128 devices in a mesh: member: 4 (over x_hi, core), cells: 32 (over y, x_lo, z).
Axes of the slice: x: 4 (x_hi: 2, x_lo: 2; x = x_hi * 2 + x_lo), y: 4, z: 4, core: 2. Of those that a mesh axis runs over, the one named last changes fastest.
Arguments:
- latent: bfloat16 [4, 8192, 1024], P('member', 'cells'), may hold values from -6 to 6
- counts: int32 [32], replicated, may hold values from 129 to 256, as said below
- w_qkv: bfloat16 [1024, 3072], replicated
- w_out: bfloat16 [1024, 1024], replicated, may hold values from -0.1875 to 0.1875
- readout_weight: bfloat16 [1024, 128], replicated, may hold values from -0.1875 to 0.1875
- target: float32 [8192, 128], P('cells'), may hold values from -6 to 6
Outputs:
- crps: float32 [8192, 128], P('cells', 'member')
- grads: float32 [1024, 4224], P(('member', 'cells'))
The draws below stay inside these ranges and needn't reach their ends.
Inputs may be any that keep to these rules, and one draw needn't show every extreme that they name: counts[b] is the number of valid slots among slots b*256 to b*256 + 255, the valid ones first; at least one block is full.
All inputs are finite; a program needn't handle non-finite values.
Results may differ from the reference program's by a relative error of at most 0.018.
Values may be sent and summed in bfloat16 or wider, within the bound.
No kernel may reach another device: no remote copies, remote signals or barrier semaphores. Data moves between devices by JAX's collectives and lax.ppermute only.
A program may use at most 128 MiB of HBM per device.

```python
import jax
import jax.numpy as jnp
from jax import lax

D = 1024
HEADS = 16
F = 128
C = 256
WIN = 256
MEMBERS = 4
BLOCKS = 32
CELLS = 8192


def draw_counts(key, part):
    key = jax.random.fold_in(key, 11)
    first_key, second_key = jax.random.split(key)
    lowered = C - jax.random.randint(first_key, (BLOCKS,), 0, C // 2)
    chosen = jax.random.randint(second_key, (), 0, BLOCKS)
    return jnp.where(jnp.arange(BLOCKS) == chosen, C, lowered).astype(jnp.int32)


def draw_w_qkv(key, part):
    key = jax.random.fold_in(key, 23)
    base = jax.random.truncated_normal(key, -4.0, 4.0, (D, 3 * D), jnp.float32) * D ** (-0.5)
    query_part = base[:, :D]
    key_part = base[:, D:2 * D]
    value_part = base[:, 2 * D:]
    return jnp.concatenate([query_part, key_part, value_part], axis=1).astype(jnp.bfloat16)


def spiked(result, key, source, target, blocks, factor):
    owner, partner = [(jnp.arange(result.shape[axis_at]) // (result.shape[axis_at] // blocks)).reshape([-1 if axis == axis_at else 1 for axis in range(result.ndim)]) for axis_at in (source, target)]
    chosen = jax.random.permutation(key, blocks)[partner]
    strong = (owner == chosen) | (owner == (partner + blocks // 2) % blocks)
    return jnp.where(strong, factor * result, result)


def levels(own_key, extent, cuts, low, largest):
    def one(position, shards_of):
        steps = jax.random.uniform(jax.random.fold_in(jax.random.fold_in(own_key, 6), position), (shards_of,), jnp.float32, low / len(cuts), largest / len(cuts))
        return jnp.repeat(jnp.exp(steps), extent[position] // shards_of).reshape((-1,) + (1,) * (len(extent) - position - 1))

    gain = one(*cuts[0])
    for cut in cuts[1:]:
        gain = gain * one(*cut)
    return gain


def normal_values(rng, extent, spread, reach, pieces=(), kind=jnp.bfloat16):
    factor_of = levels(rng, extent, pieces, -0.22, 0.18) if pieces else 1.0
    array = jax.random.normal(rng, extent, jnp.float32) * spread * factor_of
    return jnp.minimum(jnp.maximum(array, -reach), reach).astype(kind)


def heavy_noise(stream_key, shape, spread, bound, pieces, heavy, kind=jnp.bfloat16):
    array = spread * jax.random.normal(stream_key, shape, jnp.float32)
    if pieces:
        array = array * levels(stream_key, shape, pieces, -0.22, 0.18)
    return jnp.clip(spiked(array, jax.random.fold_in(stream_key, 3), *heavy), -bound, bound).astype(kind)


def setup_inputs(seed: int = 0) -> dict:
    splits = jax.random.split(jax.random.key(seed), 7)
    latent = heavy_noise(splits[0], (MEMBERS, CELLS, D), 1.0, 6.0, ((0, 4), (1, 32)), (1, 2, 32, 2.75))
    counts = draw_counts(jax.random.fold_in(splits[6], 71), 0)
    w_qkv = draw_w_qkv(jax.random.fold_in(splits[6], 71), 0)
    w_out = normal_values(splits[3], (D, D), D ** -0.5, 0.1875)
    readout_weight = normal_values(splits[4], (D, F), D ** -0.5, 0.1875)
    target = normal_values(splits[5], (CELLS, F), 1.0, 6.0, ((0, 32),), jnp.float32)
    return dict(latent=latent, counts=counts, w_qkv=w_qkv, w_out=w_out, readout_weight=readout_weight, target=target)


alpha_fair = 0.95
smooth_width = 0.0625

def smooth_abs(values):
    return jnp.sqrt(values * values + smooth_width)

def smooth_sign(values):
    return values * lax.rsqrt(values * values + smooth_width)

def layer_norm(latent_rows):
    values = latent_rows.astype(jnp.float32)
    center = values - lax.optimization_barrier(jnp.mean(values, axis=-1, keepdims=True))
    ensemble_spread = lax.optimization_barrier(jnp.mean(center * center, axis=-1, keepdims=True))
    return (center * lax.rsqrt(ensemble_spread + 1e-05)).astype(jnp.bfloat16)

def head_probs(query_heads, key_heads, allowed, scale):
    scores = jnp.einsum('qge,kge->gqk', query_heads.astype(jnp.float32), key_heads.astype(jnp.float32)) * scale
    scores = jnp.where(allowed[None], scores, -1e+30)
    row_max = lax.optimization_barrier(jnp.max(scores, axis=-1, keepdims=True))
    exponent = jnp.where(allowed[None], jnp.exp(scores - row_max), 0.0)
    return exponent / lax.optimization_barrier(jnp.sum(exponent, axis=-1, keepdims=True))

def attend_forward(query_rows, key_value, allowed, head_total):
    model_width = query_rows.shape[1]
    head_width = model_width // head_total
    scale = head_width ** (-0.5)
    outputs = []
    for group in range(head_total // 4):
        lower = group * 4 * head_width
        upper = lower + 4 * head_width
        query_heads = query_rows[:, lower:upper].reshape(-1, 4, head_width)
        key_heads = key_value[:, lower:upper].reshape(-1, 4, head_width)
        value_heads = key_value[:, model_width + lower:model_width + upper].reshape(-1, 4, head_width)
        probs = head_probs(query_heads, key_heads, allowed, scale)
        weights = lax.optimization_barrier(probs.astype(jnp.bfloat16)).astype(jnp.float32)
        mixed = jnp.einsum('gqk,kge->qge', weights, value_heads.astype(jnp.float32))
        outputs.append(mixed.reshape(-1, 4 * head_width))
    return jnp.concatenate(outputs, axis=1).astype(jnp.bfloat16)

def attend_backward(query_rows, key_value, allowed, grad_mixed, head_total):
    model_width = query_rows.shape[1]
    head_width = model_width // head_total
    scale = head_width ** (-0.5)
    query_grads, key_grads, value_grads = ([], [], [])
    for group in range(head_total // 4):
        lower = group * 4 * head_width
        upper = lower + 4 * head_width
        query_heads = query_rows[:, lower:upper].reshape(-1, 4, head_width)
        key_heads = key_value[:, lower:upper].reshape(-1, 4, head_width)
        value_heads = key_value[:, model_width + lower:model_width + upper].reshape(-1, 4, head_width)
        grad_heads = grad_mixed[:, lower:upper].reshape(-1, 4, head_width).astype(jnp.float32)
        probs = head_probs(query_heads, key_heads, allowed, scale)
        weights = lax.optimization_barrier(probs.astype(jnp.bfloat16)).astype(jnp.float32)
        dvalue = jnp.einsum('gqk,qge->kge', weights, grad_heads)
        dprob = jnp.einsum('qge,kge->gqk', grad_heads, value_heads.astype(jnp.float32))
        dscore = probs * (dprob - lax.optimization_barrier(jnp.sum(probs * dprob, axis=-1, keepdims=True))) * scale
        dscore = lax.optimization_barrier(dscore.astype(jnp.bfloat16)).astype(jnp.float32)
        dquery = jnp.einsum('gqk,kge->qge', dscore, key_heads.astype(jnp.float32))
        dkey = jnp.einsum('gqk,qge->kge', dscore, query_heads.astype(jnp.float32))
        query_grads.append(dquery.reshape(-1, 4 * head_width))
        key_grads.append(dkey.reshape(-1, 4 * head_width))
        value_grads.append(dvalue.reshape(-1, 4 * head_width))
    dquery_all = jnp.concatenate(query_grads, axis=1).astype(jnp.bfloat16)
    dkv_all = jnp.concatenate([jnp.concatenate(key_grads, axis=1), jnp.concatenate(value_grads, axis=1)], axis=1)
    return (dquery_all, dkv_all)

def unbiased_crps_score(member_prediction, target, validity_mask, variable_tally):
    member_tally = member_prediction.shape[0]
    fair_eps = (1.0 - alpha_fair) / member_tally
    spread_coefficient = (1.0 - fair_eps) / (member_tally * (member_tally - 1))
    error_term = jnp.zeros_like(target)
    ensemble_spread = jnp.zeros_like(target)
    loss_gradients = []
    for source_member in range(member_tally):
        error_term = error_term + smooth_abs(member_prediction[source_member] - target)
        attraction_term = jnp.zeros_like(target)
        for paired_member in range(member_tally):
            difference = member_prediction[source_member] - member_prediction[paired_member]
            ensemble_spread = ensemble_spread + smooth_abs(difference)
            attraction_term = attraction_term + smooth_sign(difference)
        loss_gradients.append(validity_mask / variable_tally * (smooth_sign(member_prediction[source_member] - target) / member_tally - spread_coefficient * attraction_term))
    crps = validity_mask * (error_term / member_tally - 0.5 * spread_coefficient * ensemble_spread)
    return (crps, jnp.stack(loss_gradients).astype(jnp.bfloat16))

def contract_rows(left, right):
    return lax.dot_general(left, right, (((0,), (0,)), ((), ())), preferred_element_type=jnp.float32)

def reference(latent, counts, w_qkv, w_out, readout_weight, target):
    member_tally = latent.shape[0]
    slot_total = latent.shape[1]
    model_width = w_out.shape[0]
    variable_tally = readout_weight.shape[1]
    block_total = slot_total // C
    slot_index = jnp.arange(slot_total, dtype=jnp.int32)
    owner = slot_index // C
    valid = slot_index - owner * C < counts[owner]
    valid_pad = jnp.concatenate([jnp.zeros((WIN,), dtype=bool), valid, jnp.zeros((WIN,), dtype=bool)])
    query_pos = jnp.arange(C, dtype=jnp.int32)[:, None]
    key_offset = jnp.arange(C + 2 * WIN, dtype=jnp.int32)[None, :] - WIN
    band = jnp.abs(query_pos - key_offset) <= WIN
    validity_mask = valid.astype(jnp.float32)[:, None]
    saved = []
    member_predictions = []
    for member_slot in range(member_tally):
        normed = layer_norm(latent[member_slot])
        projected = jnp.dot(normed, w_qkv, preferred_element_type=jnp.float32).astype(jnp.bfloat16)
        queries = projected[:, :model_width]
        key_value = jnp.pad(projected[:, model_width:], ((WIN, WIN), (0, 0)))

        def forward_block(carry, block):
            start = (block * C).astype(jnp.int32)
            query_block = lax.dynamic_slice_in_dim(queries, start, C, 0)
            kv_block = lax.dynamic_slice_in_dim(key_value, start, C + 2 * WIN, 0)
            allowed = band & lax.dynamic_slice_in_dim(valid_pad, start, C + 2 * WIN, 0)[None, :]
            return (carry, attend_forward(query_block, kv_block, allowed, HEADS))
        unused, attended = lax.scan(forward_block, jnp.zeros((), jnp.float32), jnp.arange(block_total, dtype=jnp.int32))
        attended = attended.reshape(slot_total, model_width)
        mixed = jnp.dot(attended, w_out, preferred_element_type=jnp.float32)
        hidden_state = (latent[member_slot].astype(jnp.float32) + mixed).astype(jnp.bfloat16)
        member_predictions.append(jnp.dot(hidden_state, readout_weight, preferred_element_type=jnp.float32))
        saved.append((normed, queries, key_value, attended, hidden_state))
    crps, loss_gradient = unbiased_crps_score(jnp.stack(member_predictions), target, validity_mask, variable_tally)
    grad_qkv = jnp.zeros((model_width, 3 * model_width), jnp.float32)
    grad_out = jnp.zeros((model_width, model_width), jnp.float32)
    grad_read = jnp.zeros((model_width, variable_tally), jnp.float32)
    for member_slot in range(member_tally):
        normed, queries, key_value, attended, hidden_state = saved[member_slot]
        dhidden = jnp.dot(loss_gradient[member_slot], readout_weight.T, preferred_element_type=jnp.float32).astype(jnp.bfloat16)
        dattended = jnp.dot(dhidden, w_out.T, preferred_element_type=jnp.float32).astype(jnp.bfloat16)

        def backward_block(total_kv, block):
            start = (block * C).astype(jnp.int32)
            query_block = lax.dynamic_slice_in_dim(queries, start, C, 0)
            kv_block = lax.dynamic_slice_in_dim(key_value, start, C + 2 * WIN, 0)
            allowed = band & lax.dynamic_slice_in_dim(valid_pad, start, C + 2 * WIN, 0)[None, :]
            grad_block = lax.dynamic_slice_in_dim(dattended, start, C, 0)
            dquery, dkv = attend_backward(query_block, kv_block, allowed, grad_block, HEADS)
            current = lax.dynamic_slice_in_dim(total_kv, start, C + 2 * WIN, 0)
            total_kv = lax.dynamic_update_slice_in_dim(total_kv, current + dkv, start, 0)
            return (total_kv, dquery)
        empty_kv = jnp.zeros((slot_total + 2 * WIN, 2 * model_width), jnp.float32)
        total_kv, dquery = lax.scan(backward_block, empty_kv, jnp.arange(block_total, dtype=jnp.int32))
        dkv = total_kv[WIN:WIN + slot_total].astype(jnp.bfloat16)
        dprojected = jnp.concatenate([dquery.reshape(slot_total, model_width), dkv], axis=1)
        grad_qkv = grad_qkv + contract_rows(normed, dprojected)
        grad_out = grad_out + contract_rows(attended, dhidden)
        grad_read = grad_read + contract_rows(hidden_state, loss_gradient[member_slot])
    return (crps, jnp.concatenate([grad_qkv, grad_out, grad_read], axis=1))
```

```python
import functools

import jax
import jax.numpy as jnp
import numpy as np
from jax import lax
from jax.experimental import pallas as pl
from jax.experimental.pallas import tpu as pltpu
from jax.sharding import PartitionSpec as P

HEADS = 16
WIN = 256
BLOCK = 256
WIDTH = 256
HEAD_WIDTH = 64
PAIR = 128
NEVER = -1e30
VMEM_BYTES = 56 * 1024 * 1024

alpha_fair = 0.95
smooth_width = 0.0625

BF = jnp.bfloat16
F32 = jnp.float32


def smooth_abs(values):
    return jnp.sqrt(values * values + smooth_width)


def smooth_sign(values):
    return values * lax.rsqrt(values * values + smooth_width)


def layer_norm(latent_rows):
    values = latent_rows.astype(F32)
    center = values - jnp.mean(values, axis=-1, keepdims=True)
    spread = jnp.mean(center * center, axis=-1, keepdims=True)
    return (center * lax.rsqrt(spread + 1e-05)).astype(BF)


def dot_nn(left, right):
    return lax.dot_general(left, right, (((1,), (0,)), ((), ())), preferred_element_type=F32)


def dot_nt(left, right):
    return lax.dot_general(left, right, (((1,), (1,)), ((), ())), preferred_element_type=F32)


def dot_tn(left, right):
    return lax.dot_general(left, right, (((0,), (0,)), ((), ())), preferred_element_type=F32)


def iota(shape, axis):
    return lax.broadcasted_iota(jnp.int32, shape, axis)


def head_part(pair_rows, half, gain=None):
    chosen = (iota(pair_rows.shape, 1) // HEAD_WIDTH) == half
    if gain is not None:
        pair_rows = pair_rows * jnp.asarray(gain, pair_rows.dtype)
    return jnp.where(chosen, pair_rows, jnp.zeros_like(pair_rows))


def project_kernel(latent_ref, weight_ref, source_ref, projected_ref, ordered_ref, normed):
    step = pl.program_id(0)

    @pl.when(step == 0)
    def _():
        normed[...] = layer_norm(latent_ref[...])

    @pl.when(step < 6)
    def _():
        projected_ref[...] = dot_nn(normed[...], weight_ref[...]).astype(BF)

    @pl.when(step >= 6)
    def _():
        order = (iota((1024, 512), 0) == source_ref[...]).astype(BF)
        ordered_ref[...] = dot_nn(normed[...], order).astype(BF)


def project(latent_own, w_qkv, source):
    rows, width = latent_own.shape
    return pl.pallas_call(
        project_kernel,
        grid=(8,),
        in_specs=[
            pl.BlockSpec((rows, width), lambda j: (0, 0)),
            pl.BlockSpec((width, 512), lambda j: (0, jnp.minimum(j, 5))),
            pl.BlockSpec((1, 512), lambda j: (0, jnp.maximum(j - 6, 0))),
        ],
        out_specs=[
            pl.BlockSpec((rows, 512), lambda j: (0, jnp.minimum(j, 5))),
            pl.BlockSpec((rows, 512), lambda j: (0, jnp.maximum(j - 6, 0))),
        ],
        out_shape=[
            jax.ShapeDtypeStruct((rows, 3 * width), BF),
            jax.ShapeDtypeStruct((rows, width), BF),
        ],
        scratch_shapes=[pltpu.VMEM((rows, width), BF)],
        compiler_params=pltpu.CompilerParams(vmem_limit_bytes=VMEM_BYTES),
        cost_estimate=pl.CostEstimate(
            flops=2 * rows * width * width * 4, bytes_accessed=8 << 20, transcendentals=0
        ),
    )(latent_own, w_qkv, source)


def forward_bias(counts_ref):
    query = iota((BLOCK, WIN), 0)
    key = iota((BLOCK, WIN), 1)
    left = jnp.where((key >= query) & (key < counts_ref[0]), 0.0, NEVER).astype(F32)
    own = jnp.where(iota((1, BLOCK), 1) < counts_ref[1], 0.0, NEVER).astype(F32)
    right = jnp.where((key <= query) & (key < counts_ref[2]), 0.0, NEVER).astype(F32)
    return left, own, right


def forward_kernel(
    counts_ref,
    left_ref,
    right_ref,
    latent_ref,
    wk_ref,
    wv_ref,
    q_ref,
    k_ref,
    v_ref,
    w_out_ref,
    readout_ref,
    normed_ref,
    khalo_ref,
    vhalo_ref,
    attended_ref,
    stats_ref,
    hidden_ref,
    forecast_ref,
):
    step = pl.program_id(0)

    @pl.when(step == 0)
    def _():
        normed_ref[:WIN] = layer_norm(left_ref[...])
        normed_ref[WIN:] = layer_norm(right_ref[...])
        stats_ref[...] = jnp.zeros_like(stats_ref)

    khalo_ref[...] = dot_nn(normed_ref[...], wk_ref[...]).astype(BF)
    vhalo_ref[...] = dot_nn(normed_ref[...], wv_ref[...]).astype(BF)
    bias_left, bias_own, bias_right = forward_bias(counts_ref)
    lane = iota((BLOCK, 128), 1)
    stats = stats_ref[...]
    for pair in range(2):
        columns = slice(pair * PAIR, (pair + 1) * PAIR)
        q_pair = q_ref[:, columns]
        halves = []
        for half in range(2):
            q_head = head_part(q_pair, half, HEAD_WIDTH ** (-0.5))
            s_left = dot_nt(q_head, khalo_ref[:WIN, columns]) + bias_left
            s_own = dot_nt(q_head, k_ref[:, columns]) + bias_own
            s_right = dot_nt(q_head, khalo_ref[WIN:, columns]) + bias_right
            top = jnp.max(
                jnp.maximum(jnp.maximum(s_left, s_own), s_right), axis=-1, keepdims=True
            )
            e_left = jnp.exp(s_left - top)
            e_own = jnp.exp(s_own - top)
            e_right = jnp.exp(s_right - top)
            total = jnp.sum(e_left + e_own + e_right, axis=-1, keepdims=True)
            mixed = dot_nn(e_left.astype(BF), vhalo_ref[:WIN, columns])
            mixed += dot_nn(e_own.astype(BF), v_ref[:, columns])
            mixed += dot_nn(e_right.astype(BF), vhalo_ref[WIN:, columns])
            halves.append(mixed / total)
            head = step * 4 + pair * 2 + half
            stats = jnp.where(lane == head, top + jnp.log(total), stats)
        both = jnp.where(lane < HEAD_WIDTH, halves[0], halves[1])
        start = pl.multiple_of(step * WIDTH + pair * PAIR, PAIR)
        attended_ref[:, pl.ds(start, PAIR)] = both
    stats_ref[...] = stats

    @pl.when(step == 3)
    def _():
        mixed = dot_nn(attended_ref[...].astype(BF), w_out_ref[...])
        hidden = (latent_ref[...].astype(F32) + mixed).astype(BF)
        hidden_ref[...] = hidden
        forecast_ref[...] = dot_nn(hidden, readout_ref[...])


def forward(counts, left, right, latent_own, w_qkv, projected, w_out, readout_weight):
    whole = lambda *shape: pl.BlockSpec(shape, lambda j: (0, 0))
    part = lambda rows, first: pl.BlockSpec((rows, WIDTH), lambda j: (0, first + j))
    return pl.pallas_call(
        forward_kernel,
        grid=(4,),
        in_specs=[
            pl.BlockSpec(memory_space=pltpu.SMEM),
            whole(WIN, 1024),
            whole(WIN, 1024),
            whole(BLOCK, 1024),
            part(1024, 4),
            part(1024, 8),
            part(BLOCK, 0),
            part(BLOCK, 4),
            part(BLOCK, 8),
            whole(1024, 1024),
            whole(1024, 128),
        ],
        out_specs=[
            whole(2 * WIN, 1024),
            part(2 * WIN, 0),
            part(2 * WIN, 0),
            whole(BLOCK, 1024),
            whole(BLOCK, 128),
            whole(BLOCK, 1024),
            whole(BLOCK, 128),
        ],
        out_shape=[
            jax.ShapeDtypeStruct((2 * WIN, 1024), BF),
            jax.ShapeDtypeStruct((2 * WIN, 1024), BF),
            jax.ShapeDtypeStruct((2 * WIN, 1024), BF),
            jax.ShapeDtypeStruct((BLOCK, 1024), F32),
            jax.ShapeDtypeStruct((BLOCK, 128), F32),
            jax.ShapeDtypeStruct((BLOCK, 1024), BF),
            jax.ShapeDtypeStruct((BLOCK, 128), F32),
        ],
        compiler_params=pltpu.CompilerParams(vmem_limit_bytes=VMEM_BYTES),
        cost_estimate=pl.CostEstimate(
            flops=6 << 30, bytes_accessed=12 << 20, transcendentals=3 << 20
        ),
    )(
        counts,
        left,
        right,
        latent_own,
        w_qkv,
        w_qkv,
        projected,
        projected,
        projected,
        w_out,
        readout_weight,
    )


def score_kernel(
    counts_ref,
    forecasts_ref,
    target_ref,
    attended_ref,
    hidden_ref,
    stats_ref,
    w_out_ref,
    readout_ref,
    crps_ref,
    slope_ref,
    grad_ref,
    stats_out_ref,
    turned_ref,
    small_ref,
):
    members = 4
    fair_eps = (1.0 - alpha_fair) / members
    coefficient = (1.0 - fair_eps) / (members * (members - 1))
    valid = (iota((BLOCK, 1), 0) < counts_ref[1]).astype(F32)
    forecasts = [forecasts_ref[member] for member in range(members)]
    own = forecasts_ref[counts_ref[3]]
    target = target_ref[...]
    error = jnp.zeros_like(target)
    for forecast in forecasts:
        error += smooth_abs(forecast - target)
    spread = jnp.full_like(target, members * smooth_width**0.5)
    for first in range(members):
        for second in range(first + 1, members):
            spread += 2.0 * smooth_abs(forecasts[first] - forecasts[second])
    crps_ref[...] = valid * (error / members - 0.5 * coefficient * spread)
    pull = jnp.zeros_like(target)
    for other in forecasts:
        pull += smooth_sign(own - other)
    slope = (
        valid / 128 * (smooth_sign(own - target) / members - coefficient * pull)
    ).astype(BF)
    slope_ref[...] = slope
    dhidden = dot_nt(slope, readout_ref[...]).astype(BF)
    dattended = dot_nt(dhidden, w_out_ref[...]).astype(BF)
    grad_ref[...] = dattended
    attended = attended_ref[...]
    product = dattended.astype(F32) * attended
    high = product.astype(BF)
    low = (product - high.astype(F32)).astype(BF)
    pick = (iota((1024, 128), 0) // HEAD_WIDTH + HEADS == iota((1024, 128), 1)).astype(BF)
    stats = stats_ref[...] + dot_nn(high, pick) + dot_nn(low, pick)
    stats_out_ref[...] = stats
    turned_ref[...] = stats.T[: 2 * HEADS]
    small_ref[:, :128] = dot_tn(attended.astype(BF), slope).astype(BF)
    small_ref[:, 128:] = dot_tn(hidden_ref[...], slope).astype(BF)


def score(counts, forecasts, target, attended, hidden, stats, w_out, readout_weight):
    vmem = pl.BlockSpec(memory_space=pltpu.VMEM)
    return pl.pallas_call(
        score_kernel,
        in_specs=[pl.BlockSpec(memory_space=pltpu.SMEM)] + [vmem] * 7,
        out_specs=[vmem] * 6,
        out_shape=[
            jax.ShapeDtypeStruct((BLOCK, 128), F32),
            jax.ShapeDtypeStruct((BLOCK, 128), BF),
            jax.ShapeDtypeStruct((BLOCK, 1024), BF),
            jax.ShapeDtypeStruct((BLOCK, 128), F32),
            jax.ShapeDtypeStruct((2 * HEADS, BLOCK), F32),
            jax.ShapeDtypeStruct((1024, 256), BF),
        ],
        compiler_params=pltpu.CompilerParams(vmem_limit_bytes=VMEM_BYTES),
    )(counts, forecasts, target, attended, hidden, stats, w_out, readout_weight)


def query_kernel(
    counts_ref, q_ref, k_ref, v_ref, khalo_ref, vhalo_ref, grad_ref, stats_ref, dq_ref
):
    step = pl.program_id(0)
    bias_left, bias_own, bias_right = forward_bias(counts_ref)
    lane = iota((BLOCK, 128), 1)
    stats = stats_ref[...]
    for pair in range(2):
        columns = slice(pair * PAIR, (pair + 1) * PAIR)
        q_pair = q_ref[:, columns]
        g_pair = grad_ref[:, columns]
        blocks = [
            (khalo_ref[:WIN, columns], vhalo_ref[:WIN, columns], bias_left),
            (k_ref[:, columns], v_ref[:, columns], bias_own),
            (khalo_ref[WIN:, columns], vhalo_ref[WIN:, columns], bias_right),
        ]
        halves = []
        for half in range(2):
            head = step * 4 + pair * 2 + half
            q_head = head_part(q_pair, half, HEAD_WIDTH ** (-0.5))
            g_head = head_part(g_pair, half)
            level = jnp.sum(jnp.where(lane == head, stats, 0.0), axis=-1, keepdims=True)
            delta = jnp.sum(jnp.where(lane == head + HEADS, stats, 0.0), axis=-1, keepdims=True)
            total = jnp.zeros((BLOCK, PAIR), F32)
            for keys, values, bias in blocks:
                probs = jnp.exp(dot_nt(q_head, keys) + bias - level)
                dscore = (probs * (dot_nt(g_head, values) - delta)).astype(BF)
                total += dot_nn(dscore, keys)
            halves.append(total)
        both = jnp.where(lane < HEAD_WIDTH, halves[0], halves[1])
        dq_ref[:, columns] = (both * HEAD_WIDTH ** (-0.5)).astype(BF)


def query_grads(counts, projected, khalo, vhalo, grad, stats):
    part = lambda rows, first: pl.BlockSpec((rows, WIDTH), lambda j: (0, first + j))
    return pl.pallas_call(
        query_kernel,
        grid=(4,),
        in_specs=[
            pl.BlockSpec(memory_space=pltpu.SMEM),
            part(BLOCK, 0),
            part(BLOCK, 4),
            part(BLOCK, 8),
            part(2 * WIN, 0),
            part(2 * WIN, 0),
            part(BLOCK, 0),
            pl.BlockSpec((BLOCK, 128), lambda j: (0, 0)),
        ],
        out_specs=part(BLOCK, 0),
        out_shape=jax.ShapeDtypeStruct((BLOCK, 1024), BF),
        compiler_params=pltpu.CompilerParams(vmem_limit_bytes=VMEM_BYTES),
        cost_estimate=pl.CostEstimate(
            flops=6 << 30, bytes_accessed=5 << 20, transcendentals=3 << 20
        ),
    )(counts, projected, projected, projected, khalo, vhalo, grad, stats)


def key_kernel(
    first_step,
    counts_ref,
    q_ref,
    k_ref,
    v_ref,
    qhalo_ref,
    grad_ref,
    ghalo_ref,
    left_ref,
    own_ref,
    right_ref,
    dk_ref,
    dv_ref,
):
    step = pl.program_id(0) + first_step
    key = iota((BLOCK, WIN), 0)
    query = iota((BLOCK, WIN), 1)
    present = key < counts_ref[1]
    bias_left = jnp.where(present & (query >= key), 0.0, NEVER).astype(F32)
    bias_own = jnp.where(present, 0.0, NEVER).astype(F32)
    bias_right = jnp.where(present & (query <= key), 0.0, NEVER).astype(F32)
    for pair in range(2):
        columns = slice(pair * PAIR, (pair + 1) * PAIR)
        keys = k_ref[:, columns]
        values = v_ref[:, columns]
        blocks = [
            (qhalo_ref[:WIN, columns], ghalo_ref[:WIN, columns], left_ref, bias_left),
            (q_ref[:, columns], grad_ref[:, columns], own_ref, bias_own),
            (qhalo_ref[WIN:, columns], ghalo_ref[WIN:, columns], right_ref, bias_right),
        ]
        dk = jnp.zeros((BLOCK, PAIR), F32)
        dv = jnp.zeros((BLOCK, PAIR), F32)
        for half in range(2):
            head = step * 4 + pair * 2 + half
            for queries, grads, turned_ref, bias in blocks:
                q_head = head_part(queries, half, HEAD_WIDTH ** (-0.5))
                g_head = head_part(grads, half)
                level = turned_ref[pl.ds(head, 1), :]
                delta = turned_ref[pl.ds(head + HEADS, 1), :]
                probs = jnp.exp(dot_nt(keys, q_head) + bias - level)
                dscore = (probs * (dot_nt(values, g_head) - delta)).astype(BF)
                dv += dot_nn(probs.astype(BF), g_head)
                dk += dot_nn(dscore, q_head)
        dk_ref[:, columns] = dk.astype(BF)
        dv_ref[:, columns] = dv.astype(BF)


def key_grads(counts, projected, qhalo, grad, ghalo, turned, first_step, steps):
    part = lambda rows, first: pl.BlockSpec(
        (rows, WIDTH), lambda j: (0, first + first_step + j)
    )
    whole = pl.BlockSpec((2 * HEADS, BLOCK), lambda j: (0, 0))
    out = pl.BlockSpec((BLOCK, WIDTH), lambda j: (0, j))
    return pl.pallas_call(
        functools.partial(key_kernel, first_step),
        grid=(steps,),
        in_specs=[
            pl.BlockSpec(memory_space=pltpu.SMEM),
            part(BLOCK, 0),
            part(BLOCK, 4),
            part(BLOCK, 8),
            part(2 * WIN, 0),
            part(BLOCK, 0),
            part(2 * WIN, 0),
            whole,
            whole,
            whole,
        ],
        out_specs=[out, out],
        out_shape=[jax.ShapeDtypeStruct((BLOCK, WIDTH * steps), BF)] * 2,
        compiler_params=pltpu.CompilerParams(vmem_limit_bytes=VMEM_BYTES),
        cost_estimate=pl.CostEstimate(
            flops=(2 << 30) * steps, bytes_accessed=5 << 20, transcendentals=3 << 20
        ),
    )(counts, projected, projected, projected, qhalo, grad, ghalo, *turned)


AXES = ("x_hi", "core", "y", "x_lo", "z")
MEMBER = ("x_hi", "core")
CELLS = ("y", "x_lo", "z")
CHIPS = ("x_hi", "y", "x_lo", "z")


def row_source(core):
    place = jnp.arange(1024, dtype=jnp.int32)
    other, chip, row = place // 512, (place % 512) // 8, place % 8
    x_hi, block = chip // 32, chip % 32
    return (x_hi * 512 + (other ^ core) * 256 + block * 8 + row)[None]


def swap_core(values):
    return lax.ppermute(values, "core", [(0, 1), (1, 0)])


def scatter_sum(partial):
    columns = partial.shape[1]
    pieces = lax.all_to_all(
        partial.reshape(64, 8, columns), CHIPS, split_axis=0, concat_axis=0
    )
    return jnp.sum(pieces.astype(F32), axis=0)


def per_device(latent, counts, w_qkv, w_out, readout_weight, target):
    latent_own = latent[0]
    cell_count = 32
    cell_index = lax.axis_index(CELLS)
    member_index = lax.axis_index(MEMBER)
    core = lax.axis_index("core")
    up = [(i, i + 1) for i in range(cell_count - 1)]
    down = [(i + 1, i) for i in range(cell_count - 1)]
    from_left = lax.ppermute(latent_own, CELLS, up)
    from_right = lax.ppermute(latent_own, CELLS, down)

    own_count = counts[cell_index]
    left_count = jnp.where(cell_index > 0, counts[jnp.maximum(cell_index - 1, 0)], 0)
    right_count = jnp.where(
        cell_index < cell_count - 1, counts[jnp.minimum(cell_index + 1, cell_count - 1)], 0
    )
    scalars = jnp.stack([left_count, own_count, right_count, member_index.astype(jnp.int32)])

    source = row_source(core)
    projected, ordered = project(latent_own, w_qkv, source)
    normed_pair = jnp.concatenate([ordered[:, :512], swap_core(ordered[:, 512:])], axis=0)
    normed_halo, khalo, vhalo, attended, stats, hidden, forecast = forward(
        scalars, from_left, from_right, latent_own, w_qkv, projected, w_out, readout_weight
    )
    forecasts = lax.all_gather(forecast, MEMBER, axis=0, tiled=False)
    qhalo = dot_nn(normed_halo, w_qkv[:, :1024]).astype(BF)
    crps_whole, slope, grad, stats, turned, small = score(
        scalars, forecasts, target, attended, hidden, stats, w_out, readout_weight
    )
    crps = lax.dynamic_slice_in_dim(crps_whole, member_index * 32, 32, 1)
    packed = jnp.concatenate([slope.astype(F32), turned.reshape(64, 128)], axis=0)
    packed_left = lax.ppermute(packed, CELLS, up)
    packed_right = lax.ppermute(packed, CELLS, down)

    dquery = query_grads(scalars, projected, khalo, vhalo, grad, stats)

    slope_halo = jnp.concatenate([packed_left[:BLOCK], packed_right[:BLOCK]], axis=0).astype(BF)
    dhidden_halo = dot_nt(slope_halo, readout_weight).astype(BF)
    ghalo = dot_nt(dhidden_halo, w_out).astype(BF)
    turned_left = packed_left[BLOCK:].reshape(2 * HEADS, BLOCK)
    turned_right = packed_right[BLOCK:].reshape(2 * HEADS, BLOCK)

    def partial_of(piece):
        paired = jnp.concatenate([piece, swap_core(piece)], axis=0)
        return dot_tn(normed_pair, paired).astype(BF)

    small = dot_tn((jnp.arange(1024)[:, None] == source).astype(BF), small).astype(BF)
    small = (small[:512].astype(F32) + swap_core(small[512:]).astype(F32)).astype(BF)
    first = scatter_sum(jnp.concatenate([partial_of(dquery), small], axis=1))
    dkey, dvalue = key_grads(
        scalars, projected, qhalo, grad, ghalo, (turned_left, turned, turned_right), 0, 4
    )
    second = scatter_sum(partial_of(jnp.concatenate([dkey, dvalue], axis=1)))
    grad_out = lax.dot_general(
        first[:, 1024:1152],
        readout_weight.astype(F32),
        (((1,), (1,)), ((), ())),
        precision=lax.Precision.HIGHEST,
        preferred_element_type=F32,
    )
    grads = jnp.concatenate([first[:, :1024], second, grad_out, first[:, 1152:]], axis=1)
    return (crps, grads)


def solution(mesh):
    fine = jax.sharding.Mesh(mesh.devices.reshape(2, 2, 4, 2, 4), AXES)
    placed = (P(MEMBER, CELLS, None), P(), P(), P(), P(), P(CELLS, None))
    return jax.shard_map(
        per_device,
        mesh=fine,
        in_specs=placed,
        out_specs=(P(CELLS, MEMBER), P(MEMBER + CELLS, None)),
        check_vma=False,
    )
```

```python
import functools

import jax
import jax.numpy as jnp
import numpy as np
from jax import lax
from jax.experimental import pallas as pl
from jax.experimental.pallas import tpu as pltpu
from jax.sharding import PartitionSpec as P

HEADS = 16
WIN = 256
BLOCK = 256
WIDTH = 256
HEAD_WIDTH = 64
PAIR = 128
NEVER = -1e30
VMEM_BYTES = 56 * 1024 * 1024

alpha_fair = 0.95
smooth_width = 0.0625

BF = jnp.bfloat16
F32 = jnp.float32


def smooth_abs(values):
    return jnp.sqrt(values * values + smooth_width)


def smooth_sign(values):
    return values * lax.rsqrt(values * values + smooth_width)


def layer_norm(latent_rows):
    values = latent_rows.astype(F32)
    center = values - jnp.mean(values, axis=-1, keepdims=True)
    spread = jnp.mean(center * center, axis=-1, keepdims=True)
    return (center * lax.rsqrt(spread + 1e-05)).astype(BF)


def dot_nn(left, right):
    return lax.dot_general(left, right, (((1,), (0,)), ((), ())), preferred_element_type=F32)


def dot_nt(left, right):
    return lax.dot_general(left, right, (((1,), (1,)), ((), ())), preferred_element_type=F32)


def dot_tn(left, right):
    return lax.dot_general(left, right, (((0,), (0,)), ((), ())), preferred_element_type=F32)


def iota(shape, axis):
    return lax.broadcasted_iota(jnp.int32, shape, axis)


def project_kernel(latent_ref, weight_ref, projected_ref, turned_ref, normed):
    step = pl.program_id(0)

    @pl.when(step == 0)
    def _():
        normed[...] = layer_norm(latent_ref[...])

    projected_ref[...] = dot_nn(normed[...], weight_ref[...]).astype(BF)

    @pl.when(step == 5)
    def _():
        turned_ref[...] = normed[...].T


def project(latent_own, w_qkv):
    rows, width = latent_own.shape
    return pl.pallas_call(
        project_kernel,
        grid=(6,),
        in_specs=[
            pl.BlockSpec((rows, width), lambda j: (0, 0)),
            pl.BlockSpec((width, 512), lambda j: (0, j)),
        ],
        out_specs=[
            pl.BlockSpec((rows, 512), lambda j: (0, j)),
            pl.BlockSpec((width, rows), lambda j: (0, 0)),
        ],
        out_shape=[
            jax.ShapeDtypeStruct((rows, 3 * width), BF),
            jax.ShapeDtypeStruct((width, rows), BF),
        ],
        scratch_shapes=[pltpu.VMEM((rows, width), BF)],
        compiler_params=pltpu.CompilerParams(vmem_limit_bytes=VMEM_BYTES),
        cost_estimate=pl.CostEstimate(
            flops=2 * rows * width * width * 4, bytes_accessed=8 << 20, transcendentals=0
        ),
    )(latent_own, w_qkv)


def spare_lane(shape):
    lane = iota(shape, len(shape) - 1)
    return lane % HEAD_WIDTH


def key_fill(count_pieces):
    fills = []
    for count, rows in count_pieces:
        spare = spare_lane((rows, PAIR))
        bias = jnp.where(iota((rows, PAIR), 0) < count, 0.0, NEVER)
        fills.append(
            jnp.where(spare < 3, 1.0, jnp.where(spare == 3, bias, 0.0)).astype(BF)
        )
    return jnp.concatenate(fills, axis=0)


def stat_spread(step, offset):
    shape = (128, WIDTH)
    lane = iota(shape, 1)
    head = step * 4 + 2 * (lane // PAIR) + jnp.where(lane % PAIR < HEAD_WIDTH, 1, 0)
    term = lane % HEAD_WIDTH
    chosen = (term < 3) & (iota(shape, 0) == term * 32 + offset + head)
    return jnp.where(chosen, -1.0, 0.0).astype(BF)


def keep_band(window, fill):
    shape = (128, 128)
    apart = iota(shape, 0) - iota(shape, 1)
    first = jnp.where(apart >= 0, window[:128], fill)
    last = jnp.where(apart <= 0, window[512:], fill)
    return first, window[128:512], last


def forward_kernel(
    counts_ref,
    left_ref,
    right_ref,
    latent_ref,
    wk_ref,
    wv_ref,
    q_ref,
    k_ref,
    v_ref,
    w_out_ref,
    readout_ref,
    normed_ref,
    kcat_ref,
    vcat_ref,
    attended_ref,
    stats_ref,
    hidden_ref,
    forecast_ref,
    probs,
    stat_rows,
):
    step = pl.program_id(0)

    @pl.when(step == 0)
    def _():
        normed_ref[:WIN] = layer_norm(left_ref[...])
        normed_ref[WIN:] = layer_norm(right_ref[...])
        probs[...] = jnp.zeros_like(probs)

    khalo = dot_nn(normed_ref[...], wk_ref[...]).astype(BF)
    kcat_ref[:WIN] = khalo[:WIN]
    kcat_ref[WIN : WIN + BLOCK] = k_ref[...]
    kcat_ref[WIN + BLOCK :] = khalo[WIN:]
    vhalo = dot_nn(normed_ref[...], wv_ref[...]).astype(BF)
    vcat_ref[:WIN] = vhalo[:WIN]
    vcat_ref[WIN : WIN + BLOCK] = v_ref[...]
    vcat_ref[WIN + BLOCK :] = vhalo[WIN:]
    fill = key_fill([(counts_ref[0], WIN), (counts_ref[1], BLOCK), (counts_ref[2], WIN)])
    low_q = iota((BLOCK, PAIR), 1) < HEAD_WIDTH
    low_k = iota(fill.shape, 1) < HEAD_WIDTH
    query_fill = (spare_lane((BLOCK, PAIR)) == 3).astype(BF)
    for pair in range(2):
        columns = slice(pair * PAIR, (pair + 1) * PAIR)
        q_pair = q_ref[:, columns] * jnp.asarray(HEAD_WIDTH ** (-0.5), BF)
        k_pair = kcat_ref[:, columns]
        v_turned = vcat_ref[:, columns].T
        halves = []
        for half in range(2):
            slot = pair * 2 + half
            if half == 0:
                q_head = jnp.where(low_q, q_pair, query_fill)
                k_head = jnp.where(low_k, k_pair, fill)
            else:
                q_head = jnp.where(low_q, query_fill, q_pair)
                k_head = jnp.where(low_k, fill, k_pair)
            scores = dot_nt(k_head, q_head)
            totals, levels = [], []
            for tile in range(2):
                rows = slice(tile * 128, tile * 128 + 640)
                lanes = slice(tile * 128, tile * 128 + 128)
                first, middle, last = keep_band(scores[rows, lanes], NEVER)
                top = jnp.maximum(
                    jnp.max(middle, axis=0, keepdims=True),
                    jnp.max(jnp.maximum(first, last), axis=0, keepdims=True),
                )
                first = jnp.exp(first - top)
                middle = jnp.exp(middle - top)
                last = jnp.exp(last - top)
                total = jnp.sum(middle, axis=0, keepdims=True) + jnp.sum(
                    first + last, axis=0, keepdims=True
                )
                start = tile * 128
                probs[slot, start : start + 128, lanes] = first.astype(BF)
                probs[slot, start + 128 : start + 512, lanes] = middle.astype(BF)
                probs[slot, start + 512 : start + 640, lanes] = last.astype(BF)
                totals.append(total)
                levels.append(top + jnp.log(total))
            total = jnp.concatenate(totals, axis=1)
            mixed = dot_nn(
                v_turned[half * HEAD_WIDTH : (half + 1) * HEAD_WIDTH], probs[slot]
            )
            halves.append(mixed * (1.0 / total))
            stat_rows[pl.ds(step * 4 + slot, 1), :] = jnp.concatenate(levels, axis=1)
        both = jnp.concatenate(halves, axis=0).T
        start = pl.multiple_of(step * WIDTH + pair * PAIR, PAIR)
        attended_ref[:, pl.ds(start, PAIR)] = both

    @pl.when(step == 3)
    def _():
        mixed = dot_nn(attended_ref[...].astype(BF), w_out_ref[...])
        hidden = (latent_ref[...].astype(F32) + mixed).astype(BF)
        hidden_ref[...] = hidden
        forecast_ref[...] = dot_nn(hidden, readout_ref[...])
        stat_rows[HEADS:] = jnp.zeros((128 - HEADS, BLOCK), F32)
        stats_ref[...] = stat_rows[...].T


def forward(counts, left, right, latent_own, w_qkv, projected, w_out, readout_weight):
    whole = lambda *shape: pl.BlockSpec(shape, lambda j: (0, 0))
    part = lambda rows, first: pl.BlockSpec((rows, WIDTH), lambda j: (0, first + j))
    window = 2 * WIN + BLOCK
    return pl.pallas_call(
        forward_kernel,
        grid=(4,),
        in_specs=[
            pl.BlockSpec(memory_space=pltpu.SMEM),
            whole(WIN, 1024),
            whole(WIN, 1024),
            whole(BLOCK, 1024),
            part(1024, 4),
            part(1024, 8),
            part(BLOCK, 0),
            part(BLOCK, 4),
            part(BLOCK, 8),
            whole(1024, 1024),
            whole(1024, 128),
        ],
        out_specs=[
            whole(2 * WIN, 1024),
            part(window, 0),
            part(window, 0),
            whole(BLOCK, 1024),
            whole(BLOCK, 128),
            whole(BLOCK, 1024),
            whole(BLOCK, 128),
        ],
        out_shape=[
            jax.ShapeDtypeStruct((2 * WIN, 1024), BF),
            jax.ShapeDtypeStruct((window, 1024), BF),
            jax.ShapeDtypeStruct((window, 1024), BF),
            jax.ShapeDtypeStruct((BLOCK, 1024), F32),
            jax.ShapeDtypeStruct((BLOCK, 128), F32),
            jax.ShapeDtypeStruct((BLOCK, 1024), BF),
            jax.ShapeDtypeStruct((BLOCK, 128), F32),
        ],
        scratch_shapes=[pltpu.VMEM((4, window, BLOCK), BF), pltpu.VMEM((128, BLOCK), F32)],
        compiler_params=pltpu.CompilerParams(vmem_limit_bytes=VMEM_BYTES),
        cost_estimate=pl.CostEstimate(
            flops=6 << 30, bytes_accessed=12 << 20, transcendentals=3 << 20
        ),
    )(
        counts,
        left,
        right,
        latent_own,
        w_qkv,
        w_qkv,
        projected,
        projected,
        projected,
        w_out,
        readout_weight,
    )


def score_kernel(
    counts_ref,
    own_ref,
    near_ref,
    others_ref,
    target_ref,
    attended_ref,
    hidden_ref,
    stats_ref,
    w_out_ref,
    readout_ref,
    crps_ref,
    packed_ref,
    grad_ref,
    small_ref,
):
    members = 4
    fair_eps = (1.0 - alpha_fair) / members
    coefficient = (1.0 - fair_eps) / (members * (members - 1))
    valid = (iota((BLOCK, 1), 0) < counts_ref[1]).astype(F32)
    own = own_ref[...]
    forecasts = [own, near_ref[...], others_ref[0], others_ref[1]]
    target = target_ref[...]
    error = jnp.zeros_like(target)
    for forecast in forecasts:
        error += smooth_abs(forecast - target)
    spread = jnp.full_like(target, members * smooth_width**0.5)
    for first in range(members):
        for second in range(first + 1, members):
            spread += 2.0 * smooth_abs(forecasts[first] - forecasts[second])
    crps_ref[...] = valid * (error / members - 0.5 * coefficient * spread)
    pull = jnp.zeros_like(target)
    for other in forecasts[1:]:
        pull += smooth_sign(own - other)
    slope = (
        valid / 128 * (smooth_sign(own - target) / members - coefficient * pull)
    ).astype(BF)
    dhidden = dot_nt(slope, readout_ref[...]).astype(BF)
    dattended = dot_nt(dhidden, w_out_ref[...]).astype(BF)
    grad_ref[...] = dattended
    attended = attended_ref[...]
    product = dattended.astype(F32) * attended
    high = product.astype(BF)
    low = (product - high.astype(F32)).astype(BF)
    pick = (iota((1024, 128), 0) // HEAD_WIDTH + HEADS == iota((1024, 128), 1)).astype(BF)
    stats = stats_ref[...] + dot_nn(high, pick) + dot_nn(low, pick)
    first = stats.astype(BF)
    rest = stats - first.astype(F32)
    second = rest.astype(BF)
    third = (rest - second.astype(F32)).astype(BF)
    terms = jnp.zeros((BLOCK, 128), F32)
    for place, term in enumerate((first, second, third)):
        shift = (iota((128, 128), 0) + 32 * place == iota((128, 128), 1)) & (
            iota((128, 128), 0) < 32
        )
        terms += dot_nn(term, shift.astype(BF))
    packed_ref[:, :128] = slope
    packed_ref[:, 128:] = terms.astype(BF)
    small_ref[:, :128] = dot_tn(attended.astype(BF), slope).astype(BF)
    small_ref[:, 128:] = dot_tn(hidden_ref[...], slope).astype(BF)


def score(counts, own, near, others, target, attended, hidden, stats, w_out, readout_weight):
    vmem = pl.BlockSpec(memory_space=pltpu.VMEM)
    return pl.pallas_call(
        score_kernel,
        in_specs=[pl.BlockSpec(memory_space=pltpu.SMEM)] + [vmem] * 9,
        out_specs=[vmem] * 4,
        out_shape=[
            jax.ShapeDtypeStruct((BLOCK, 128), F32),
            jax.ShapeDtypeStruct((BLOCK, 256), BF),
            jax.ShapeDtypeStruct((BLOCK, 1024), BF),
            jax.ShapeDtypeStruct((1024, 256), BF),
        ],
        compiler_params=pltpu.CompilerParams(vmem_limit_bytes=VMEM_BYTES),
    )(counts, own, near, others, target, attended, hidden, stats, w_out, readout_weight)


def query_kernel(
    counts_ref, q_ref, kcat_ref, vcat_ref, grad_ref, packed_ref, dq_ref, dscores
):
    step = pl.program_id(0)

    @pl.when(step == 0)
    def _():
        dscores[...] = jnp.zeros_like(dscores)

    fill = key_fill([(counts_ref[0], WIN), (counts_ref[1], BLOCK), (counts_ref[2], WIN)])
    value_fill = (spare_lane(fill.shape) < 3).astype(BF)
    low_q = iota((BLOCK, PAIR), 1) < HEAD_WIDTH
    low_k = iota(fill.shape, 1) < HEAD_WIDTH
    terms = packed_ref[:, 128:]
    ones = (spare_lane((BLOCK, WIDTH)) == 3).astype(F32)
    q_fill = (dot_nn(terms, stat_spread(step, 0)) + ones).astype(BF)
    g_fill = dot_nn(terms, stat_spread(step, HEADS)).astype(BF)
    for pair in range(2):
        columns = slice(pair * PAIR, (pair + 1) * PAIR)
        q_pair = q_ref[:, columns] * jnp.asarray(HEAD_WIDTH ** (-0.5), BF)
        g_pair = grad_ref[:, columns]
        k_pair = kcat_ref[:, columns]
        v_pair = vcat_ref[:, columns]
        k_turned = k_pair.T
        for half in range(2):
            slot = pair * 2 + half
            pick_q = low_q if half == 0 else ~low_q
            pick_k = low_k if half == 0 else ~low_k
            q_head = jnp.where(pick_q, q_pair, q_fill[:, columns])
            g_head = jnp.where(pick_q, g_pair, g_fill[:, columns])
            k_head = jnp.where(pick_k, k_pair, fill)
            v_head = jnp.where(pick_k, v_pair, value_fill)
            scores = dot_nt(k_head, q_head)
            change = dot_nt(v_head, g_head)
            for tile in range(2):
                rows = slice(tile * 128, tile * 128 + 640)
                lanes = slice(tile * 128, tile * 128 + 128)
                ends = jnp.exp(scores[rows, lanes]) * change[rows, lanes]
                first, middle, last = keep_band(ends, 0.0)
                start = tile * 128
                dscores[slot, start : start + 128, lanes] = first.astype(BF)
                dscores[slot, start + 128 : start + 512, lanes] = middle.astype(BF)
                dscores[slot, start + 512 : start + 640, lanes] = last.astype(BF)
            turned = dot_nn(
                k_turned[half * HEAD_WIDTH : (half + 1) * HEAD_WIDTH], dscores[slot]
            )
            dq_ref[slot * HEAD_WIDTH : (slot + 1) * HEAD_WIDTH] = (
                turned * HEAD_WIDTH ** (-0.5)
            ).astype(BF)


def query_grads(counts, projected, kcat, vcat, grad, packed):
    part = lambda rows, first: pl.BlockSpec((rows, WIDTH), lambda j: (0, first + j))
    window = 2 * WIN + BLOCK
    return pl.pallas_call(
        query_kernel,
        grid=(4,),
        in_specs=[
            pl.BlockSpec(memory_space=pltpu.SMEM),
            part(BLOCK, 0),
            part(window, 0),
            part(window, 0),
            part(BLOCK, 0),
            pl.BlockSpec((BLOCK, 256), lambda j: (0, 0)),
        ],
        out_specs=pl.BlockSpec((WIDTH, BLOCK), lambda j: (j, 0)),
        out_shape=jax.ShapeDtypeStruct((1024, BLOCK), BF),
        scratch_shapes=[pltpu.VMEM((4, window, BLOCK), BF)],
        compiler_params=pltpu.CompilerParams(vmem_limit_bytes=VMEM_BYTES),
        cost_estimate=pl.CostEstimate(
            flops=6 << 30, bytes_accessed=5 << 20, transcendentals=3 << 20
        ),
    )(counts, projected, kcat, vcat, grad, packed)


def key_kernel(
    counts_ref,
    q_ref,
    k_ref,
    v_ref,
    qhalo_ref,
    grad_ref,
    own_ref,
    left_ref,
    right_ref,
    w_out_ref,
    readout_ref,
    out_ref,
    probs,
    dscores,
    dhidden,
):
    step = pl.program_id(0)

    @pl.when(step == 0)
    def _():
        probs[...] = jnp.zeros_like(probs)
        dscores[...] = jnp.zeros_like(dscores)
        dhidden[:WIN] = dot_nt(left_ref[:, :128], readout_ref[...]).astype(BF)
        dhidden[WIN:] = dot_nt(right_ref[:, :128], readout_ref[...]).astype(BF)

    ghalo = dot_nt(dhidden[...], w_out_ref[...]).astype(BF)
    terms = jnp.concatenate(
        [left_ref[:, 128:], own_ref[:, 128:], right_ref[:, 128:]], axis=0
    )
    window = terms.shape[0]
    fill = key_fill([(counts_ref[1], BLOCK)])
    value_fill = (spare_lane(fill.shape) < 3).astype(BF)
    low_q = iota((window, PAIR), 1) < HEAD_WIDTH
    low_k = iota(fill.shape, 1) < HEAD_WIDTH
    ones = (spare_lane((window, WIDTH)) == 3).astype(F32)
    q_fill = (dot_nn(terms, stat_spread(step, 0)) + ones).astype(BF)
    g_fill = dot_nn(terms, stat_spread(step, HEADS)).astype(BF)
    for pair in range(2):
        columns = slice(pair * PAIR, (pair + 1) * PAIR)
        q_pair = jnp.concatenate(
            [qhalo_ref[:WIN, columns], q_ref[:, columns], qhalo_ref[WIN:, columns]], axis=0
        ) * jnp.asarray(HEAD_WIDTH ** (-0.5), BF)
        g_pair = jnp.concatenate(
            [ghalo[:WIN, columns], grad_ref[:, columns], ghalo[WIN:, columns]], axis=0
        )
        k_pair = k_ref[:, columns]
        v_pair = v_ref[:, columns]
        q_turned = q_pair.T
        g_turned = g_pair.T
        for half in range(2):
            slot = pair * 2 + half
            pick_q = low_q if half == 0 else ~low_q
            pick_k = low_k if half == 0 else ~low_k
            q_head = jnp.where(pick_q, q_pair, q_fill[:, columns])
            g_head = jnp.where(pick_q, g_pair, g_fill[:, columns])
            k_head = jnp.where(pick_k, k_pair, fill)
            v_head = jnp.where(pick_k, v_pair, value_fill)
            scores = dot_nt(q_head, k_head)
            change = dot_nt(g_head, v_head)
            for tile in range(2):
                rows = slice(tile * 128, tile * 128 + 640)
                lanes = slice(tile * 128, tile * 128 + 128)
                weight = keep_band(jnp.exp(scores[rows, lanes]), 0.0)
                moved = change[rows, lanes]
                start = tile * 128
                for piece, (low, high) in zip(weight, ((0, 128), (128, 512), (512, 640))):
                    place = slice(start + low, start + high)
                    probs[slot, place, lanes] = piece.astype(BF)
                    dscores[slot, place, lanes] = (piece * moved[low:high]).astype(BF)
            lanes = slice(half * HEAD_WIDTH, (half + 1) * HEAD_WIDTH)
            place = slice(slot * HEAD_WIDTH, (slot + 1) * HEAD_WIDTH)
            out_ref[0, place] = dot_nn(q_turned[lanes], dscores[slot]).astype(BF)
            out_ref[1, place] = dot_nn(g_turned[lanes], probs[slot]).astype(BF)


def key_grads(counts, projected, qhalo, grad, own, left, right, w_out, readout_weight):
    part = lambda rows, first: pl.BlockSpec((rows, WIDTH), lambda j: (0, first + j))
    whole = lambda *shape: pl.BlockSpec(shape, lambda j: (0, 0))
    window = 2 * WIN + BLOCK
    return pl.pallas_call(
        key_kernel,
        grid=(4,),
        in_specs=[
            pl.BlockSpec(memory_space=pltpu.SMEM),
            part(BLOCK, 0),
            part(BLOCK, 4),
            part(BLOCK, 8),
            part(2 * WIN, 0),
            part(BLOCK, 0),
            whole(BLOCK, 256),
            whole(BLOCK, 256),
            whole(BLOCK, 256),
            pl.BlockSpec((WIDTH, 1024), lambda j: (j, 0)),
            whole(1024, 128),
        ],
        out_specs=pl.BlockSpec((2, WIDTH, BLOCK), lambda j: (0, j, 0)),
        out_shape=jax.ShapeDtypeStruct((2, 1024, BLOCK), BF),
        scratch_shapes=[
            pltpu.VMEM((4, window, BLOCK), BF),
            pltpu.VMEM((4, window, BLOCK), BF),
            pltpu.VMEM((2 * WIN, 1024), BF),
        ],
        compiler_params=pltpu.CompilerParams(vmem_limit_bytes=VMEM_BYTES),
        cost_estimate=pl.CostEstimate(
            flops=9 << 30, bytes_accessed=5 << 20, transcendentals=3 << 20
        ),
    )(
        counts,
        projected,
        projected,
        projected,
        qhalo,
        grad,
        own,
        left,
        right,
        w_out,
        readout_weight,
    )


AXES = ("x_hi", "core", "y", "x_lo", "z")
MEMBER = ("x_hi", "core")
CELLS = ("y", "x_lo", "z")
CHIPS = ("x_hi", "y", "x_lo", "z")
SWAP = [(0, 1), (1, 0)]


def swap_core(values):
    return lax.ppermute(values, "core", SWAP)


def core_rows(values, core):
    rows, columns = values.shape
    chosen = lax.dynamic_slice_in_dim(values.reshape(2, 2, rows // 4, columns), core, 1, 1)
    return chosen.reshape(rows // 2, columns)


def scatter_sum(partial):
    columns = partial.shape[1]
    pieces = lax.all_to_all(
        partial.reshape(64, 8, columns), CHIPS, split_axis=0, concat_axis=0
    )
    return jnp.sum(pieces.astype(F32), axis=0)


def per_device(latent, counts, w_qkv, w_out, readout_weight, target):
    latent_own = latent[0]
    cell_count = 32
    cell_index = lax.axis_index(CELLS)
    member_index = lax.axis_index(MEMBER)
    core = lax.axis_index("core")
    up = [(i, i + 1) for i in range(cell_count - 1)]
    down = [(i + 1, i) for i in range(cell_count - 1)]
    from_left = lax.ppermute(latent_own, CELLS, up)
    from_right = lax.ppermute(latent_own, CELLS, down)

    own_count = counts[cell_index]
    left_count = jnp.where(cell_index > 0, counts[jnp.maximum(cell_index - 1, 0)], 0)
    right_count = jnp.where(
        cell_index < cell_count - 1, counts[jnp.minimum(cell_index + 1, cell_count - 1)], 0
    )
    scalars = jnp.stack([left_count, own_count, right_count])

    projected, turned = project(latent_own, w_qkv)
    turned_own = core_rows(turned, core)
    turned_other = swap_core(core_rows(turned, 1 - core))
    normed_halo, kcat, vcat, attended, stats, hidden, forecast = forward(
        scalars, from_left, from_right, latent_own, w_qkv, projected, w_out, readout_weight
    )
    near = lax.ppermute(forecast, "x_hi", SWAP)
    others = swap_core(jnp.stack([forecast, near]))
    qhalo = dot_nn(normed_halo, w_qkv[:, :1024]).astype(BF)
    crps_whole, packed, grad, small = score(
        scalars, forecast, near, others, target, attended, hidden, stats, w_out, readout_weight
    )
    crps = lax.dynamic_slice_in_dim(crps_whole, member_index * 32, 32, 1)
    packed_left = lax.ppermute(packed, CELLS, up)
    packed_right = lax.ppermute(packed, CELLS, down)

    dquery = query_grads(scalars, projected, kcat, vcat, grad, packed)

    def partial_of(piece):
        return dot_nt(turned_own, piece) + dot_nt(turned_other, swap_core(piece))

    small_sum = core_rows(small, core).astype(F32) + swap_core(
        core_rows(small, 1 - core)
    ).astype(F32)
    first_part = jnp.concatenate([partial_of(dquery), small_sum], axis=1).astype(BF)
    first_part, scalars = lax.optimization_barrier((first_part, scalars))
    first = scatter_sum(first_part)
    pairs = key_grads(
        scalars,
        projected,
        qhalo,
        grad,
        packed,
        packed_left,
        packed_right,
        w_out,
        readout_weight,
    )
    second = scatter_sum(partial_of(pairs.reshape(2048, BLOCK)).astype(BF))
    grad_out = lax.dot_general(
        first[:, 1024:1152],
        readout_weight.astype(F32),
        (((1,), (1,)), ((), ())),
        precision=lax.Precision.HIGHEST,
        preferred_element_type=F32,
    )
    grads = jnp.concatenate([first[:, :1024], second, grad_out, first[:, 1152:]], axis=1)
    return (crps, grads)


def solution(mesh):
    fine = jax.sharding.Mesh(mesh.devices.reshape(2, 2, 4, 2, 4), AXES)
    placed = (P(MEMBER, CELLS, None), P(), P(), P(), P(), P(CELLS, None))
    return jax.shard_map(
        per_device,
        mesh=fine,
        in_specs=placed,
        out_specs=(P(CELLS, MEMBER), P(MEMBER + CELLS, None)),
        check_vma=False,
    )
```

```python
import functools

import jax
import jax.numpy as jnp
import numpy as np
from jax import lax
from jax.experimental import pallas as pl
from jax.experimental.pallas import tpu as pltpu
from jax.sharding import PartitionSpec as P

HEADS = 16
WIN = 256
BLOCK = 256
WIDTH = 256
HEAD_WIDTH = 64
PAIR = 128
NEVER = -1e30
VMEM_BYTES = 56 * 1024 * 1024

alpha_fair = 0.95
smooth_width = 0.0625

BF = jnp.bfloat16
F32 = jnp.float32


def smooth_abs(values):
    return jnp.sqrt(values * values + smooth_width)


def smooth_sign(values):
    return values * lax.rsqrt(values * values + smooth_width)


def layer_norm(latent_rows):
    values = latent_rows.astype(F32)
    center = values - jnp.mean(values, axis=-1, keepdims=True)
    spread = jnp.mean(center * center, axis=-1, keepdims=True)
    return (center * lax.rsqrt(spread + 1e-05)).astype(BF)


def dot_nn(left, right):
    return lax.dot_general(left, right, (((1,), (0,)), ((), ())), preferred_element_type=F32)


def dot_nt(left, right):
    return lax.dot_general(left, right, (((1,), (1,)), ((), ())), preferred_element_type=F32)


def dot_tn(left, right):
    return lax.dot_general(left, right, (((0,), (0,)), ((), ())), preferred_element_type=F32)


def iota(shape, axis):
    return lax.broadcasted_iota(jnp.int32, shape, axis)


def project_kernel(latent_ref, weight_ref, projected_ref, turned_ref, normed):
    step = pl.program_id(0)

    @pl.when(step == 0)
    def _():
        normed[...] = layer_norm(latent_ref[...])

    projected_ref[...] = dot_nn(normed[...], weight_ref[...]).astype(BF)

    @pl.when(step == 5)
    def _():
        turned_ref[...] = normed[...].T


def project(latent_own, w_qkv):
    rows, width = latent_own.shape
    return pl.pallas_call(
        project_kernel,
        grid=(6,),
        in_specs=[
            pl.BlockSpec((rows, width), lambda j: (0, 0)),
            pl.BlockSpec((width, 512), lambda j: (0, j)),
        ],
        out_specs=[
            pl.BlockSpec((rows, 512), lambda j: (0, j)),
            pl.BlockSpec((width, rows), lambda j: (0, 0)),
        ],
        out_shape=[
            jax.ShapeDtypeStruct((rows, 3 * width), BF),
            jax.ShapeDtypeStruct((width, rows), BF),
        ],
        scratch_shapes=[pltpu.VMEM((rows, width), BF)],
        compiler_params=pltpu.CompilerParams(vmem_limit_bytes=VMEM_BYTES),
        cost_estimate=pl.CostEstimate(
            flops=2 * rows * width * width * 4, bytes_accessed=8 << 20, transcendentals=0
        ),
    )(latent_own, w_qkv)


def spare_lane(shape):
    lane = iota(shape, len(shape) - 1)
    return lane % HEAD_WIDTH


def key_fill(count_pieces):
    fills = []
    for count, rows in count_pieces:
        spare = spare_lane((rows, PAIR))
        bias = jnp.where(iota((rows, PAIR), 0) < count, 0.0, NEVER)
        fills.append(
            jnp.where(spare < 3, 1.0, jnp.where(spare == 3, bias, 0.0)).astype(BF)
        )
    return jnp.concatenate(fills, axis=0)


def stat_spread(step, offset):
    shape = (128, WIDTH)
    lane = iota(shape, 1)
    head = step * 4 + 2 * (lane // PAIR) + jnp.where(lane % PAIR < HEAD_WIDTH, 1, 0)
    term = lane % HEAD_WIDTH
    chosen = (term < 3) & (iota(shape, 0) == term * 32 + offset + head)
    return jnp.where(chosen, -1.0, 0.0).astype(BF)


def keep_band(window, fill):
    shape = (128, 128)
    apart = iota(shape, 0) - iota(shape, 1)
    first = jnp.where(apart >= 0, window[:128], fill)
    last = jnp.where(apart <= 0, window[512:], fill)
    return first, window[128:512], last


def forward_kernel(
    counts_ref,
    left_ref,
    right_ref,
    latent_ref,
    wk_ref,
    wv_ref,
    q_ref,
    k_ref,
    v_ref,
    w_out_ref,
    readout_ref,
    normed_ref,
    kcat_ref,
    vcat_ref,
    attended_ref,
    stats_ref,
    hidden_ref,
    forecast_ref,
    probs,
    stat_rows,
):
    step = pl.program_id(0)

    @pl.when(step == 0)
    def _():
        normed_ref[:WIN] = layer_norm(left_ref[...])
        normed_ref[WIN:] = layer_norm(right_ref[...])
        probs[...] = jnp.zeros_like(probs)

    khalo = dot_nn(normed_ref[...], wk_ref[...]).astype(BF)
    kcat_ref[:WIN] = khalo[:WIN]
    kcat_ref[WIN : WIN + BLOCK] = k_ref[...]
    kcat_ref[WIN + BLOCK :] = khalo[WIN:]
    vhalo = dot_nn(normed_ref[...], wv_ref[...]).astype(BF)
    vcat_ref[:WIN] = vhalo[:WIN]
    vcat_ref[WIN : WIN + BLOCK] = v_ref[...]
    vcat_ref[WIN + BLOCK :] = vhalo[WIN:]
    fill = key_fill([(counts_ref[0], WIN), (counts_ref[1], BLOCK), (counts_ref[2], WIN)])
    low_q = iota((BLOCK, PAIR), 1) < HEAD_WIDTH
    low_k = iota(fill.shape, 1) < HEAD_WIDTH
    query_fill = (spare_lane((BLOCK, PAIR)) == 3).astype(BF)
    scores, turned = [], []
    for pair in range(2):
        columns = slice(pair * PAIR, (pair + 1) * PAIR)
        q_pair = q_ref[:, columns] * jnp.asarray(HEAD_WIDTH ** (-0.5), BF)
        k_pair = kcat_ref[:, columns]
        turned.append(vcat_ref[:, columns].T)
        for half in range(2):
            if half == 0:
                q_head = jnp.where(low_q, q_pair, query_fill)
                k_head = jnp.where(low_k, k_pair, fill)
            else:
                q_head = jnp.where(low_q, query_fill, q_pair)
                k_head = jnp.where(low_k, fill, k_pair)
            scores.append(dot_nt(k_head, q_head))
    scales = []
    for slot in range(4):
        totals, levels = [], []
        for tile in range(2):
            rows = slice(tile * 128, tile * 128 + 640)
            lanes = slice(tile * 128, tile * 128 + 128)
            first, middle, last = keep_band(scores[slot][rows, lanes], NEVER)
            top = jnp.maximum(
                jnp.max(middle, axis=0, keepdims=True),
                jnp.max(jnp.maximum(first, last), axis=0, keepdims=True),
            )
            first = jnp.exp(first - top)
            middle = jnp.exp(middle - top)
            last = jnp.exp(last - top)
            total = jnp.sum(middle, axis=0, keepdims=True) + jnp.sum(
                first + last, axis=0, keepdims=True
            )
            start = tile * 128
            probs[slot, start : start + 128, lanes] = first.astype(BF)
            probs[slot, start + 128 : start + 512, lanes] = middle.astype(BF)
            probs[slot, start + 512 : start + 640, lanes] = last.astype(BF)
            totals.append(total)
            levels.append(top + jnp.log(total))
        scales.append(1.0 / jnp.concatenate(totals, axis=1))
        stat_rows[pl.ds(step * 4 + slot, 1), :] = jnp.concatenate(levels, axis=1)
    for pair in range(2):
        halves = []
        for half in range(2):
            slot = pair * 2 + half
            lanes = slice(half * HEAD_WIDTH, (half + 1) * HEAD_WIDTH)
            halves.append(dot_nn(turned[pair][lanes], probs[slot]) * scales[slot])
        start = pl.multiple_of(step * WIDTH + pair * PAIR, PAIR)
        attended_ref[:, pl.ds(start, PAIR)] = jnp.concatenate(halves, axis=0).T

    @pl.when(step == 3)
    def _():
        mixed = dot_nn(attended_ref[...].astype(BF), w_out_ref[...])
        hidden = (latent_ref[...].astype(F32) + mixed).astype(BF)
        hidden_ref[...] = hidden
        forecast_ref[...] = dot_nn(hidden, readout_ref[...])
        stat_rows[HEADS:] = jnp.zeros((128 - HEADS, BLOCK), F32)
        stats_ref[...] = stat_rows[...].T


def forward(counts, left, right, latent_own, w_qkv, projected, w_out, readout_weight):
    whole = lambda *shape: pl.BlockSpec(shape, lambda j: (0, 0))
    part = lambda rows, first: pl.BlockSpec((rows, WIDTH), lambda j: (0, first + j))
    window = 2 * WIN + BLOCK
    return pl.pallas_call(
        forward_kernel,
        grid=(4,),
        in_specs=[
            pl.BlockSpec(memory_space=pltpu.SMEM),
            whole(WIN, 1024),
            whole(WIN, 1024),
            whole(BLOCK, 1024),
            part(1024, 4),
            part(1024, 8),
            part(BLOCK, 0),
            part(BLOCK, 4),
            part(BLOCK, 8),
            whole(1024, 1024),
            whole(1024, 128),
        ],
        out_specs=[
            whole(2 * WIN, 1024),
            part(window, 0),
            part(window, 0),
            whole(BLOCK, 1024),
            whole(BLOCK, 128),
            whole(BLOCK, 1024),
            whole(BLOCK, 128),
        ],
        out_shape=[
            jax.ShapeDtypeStruct((2 * WIN, 1024), BF),
            jax.ShapeDtypeStruct((window, 1024), BF),
            jax.ShapeDtypeStruct((window, 1024), BF),
            jax.ShapeDtypeStruct((BLOCK, 1024), F32),
            jax.ShapeDtypeStruct((BLOCK, 128), F32),
            jax.ShapeDtypeStruct((BLOCK, 1024), BF),
            jax.ShapeDtypeStruct((BLOCK, 128), F32),
        ],
        scratch_shapes=[pltpu.VMEM((4, window, BLOCK), BF), pltpu.VMEM((128, BLOCK), F32)],
        compiler_params=pltpu.CompilerParams(vmem_limit_bytes=VMEM_BYTES),
        cost_estimate=pl.CostEstimate(
            flops=6 << 30, bytes_accessed=12 << 20, transcendentals=3 << 20
        ),
    )(
        counts,
        left,
        right,
        latent_own,
        w_qkv,
        w_qkv,
        projected,
        projected,
        projected,
        w_out,
        readout_weight,
    )


def score_kernel(
    counts_ref,
    own_ref,
    near_ref,
    others_ref,
    target_ref,
    attended_ref,
    hidden_ref,
    stats_ref,
    w_out_ref,
    readout_ref,
    crps_ref,
    packed_ref,
    grad_ref,
    small_ref,
):
    members = 4
    fair_eps = (1.0 - alpha_fair) / members
    coefficient = (1.0 - fair_eps) / (members * (members - 1))
    valid = (iota((BLOCK, 1), 0) < counts_ref[1]).astype(F32)
    own = own_ref[...]
    forecasts = [own, near_ref[...], others_ref[0], others_ref[1]]
    target = target_ref[...]
    error = jnp.zeros_like(target)
    for forecast in forecasts:
        error += smooth_abs(forecast - target)
    spread = jnp.full_like(target, members * smooth_width**0.5)
    for first in range(members):
        for second in range(first + 1, members):
            spread += 2.0 * smooth_abs(forecasts[first] - forecasts[second])
    crps_ref[...] = valid * (error / members - 0.5 * coefficient * spread)
    pull = jnp.zeros_like(target)
    for other in forecasts[1:]:
        pull += smooth_sign(own - other)
    slope = (
        valid / 128 * (smooth_sign(own - target) / members - coefficient * pull)
    ).astype(BF)
    dhidden = dot_nt(slope, readout_ref[...]).astype(BF)
    dattended = dot_nt(dhidden, w_out_ref[...]).astype(BF)
    grad_ref[...] = dattended
    attended = attended_ref[...]
    product = dattended.astype(F32) * attended
    high = product.astype(BF)
    low = (product - high.astype(F32)).astype(BF)
    pick = (iota((1024, 128), 0) // HEAD_WIDTH + HEADS == iota((1024, 128), 1)).astype(BF)
    stats = stats_ref[...] + dot_nn(high, pick) + dot_nn(low, pick)
    first = stats.astype(BF)
    rest = stats - first.astype(F32)
    second = rest.astype(BF)
    third = (rest - second.astype(F32)).astype(BF)
    terms = jnp.zeros((BLOCK, 128), F32)
    for place, term in enumerate((first, second, third)):
        shift = (iota((128, 128), 0) + 32 * place == iota((128, 128), 1)) & (
            iota((128, 128), 0) < 32
        )
        terms += dot_nn(term, shift.astype(BF))
    packed_ref[:, :128] = slope
    packed_ref[:, 128:] = terms.astype(BF)
    small_ref[:, :128] = dot_tn(attended.astype(BF), slope).astype(BF)
    small_ref[:, 128:] = dot_tn(hidden_ref[...], slope).astype(BF)


def score(counts, own, near, others, target, attended, hidden, stats, w_out, readout_weight):
    vmem = pl.BlockSpec(memory_space=pltpu.VMEM)
    return pl.pallas_call(
        score_kernel,
        in_specs=[pl.BlockSpec(memory_space=pltpu.SMEM)] + [vmem] * 9,
        out_specs=[vmem] * 4,
        out_shape=[
            jax.ShapeDtypeStruct((BLOCK, 128), F32),
            jax.ShapeDtypeStruct((BLOCK, 256), BF),
            jax.ShapeDtypeStruct((BLOCK, 1024), BF),
            jax.ShapeDtypeStruct((1024, 256), BF),
        ],
        compiler_params=pltpu.CompilerParams(vmem_limit_bytes=VMEM_BYTES),
    )(counts, own, near, others, target, attended, hidden, stats, w_out, readout_weight)


def query_kernel(
    counts_ref, q_ref, kcat_ref, vcat_ref, grad_ref, packed_ref, dq_ref, dscores
):
    step = pl.program_id(0)

    @pl.when(step == 0)
    def _():
        dscores[...] = jnp.zeros_like(dscores)

    fill = key_fill([(counts_ref[0], WIN), (counts_ref[1], BLOCK), (counts_ref[2], WIN)])
    value_fill = (spare_lane(fill.shape) < 3).astype(BF)
    low_q = iota((BLOCK, PAIR), 1) < HEAD_WIDTH
    low_k = iota(fill.shape, 1) < HEAD_WIDTH
    terms = packed_ref[:, 128:]
    ones = (spare_lane((BLOCK, WIDTH)) == 3).astype(F32)
    q_fill = (dot_nn(terms, stat_spread(step, 0)) + ones).astype(BF)
    g_fill = dot_nn(terms, stat_spread(step, HEADS)).astype(BF)
    turned = []
    for pair in range(2):
        columns = slice(pair * PAIR, (pair + 1) * PAIR)
        q_pair = q_ref[:, columns] * jnp.asarray(HEAD_WIDTH ** (-0.5), BF)
        g_pair = grad_ref[:, columns]
        k_pair = kcat_ref[:, columns]
        v_pair = vcat_ref[:, columns]
        k_turned = k_pair.T
        for half in range(2):
            slot = pair * 2 + half
            pick_q = low_q if half == 0 else ~low_q
            pick_k = low_k if half == 0 else ~low_k
            q_head = jnp.where(pick_q, q_pair, q_fill[:, columns])
            g_head = jnp.where(pick_q, g_pair, g_fill[:, columns])
            k_head = jnp.where(pick_k, k_pair, fill)
            v_head = jnp.where(pick_k, v_pair, value_fill)
            scores = dot_nt(k_head, q_head)
            change = dot_nt(v_head, g_head)
            for tile in range(2):
                rows = slice(tile * 128, tile * 128 + 640)
                lanes = slice(tile * 128, tile * 128 + 128)
                ends = jnp.exp(scores[rows, lanes]) * change[rows, lanes]
                first, middle, last = keep_band(ends, 0.0)
                start = tile * 128
                dscores[slot, start : start + 128, lanes] = first.astype(BF)
                dscores[slot, start + 128 : start + 512, lanes] = middle.astype(BF)
                dscores[slot, start + 512 : start + 640, lanes] = last.astype(BF)
            turned.append(k_turned[half * HEAD_WIDTH : (half + 1) * HEAD_WIDTH])
    for slot in range(4):
        dquery = dot_nn(turned[slot], dscores[slot]) * HEAD_WIDTH ** (-0.5)
        dq_ref[slot * HEAD_WIDTH : (slot + 1) * HEAD_WIDTH] = dquery.astype(BF)


def query_grads(counts, projected, kcat, vcat, grad, packed):
    part = lambda rows, first: pl.BlockSpec((rows, WIDTH), lambda j: (0, first + j))
    window = 2 * WIN + BLOCK
    return pl.pallas_call(
        query_kernel,
        grid=(4,),
        in_specs=[
            pl.BlockSpec(memory_space=pltpu.SMEM),
            part(BLOCK, 0),
            part(window, 0),
            part(window, 0),
            part(BLOCK, 0),
            pl.BlockSpec((BLOCK, 256), lambda j: (0, 0)),
        ],
        out_specs=pl.BlockSpec((WIDTH, BLOCK), lambda j: (j, 0)),
        out_shape=jax.ShapeDtypeStruct((1024, BLOCK), BF),
        scratch_shapes=[pltpu.VMEM((4, window, BLOCK), BF)],
        compiler_params=pltpu.CompilerParams(vmem_limit_bytes=VMEM_BYTES),
        cost_estimate=pl.CostEstimate(
            flops=6 << 30, bytes_accessed=5 << 20, transcendentals=3 << 20
        ),
    )(counts, projected, kcat, vcat, grad, packed)


def key_kernel(
    counts_ref,
    q_ref,
    k_ref,
    v_ref,
    qhalo_ref,
    grad_ref,
    own_ref,
    left_ref,
    right_ref,
    w_out_ref,
    readout_ref,
    out_ref,
    probs,
    dscores,
    dhidden,
):
    step = pl.program_id(0)

    @pl.when(step == 0)
    def _():
        probs[...] = jnp.zeros_like(probs)
        dscores[...] = jnp.zeros_like(dscores)
        dhidden[:WIN] = dot_nt(left_ref[:, :128], readout_ref[...]).astype(BF)
        dhidden[WIN:] = dot_nt(right_ref[:, :128], readout_ref[...]).astype(BF)

    ghalo = dot_nt(dhidden[...], w_out_ref[...]).astype(BF)
    terms = jnp.concatenate(
        [left_ref[:, 128:], own_ref[:, 128:], right_ref[:, 128:]], axis=0
    )
    window = terms.shape[0]
    fill = key_fill([(counts_ref[1], BLOCK)])
    value_fill = (spare_lane(fill.shape) < 3).astype(BF)
    low_q = iota((window, PAIR), 1) < HEAD_WIDTH
    low_k = iota(fill.shape, 1) < HEAD_WIDTH
    ones = (spare_lane((window, WIDTH)) == 3).astype(F32)
    q_fill = (dot_nn(terms, stat_spread(step, 0)) + ones).astype(BF)
    g_fill = dot_nn(terms, stat_spread(step, HEADS)).astype(BF)
    turned = []
    for pair in range(2):
        columns = slice(pair * PAIR, (pair + 1) * PAIR)
        q_pair = jnp.concatenate(
            [qhalo_ref[:WIN, columns], q_ref[:, columns], qhalo_ref[WIN:, columns]], axis=0
        ) * jnp.asarray(HEAD_WIDTH ** (-0.5), BF)
        g_pair = jnp.concatenate(
            [ghalo[:WIN, columns], grad_ref[:, columns], ghalo[WIN:, columns]], axis=0
        )
        k_pair = k_ref[:, columns]
        v_pair = v_ref[:, columns]
        q_turned = q_pair.T
        g_turned = g_pair.T
        for half in range(2):
            slot = pair * 2 + half
            pick_q = low_q if half == 0 else ~low_q
            pick_k = low_k if half == 0 else ~low_k
            q_head = jnp.where(pick_q, q_pair, q_fill[:, columns])
            g_head = jnp.where(pick_q, g_pair, g_fill[:, columns])
            k_head = jnp.where(pick_k, k_pair, fill)
            v_head = jnp.where(pick_k, v_pair, value_fill)
            scores = dot_nt(q_head, k_head)
            change = dot_nt(g_head, v_head)
            for tile in range(2):
                rows = slice(tile * 128, tile * 128 + 640)
                lanes = slice(tile * 128, tile * 128 + 128)
                weight = keep_band(jnp.exp(scores[rows, lanes]), 0.0)
                moved = change[rows, lanes]
                start = tile * 128
                for piece, (low, high) in zip(weight, ((0, 128), (128, 512), (512, 640))):
                    place = slice(start + low, start + high)
                    probs[slot, place, lanes] = piece.astype(BF)
                    dscores[slot, place, lanes] = (piece * moved[low:high]).astype(BF)
            lanes = slice(half * HEAD_WIDTH, (half + 1) * HEAD_WIDTH)
            turned.append((q_turned[lanes], g_turned[lanes]))
    for slot in range(4):
        place = slice(slot * HEAD_WIDTH, (slot + 1) * HEAD_WIDTH)
        out_ref[0, place] = dot_nn(turned[slot][0], dscores[slot]).astype(BF)
        out_ref[1, place] = dot_nn(turned[slot][1], probs[slot]).astype(BF)


def key_grads(counts, projected, qhalo, grad, own, left, right, w_out, readout_weight):
    part = lambda rows, first: pl.BlockSpec((rows, WIDTH), lambda j: (0, first + j))
    whole = lambda *shape: pl.BlockSpec(shape, lambda j: (0, 0))
    window = 2 * WIN + BLOCK
    return pl.pallas_call(
        key_kernel,
        grid=(4,),
        in_specs=[
            pl.BlockSpec(memory_space=pltpu.SMEM),
            part(BLOCK, 0),
            part(BLOCK, 4),
            part(BLOCK, 8),
            part(2 * WIN, 0),
            part(BLOCK, 0),
            whole(BLOCK, 256),
            whole(BLOCK, 256),
            whole(BLOCK, 256),
            pl.BlockSpec((WIDTH, 1024), lambda j: (j, 0)),
            whole(1024, 128),
        ],
        out_specs=pl.BlockSpec((2, WIDTH, BLOCK), lambda j: (0, j, 0)),
        out_shape=jax.ShapeDtypeStruct((2, 1024, BLOCK), BF),
        scratch_shapes=[
            pltpu.VMEM((4, window, BLOCK), BF),
            pltpu.VMEM((4, window, BLOCK), BF),
            pltpu.VMEM((2 * WIN, 1024), BF),
        ],
        compiler_params=pltpu.CompilerParams(vmem_limit_bytes=VMEM_BYTES),
        cost_estimate=pl.CostEstimate(
            flops=9 << 30, bytes_accessed=5 << 20, transcendentals=3 << 20
        ),
    )(
        counts,
        projected,
        projected,
        projected,
        qhalo,
        grad,
        own,
        left,
        right,
        w_out,
        readout_weight,
    )


AXES = ("x_hi", "core", "y", "x_lo", "z")
MEMBER = ("x_hi", "core")
CELLS = ("y", "x_lo", "z")
CHIPS = ("x_hi", "y", "x_lo", "z")
SWAP = [(0, 1), (1, 0)]


def swap_core(values):
    return lax.ppermute(values, "core", SWAP)


def core_rows(values, core):
    rows, columns = values.shape
    chosen = lax.dynamic_slice_in_dim(values.reshape(2, 2, rows // 4, columns), core, 1, 1)
    return chosen.reshape(rows // 2, columns)


def scatter(partial):
    columns = partial.shape[1]
    return lax.all_to_all(partial.reshape(64, 8, columns), CHIPS, split_axis=0, concat_axis=0)


def add_up(pieces):
    return jnp.sum(pieces.astype(F32), axis=0)


def per_device(latent, counts, w_qkv, w_out, readout_weight, target):
    latent_own = latent[0]
    cell_count = 32
    cell_index = lax.axis_index(CELLS)
    member_index = lax.axis_index(MEMBER)
    core = lax.axis_index("core")
    up = [(i, i + 1) for i in range(cell_count - 1)]
    down = [(i + 1, i) for i in range(cell_count - 1)]
    from_left = lax.ppermute(latent_own, CELLS, up)
    from_right = lax.ppermute(latent_own, CELLS, down)

    own_count = counts[cell_index]
    left_count = jnp.where(cell_index > 0, counts[jnp.maximum(cell_index - 1, 0)], 0)
    right_count = jnp.where(
        cell_index < cell_count - 1, counts[jnp.minimum(cell_index + 1, cell_count - 1)], 0
    )
    scalars = jnp.stack([left_count, own_count, right_count])

    projected, turned = project(latent_own, w_qkv)
    turned_own = core_rows(turned, core)
    turned_other = swap_core(core_rows(turned, 1 - core))
    normed_halo, kcat, vcat, attended, stats, hidden, forecast = forward(
        scalars, from_left, from_right, latent_own, w_qkv, projected, w_out, readout_weight
    )
    near = lax.ppermute(forecast, "x_hi", SWAP)
    others = swap_core(jnp.stack([forecast, near]))
    qhalo = dot_nn(normed_halo, w_qkv[:, :1024]).astype(BF)
    others, qhalo = lax.optimization_barrier((others, qhalo))
    crps_whole, packed, grad, small = score(
        scalars, forecast, near, others, target, attended, hidden, stats, w_out, readout_weight
    )
    crps = lax.dynamic_slice_in_dim(crps_whole, member_index * 32, 32, 1)
    packed_left = lax.ppermute(packed, CELLS, up)
    packed_right = lax.ppermute(packed, CELLS, down)

    dquery = query_grads(scalars, projected, kcat, vcat, grad, packed)
    dquery, packed_left, packed_right = lax.optimization_barrier(
        (dquery, packed_left, packed_right)
    )

    def partial_of(piece):
        return dot_nt(turned_own, piece) + dot_nt(turned_other, swap_core(piece))

    small_sum = core_rows(small, core).astype(F32) + swap_core(
        core_rows(small, 1 - core)
    ).astype(F32)
    first_part = jnp.concatenate([partial_of(dquery), small_sum], axis=1).astype(BF)
    first_part, scalars = lax.optimization_barrier((first_part, scalars))
    first = scatter(first_part)
    pairs = key_grads(
        scalars,
        projected,
        qhalo,
        grad,
        packed,
        packed_left,
        packed_right,
        w_out,
        readout_weight,
    )
    pairs, first = lax.optimization_barrier((pairs, first))
    second = add_up(scatter(partial_of(pairs.reshape(2048, BLOCK)).astype(BF)))
    first = add_up(first)
    grad_out = lax.dot_general(
        first[:, 1024:1152],
        readout_weight.astype(F32),
        (((1,), (1,)), ((), ())),
        precision=lax.Precision.HIGHEST,
        preferred_element_type=F32,
    )
    grads = jnp.concatenate([first[:, :1024], second, grad_out, first[:, 1152:]], axis=1)
    return (crps, grads)


def solution(mesh):
    fine = jax.sharding.Mesh(mesh.devices.reshape(2, 2, 4, 2, 4), AXES)
    placed = (P(MEMBER, CELLS, None), P(), P(), P(), P(), P(CELLS, None))
    return jax.shard_map(
        per_device,
        mesh=fine,
        in_specs=placed,
        out_specs=(P(CELLS, MEMBER), P(MEMBER + CELLS, None)),
        check_vma=False,
    )
```

```python
import functools

import jax
import jax.numpy as jnp
import numpy as np
from jax import lax
from jax.experimental import pallas as pl
from jax.experimental.pallas import tpu as pltpu
from jax.sharding import PartitionSpec as P

HEADS = 16
WIN = 256
BLOCK = 256
WIDTH = 256
HEAD_WIDTH = 64
PAIR = 128
NEVER = -1e30

alpha_fair = 0.95
smooth_width = 0.0625

BF = jnp.bfloat16
F32 = jnp.float32


def smooth_abs(values):
    return jnp.sqrt(values * values + smooth_width)


def smooth_sign(values):
    return values * lax.rsqrt(values * values + smooth_width)


def layer_norm(latent_rows):
    values = latent_rows.astype(F32)
    center = values - jnp.mean(values, axis=-1, keepdims=True)
    spread = jnp.mean(center * center, axis=-1, keepdims=True)
    return (center * lax.rsqrt(spread + 1e-05)).astype(BF)


def dot_nn(left, right):
    return lax.dot_general(left, right, (((1,), (0,)), ((), ())), preferred_element_type=F32)


def dot_nt(left, right):
    return lax.dot_general(left, right, (((1,), (1,)), ((), ())), preferred_element_type=F32)


def dot_tn(left, right):
    return lax.dot_general(left, right, (((0,), (0,)), ((), ())), preferred_element_type=F32)


def iota(shape, axis):
    return lax.broadcasted_iota(jnp.int32, shape, axis)


def project_kernel(latent_ref, weight_ref, projected_ref, turned_ref, normed):
    step = pl.program_id(0)

    @pl.when(step == 0)
    def _():
        normed[...] = layer_norm(latent_ref[...])

    projected_ref[...] = dot_nn(normed[...], weight_ref[...]).astype(BF)

    @pl.when(step == 5)
    def _():
        turned_ref[...] = normed[...].T


def project(latent_own, w_qkv):
    rows, width = latent_own.shape
    return pl.pallas_call(
        project_kernel,
        grid=(6,),
        in_specs=[
            pl.BlockSpec((rows, width), lambda j: (0, 0)),
            pl.BlockSpec((width, 512), lambda j: (0, j)),
        ],
        out_specs=[
            pl.BlockSpec((rows, 512), lambda j: (0, j)),
            pl.BlockSpec((width, rows), lambda j: (0, 0)),
        ],
        out_shape=[
            jax.ShapeDtypeStruct((rows, 3 * width), BF),
            jax.ShapeDtypeStruct((width, rows), BF),
        ],
        scratch_shapes=[pltpu.VMEM((rows, width), BF)],
        compiler_params=pltpu.CompilerParams(vmem_limit_bytes=10 * 1024 * 1024),
        cost_estimate=pl.CostEstimate(
            flops=2 * rows * width * width * 4, bytes_accessed=8 << 20, transcendentals=0
        ),
    )(latent_own, w_qkv)


def spare_lane(shape):
    lane = iota(shape, len(shape) - 1)
    return lane % HEAD_WIDTH


def key_fill(count_pieces):
    fills = []
    for count, rows in count_pieces:
        spare = spare_lane((rows, PAIR))
        bias = jnp.where(iota((rows, PAIR), 0) < count, 0.0, NEVER)
        fills.append(
            jnp.where(spare < 3, 1.0, jnp.where(spare == 3, bias, 0.0)).astype(BF)
        )
    return jnp.concatenate(fills, axis=0)


def stat_spread(step, offset):
    shape = (128, WIDTH)
    lane = iota(shape, 1)
    head = step * 4 + 2 * (lane // PAIR) + jnp.where(lane % PAIR < HEAD_WIDTH, 1, 0)
    term = lane % HEAD_WIDTH
    chosen = (term < 3) & (iota(shape, 0) == term * 32 + offset + head)
    return jnp.where(chosen, -1.0, 0.0).astype(BF)


def keep_band(window, fill):
    shape = (128, 128)
    apart = iota(shape, 0) - iota(shape, 1)
    first = jnp.where(apart >= 0, window[:128], fill)
    last = jnp.where(apart <= 0, window[512:], fill)
    return first, window[128:512], last


def forward_kernel(
    counts_ref,
    left_ref,
    right_ref,
    latent_ref,
    wk_ref,
    wv_ref,
    q_ref,
    k_ref,
    v_ref,
    w_out_ref,
    readout_ref,
    normed_ref,
    kcat_ref,
    vcat_ref,
    attended_ref,
    stats_ref,
    hidden_ref,
    forecast_ref,
    probs,
    stat_rows,
):
    step = pl.program_id(0)

    @pl.when(step == 0)
    def _():
        normed_ref[:WIN] = layer_norm(left_ref[...])
        normed_ref[WIN:] = layer_norm(right_ref[...])
        probs[...] = jnp.zeros_like(probs)

    khalo = dot_nn(normed_ref[...], wk_ref[...]).astype(BF)
    kcat_ref[:WIN] = khalo[:WIN]
    kcat_ref[WIN : WIN + BLOCK] = k_ref[...]
    kcat_ref[WIN + BLOCK :] = khalo[WIN:]
    vhalo = dot_nn(normed_ref[...], wv_ref[...]).astype(BF)
    vcat_ref[:WIN] = vhalo[:WIN]
    vcat_ref[WIN : WIN + BLOCK] = v_ref[...]
    vcat_ref[WIN + BLOCK :] = vhalo[WIN:]
    fill = key_fill([(counts_ref[0], WIN), (counts_ref[1], BLOCK), (counts_ref[2], WIN)])
    low_q = iota((BLOCK, PAIR), 1) < HEAD_WIDTH
    low_k = iota(fill.shape, 1) < HEAD_WIDTH
    query_fill = (spare_lane((BLOCK, PAIR)) == 3).astype(BF)
    scores, turned = [], []
    for pair in range(2):
        columns = slice(pair * PAIR, (pair + 1) * PAIR)
        q_pair = q_ref[:, columns] * jnp.asarray(HEAD_WIDTH ** (-0.5), BF)
        k_pair = kcat_ref[:, columns]
        turned.append(vcat_ref[:, columns].T)
        for half in range(2):
            if half == 0:
                q_head = jnp.where(low_q, q_pair, query_fill)
                k_head = jnp.where(low_k, k_pair, fill)
            else:
                q_head = jnp.where(low_q, query_fill, q_pair)
                k_head = jnp.where(low_k, fill, k_pair)
            scores.append(dot_nt(k_head, q_head))
    scales = []
    for slot in range(4):
        totals, levels = [], []
        for tile in range(2):
            rows = slice(tile * 128, tile * 128 + 640)
            lanes = slice(tile * 128, tile * 128 + 128)
            first, middle, last = keep_band(scores[slot][rows, lanes], NEVER)
            top = jnp.maximum(
                jnp.max(middle, axis=0, keepdims=True),
                jnp.max(jnp.maximum(first, last), axis=0, keepdims=True),
            )
            first = jnp.exp(first - top)
            middle = jnp.exp(middle - top)
            last = jnp.exp(last - top)
            total = jnp.sum(middle, axis=0, keepdims=True) + jnp.sum(
                first + last, axis=0, keepdims=True
            )
            start = tile * 128
            probs[slot, start : start + 128, lanes] = first.astype(BF)
            probs[slot, start + 128 : start + 512, lanes] = middle.astype(BF)
            probs[slot, start + 512 : start + 640, lanes] = last.astype(BF)
            totals.append(total)
            levels.append(top + jnp.log(total))
        scales.append(1.0 / jnp.concatenate(totals, axis=1))
        stat_rows[pl.ds(step * 4 + slot, 1), :] = jnp.concatenate(levels, axis=1)
    for pair in range(2):
        halves = []
        for half in range(2):
            slot = pair * 2 + half
            lanes = slice(half * HEAD_WIDTH, (half + 1) * HEAD_WIDTH)
            halves.append(dot_nn(turned[pair][lanes], probs[slot]) * scales[slot])
        start = pl.multiple_of(step * WIDTH + pair * PAIR, PAIR)
        attended_ref[:, pl.ds(start, PAIR)] = jnp.concatenate(halves, axis=0).T

    @pl.when(step == 3)
    def _():
        mixed = dot_nn(attended_ref[...].astype(BF), w_out_ref[...])
        hidden = (latent_ref[...].astype(F32) + mixed).astype(BF)
        hidden_ref[...] = hidden
        forecast_ref[...] = dot_nn(hidden, readout_ref[...])
        stat_rows[HEADS:] = jnp.zeros((128 - HEADS, BLOCK), F32)
        stats_ref[...] = stat_rows[...].T


def forward(counts, left, right, latent_own, w_qkv, projected, w_out, readout_weight):
    whole = lambda *shape: pl.BlockSpec(shape, lambda j: (0, 0))
    part = lambda rows, first: pl.BlockSpec((rows, WIDTH), lambda j: (0, first + j))
    window = 2 * WIN + BLOCK
    return pl.pallas_call(
        forward_kernel,
        grid=(4,),
        in_specs=[
            pl.BlockSpec(memory_space=pltpu.SMEM),
            whole(WIN, 1024),
            whole(WIN, 1024),
            whole(BLOCK, 1024),
            part(1024, 4),
            part(1024, 8),
            part(BLOCK, 0),
            part(BLOCK, 4),
            part(BLOCK, 8),
            whole(1024, 1024),
            whole(1024, 128),
        ],
        out_specs=[
            whole(2 * WIN, 1024),
            part(window, 0),
            part(window, 0),
            whole(BLOCK, 1024),
            whole(BLOCK, 128),
            whole(BLOCK, 1024),
            whole(BLOCK, 128),
        ],
        out_shape=[
            jax.ShapeDtypeStruct((2 * WIN, 1024), BF),
            jax.ShapeDtypeStruct((window, 1024), BF),
            jax.ShapeDtypeStruct((window, 1024), BF),
            jax.ShapeDtypeStruct((BLOCK, 1024), F32),
            jax.ShapeDtypeStruct((BLOCK, 128), F32),
            jax.ShapeDtypeStruct((BLOCK, 1024), BF),
            jax.ShapeDtypeStruct((BLOCK, 128), F32),
        ],
        scratch_shapes=[pltpu.VMEM((4, window, BLOCK), BF), pltpu.VMEM((128, BLOCK), F32)],
        compiler_params=pltpu.CompilerParams(vmem_limit_bytes=28 * 1024 * 1024),
        cost_estimate=pl.CostEstimate(
            flops=6 << 30, bytes_accessed=12 << 20, transcendentals=3 << 20
        ),
    )(
        counts,
        left,
        right,
        latent_own,
        w_qkv,
        w_qkv,
        projected,
        projected,
        projected,
        w_out,
        readout_weight,
    )


def score_kernel(
    counts_ref,
    own_ref,
    near_ref,
    others_ref,
    target_ref,
    attended_ref,
    hidden_ref,
    stats_ref,
    w_out_ref,
    readout_ref,
    crps_ref,
    packed_ref,
    grad_ref,
    small_ref,
):
    members = 4
    fair_eps = (1.0 - alpha_fair) / members
    coefficient = (1.0 - fair_eps) / (members * (members - 1))
    valid = (iota((BLOCK, 1), 0) < counts_ref[1]).astype(F32)
    own = own_ref[...]
    forecasts = [own, near_ref[...], others_ref[0], others_ref[1]]
    target = target_ref[...]
    error = jnp.zeros_like(target)
    for forecast in forecasts:
        error += smooth_abs(forecast - target)
    spread = jnp.full_like(target, members * smooth_width**0.5)
    for first in range(members):
        for second in range(first + 1, members):
            spread += 2.0 * smooth_abs(forecasts[first] - forecasts[second])
    crps_ref[...] = valid * (error / members - 0.5 * coefficient * spread)
    pull = jnp.zeros_like(target)
    for other in forecasts[1:]:
        pull += smooth_sign(own - other)
    slope = (
        valid / 128 * (smooth_sign(own - target) / members - coefficient * pull)
    ).astype(BF)
    dhidden = dot_nt(slope, readout_ref[...]).astype(BF)
    dattended = dot_nt(dhidden, w_out_ref[...]).astype(BF)
    grad_ref[...] = dattended
    attended = attended_ref[...]
    product = dattended.astype(F32) * attended
    high = product.astype(BF)
    low = (product - high.astype(F32)).astype(BF)
    pick = (iota((1024, 128), 0) // HEAD_WIDTH + HEADS == iota((1024, 128), 1)).astype(BF)
    stats = stats_ref[...] + dot_nn(high, pick) + dot_nn(low, pick)
    first = stats.astype(BF)
    rest = stats - first.astype(F32)
    second = rest.astype(BF)
    third = (rest - second.astype(F32)).astype(BF)
    terms = jnp.zeros((BLOCK, 128), F32)
    for place, term in enumerate((first, second, third)):
        shift = (iota((128, 128), 0) + 32 * place == iota((128, 128), 1)) & (
            iota((128, 128), 0) < 32
        )
        terms += dot_nn(term, shift.astype(BF))
    packed_ref[:, :128] = slope
    packed_ref[:, 128:] = terms.astype(BF)
    small_ref[:, :128] = dot_tn(attended.astype(BF), slope).astype(BF)
    small_ref[:, 128:] = dot_tn(hidden_ref[...], slope).astype(BF)


def score(counts, own, near, others, target, attended, hidden, stats, w_out, readout_weight):
    vmem = pl.BlockSpec(memory_space=pltpu.VMEM)
    return pl.pallas_call(
        score_kernel,
        in_specs=[pl.BlockSpec(memory_space=pltpu.SMEM)] + [vmem] * 9,
        out_specs=[vmem] * 4,
        out_shape=[
            jax.ShapeDtypeStruct((BLOCK, 128), F32),
            jax.ShapeDtypeStruct((BLOCK, 256), BF),
            jax.ShapeDtypeStruct((BLOCK, 1024), BF),
            jax.ShapeDtypeStruct((1024, 256), BF),
        ],
        compiler_params=pltpu.CompilerParams(vmem_limit_bytes=12 * 1024 * 1024),
    )(counts, own, near, others, target, attended, hidden, stats, w_out, readout_weight)


def query_kernel(
    counts_ref, q_ref, kcat_ref, vcat_ref, grad_ref, packed_ref, dq_ref, dscores
):
    step = pl.program_id(0)

    @pl.when(step == 0)
    def _():
        dscores[...] = jnp.zeros_like(dscores)

    fill = key_fill([(counts_ref[0], WIN), (counts_ref[1], BLOCK), (counts_ref[2], WIN)])
    value_fill = (spare_lane(fill.shape) < 3).astype(BF)
    low_q = iota((BLOCK, PAIR), 1) < HEAD_WIDTH
    low_k = iota(fill.shape, 1) < HEAD_WIDTH
    terms = packed_ref[:, 128:]
    ones = (spare_lane((BLOCK, WIDTH)) == 3).astype(F32)
    q_fill = (dot_nn(terms, stat_spread(step, 0)) + ones).astype(BF)
    g_fill = dot_nn(terms, stat_spread(step, HEADS)).astype(BF)
    turned = []
    for pair in range(2):
        columns = slice(pair * PAIR, (pair + 1) * PAIR)
        q_pair = q_ref[:, columns] * jnp.asarray(HEAD_WIDTH ** (-0.5), BF)
        g_pair = grad_ref[:, columns]
        k_pair = kcat_ref[:, columns]
        v_pair = vcat_ref[:, columns]
        k_turned = k_pair.T
        for half in range(2):
            slot = pair * 2 + half
            pick_q = low_q if half == 0 else ~low_q
            pick_k = low_k if half == 0 else ~low_k
            q_head = jnp.where(pick_q, q_pair, q_fill[:, columns])
            g_head = jnp.where(pick_q, g_pair, g_fill[:, columns])
            k_head = jnp.where(pick_k, k_pair, fill)
            v_head = jnp.where(pick_k, v_pair, value_fill)
            scores = dot_nt(k_head, q_head)
            change = dot_nt(v_head, g_head)
            for tile in range(2):
                rows = slice(tile * 128, tile * 128 + 640)
                lanes = slice(tile * 128, tile * 128 + 128)
                ends = jnp.exp(scores[rows, lanes]) * change[rows, lanes]
                first, middle, last = keep_band(ends, 0.0)
                start = tile * 128
                dscores[slot, start : start + 128, lanes] = first.astype(BF)
                dscores[slot, start + 128 : start + 512, lanes] = middle.astype(BF)
                dscores[slot, start + 512 : start + 640, lanes] = last.astype(BF)
            turned.append(k_turned[half * HEAD_WIDTH : (half + 1) * HEAD_WIDTH])
    for slot in range(4):
        dquery = dot_nn(turned[slot], dscores[slot]) * HEAD_WIDTH ** (-0.5)
        dq_ref[slot * HEAD_WIDTH : (slot + 1) * HEAD_WIDTH] = dquery.astype(BF)


def query_grads(counts, projected, kcat, vcat, grad, packed):
    part = lambda rows, first: pl.BlockSpec((rows, WIDTH), lambda j: (0, first + j))
    window = 2 * WIN + BLOCK
    return pl.pallas_call(
        query_kernel,
        grid=(4,),
        in_specs=[
            pl.BlockSpec(memory_space=pltpu.SMEM),
            part(BLOCK, 0),
            part(window, 0),
            part(window, 0),
            part(BLOCK, 0),
            pl.BlockSpec((BLOCK, 256), lambda j: (0, 0)),
        ],
        out_specs=pl.BlockSpec((WIDTH, BLOCK), lambda j: (j, 0)),
        out_shape=jax.ShapeDtypeStruct((1024, BLOCK), BF),
        scratch_shapes=[pltpu.VMEM((4, window, BLOCK), BF)],
        compiler_params=pltpu.CompilerParams(vmem_limit_bytes=12 * 1024 * 1024),
        cost_estimate=pl.CostEstimate(
            flops=6 << 30, bytes_accessed=5 << 20, transcendentals=3 << 20
        ),
    )(counts, projected, kcat, vcat, grad, packed)


def key_kernel(
    counts_ref,
    q_ref,
    k_ref,
    v_ref,
    qhalo_ref,
    grad_ref,
    own_ref,
    left_ref,
    right_ref,
    w_out_ref,
    readout_ref,
    out_ref,
    probs,
    dscores,
    dhidden,
):
    step = pl.program_id(0)

    @pl.when(step == 0)
    def _():
        probs[...] = jnp.zeros_like(probs)
        dscores[...] = jnp.zeros_like(dscores)
        dhidden[:WIN] = dot_nt(left_ref[:, :128], readout_ref[...]).astype(BF)
        dhidden[WIN:] = dot_nt(right_ref[:, :128], readout_ref[...]).astype(BF)

    ghalo = dot_nt(dhidden[...], w_out_ref[...]).astype(BF)
    terms = jnp.concatenate(
        [left_ref[:, 128:], own_ref[:, 128:], right_ref[:, 128:]], axis=0
    )
    window = terms.shape[0]
    fill = key_fill([(counts_ref[1], BLOCK)])
    value_fill = (spare_lane(fill.shape) < 3).astype(BF)
    low_q = iota((window, PAIR), 1) < HEAD_WIDTH
    low_k = iota(fill.shape, 1) < HEAD_WIDTH
    ones = (spare_lane((window, WIDTH)) == 3).astype(F32)
    q_fill = (dot_nn(terms, stat_spread(step, 0)) + ones).astype(BF)
    g_fill = dot_nn(terms, stat_spread(step, HEADS)).astype(BF)
    turned = []
    for pair in range(2):
        columns = slice(pair * PAIR, (pair + 1) * PAIR)
        q_pair = jnp.concatenate(
            [qhalo_ref[:WIN, columns], q_ref[:, columns], qhalo_ref[WIN:, columns]], axis=0
        ) * jnp.asarray(HEAD_WIDTH ** (-0.5), BF)
        g_pair = jnp.concatenate(
            [ghalo[:WIN, columns], grad_ref[:, columns], ghalo[WIN:, columns]], axis=0
        )
        k_pair = k_ref[:, columns]
        v_pair = v_ref[:, columns]
        q_turned = q_pair.T
        g_turned = g_pair.T
        for half in range(2):
            slot = pair * 2 + half
            pick_q = low_q if half == 0 else ~low_q
            pick_k = low_k if half == 0 else ~low_k
            q_head = jnp.where(pick_q, q_pair, q_fill[:, columns])
            g_head = jnp.where(pick_q, g_pair, g_fill[:, columns])
            k_head = jnp.where(pick_k, k_pair, fill)
            v_head = jnp.where(pick_k, v_pair, value_fill)
            scores = dot_nt(q_head, k_head)
            change = dot_nt(g_head, v_head)
            for tile in range(2):
                rows = slice(tile * 128, tile * 128 + 640)
                lanes = slice(tile * 128, tile * 128 + 128)
                weight = keep_band(jnp.exp(scores[rows, lanes]), 0.0)
                moved = change[rows, lanes]
                start = tile * 128
                for piece, (low, high) in zip(weight, ((0, 128), (128, 512), (512, 640))):
                    place = slice(start + low, start + high)
                    probs[slot, place, lanes] = piece.astype(BF)
                    dscores[slot, place, lanes] = (piece * moved[low:high]).astype(BF)
            lanes = slice(half * HEAD_WIDTH, (half + 1) * HEAD_WIDTH)
            turned.append((q_turned[lanes], g_turned[lanes]))
    for slot in range(4):
        place = slice(slot * HEAD_WIDTH, (slot + 1) * HEAD_WIDTH)
        out_ref[0, place] = dot_nn(turned[slot][0], dscores[slot]).astype(BF)
        out_ref[1, place] = dot_nn(turned[slot][1], probs[slot]).astype(BF)


def key_grads(counts, projected, qhalo, grad, own, left, right, w_out, readout_weight):
    part = lambda rows, first: pl.BlockSpec((rows, WIDTH), lambda j: (0, first + j))
    whole = lambda *shape: pl.BlockSpec(shape, lambda j: (0, 0))
    window = 2 * WIN + BLOCK
    return pl.pallas_call(
        key_kernel,
        grid=(4,),
        in_specs=[
            pl.BlockSpec(memory_space=pltpu.SMEM),
            part(BLOCK, 0),
            part(BLOCK, 4),
            part(BLOCK, 8),
            part(2 * WIN, 0),
            part(BLOCK, 0),
            whole(BLOCK, 256),
            whole(BLOCK, 256),
            whole(BLOCK, 256),
            pl.BlockSpec((WIDTH, 1024), lambda j: (j, 0)),
            whole(1024, 128),
        ],
        out_specs=pl.BlockSpec((2, WIDTH, BLOCK), lambda j: (0, j, 0)),
        out_shape=jax.ShapeDtypeStruct((2, 1024, BLOCK), BF),
        scratch_shapes=[
            pltpu.VMEM((4, window, BLOCK), BF),
            pltpu.VMEM((4, window, BLOCK), BF),
            pltpu.VMEM((2 * WIN, 1024), BF),
        ],
        compiler_params=pltpu.CompilerParams(vmem_limit_bytes=18 * 1024 * 1024),
        cost_estimate=pl.CostEstimate(
            flops=9 << 30, bytes_accessed=5 << 20, transcendentals=3 << 20
        ),
    )(
        counts,
        projected,
        projected,
        projected,
        qhalo,
        grad,
        own,
        left,
        right,
        w_out,
        readout_weight,
    )


AXES = ("x_hi", "core", "y", "x_lo", "z")
MEMBER = ("x_hi", "core")
CELLS = ("y", "x_lo", "z")
CHIPS = ("x_hi", "y", "x_lo", "z")
SWAP = [(0, 1), (1, 0)]


def swap_core(values):
    return lax.ppermute(values, "core", SWAP)


def core_rows(values, core):
    rows, columns = values.shape
    chosen = lax.dynamic_slice_in_dim(values.reshape(2, 2, rows // 4, columns), core, 1, 1)
    return chosen.reshape(rows // 2, columns)


def scatter(partial):
    columns = partial.shape[1]
    return lax.all_to_all(partial.reshape(64, 8, columns), CHIPS, split_axis=0, concat_axis=0)


def add_up(pieces):
    return jnp.sum(pieces.astype(F32), axis=0)


def per_device(latent, counts, w_qkv, w_out, readout_weight, target):
    latent_own = latent[0]
    cell_count = 32
    cell_index = lax.axis_index(CELLS)
    member_index = lax.axis_index(MEMBER)
    core = lax.axis_index("core")
    up = [(i, i + 1) for i in range(cell_count - 1)]
    down = [(i + 1, i) for i in range(cell_count - 1)]
    from_left = lax.ppermute(latent_own, CELLS, up)
    from_right = lax.ppermute(latent_own, CELLS, down)

    own_count = counts[cell_index]
    left_count = jnp.where(cell_index > 0, counts[jnp.maximum(cell_index - 1, 0)], 0)
    right_count = jnp.where(
        cell_index < cell_count - 1, counts[jnp.minimum(cell_index + 1, cell_count - 1)], 0
    )
    scalars = jnp.stack([left_count, own_count, right_count])

    projected, turned = project(latent_own, w_qkv)
    turned_own = core_rows(turned, core)
    turned_other = swap_core(core_rows(turned, 1 - core))
    normed_halo, kcat, vcat, attended, stats, hidden, forecast = forward(
        scalars, from_left, from_right, latent_own, w_qkv, projected, w_out, readout_weight
    )
    near = lax.ppermute(forecast, "x_hi", SWAP)
    qhalo = dot_nn(normed_halo, w_qkv[:, :1024]).astype(BF)
    near, qhalo = lax.optimization_barrier((near, qhalo))
    others = swap_core(jnp.stack([forecast, near]))
    crps_whole, packed, grad, small = score(
        scalars, forecast, near, others, target, attended, hidden, stats, w_out, readout_weight
    )
    crps = lax.dynamic_slice_in_dim(crps_whole, member_index * 32, 32, 1)
    packed_left = lax.ppermute(packed, CELLS, up)
    packed_right = lax.ppermute(packed, CELLS, down)

    dquery = query_grads(scalars, projected, kcat, vcat, grad, packed)
    dquery, packed_left, packed_right = lax.optimization_barrier(
        (dquery, packed_left, packed_right)
    )

    def partial_of(piece):
        return dot_nt(turned_own, piece) + dot_nt(turned_other, swap_core(piece))

    small_sum = core_rows(small, core).astype(F32) + swap_core(
        core_rows(small, 1 - core)
    ).astype(F32)
    first_part = jnp.concatenate([partial_of(dquery), small_sum], axis=1).astype(BF)
    first_part, scalars = lax.optimization_barrier((first_part, scalars))
    first = scatter(first_part)
    pairs = key_grads(
        scalars,
        projected,
        qhalo,
        grad,
        packed,
        packed_left,
        packed_right,
        w_out,
        readout_weight,
    )
    second_part = partial_of(pairs.reshape(2048, BLOCK)).astype(BF)
    second_part, first = lax.optimization_barrier((second_part, first))
    second = add_up(scatter(second_part))
    first = add_up(first)
    grad_out = lax.dot_general(
        first[:, 1024:1152],
        readout_weight.astype(F32),
        (((1,), (1,)), ((), ())),
        precision=lax.Precision.HIGHEST,
        preferred_element_type=F32,
    )
    grads = jnp.concatenate([first[:, :1024], second, grad_out, first[:, 1152:]], axis=1)
    return (crps, grads)


def solution(mesh):
    fine = jax.sharding.Mesh(mesh.devices.reshape(2, 2, 4, 2, 4), AXES)
    placed = (P(MEMBER, CELLS, None), P(), P(), P(), P(), P(CELLS, None))
    return jax.shard_map(
        per_device,
        mesh=fine,
        in_specs=placed,
        out_specs=(P(CELLS, MEMBER), P(MEMBER + CELLS, None)),
        check_vma=False,
    )
```

```python
import functools

import jax
import jax.numpy as jnp
import numpy as np
from jax import lax
from jax.experimental import pallas as pl
from jax.experimental.pallas import tpu as pltpu
from jax.sharding import PartitionSpec as P

HEADS = 16
WIN = 256
BLOCK = 256
WIDTH = 256
HEAD_WIDTH = 64
PAIR = 128
NEVER = -1e30

alpha_fair = 0.95
smooth_width = 0.0625

BF = jnp.bfloat16
F32 = jnp.float32


def smooth_abs(values):
    return jnp.sqrt(values * values + smooth_width)


def smooth_sign(values):
    return values * lax.rsqrt(values * values + smooth_width)


def layer_norm(latent_rows):
    values = latent_rows.astype(F32)
    center = values - jnp.mean(values, axis=-1, keepdims=True)
    spread = jnp.mean(center * center, axis=-1, keepdims=True)
    return (center * lax.rsqrt(spread + 1e-05)).astype(BF)


def dot_nn(left, right):
    return lax.dot_general(left, right, (((1,), (0,)), ((), ())), preferred_element_type=F32)


def dot_nt(left, right):
    return lax.dot_general(left, right, (((1,), (1,)), ((), ())), preferred_element_type=F32)


def dot_tn(left, right):
    return lax.dot_general(left, right, (((0,), (0,)), ((), ())), preferred_element_type=F32)


def iota(shape, axis):
    return lax.broadcasted_iota(jnp.int32, shape, axis)


FREE = pl.CostEstimate(flops=0, bytes_accessed=0, transcendentals=0)
HBM = pl.BlockSpec(memory_space=pltpu.HBM)


def fetches(weight_ref, buffer, arrived, width, first):
    return [
        pltpu.make_async_copy(
            weight_ref.at[:, pl.ds(first + place * width, width)],
            buffer.at[place],
            arrived.at[place],
        )
        for place in range(buffer.shape[0])
    ]


def fetch_one(weight_ref, buffer, arrived, width, first, place):
    start = pl.multiple_of(first + place * width, width)
    return pltpu.make_async_copy(
        weight_ref.at[:, pl.ds(start, width)], buffer.at[place], arrived.at[place]
    )


def project_kernel(latent_ref, weight_ref, projected_ref, turned_ref, normed, buffer, arrived):
    step = pl.program_id(0)

    @pl.when(step == 0)
    def _():
        for copy in fetches(weight_ref, buffer, arrived, 512, 0):
            copy.start()
        normed[...] = layer_norm(latent_ref[...])
        turned_ref[...] = normed[...].T

    fetch_one(weight_ref, buffer, arrived, 512, 0, step).wait()
    projected_ref[...] = dot_nn(normed[...], buffer[step]).astype(BF)


def project(latent_own, w_qkv):
    rows, width = latent_own.shape
    return pl.pallas_call(
        project_kernel,
        grid=(6,),
        in_specs=[pl.BlockSpec((rows, width), lambda j: (0, 0)), HBM],
        out_specs=[
            pl.BlockSpec((rows, 512), lambda j: (0, j)),
            pl.BlockSpec((width, rows), lambda j: (0, 0)),
        ],
        out_shape=[
            jax.ShapeDtypeStruct((rows, 3 * width), BF),
            jax.ShapeDtypeStruct((width, rows), BF),
        ],
        scratch_shapes=[
            pltpu.VMEM((rows, width), BF),
            pltpu.VMEM((6, width, 512), BF),
            pltpu.SemaphoreType.DMA((6,)),
        ],
        compiler_params=pltpu.CompilerParams(vmem_limit_bytes=16 * 1024 * 1024),
        cost_estimate=pl.CostEstimate(
            flops=2 * rows * width * width * 4, bytes_accessed=8 << 20, transcendentals=0
        ),
    )(latent_own, w_qkv)


def halo_query_kernel(normed_ref, weight_ref, out_ref, buffer, arrived):
    step = pl.program_id(0)

    @pl.when(step == 0)
    def _():
        for copy in fetches(weight_ref, buffer, arrived, 256, 0):
            copy.start()

    fetch_one(weight_ref, buffer, arrived, 256, 0, step).wait()
    out_ref[...] = dot_nn(normed_ref[...], buffer[step]).astype(BF)


def halo_queries(normed_halo, w_qkv):
    rows, width = normed_halo.shape
    return pl.pallas_call(
        halo_query_kernel,
        grid=(4,),
        in_specs=[pl.BlockSpec((rows, width), lambda j: (0, 0)), HBM],
        out_specs=pl.BlockSpec((rows, 256), lambda j: (0, j)),
        out_shape=jax.ShapeDtypeStruct((rows, width), BF),
        scratch_shapes=[
            pltpu.VMEM((4, width, 256), BF),
            pltpu.SemaphoreType.DMA((4,)),
        ],
        compiler_params=pltpu.CompilerParams(vmem_limit_bytes=12 * 1024 * 1024),
        cost_estimate=FREE,
    )(normed_halo, w_qkv)


def partial_kernel(
    core_ref, normed_ref, normed_other_ref, piece_ref, other_ref, small_ref, small_other_ref,
    out_ref,
):
    core = core_ref[0]
    for top in range(2):
        rows = slice(top * 256, (top + 1) * 256)
        own = normed_ref[top, core]
        near = normed_other_ref[top, core]
        for first in range(0, piece_ref.shape[0], 512):
            columns = slice(first, first + 512)
            out_ref[rows, columns] = (
                dot_nt(own, piece_ref[columns]) + dot_nt(near, other_ref[columns])
            ).astype(BF)
        if small_ref is not None:
            out_ref[rows, piece_ref.shape[0] :] = (
                small_ref[top, core].astype(F32) + small_other_ref[top, core].astype(F32)
            ).astype(BF)


def plain_partial_kernel(core_ref, normed_ref, normed_other_ref, piece_ref, other_ref, out_ref):
    partial_kernel(
        core_ref, normed_ref, normed_other_ref, piece_ref, other_ref, None, None, out_ref
    )


def partial_sums(core, turned, turned_other, piece, other, smalls=()):
    by_core = lambda values: values.reshape(2, 2, 256, 256)
    vmem = pl.BlockSpec(memory_space=pltpu.VMEM)
    columns = piece.shape[0] + 256 * (len(smalls) // 2)
    return pl.pallas_call(
        partial_kernel if smalls else plain_partial_kernel,
        in_specs=[pl.BlockSpec(memory_space=pltpu.SMEM)] + [vmem] * (4 + len(smalls)),
        out_specs=vmem,
        out_shape=jax.ShapeDtypeStruct((512, columns), BF),
        compiler_params=pltpu.CompilerParams(vmem_limit_bytes=12 * 1024 * 1024),
        cost_estimate=FREE,
    )(
        core.astype(jnp.int32).reshape(1),
        by_core(turned),
        by_core(turned_other),
        piece,
        other,
        *(by_core(small) for small in smalls),
    )


def spare_lane(shape):
    lane = iota(shape, len(shape) - 1)
    return lane % HEAD_WIDTH


def key_fill(count_pieces):
    fills = []
    for count, rows in count_pieces:
        spare = spare_lane((rows, PAIR))
        bias = jnp.where(iota((rows, PAIR), 0) < count, 0.0, NEVER)
        fills.append(
            jnp.where(spare < 3, 1.0, jnp.where(spare == 3, bias, 0.0)).astype(BF)
        )
    return jnp.concatenate(fills, axis=0)


def stat_spread(step, offset):
    shape = (128, WIDTH)
    lane = iota(shape, 1)
    head = step * 4 + 2 * (lane // PAIR) + jnp.where(lane % PAIR < HEAD_WIDTH, 1, 0)
    term = lane % HEAD_WIDTH
    chosen = (term < 3) & (iota(shape, 0) == term * 32 + offset + head)
    return jnp.where(chosen, -1.0, 0.0).astype(BF)


def keep_band(window, fill):
    shape = (128, 128)
    apart = iota(shape, 0) - iota(shape, 1)
    first = jnp.where(apart >= 0, window[:128], fill)
    last = jnp.where(apart <= 0, window[512:], fill)
    return first, window[128:512], last


def forward_kernel(
    counts_ref,
    left_ref,
    right_ref,
    latent_ref,
    weight_ref,
    q_ref,
    k_ref,
    v_ref,
    w_out_ref,
    readout_ref,
    normed_ref,
    kcat_ref,
    vcat_ref,
    attended_ref,
    stats_ref,
    hidden_ref,
    forecast_ref,
    probs,
    stat_rows,
    buffer,
    arrived,
):
    step = pl.program_id(0)

    @pl.when(step == 0)
    def _():
        copies = fetches(weight_ref, buffer, arrived, WIDTH, 1024)
        for place in (0, 4, 1, 5, 2, 6, 3, 7):
            copies[place].start()
        normed_ref[:WIN] = layer_norm(left_ref[...])
        normed_ref[WIN:] = layer_norm(right_ref[...])
        probs[...] = jnp.zeros_like(probs)

    fetch_one(weight_ref, buffer, arrived, WIDTH, 1024, step).wait()
    fetch_one(weight_ref, buffer, arrived, WIDTH, 1024, step + 4).wait()
    khalo = dot_nn(normed_ref[...], buffer[step]).astype(BF)
    kcat_ref[:WIN] = khalo[:WIN]
    kcat_ref[WIN : WIN + BLOCK] = k_ref[...]
    kcat_ref[WIN + BLOCK :] = khalo[WIN:]
    vhalo = dot_nn(normed_ref[...], buffer[step + 4]).astype(BF)
    vcat_ref[:WIN] = vhalo[:WIN]
    vcat_ref[WIN : WIN + BLOCK] = v_ref[...]
    vcat_ref[WIN + BLOCK :] = vhalo[WIN:]
    fill = key_fill([(counts_ref[0], WIN), (counts_ref[1], BLOCK), (counts_ref[2], WIN)])
    low_q = iota((BLOCK, PAIR), 1) < HEAD_WIDTH
    low_k = iota(fill.shape, 1) < HEAD_WIDTH
    query_fill = (spare_lane((BLOCK, PAIR)) == 3).astype(BF)
    scores, turned = [], []
    for pair in range(2):
        columns = slice(pair * PAIR, (pair + 1) * PAIR)
        q_pair = q_ref[:, columns] * jnp.asarray(HEAD_WIDTH ** (-0.5), BF)
        k_pair = kcat_ref[:, columns]
        turned.append(vcat_ref[:, columns].T)
        for half in range(2):
            if half == 0:
                q_head = jnp.where(low_q, q_pair, query_fill)
                k_head = jnp.where(low_k, k_pair, fill)
            else:
                q_head = jnp.where(low_q, query_fill, q_pair)
                k_head = jnp.where(low_k, fill, k_pair)
            scores.append(dot_nt(k_head, q_head))
    scales = []
    for slot in range(4):
        totals, levels = [], []
        for tile in range(2):
            rows = slice(tile * 128, tile * 128 + 640)
            lanes = slice(tile * 128, tile * 128 + 128)
            first, middle, last = keep_band(scores[slot][rows, lanes], NEVER)
            top = jnp.maximum(
                jnp.max(middle, axis=0, keepdims=True),
                jnp.max(jnp.maximum(first, last), axis=0, keepdims=True),
            )
            first = jnp.exp(first - top)
            middle = jnp.exp(middle - top)
            last = jnp.exp(last - top)
            total = jnp.sum(middle, axis=0, keepdims=True) + jnp.sum(
                first + last, axis=0, keepdims=True
            )
            start = tile * 128
            probs[slot, start : start + 128, lanes] = first.astype(BF)
            probs[slot, start + 128 : start + 512, lanes] = middle.astype(BF)
            probs[slot, start + 512 : start + 640, lanes] = last.astype(BF)
            totals.append(total)
            levels.append(top + jnp.log(total))
        scales.append(1.0 / jnp.concatenate(totals, axis=1))
        stat_rows[pl.ds(step * 4 + slot, 1), :] = jnp.concatenate(levels, axis=1)
    for pair in range(2):
        halves = []
        for half in range(2):
            slot = pair * 2 + half
            lanes = slice(half * HEAD_WIDTH, (half + 1) * HEAD_WIDTH)
            halves.append(dot_nn(turned[pair][lanes], probs[slot]) * scales[slot])
        start = pl.multiple_of(step * WIDTH + pair * PAIR, PAIR)
        attended_ref[:, pl.ds(start, PAIR)] = jnp.concatenate(halves, axis=0).T

    @pl.when(step == 3)
    def _():
        mixed = dot_nn(attended_ref[...].astype(BF), w_out_ref[...])
        hidden = (latent_ref[...].astype(F32) + mixed).astype(BF)
        hidden_ref[...] = hidden
        forecast_ref[...] = dot_nn(hidden, readout_ref[...])
        stat_rows[HEADS:] = jnp.zeros((128 - HEADS, BLOCK), F32)
        stats_ref[...] = stat_rows[...].T


def forward(counts, left, right, latent_own, w_qkv, projected, w_out, readout_weight):
    whole = lambda *shape: pl.BlockSpec(shape, lambda j: (0, 0))
    part = lambda rows, first: pl.BlockSpec((rows, WIDTH), lambda j: (0, first + j))
    window = 2 * WIN + BLOCK
    return pl.pallas_call(
        forward_kernel,
        grid=(4,),
        in_specs=[
            pl.BlockSpec(memory_space=pltpu.SMEM),
            whole(WIN, 1024),
            whole(WIN, 1024),
            whole(BLOCK, 1024),
            HBM,
            part(BLOCK, 0),
            part(BLOCK, 4),
            part(BLOCK, 8),
            whole(1024, 1024),
            whole(1024, 128),
        ],
        out_specs=[
            whole(2 * WIN, 1024),
            part(window, 0),
            part(window, 0),
            whole(BLOCK, 1024),
            whole(BLOCK, 128),
            whole(BLOCK, 1024),
            whole(BLOCK, 128),
        ],
        out_shape=[
            jax.ShapeDtypeStruct((2 * WIN, 1024), BF),
            jax.ShapeDtypeStruct((window, 1024), BF),
            jax.ShapeDtypeStruct((window, 1024), BF),
            jax.ShapeDtypeStruct((BLOCK, 1024), F32),
            jax.ShapeDtypeStruct((BLOCK, 128), F32),
            jax.ShapeDtypeStruct((BLOCK, 1024), BF),
            jax.ShapeDtypeStruct((BLOCK, 128), F32),
        ],
        scratch_shapes=[
            pltpu.VMEM((4, window, BLOCK), BF),
            pltpu.VMEM((128, BLOCK), F32),
            pltpu.VMEM((8, 1024, WIDTH), BF),
            pltpu.SemaphoreType.DMA((8,)),
        ],
        compiler_params=pltpu.CompilerParams(vmem_limit_bytes=28 * 1024 * 1024),
        cost_estimate=pl.CostEstimate(
            flops=6 << 30, bytes_accessed=12 << 20, transcendentals=3 << 20
        ),
    )(
        counts,
        left,
        right,
        latent_own,
        w_qkv,
        projected,
        projected,
        projected,
        w_out,
        readout_weight,
    )


def score_kernel(
    counts_ref,
    own_ref,
    near_ref,
    others_ref,
    target_ref,
    attended_ref,
    hidden_ref,
    stats_ref,
    w_out_ref,
    readout_ref,
    crps_ref,
    packed_ref,
    grad_ref,
    small_ref,
):
    members = 4
    fair_eps = (1.0 - alpha_fair) / members
    coefficient = (1.0 - fair_eps) / (members * (members - 1))
    valid = (iota((BLOCK, 1), 0) < counts_ref[1]).astype(F32)
    own = own_ref[...]
    forecasts = [own, near_ref[...], others_ref[0], others_ref[1]]
    target = target_ref[...]
    error = jnp.zeros_like(target)
    for forecast in forecasts:
        error += smooth_abs(forecast - target)
    spread = jnp.full_like(target, members * smooth_width**0.5)
    for first in range(members):
        for second in range(first + 1, members):
            spread += 2.0 * smooth_abs(forecasts[first] - forecasts[second])
    crps_ref[...] = valid * (error / members - 0.5 * coefficient * spread)
    pull = jnp.zeros_like(target)
    for other in forecasts[1:]:
        pull += smooth_sign(own - other)
    slope = (
        valid / 128 * (smooth_sign(own - target) / members - coefficient * pull)
    ).astype(BF)
    dhidden = dot_nt(slope, readout_ref[...]).astype(BF)
    dattended = dot_nt(dhidden, w_out_ref[...]).astype(BF)
    grad_ref[...] = dattended
    attended = attended_ref[...]
    product = dattended.astype(F32) * attended
    high = product.astype(BF)
    low = (product - high.astype(F32)).astype(BF)
    pick = (iota((1024, 128), 0) // HEAD_WIDTH + HEADS == iota((1024, 128), 1)).astype(BF)
    stats = stats_ref[...] + dot_nn(high, pick) + dot_nn(low, pick)
    first = stats.astype(BF)
    rest = stats - first.astype(F32)
    second = rest.astype(BF)
    third = (rest - second.astype(F32)).astype(BF)
    terms = jnp.zeros((BLOCK, 128), F32)
    for place, term in enumerate((first, second, third)):
        shift = (iota((128, 128), 0) + 32 * place == iota((128, 128), 1)) & (
            iota((128, 128), 0) < 32
        )
        terms += dot_nn(term, shift.astype(BF))
    packed_ref[:, :128] = slope
    packed_ref[:, 128:] = terms.astype(BF)
    small_ref[:, :128] = dot_tn(attended.astype(BF), slope).astype(BF)
    small_ref[:, 128:] = dot_tn(hidden_ref[...], slope).astype(BF)


def score(counts, own, near, others, target, attended, hidden, stats, w_out, readout_weight):
    vmem = pl.BlockSpec(memory_space=pltpu.VMEM)
    return pl.pallas_call(
        score_kernel,
        in_specs=[pl.BlockSpec(memory_space=pltpu.SMEM)] + [vmem] * 9,
        out_specs=[vmem] * 4,
        out_shape=[
            jax.ShapeDtypeStruct((BLOCK, 128), F32),
            jax.ShapeDtypeStruct((BLOCK, 256), BF),
            jax.ShapeDtypeStruct((BLOCK, 1024), BF),
            jax.ShapeDtypeStruct((1024, 256), BF),
        ],
        compiler_params=pltpu.CompilerParams(vmem_limit_bytes=12 * 1024 * 1024),
    )(counts, own, near, others, target, attended, hidden, stats, w_out, readout_weight)


def query_kernel(
    counts_ref, q_ref, kcat_ref, vcat_ref, grad_ref, packed_ref, dq_ref, dscores
):
    step = pl.program_id(0)

    @pl.when(step == 0)
    def _():
        dscores[...] = jnp.zeros_like(dscores)

    fill = key_fill([(counts_ref[0], WIN), (counts_ref[1], BLOCK), (counts_ref[2], WIN)])
    value_fill = (spare_lane(fill.shape) < 3).astype(BF)
    low_q = iota((BLOCK, PAIR), 1) < HEAD_WIDTH
    low_k = iota(fill.shape, 1) < HEAD_WIDTH
    terms = packed_ref[:, 128:]
    ones = (spare_lane((BLOCK, WIDTH)) == 3).astype(F32)
    q_fill = (dot_nn(terms, stat_spread(step, 0)) + ones).astype(BF)
    g_fill = dot_nn(terms, stat_spread(step, HEADS)).astype(BF)
    turned = []
    for pair in range(2):
        columns = slice(pair * PAIR, (pair + 1) * PAIR)
        q_pair = q_ref[:, columns] * jnp.asarray(HEAD_WIDTH ** (-0.5), BF)
        g_pair = grad_ref[:, columns]
        k_pair = kcat_ref[:, columns]
        v_pair = vcat_ref[:, columns]
        k_turned = k_pair.T
        for half in range(2):
            slot = pair * 2 + half
            pick_q = low_q if half == 0 else ~low_q
            pick_k = low_k if half == 0 else ~low_k
            q_head = jnp.where(pick_q, q_pair, q_fill[:, columns])
            g_head = jnp.where(pick_q, g_pair, g_fill[:, columns])
            k_head = jnp.where(pick_k, k_pair, fill)
            v_head = jnp.where(pick_k, v_pair, value_fill)
            scores = dot_nt(k_head, q_head)
            change = dot_nt(v_head, g_head)
            for tile in range(2):
                rows = slice(tile * 128, tile * 128 + 640)
                lanes = slice(tile * 128, tile * 128 + 128)
                ends = jnp.exp(scores[rows, lanes]) * change[rows, lanes]
                first, middle, last = keep_band(ends, 0.0)
                start = tile * 128
                dscores[slot, start : start + 128, lanes] = first.astype(BF)
                dscores[slot, start + 128 : start + 512, lanes] = middle.astype(BF)
                dscores[slot, start + 512 : start + 640, lanes] = last.astype(BF)
            turned.append(k_turned[half * HEAD_WIDTH : (half + 1) * HEAD_WIDTH])
    for slot in range(4):
        dquery = dot_nn(turned[slot], dscores[slot]) * HEAD_WIDTH ** (-0.5)
        dq_ref[slot * HEAD_WIDTH : (slot + 1) * HEAD_WIDTH] = dquery.astype(BF)


def query_grads(counts, projected, kcat, vcat, grad, packed):
    part = lambda rows, first: pl.BlockSpec((rows, WIDTH), lambda j: (0, first + j))
    window = 2 * WIN + BLOCK
    return pl.pallas_call(
        query_kernel,
        grid=(4,),
        in_specs=[
            pl.BlockSpec(memory_space=pltpu.SMEM),
            part(BLOCK, 0),
            part(window, 0),
            part(window, 0),
            part(BLOCK, 0),
            pl.BlockSpec((BLOCK, 256), lambda j: (0, 0)),
        ],
        out_specs=pl.BlockSpec((WIDTH, BLOCK), lambda j: (j, 0)),
        out_shape=jax.ShapeDtypeStruct((1024, BLOCK), BF),
        scratch_shapes=[pltpu.VMEM((4, window, BLOCK), BF)],
        compiler_params=pltpu.CompilerParams(vmem_limit_bytes=12 * 1024 * 1024),
        cost_estimate=pl.CostEstimate(
            flops=6 << 30, bytes_accessed=5 << 20, transcendentals=3 << 20
        ),
    )(counts, projected, kcat, vcat, grad, packed)


def key_kernel(
    counts_ref,
    q_ref,
    k_ref,
    v_ref,
    qhalo_ref,
    grad_ref,
    own_ref,
    left_ref,
    right_ref,
    w_out_ref,
    readout_ref,
    out_ref,
    probs,
    dscores,
    dhidden,
):
    step = pl.program_id(0)

    @pl.when(step == 0)
    def _():
        probs[...] = jnp.zeros_like(probs)
        dscores[...] = jnp.zeros_like(dscores)
        dhidden[:WIN] = dot_nt(left_ref[:, :128], readout_ref[...]).astype(BF)
        dhidden[WIN:] = dot_nt(right_ref[:, :128], readout_ref[...]).astype(BF)

    ghalo = dot_nt(dhidden[...], w_out_ref[...]).astype(BF)
    terms = jnp.concatenate(
        [left_ref[:, 128:], own_ref[:, 128:], right_ref[:, 128:]], axis=0
    )
    window = terms.shape[0]
    fill = key_fill([(counts_ref[1], BLOCK)])
    value_fill = (spare_lane(fill.shape) < 3).astype(BF)
    low_q = iota((window, PAIR), 1) < HEAD_WIDTH
    low_k = iota(fill.shape, 1) < HEAD_WIDTH
    ones = (spare_lane((window, WIDTH)) == 3).astype(F32)
    q_fill = (dot_nn(terms, stat_spread(step, 0)) + ones).astype(BF)
    g_fill = dot_nn(terms, stat_spread(step, HEADS)).astype(BF)
    turned = []
    for pair in range(2):
        columns = slice(pair * PAIR, (pair + 1) * PAIR)
        q_pair = jnp.concatenate(
            [qhalo_ref[:WIN, columns], q_ref[:, columns], qhalo_ref[WIN:, columns]], axis=0
        ) * jnp.asarray(HEAD_WIDTH ** (-0.5), BF)
        g_pair = jnp.concatenate(
            [ghalo[:WIN, columns], grad_ref[:, columns], ghalo[WIN:, columns]], axis=0
        )
        k_pair = k_ref[:, columns]
        v_pair = v_ref[:, columns]
        q_turned = q_pair.T
        g_turned = g_pair.T
        for half in range(2):
            slot = pair * 2 + half
            pick_q = low_q if half == 0 else ~low_q
            pick_k = low_k if half == 0 else ~low_k
            q_head = jnp.where(pick_q, q_pair, q_fill[:, columns])
            g_head = jnp.where(pick_q, g_pair, g_fill[:, columns])
            k_head = jnp.where(pick_k, k_pair, fill)
            v_head = jnp.where(pick_k, v_pair, value_fill)
            scores = dot_nt(q_head, k_head)
            change = dot_nt(g_head, v_head)
            for tile in range(2):
                rows = slice(tile * 128, tile * 128 + 640)
                lanes = slice(tile * 128, tile * 128 + 128)
                weight = keep_band(jnp.exp(scores[rows, lanes]), 0.0)
                moved = change[rows, lanes]
                start = tile * 128
                for piece, (low, high) in zip(weight, ((0, 128), (128, 512), (512, 640))):
                    place = slice(start + low, start + high)
                    probs[slot, place, lanes] = piece.astype(BF)
                    dscores[slot, place, lanes] = (piece * moved[low:high]).astype(BF)
            lanes = slice(half * HEAD_WIDTH, (half + 1) * HEAD_WIDTH)
            turned.append((q_turned[lanes], g_turned[lanes]))
    for slot in range(4):
        place = slice(slot * HEAD_WIDTH, (slot + 1) * HEAD_WIDTH)
        out_ref[0, place] = dot_nn(turned[slot][0], dscores[slot]).astype(BF)
        out_ref[1, place] = dot_nn(turned[slot][1], probs[slot]).astype(BF)


def key_grads(counts, projected, qhalo, grad, own, left, right, w_out, readout_weight):
    part = lambda rows, first: pl.BlockSpec((rows, WIDTH), lambda j: (0, first + j))
    whole = lambda *shape: pl.BlockSpec(shape, lambda j: (0, 0))
    window = 2 * WIN + BLOCK
    return pl.pallas_call(
        key_kernel,
        grid=(4,),
        in_specs=[
            pl.BlockSpec(memory_space=pltpu.SMEM),
            part(BLOCK, 0),
            part(BLOCK, 4),
            part(BLOCK, 8),
            part(2 * WIN, 0),
            part(BLOCK, 0),
            whole(BLOCK, 256),
            whole(BLOCK, 256),
            whole(BLOCK, 256),
            pl.BlockSpec((WIDTH, 1024), lambda j: (j, 0)),
            whole(1024, 128),
        ],
        out_specs=pl.BlockSpec((2, WIDTH, BLOCK), lambda j: (0, j, 0)),
        out_shape=jax.ShapeDtypeStruct((2, 1024, BLOCK), BF),
        scratch_shapes=[
            pltpu.VMEM((4, window, BLOCK), BF),
            pltpu.VMEM((4, window, BLOCK), BF),
            pltpu.VMEM((2 * WIN, 1024), BF),
        ],
        compiler_params=pltpu.CompilerParams(vmem_limit_bytes=18 * 1024 * 1024),
        cost_estimate=FREE,
    )(
        counts,
        projected,
        projected,
        projected,
        qhalo,
        grad,
        own,
        left,
        right,
        w_out,
        readout_weight,
    )


AXES = ("x_hi", "core", "y", "x_lo", "z")
MEMBER = ("x_hi", "core")
CELLS = ("y", "x_lo", "z")
CHIPS = ("x_hi", "y", "x_lo", "z")
SWAP = [(0, 1), (1, 0)]


def swap_core(values):
    return lax.ppermute(values, "core", SWAP)


def scatter(partial):
    columns = partial.shape[1]
    return lax.all_to_all(partial.reshape(64, 8, columns), CHIPS, split_axis=0, concat_axis=0)


def add_up(pieces):
    return jnp.sum(pieces.astype(F32), axis=0)


def per_device(latent, counts, w_qkv, w_out, readout_weight, target):
    latent_own = latent[0]
    cell_count = 32
    cell_index = lax.axis_index(CELLS)
    member_index = lax.axis_index(MEMBER)
    core = lax.axis_index("core")
    up = [(i, i + 1) for i in range(cell_count - 1)]
    down = [(i + 1, i) for i in range(cell_count - 1)]
    from_left = lax.ppermute(latent_own, CELLS, up)
    from_right = lax.ppermute(latent_own, CELLS, down)

    own_count = counts[cell_index]
    left_count = jnp.where(cell_index > 0, counts[jnp.maximum(cell_index - 1, 0)], 0)
    right_count = jnp.where(
        cell_index < cell_count - 1, counts[jnp.minimum(cell_index + 1, cell_count - 1)], 0
    )
    scalars = jnp.stack([left_count, own_count, right_count])

    projected, turned = project(latent_own, w_qkv)
    turned_other = swap_core(turned)
    normed_halo, kcat, vcat, attended, stats, hidden, forecast = forward(
        scalars, from_left, from_right, latent_own, w_qkv, projected, w_out, readout_weight
    )
    near = lax.ppermute(forecast, "x_hi", SWAP)
    qhalo = halo_queries(normed_halo, w_qkv)
    near, qhalo = lax.optimization_barrier((near, qhalo))
    others = swap_core(jnp.stack([forecast, near]))
    crps_whole, packed, grad, small = score(
        scalars, forecast, near, others, target, attended, hidden, stats, w_out, readout_weight
    )
    crps = lax.dynamic_slice_in_dim(crps_whole, member_index * 32, 32, 1)
    packed_left = lax.ppermute(packed, CELLS, up)
    packed_right = lax.ppermute(packed, CELLS, down)

    dquery = query_grads(scalars, projected, kcat, vcat, grad, packed)
    dquery, packed_left, packed_right = lax.optimization_barrier(
        (dquery, packed_left, packed_right)
    )

    first_part = partial_sums(
        core, turned, turned_other, dquery, swap_core(dquery), (small, swap_core(small))
    )
    first_part, scalars = lax.optimization_barrier((first_part, scalars))
    first = scatter(first_part)
    pairs = key_grads(
        scalars,
        projected,
        qhalo,
        grad,
        packed,
        packed_left,
        packed_right,
        w_out,
        readout_weight,
    )
    pairs = pairs.reshape(2048, BLOCK)
    second_part = partial_sums(core, turned, turned_other, pairs, swap_core(pairs))
    second_part, first = lax.optimization_barrier((second_part, first))
    second = add_up(scatter(second_part))
    first = add_up(first)
    grad_out = lax.dot_general(
        first[:, 1024:1152],
        readout_weight.astype(F32),
        (((1,), (1,)), ((), ())),
        precision=lax.Precision.HIGHEST,
        preferred_element_type=F32,
    )
    grads = jnp.concatenate([first[:, :1024], second, grad_out, first[:, 1152:]], axis=1)
    return (crps, grads)


def solution(mesh):
    fine = jax.sharding.Mesh(mesh.devices.reshape(2, 2, 4, 2, 4), AXES)
    placed = (P(MEMBER, CELLS, None), P(), P(), P(), P(), P(CELLS, None))
    return jax.shard_map(
        per_device,
        mesh=fine,
        in_specs=placed,
        out_specs=(P(CELLS, MEMBER), P(MEMBER + CELLS, None)),
        check_vma=False,
    )
```

```python
import functools

import jax
import jax.numpy as jnp
import numpy as np
from jax import lax
from jax.experimental import pallas as pl
from jax.experimental.pallas import tpu as pltpu
from jax.sharding import PartitionSpec as P

HEADS = 16
WIN = 256
BLOCK = 256
WIDTH = 256
HEAD_WIDTH = 64
PAIR = 128
NEVER = -1e30

alpha_fair = 0.95
smooth_width = 0.0625

BF = jnp.bfloat16
F32 = jnp.float32


def smooth_abs(values):
    return jnp.sqrt(values * values + smooth_width)


def smooth_sign(values):
    return values * lax.rsqrt(values * values + smooth_width)


def layer_norm(latent_rows):
    values = latent_rows.astype(F32)
    center = values - jnp.mean(values, axis=-1, keepdims=True)
    spread = jnp.mean(center * center, axis=-1, keepdims=True)
    return (center * lax.rsqrt(spread + 1e-05)).astype(BF)


def dot_nn(left, right):
    return lax.dot_general(left, right, (((1,), (0,)), ((), ())), preferred_element_type=F32)


def dot_nt(left, right):
    return lax.dot_general(left, right, (((1,), (1,)), ((), ())), preferred_element_type=F32)


def dot_tn(left, right):
    return lax.dot_general(left, right, (((0,), (0,)), ((), ())), preferred_element_type=F32)


def iota(shape, axis):
    return lax.broadcasted_iota(jnp.int32, shape, axis)


FREE = pl.CostEstimate(flops=0, bytes_accessed=0, transcendentals=0)
HBM = pl.BlockSpec(memory_space=pltpu.HBM)


def fetches(weight_ref, buffer, arrived, width, first):
    return [
        pltpu.make_async_copy(
            weight_ref.at[:, pl.ds(first + place * width, width)],
            buffer.at[place],
            arrived.at[place],
        )
        for place in range(buffer.shape[0])
    ]


def fetch_one(weight_ref, buffer, arrived, width, first, place):
    start = pl.multiple_of(first + place * width, width)
    return pltpu.make_async_copy(
        weight_ref.at[:, pl.ds(start, width)], buffer.at[place], arrived.at[place]
    )


def project_kernel(latent_ref, weight_ref, projected_ref, turned_ref, normed, buffer, arrived):
    step = pl.program_id(0)

    @pl.when(step == 0)
    def _():
        for copy in fetches(weight_ref, buffer, arrived, 512, 0):
            copy.start()
        normed[...] = layer_norm(latent_ref[...])
        turned_ref[...] = normed[...].T

    fetch_one(weight_ref, buffer, arrived, 512, 0, step).wait()
    projected_ref[...] = dot_nn(normed[...], buffer[step]).astype(BF)


def project(latent_own, w_qkv):
    rows, width = latent_own.shape
    return pl.pallas_call(
        project_kernel,
        grid=(6,),
        in_specs=[pl.BlockSpec((rows, width), lambda j: (0, 0)), HBM],
        out_specs=[
            pl.BlockSpec((rows, 512), lambda j: (0, j)),
            pl.BlockSpec((width, rows), lambda j: (0, 0)),
        ],
        out_shape=[
            jax.ShapeDtypeStruct((rows, 3 * width), BF),
            jax.ShapeDtypeStruct((width, rows), BF),
        ],
        scratch_shapes=[
            pltpu.VMEM((rows, width), BF),
            pltpu.VMEM((6, width, 512), BF),
            pltpu.SemaphoreType.DMA((6,)),
        ],
        compiler_params=pltpu.CompilerParams(vmem_limit_bytes=56 * 1024 * 1024),
        cost_estimate=pl.CostEstimate(
            flops=2 * rows * width * width * 4, bytes_accessed=8 << 20, transcendentals=0
        ),
    )(latent_own, w_qkv)


def halo_query_kernel(normed_ref, weight_ref, out_ref, buffer, arrived):
    step = pl.program_id(0)

    @pl.when(step == 0)
    def _():
        for copy in fetches(weight_ref, buffer, arrived, 256, 0):
            copy.start()

    fetch_one(weight_ref, buffer, arrived, 256, 0, step).wait()
    out_ref[...] = dot_nn(normed_ref[...], buffer[step]).astype(BF)


def halo_queries(normed_halo, w_qkv):
    rows, width = normed_halo.shape
    return pl.pallas_call(
        halo_query_kernel,
        grid=(4,),
        in_specs=[pl.BlockSpec((rows, width), lambda j: (0, 0)), HBM],
        out_specs=pl.BlockSpec((rows, 256), lambda j: (0, j)),
        out_shape=jax.ShapeDtypeStruct((rows, width), BF),
        scratch_shapes=[
            pltpu.VMEM((4, width, 256), BF),
            pltpu.SemaphoreType.DMA((4,)),
        ],
        compiler_params=pltpu.CompilerParams(vmem_limit_bytes=52 * 1024 * 1024),
        cost_estimate=FREE,
    )(normed_halo, w_qkv)


def partial_kernel(
    core_ref, normed_ref, normed_other_ref, piece_ref, other_ref, small_ref, small_other_ref,
    out_ref,
):
    core = core_ref[0]
    for top in range(2):
        rows = slice(top * 256, (top + 1) * 256)
        own = normed_ref[top, core]
        near = normed_other_ref[top, core]
        for first in range(0, piece_ref.shape[0], 512):
            columns = slice(first, first + 512)
            out_ref[rows, columns] = (
                dot_nt(own, piece_ref[columns]) + dot_nt(near, other_ref[columns])
            ).astype(BF)
        if small_ref is not None:
            out_ref[rows, piece_ref.shape[0] :] = (
                small_ref[top, core].astype(F32) + small_other_ref[top, core].astype(F32)
            ).astype(BF)


def plain_partial_kernel(core_ref, normed_ref, normed_other_ref, piece_ref, other_ref, out_ref):
    partial_kernel(
        core_ref, normed_ref, normed_other_ref, piece_ref, other_ref, None, None, out_ref
    )


def partial_sums(core, turned, turned_other, piece, other, smalls=()):
    by_core = lambda values: values.reshape(2, 2, 256, 256)
    vmem = pl.BlockSpec(memory_space=pltpu.VMEM)
    columns = piece.shape[0] + 256 * (len(smalls) // 2)
    return pl.pallas_call(
        partial_kernel if smalls else plain_partial_kernel,
        in_specs=[pl.BlockSpec(memory_space=pltpu.SMEM)] + [vmem] * (4 + len(smalls)),
        out_specs=vmem,
        out_shape=jax.ShapeDtypeStruct((512, columns), BF),
        compiler_params=pltpu.CompilerParams(vmem_limit_bytes=12 * 1024 * 1024),
        cost_estimate=FREE,
    )(
        core.astype(jnp.int32).reshape(1),
        by_core(turned),
        by_core(turned_other),
        piece,
        other,
        *(by_core(small) for small in smalls),
    )


def spare_lane(shape):
    lane = iota(shape, len(shape) - 1)
    return lane % HEAD_WIDTH


def key_fill(count_pieces):
    fills = []
    for count, rows in count_pieces:
        spare = spare_lane((rows, PAIR))
        bias = jnp.where(iota((rows, PAIR), 0) < count, 0.0, NEVER)
        fills.append(
            jnp.where(spare < 3, 1.0, jnp.where(spare == 3, bias, 0.0)).astype(BF)
        )
    return jnp.concatenate(fills, axis=0)


def stat_spread(step, offset):
    shape = (128, WIDTH)
    lane = iota(shape, 1)
    head = step * 4 + 2 * (lane // PAIR) + jnp.where(lane % PAIR < HEAD_WIDTH, 1, 0)
    term = lane % HEAD_WIDTH
    chosen = (term < 3) & (iota(shape, 0) == term * 32 + offset + head)
    return jnp.where(chosen, -1.0, 0.0).astype(BF)


def keep_band(window, fill):
    shape = (128, 128)
    apart = iota(shape, 0) - iota(shape, 1)
    first = jnp.where(apart >= 0, window[:128], fill)
    last = jnp.where(apart <= 0, window[512:], fill)
    return first, window[128:512], last


def forward_kernel(
    counts_ref,
    left_ref,
    right_ref,
    latent_ref,
    weight_ref,
    q_ref,
    k_ref,
    v_ref,
    w_out_ref,
    readout_ref,
    normed_ref,
    kcat_ref,
    vcat_ref,
    attended_ref,
    stats_ref,
    hidden_ref,
    forecast_ref,
    probs,
    stat_rows,
    buffer,
    arrived,
):
    step = pl.program_id(0)

    @pl.when(step == 0)
    def _():
        copies = fetches(weight_ref, buffer, arrived, WIDTH, 1024)
        for place in (0, 4, 1, 5, 2, 6, 3, 7):
            copies[place].start()
        normed_ref[:WIN] = layer_norm(left_ref[...])
        normed_ref[WIN:] = layer_norm(right_ref[...])
        probs[...] = jnp.zeros_like(probs)

    fetch_one(weight_ref, buffer, arrived, WIDTH, 1024, step).wait()
    fetch_one(weight_ref, buffer, arrived, WIDTH, 1024, step + 4).wait()
    khalo = dot_nn(normed_ref[...], buffer[step]).astype(BF)
    kcat_ref[:WIN] = khalo[:WIN]
    kcat_ref[WIN : WIN + BLOCK] = k_ref[...]
    kcat_ref[WIN + BLOCK :] = khalo[WIN:]
    vhalo = dot_nn(normed_ref[...], buffer[step + 4]).astype(BF)
    vcat_ref[:WIN] = vhalo[:WIN]
    vcat_ref[WIN : WIN + BLOCK] = v_ref[...]
    vcat_ref[WIN + BLOCK :] = vhalo[WIN:]
    fill = key_fill([(counts_ref[0], WIN), (counts_ref[1], BLOCK), (counts_ref[2], WIN)])
    low_q = iota((BLOCK, PAIR), 1) < HEAD_WIDTH
    low_k = iota(fill.shape, 1) < HEAD_WIDTH
    query_fill = (spare_lane((BLOCK, PAIR)) == 3).astype(BF)
    scores, turned = [], []
    for pair in range(2):
        columns = slice(pair * PAIR, (pair + 1) * PAIR)
        q_pair = q_ref[:, columns] * jnp.asarray(HEAD_WIDTH ** (-0.5), BF)
        k_pair = kcat_ref[:, columns]
        turned.append(vcat_ref[:, columns].T)
        for half in range(2):
            if half == 0:
                q_head = jnp.where(low_q, q_pair, query_fill)
                k_head = jnp.where(low_k, k_pair, fill)
            else:
                q_head = jnp.where(low_q, query_fill, q_pair)
                k_head = jnp.where(low_k, fill, k_pair)
            scores.append(dot_nt(k_head, q_head))
    scales = []
    for slot in range(4):
        totals, levels = [], []
        for tile in range(2):
            rows = slice(tile * 128, tile * 128 + 640)
            lanes = slice(tile * 128, tile * 128 + 128)
            first, middle, last = keep_band(scores[slot][rows, lanes], NEVER)
            top = jnp.maximum(
                jnp.max(middle, axis=0, keepdims=True),
                jnp.max(jnp.maximum(first, last), axis=0, keepdims=True),
            )
            first = jnp.exp(first - top)
            middle = jnp.exp(middle - top)
            last = jnp.exp(last - top)
            total = jnp.sum(middle, axis=0, keepdims=True) + jnp.sum(
                first + last, axis=0, keepdims=True
            )
            start = tile * 128
            probs[slot, start : start + 128, lanes] = first.astype(BF)
            probs[slot, start + 128 : start + 512, lanes] = middle.astype(BF)
            probs[slot, start + 512 : start + 640, lanes] = last.astype(BF)
            totals.append(total)
            levels.append(top + jnp.log(total))
        scales.append(1.0 / jnp.concatenate(totals, axis=1))
        stat_rows[pl.ds(step * 4 + slot, 1), :] = jnp.concatenate(levels, axis=1)
    for pair in range(2):
        halves = []
        for half in range(2):
            slot = pair * 2 + half
            lanes = slice(half * HEAD_WIDTH, (half + 1) * HEAD_WIDTH)
            halves.append(dot_nn(turned[pair][lanes], probs[slot]) * scales[slot])
        start = pl.multiple_of(step * WIDTH + pair * PAIR, PAIR)
        attended_ref[:, pl.ds(start, PAIR)] = jnp.concatenate(halves, axis=0).T

    @pl.when(step == 3)
    def _():
        mixed = dot_nn(attended_ref[...].astype(BF), w_out_ref[...])
        hidden = (latent_ref[...].astype(F32) + mixed).astype(BF)
        hidden_ref[...] = hidden
        forecast_ref[...] = dot_nn(hidden, readout_ref[...])
        stat_rows[HEADS:] = jnp.zeros((128 - HEADS, BLOCK), F32)
        stats_ref[...] = stat_rows[...].T


def forward(counts, left, right, latent_own, w_qkv, projected, w_out, readout_weight):
    whole = lambda *shape: pl.BlockSpec(shape, lambda j: (0, 0))
    part = lambda rows, first: pl.BlockSpec((rows, WIDTH), lambda j: (0, first + j))
    window = 2 * WIN + BLOCK
    return pl.pallas_call(
        forward_kernel,
        grid=(4,),
        in_specs=[
            pl.BlockSpec(memory_space=pltpu.SMEM),
            whole(WIN, 1024),
            whole(WIN, 1024),
            whole(BLOCK, 1024),
            HBM,
            part(BLOCK, 0),
            part(BLOCK, 4),
            part(BLOCK, 8),
            whole(1024, 1024),
            whole(1024, 128),
        ],
        out_specs=[
            whole(2 * WIN, 1024),
            part(window, 0),
            part(window, 0),
            whole(BLOCK, 1024),
            whole(BLOCK, 128),
            whole(BLOCK, 1024),
            whole(BLOCK, 128),
        ],
        out_shape=[
            jax.ShapeDtypeStruct((2 * WIN, 1024), BF),
            jax.ShapeDtypeStruct((window, 1024), BF),
            jax.ShapeDtypeStruct((window, 1024), BF),
            jax.ShapeDtypeStruct((BLOCK, 1024), F32),
            jax.ShapeDtypeStruct((BLOCK, 128), F32),
            jax.ShapeDtypeStruct((BLOCK, 1024), BF),
            jax.ShapeDtypeStruct((BLOCK, 128), F32),
        ],
        scratch_shapes=[
            pltpu.VMEM((4, window, BLOCK), BF),
            pltpu.VMEM((128, BLOCK), F32),
            pltpu.VMEM((8, 1024, WIDTH), BF),
            pltpu.SemaphoreType.DMA((8,)),
        ],
        compiler_params=pltpu.CompilerParams(vmem_limit_bytes=48 * 1024 * 1024),
        cost_estimate=pl.CostEstimate(
            flops=6 << 30, bytes_accessed=12 << 20, transcendentals=3 << 20
        ),
    )(
        counts,
        left,
        right,
        latent_own,
        w_qkv,
        projected,
        projected,
        projected,
        w_out,
        readout_weight,
    )


def score_kernel(
    counts_ref,
    own_ref,
    near_ref,
    others_ref,
    target_ref,
    attended_ref,
    hidden_ref,
    stats_ref,
    w_out_ref,
    readout_ref,
    crps_ref,
    packed_ref,
    grad_ref,
    small_ref,
):
    members = 4
    fair_eps = (1.0 - alpha_fair) / members
    coefficient = (1.0 - fair_eps) / (members * (members - 1))
    valid = (iota((BLOCK, 1), 0) < counts_ref[1]).astype(F32)
    own = own_ref[...]
    forecasts = [own, near_ref[...], others_ref[0], others_ref[1]]
    target = target_ref[...]
    error = jnp.zeros_like(target)
    for forecast in forecasts:
        error += smooth_abs(forecast - target)
    spread = jnp.full_like(target, members * smooth_width**0.5)
    for first in range(members):
        for second in range(first + 1, members):
            spread += 2.0 * smooth_abs(forecasts[first] - forecasts[second])
    crps_ref[...] = valid * (error / members - 0.5 * coefficient * spread)
    pull = jnp.zeros_like(target)
    for other in forecasts[1:]:
        pull += smooth_sign(own - other)
    slope = (
        valid / 128 * (smooth_sign(own - target) / members - coefficient * pull)
    ).astype(BF)
    dhidden = dot_nt(slope, readout_ref[...]).astype(BF)
    dattended = dot_nt(dhidden, w_out_ref[...]).astype(BF)
    grad_ref[...] = dattended
    attended = attended_ref[...]
    product = dattended.astype(F32) * attended
    high = product.astype(BF)
    low = (product - high.astype(F32)).astype(BF)
    pick = (iota((1024, 128), 0) // HEAD_WIDTH + HEADS == iota((1024, 128), 1)).astype(BF)
    stats = stats_ref[...] + dot_nn(high, pick) + dot_nn(low, pick)
    first = stats.astype(BF)
    rest = stats - first.astype(F32)
    second = rest.astype(BF)
    third = (rest - second.astype(F32)).astype(BF)
    terms = jnp.zeros((BLOCK, 128), F32)
    for place, term in enumerate((first, second, third)):
        shift = (iota((128, 128), 0) + 32 * place == iota((128, 128), 1)) & (
            iota((128, 128), 0) < 32
        )
        terms += dot_nn(term, shift.astype(BF))
    packed_ref[:, :128] = slope
    packed_ref[:, 128:] = terms.astype(BF)
    small_ref[:, :128] = dot_tn(attended.astype(BF), slope).astype(BF)
    small_ref[:, 128:] = dot_tn(hidden_ref[...], slope).astype(BF)


def score(counts, own, near, others, target, attended, hidden, stats, w_out, readout_weight):
    vmem = pl.BlockSpec(memory_space=pltpu.VMEM)
    return pl.pallas_call(
        score_kernel,
        in_specs=[pl.BlockSpec(memory_space=pltpu.SMEM)] + [vmem] * 9,
        out_specs=[vmem] * 4,
        out_shape=[
            jax.ShapeDtypeStruct((BLOCK, 128), F32),
            jax.ShapeDtypeStruct((BLOCK, 256), BF),
            jax.ShapeDtypeStruct((BLOCK, 1024), BF),
            jax.ShapeDtypeStruct((1024, 256), BF),
        ],
        compiler_params=pltpu.CompilerParams(vmem_limit_bytes=12 * 1024 * 1024),
    )(counts, own, near, others, target, attended, hidden, stats, w_out, readout_weight)


def query_kernel(
    counts_ref, q_ref, kcat_ref, vcat_ref, grad_ref, packed_ref, dq_ref, dscores
):
    step = pl.program_id(0)

    @pl.when(step == 0)
    def _():
        dscores[...] = jnp.zeros_like(dscores)

    fill = key_fill([(counts_ref[0], WIN), (counts_ref[1], BLOCK), (counts_ref[2], WIN)])
    value_fill = (spare_lane(fill.shape) < 3).astype(BF)
    low_q = iota((BLOCK, PAIR), 1) < HEAD_WIDTH
    low_k = iota(fill.shape, 1) < HEAD_WIDTH
    terms = packed_ref[:, 128:]
    ones = (spare_lane((BLOCK, WIDTH)) == 3).astype(F32)
    q_fill = (dot_nn(terms, stat_spread(step, 0)) + ones).astype(BF)
    g_fill = dot_nn(terms, stat_spread(step, HEADS)).astype(BF)
    turned = []
    for pair in range(2):
        columns = slice(pair * PAIR, (pair + 1) * PAIR)
        q_pair = q_ref[:, columns] * jnp.asarray(HEAD_WIDTH ** (-0.5), BF)
        g_pair = grad_ref[:, columns]
        k_pair = kcat_ref[:, columns]
        v_pair = vcat_ref[:, columns]
        k_turned = k_pair.T
        for half in range(2):
            slot = pair * 2 + half
            pick_q = low_q if half == 0 else ~low_q
            pick_k = low_k if half == 0 else ~low_k
            q_head = jnp.where(pick_q, q_pair, q_fill[:, columns])
            g_head = jnp.where(pick_q, g_pair, g_fill[:, columns])
            k_head = jnp.where(pick_k, k_pair, fill)
            v_head = jnp.where(pick_k, v_pair, value_fill)
            scores = dot_nt(k_head, q_head)
            change = dot_nt(v_head, g_head)
            for tile in range(2):
                rows = slice(tile * 128, tile * 128 + 640)
                lanes = slice(tile * 128, tile * 128 + 128)
                ends = jnp.exp(scores[rows, lanes]) * change[rows, lanes]
                first, middle, last = keep_band(ends, 0.0)
                start = tile * 128
                dscores[slot, start : start + 128, lanes] = first.astype(BF)
                dscores[slot, start + 128 : start + 512, lanes] = middle.astype(BF)
                dscores[slot, start + 512 : start + 640, lanes] = last.astype(BF)
            turned.append(k_turned[half * HEAD_WIDTH : (half + 1) * HEAD_WIDTH])
    for slot in range(4):
        dquery = dot_nn(turned[slot], dscores[slot]) * HEAD_WIDTH ** (-0.5)
        dq_ref[slot * HEAD_WIDTH : (slot + 1) * HEAD_WIDTH] = dquery.astype(BF)


def query_grads(counts, projected, kcat, vcat, grad, packed):
    part = lambda rows, first: pl.BlockSpec((rows, WIDTH), lambda j: (0, first + j))
    window = 2 * WIN + BLOCK
    return pl.pallas_call(
        query_kernel,
        grid=(4,),
        in_specs=[
            pl.BlockSpec(memory_space=pltpu.SMEM),
            part(BLOCK, 0),
            part(window, 0),
            part(window, 0),
            part(BLOCK, 0),
            pl.BlockSpec((BLOCK, 256), lambda j: (0, 0)),
        ],
        out_specs=pl.BlockSpec((WIDTH, BLOCK), lambda j: (j, 0)),
        out_shape=jax.ShapeDtypeStruct((1024, BLOCK), BF),
        scratch_shapes=[pltpu.VMEM((4, window, BLOCK), BF)],
        compiler_params=pltpu.CompilerParams(vmem_limit_bytes=12 * 1024 * 1024),
        cost_estimate=pl.CostEstimate(
            flops=6 << 30, bytes_accessed=5 << 20, transcendentals=3 << 20
        ),
    )(counts, projected, kcat, vcat, grad, packed)


def key_kernel(
    counts_ref,
    q_ref,
    k_ref,
    v_ref,
    qhalo_ref,
    grad_ref,
    own_ref,
    left_ref,
    right_ref,
    w_out_ref,
    readout_ref,
    out_ref,
    probs,
    dscores,
    dhidden,
):
    step = pl.program_id(0)

    @pl.when(step == 0)
    def _():
        probs[...] = jnp.zeros_like(probs)
        dscores[...] = jnp.zeros_like(dscores)
        dhidden[:WIN] = dot_nt(left_ref[:, :128], readout_ref[...]).astype(BF)
        dhidden[WIN:] = dot_nt(right_ref[:, :128], readout_ref[...]).astype(BF)

    ghalo = dot_nt(dhidden[...], w_out_ref[...]).astype(BF)
    terms = jnp.concatenate(
        [left_ref[:, 128:], own_ref[:, 128:], right_ref[:, 128:]], axis=0
    )
    window = terms.shape[0]
    fill = key_fill([(counts_ref[1], BLOCK)])
    value_fill = (spare_lane(fill.shape) < 3).astype(BF)
    low_q = iota((window, PAIR), 1) < HEAD_WIDTH
    low_k = iota(fill.shape, 1) < HEAD_WIDTH
    ones = (spare_lane((window, WIDTH)) == 3).astype(F32)
    q_fill = (dot_nn(terms, stat_spread(step, 0)) + ones).astype(BF)
    g_fill = dot_nn(terms, stat_spread(step, HEADS)).astype(BF)
    turned = []
    for pair in range(2):
        columns = slice(pair * PAIR, (pair + 1) * PAIR)
        q_pair = jnp.concatenate(
            [qhalo_ref[:WIN, columns], q_ref[:, columns], qhalo_ref[WIN:, columns]], axis=0
        ) * jnp.asarray(HEAD_WIDTH ** (-0.5), BF)
        g_pair = jnp.concatenate(
            [ghalo[:WIN, columns], grad_ref[:, columns], ghalo[WIN:, columns]], axis=0
        )
        k_pair = k_ref[:, columns]
        v_pair = v_ref[:, columns]
        q_turned = q_pair.T
        g_turned = g_pair.T
        for half in range(2):
            slot = pair * 2 + half
            pick_q = low_q if half == 0 else ~low_q
            pick_k = low_k if half == 0 else ~low_k
            q_head = jnp.where(pick_q, q_pair, q_fill[:, columns])
            g_head = jnp.where(pick_q, g_pair, g_fill[:, columns])
            k_head = jnp.where(pick_k, k_pair, fill)
            v_head = jnp.where(pick_k, v_pair, value_fill)
            scores = dot_nt(q_head, k_head)
            change = dot_nt(g_head, v_head)
            for tile in range(2):
                rows = slice(tile * 128, tile * 128 + 640)
                lanes = slice(tile * 128, tile * 128 + 128)
                weight = keep_band(jnp.exp(scores[rows, lanes]), 0.0)
                moved = change[rows, lanes]
                start = tile * 128
                for piece, (low, high) in zip(weight, ((0, 128), (128, 512), (512, 640))):
                    place = slice(start + low, start + high)
                    probs[slot, place, lanes] = piece.astype(BF)
                    dscores[slot, place, lanes] = (piece * moved[low:high]).astype(BF)
            lanes = slice(half * HEAD_WIDTH, (half + 1) * HEAD_WIDTH)
            turned.append((q_turned[lanes], g_turned[lanes]))
    for slot in range(4):
        place = slice(slot * HEAD_WIDTH, (slot + 1) * HEAD_WIDTH)
        out_ref[0, place] = dot_nn(turned[slot][0], dscores[slot]).astype(BF)
        out_ref[1, place] = dot_nn(turned[slot][1], probs[slot]).astype(BF)


def key_grads(counts, projected, qhalo, grad, own, left, right, w_out, readout_weight):
    part = lambda rows, first: pl.BlockSpec((rows, WIDTH), lambda j: (0, first + j))
    whole = lambda *shape: pl.BlockSpec(shape, lambda j: (0, 0))
    window = 2 * WIN + BLOCK
    return pl.pallas_call(
        key_kernel,
        grid=(4,),
        in_specs=[
            pl.BlockSpec(memory_space=pltpu.SMEM),
            part(BLOCK, 0),
            part(BLOCK, 4),
            part(BLOCK, 8),
            part(2 * WIN, 0),
            part(BLOCK, 0),
            whole(BLOCK, 256),
            whole(BLOCK, 256),
            whole(BLOCK, 256),
            pl.BlockSpec((WIDTH, 1024), lambda j: (j, 0)),
            whole(1024, 128),
        ],
        out_specs=pl.BlockSpec((2, WIDTH, BLOCK), lambda j: (0, j, 0)),
        out_shape=jax.ShapeDtypeStruct((2, 1024, BLOCK), BF),
        scratch_shapes=[
            pltpu.VMEM((4, window, BLOCK), BF),
            pltpu.VMEM((4, window, BLOCK), BF),
            pltpu.VMEM((2 * WIN, 1024), BF),
        ],
        compiler_params=pltpu.CompilerParams(vmem_limit_bytes=56 * 1024 * 1024),
        cost_estimate=FREE,
    )(
        counts,
        projected,
        projected,
        projected,
        qhalo,
        grad,
        own,
        left,
        right,
        w_out,
        readout_weight,
    )


AXES = ("x_hi", "core", "y", "x_lo", "z")
MEMBER = ("x_hi", "core")
CELLS = ("y", "x_lo", "z")
CHIPS = ("x_hi", "y", "x_lo", "z")
SWAP = [(0, 1), (1, 0)]


def swap_core(values):
    return lax.ppermute(values, "core", SWAP)


def scatter(partial):
    columns = partial.shape[1]
    return lax.all_to_all(partial.reshape(64, 8, columns), CHIPS, split_axis=0, concat_axis=0)


def add_up(pieces):
    return jnp.sum(pieces.astype(F32), axis=0)


def per_device(latent, counts, w_qkv, w_out, readout_weight, target):
    latent_own = latent[0]
    cell_count = 32
    cell_index = lax.axis_index(CELLS)
    member_index = lax.axis_index(MEMBER)
    core = lax.axis_index("core")
    up = [(i, i + 1) for i in range(cell_count - 1)]
    down = [(i + 1, i) for i in range(cell_count - 1)]
    from_left = lax.ppermute(latent_own, CELLS, up)
    from_right = lax.ppermute(latent_own, CELLS, down)

    own_count = counts[cell_index]
    left_count = jnp.where(cell_index > 0, counts[jnp.maximum(cell_index - 1, 0)], 0)
    right_count = jnp.where(
        cell_index < cell_count - 1, counts[jnp.minimum(cell_index + 1, cell_count - 1)], 0
    )
    scalars = jnp.stack([left_count, own_count, right_count])

    projected, turned = project(latent_own, w_qkv)
    turned_other = swap_core(turned)
    normed_halo, kcat, vcat, attended, stats, hidden, forecast = forward(
        scalars, from_left, from_right, latent_own, w_qkv, projected, w_out, readout_weight
    )
    near = lax.ppermute(forecast, "x_hi", SWAP)
    qhalo = halo_queries(normed_halo, w_qkv)
    near, qhalo = lax.optimization_barrier((near, qhalo))
    others = swap_core(jnp.stack([forecast, near]))
    crps_whole, packed, grad, small = score(
        scalars, forecast, near, others, target, attended, hidden, stats, w_out, readout_weight
    )
    crps = lax.dynamic_slice_in_dim(crps_whole, member_index * 32, 32, 1)
    packed_left = lax.ppermute(packed, CELLS, up)
    packed_right = lax.ppermute(packed, CELLS, down)

    dquery = query_grads(scalars, projected, kcat, vcat, grad, packed)
    dquery, packed_left, packed_right = lax.optimization_barrier(
        (dquery, packed_left, packed_right)
    )

    first_part = partial_sums(
        core, turned, turned_other, dquery, swap_core(dquery), (small, swap_core(small))
    )
    first_part, scalars = lax.optimization_barrier((first_part, scalars))
    first = scatter(first_part)
    pairs = key_grads(
        scalars,
        projected,
        qhalo,
        grad,
        packed,
        packed_left,
        packed_right,
        w_out,
        readout_weight,
    )
    pairs = pairs.reshape(2048, BLOCK)
    second_part = partial_sums(core, turned, turned_other, pairs, swap_core(pairs))
    second_part, first = lax.optimization_barrier((second_part, first))
    second = add_up(scatter(second_part))
    first = add_up(first)
    grad_out = lax.dot_general(
        first[:, 1024:1152],
        readout_weight.astype(F32),
        (((1,), (1,)), ((), ())),
        precision=lax.Precision.HIGHEST,
        preferred_element_type=F32,
    )
    grads = jnp.concatenate([first[:, :1024], second, grad_out, first[:, 1152:]], axis=1)
    return (crps, grads)


def solution(mesh):
    fine = jax.sharding.Mesh(mesh.devices.reshape(2, 2, 4, 2, 4), AXES)
    placed = (P(MEMBER, CELLS, None), P(), P(), P(), P(), P(CELLS, None))
    return jax.shard_map(
        per_device,
        mesh=fine,
        in_specs=placed,
        out_specs=(P(CELLS, MEMBER), P(MEMBER + CELLS, None)),
        check_vma=False,
    )
```

```python
import functools

import jax
import jax.numpy as jnp
import numpy as np
from jax import lax
from jax.experimental import pallas as pl
from jax.experimental.pallas import tpu as pltpu
from jax.sharding import PartitionSpec as P

HEADS = 16
WIN = 256
BLOCK = 256
WIDTH = 256
HEAD_WIDTH = 64
PAIR = 128
NEVER = -1e30

alpha_fair = 0.95
smooth_width = 0.0625

BF = jnp.bfloat16
F32 = jnp.float32


def smooth_abs(values):
    return jnp.sqrt(values * values + smooth_width)


def smooth_sign(values):
    return values * lax.rsqrt(values * values + smooth_width)


def layer_norm(latent_rows):
    values = latent_rows.astype(F32)
    center = values - jnp.mean(values, axis=-1, keepdims=True)
    spread = jnp.mean(center * center, axis=-1, keepdims=True)
    return (center * lax.rsqrt(spread + 1e-05)).astype(BF)


def dot_nn(left, right):
    return lax.dot_general(left, right, (((1,), (0,)), ((), ())), preferred_element_type=F32)


def dot_nt(left, right):
    return lax.dot_general(left, right, (((1,), (1,)), ((), ())), preferred_element_type=F32)


def dot_tn(left, right):
    return lax.dot_general(left, right, (((0,), (0,)), ((), ())), preferred_element_type=F32)


def iota(shape, axis):
    return lax.broadcasted_iota(jnp.int32, shape, axis)


FREE = pl.CostEstimate(flops=0, bytes_accessed=0, transcendentals=0)
HBM = pl.BlockSpec(memory_space=pltpu.HBM)


def fetches(weight_ref, buffer, arrived, width, first):
    return [
        pltpu.make_async_copy(
            weight_ref.at[:, pl.ds(first + place * width, width)],
            buffer.at[place],
            arrived.at[place],
        )
        for place in range(buffer.shape[0])
    ]


def fetch_one(weight_ref, buffer, arrived, width, first, place):
    start = pl.multiple_of(first + place * width, width)
    return pltpu.make_async_copy(
        weight_ref.at[:, pl.ds(start, width)], buffer.at[place], arrived.at[place]
    )


def project_kernel(latent_ref, weight_ref, projected_ref, turned_ref, normed, buffer, arrived):
    step = pl.program_id(0)

    @pl.when(step == 0)
    def _():
        for copy in fetches(weight_ref, buffer, arrived, 512, 0):
            copy.start()
        normed[...] = layer_norm(latent_ref[...])
        turned_ref[...] = normed[...].T

    fetch_one(weight_ref, buffer, arrived, 512, 0, step).wait()
    projected_ref[...] = dot_nn(normed[...], buffer[step]).astype(BF)


def project(latent_own, w_qkv):
    rows, width = latent_own.shape
    return pl.pallas_call(
        project_kernel,
        grid=(6,),
        in_specs=[pl.BlockSpec((rows, width), lambda j: (0, 0)), HBM],
        out_specs=[
            pl.BlockSpec((rows, 512), lambda j: (0, j)),
            pl.BlockSpec((width, rows), lambda j: (0, 0)),
        ],
        out_shape=[
            jax.ShapeDtypeStruct((rows, 3 * width), BF),
            jax.ShapeDtypeStruct((width, rows), BF),
        ],
        scratch_shapes=[
            pltpu.VMEM((rows, width), BF),
            pltpu.VMEM((6, width, 512), BF),
            pltpu.SemaphoreType.DMA((6,)),
        ],
        compiler_params=pltpu.CompilerParams(vmem_limit_bytes=56 * 1024 * 1024),
        cost_estimate=pl.CostEstimate(
            flops=2 * rows * width * width * 4, bytes_accessed=8 << 20, transcendentals=0
        ),
    )(latent_own, w_qkv)


def halo_query_kernel(normed_ref, weight_ref, out_ref, buffer, arrived):
    step = pl.program_id(0)

    @pl.when(step == 0)
    def _():
        for copy in fetches(weight_ref, buffer, arrived, 256, 0):
            copy.start()

    fetch_one(weight_ref, buffer, arrived, 256, 0, step).wait()
    out_ref[...] = dot_nn(normed_ref[...], buffer[step]).astype(BF)


def halo_queries(normed_halo, w_qkv):
    rows, width = normed_halo.shape
    return pl.pallas_call(
        halo_query_kernel,
        grid=(4,),
        in_specs=[pl.BlockSpec((rows, width), lambda j: (0, 0)), HBM],
        out_specs=pl.BlockSpec((rows, 256), lambda j: (0, j)),
        out_shape=jax.ShapeDtypeStruct((rows, width), BF),
        scratch_shapes=[
            pltpu.VMEM((4, width, 256), BF),
            pltpu.SemaphoreType.DMA((4,)),
        ],
        compiler_params=pltpu.CompilerParams(vmem_limit_bytes=52 * 1024 * 1024),
        cost_estimate=FREE,
    )(normed_halo, w_qkv)


def partial_kernel(
    core_ref, normed_ref, normed_other_ref, piece_ref, other_ref, small_ref, small_other_ref,
    out_ref,
):
    core = core_ref[0]
    for top in range(2):
        rows = slice(top * 256, (top + 1) * 256)
        own = normed_ref[top, core]
        near = normed_other_ref[top, core]
        for first in range(0, piece_ref.shape[0], 512):
            columns = slice(first, first + 512)
            out_ref[rows, columns] = (
                dot_nt(own, piece_ref[columns]) + dot_nt(near, other_ref[columns])
            ).astype(BF)
        if small_ref is not None:
            out_ref[rows, piece_ref.shape[0] :] = (
                small_ref[top, core].astype(F32) + small_other_ref[top, core].astype(F32)
            ).astype(BF)


def plain_partial_kernel(core_ref, normed_ref, normed_other_ref, piece_ref, other_ref, out_ref):
    partial_kernel(
        core_ref, normed_ref, normed_other_ref, piece_ref, other_ref, None, None, out_ref
    )


def partial_sums(core, turned, turned_other, piece, other, smalls=()):
    by_core = lambda values: values.reshape(2, 2, 256, 256)
    vmem = pl.BlockSpec(memory_space=pltpu.VMEM)
    columns = piece.shape[0] + 256 * (len(smalls) // 2)
    return pl.pallas_call(
        partial_kernel if smalls else plain_partial_kernel,
        in_specs=[pl.BlockSpec(memory_space=pltpu.SMEM)] + [vmem] * (4 + len(smalls)),
        out_specs=vmem,
        out_shape=jax.ShapeDtypeStruct((512, columns), BF),
        compiler_params=pltpu.CompilerParams(vmem_limit_bytes=12 * 1024 * 1024),
        cost_estimate=FREE,
    )(
        core.astype(jnp.int32).reshape(1),
        by_core(turned),
        by_core(turned_other),
        piece,
        other,
        *(by_core(small) for small in smalls),
    )


def spare_lane(shape):
    lane = iota(shape, len(shape) - 1)
    return lane % HEAD_WIDTH


def key_fill(count_pieces):
    fills = []
    for count, rows in count_pieces:
        spare = spare_lane((rows, PAIR))
        bias = jnp.where(iota((rows, PAIR), 0) < count, 0.0, NEVER)
        fills.append(
            jnp.where(spare < 3, 1.0, jnp.where(spare == 3, bias, 0.0)).astype(BF)
        )
    return jnp.concatenate(fills, axis=0)


def stat_spread(step, offset):
    shape = (128, WIDTH)
    lane = iota(shape, 1)
    head = step * 4 + 2 * (lane // PAIR) + jnp.where(lane % PAIR < HEAD_WIDTH, 1, 0)
    term = lane % HEAD_WIDTH
    chosen = (term < 3) & (iota(shape, 0) == term * 32 + offset + head)
    return jnp.where(chosen, -1.0, 0.0).astype(BF)


def keep_band(window, fill):
    shape = (128, 128)
    apart = iota(shape, 0) - iota(shape, 1)
    first = jnp.where(apart >= 0, window[:128], fill)
    last = jnp.where(apart <= 0, window[512:], fill)
    return first, window[128:512], last


def forward_kernel(
    counts_ref,
    left_ref,
    right_ref,
    latent_ref,
    weight_ref,
    q_ref,
    k_ref,
    v_ref,
    w_out_ref,
    readout_ref,
    normed_ref,
    kcat_ref,
    vcat_ref,
    attended_ref,
    stats_ref,
    hidden_ref,
    forecast_ref,
    probs,
    inverse_ref,
    stat_rows,
    buffer,
    arrived,
):
    step = pl.program_id(0)

    @pl.when(step == 0)
    def _():
        copies = fetches(weight_ref, buffer, arrived, WIDTH, 1024)
        for place in (0, 4, 1, 5, 2, 6, 3, 7):
            copies[place].start()
        normed_ref[:WIN] = layer_norm(left_ref[...])
        normed_ref[WIN:] = layer_norm(right_ref[...])

    fetch_one(weight_ref, buffer, arrived, WIDTH, 1024, step).wait()
    fetch_one(weight_ref, buffer, arrived, WIDTH, 1024, step + 4).wait()
    khalo = dot_nn(normed_ref[...], buffer[step]).astype(BF)
    kcat_ref[:WIN] = khalo[:WIN]
    kcat_ref[WIN : WIN + BLOCK] = k_ref[...]
    kcat_ref[WIN + BLOCK :] = khalo[WIN:]
    vhalo = dot_nn(normed_ref[...], buffer[step + 4]).astype(BF)
    vcat_ref[:WIN] = vhalo[:WIN]
    vcat_ref[WIN : WIN + BLOCK] = v_ref[...]
    vcat_ref[WIN + BLOCK :] = vhalo[WIN:]
    fill = key_fill([(counts_ref[0], WIN), (counts_ref[1], BLOCK), (counts_ref[2], WIN)])
    low_q = iota((BLOCK, PAIR), 1) < HEAD_WIDTH
    low_k = iota(fill.shape, 1) < HEAD_WIDTH
    query_fill = (spare_lane((BLOCK, PAIR)) == 3).astype(BF)
    scores, turned = [], []
    for pair in range(2):
        columns = slice(pair * PAIR, (pair + 1) * PAIR)
        q_pair = q_ref[:, columns] * jnp.asarray(HEAD_WIDTH ** (-0.5), BF)
        k_pair = kcat_ref[:, columns]
        turned.append(vcat_ref[:, columns].T)
        for half in range(2):
            if half == 0:
                q_head = jnp.where(low_q, q_pair, query_fill)
                k_head = jnp.where(low_k, k_pair, fill)
            else:
                q_head = jnp.where(low_q, query_fill, q_pair)
                k_head = jnp.where(low_k, fill, k_pair)
            scores.append(dot_nt(k_head, q_head))
    tops = []
    for slot in range(4):
        levels = []
        for tile in range(2):
            rows = slice(tile * 128, tile * 128 + 640)
            lanes = slice(tile * 128, tile * 128 + 128)
            first, middle, last = keep_band(scores[slot][rows, lanes], NEVER)
            top = jnp.maximum(
                jnp.max(middle, axis=0, keepdims=True),
                jnp.max(jnp.maximum(first, last), axis=0, keepdims=True),
            )
            start = tile * 128
            probs[slot, start : start + 128, lanes] = jnp.exp(first - top).astype(BF)
            probs[slot, start + 128 : start + 512, lanes] = jnp.exp(middle - top).astype(BF)
            probs[slot, start + 512 : start + 640, lanes] = jnp.exp(last - top).astype(BF)
            levels.append(top)
        probs[slot, :128, 128:] = jnp.zeros((128, 128), BF)
        probs[slot, 640:, :128] = jnp.zeros((128, 128), BF)
        tops.append(jnp.concatenate(levels, axis=1))
    ones = jnp.ones((16, fill.shape[0]), BF)
    for pair in range(2):
        halves = []
        for half in range(2):
            slot = pair * 2 + half
            lanes = slice(half * HEAD_WIDTH, (half + 1) * HEAD_WIDTH)
            values = jnp.concatenate([turned[pair][lanes], ones], axis=0)
            mixed = dot_nn(values, probs[slot])
            total = mixed[HEAD_WIDTH : HEAD_WIDTH + 1]
            inverse = 1.0 / total
            halves.append(mixed[:HEAD_WIDTH] * inverse)
            head = step * 4 + slot
            inverse_ref[pl.ds(head, 1), :] = inverse
            stat_rows[pl.ds(head, 1), :] = tops[slot] + jnp.log(total)
        start = pl.multiple_of(step * WIDTH + pair * PAIR, PAIR)
        attended_ref[:, pl.ds(start, PAIR)] = jnp.concatenate(halves, axis=0).T

    @pl.when(step == 3)
    def _():
        mixed = dot_nn(attended_ref[...].astype(BF), w_out_ref[...])
        hidden = (latent_ref[...].astype(F32) + mixed).astype(BF)
        hidden_ref[...] = hidden
        forecast_ref[...] = dot_nn(hidden, readout_ref[...])
        stat_rows[HEADS:] = jnp.zeros((128 - HEADS, BLOCK), F32)
        stats_ref[...] = stat_rows[...].T


def forward(counts, left, right, latent_own, w_qkv, projected, w_out, readout_weight):
    whole = lambda *shape: pl.BlockSpec(shape, lambda j: (0, 0))
    part = lambda rows, first: pl.BlockSpec((rows, WIDTH), lambda j: (0, first + j))
    window = 2 * WIN + BLOCK
    return pl.pallas_call(
        forward_kernel,
        grid=(4,),
        in_specs=[
            pl.BlockSpec(memory_space=pltpu.SMEM),
            whole(WIN, 1024),
            whole(WIN, 1024),
            whole(BLOCK, 1024),
            HBM,
            part(BLOCK, 0),
            part(BLOCK, 4),
            part(BLOCK, 8),
            whole(1024, 1024),
            whole(1024, 128),
        ],
        out_specs=[
            whole(2 * WIN, 1024),
            part(window, 0),
            part(window, 0),
            whole(BLOCK, 1024),
            whole(BLOCK, 128),
            whole(BLOCK, 1024),
            whole(BLOCK, 128),
            pl.BlockSpec((4, window, BLOCK), lambda j: (j, 0, 0)),
            whole(HEADS, BLOCK),
        ],
        out_shape=[
            jax.ShapeDtypeStruct((2 * WIN, 1024), BF),
            jax.ShapeDtypeStruct((window, 1024), BF),
            jax.ShapeDtypeStruct((window, 1024), BF),
            jax.ShapeDtypeStruct((BLOCK, 1024), F32),
            jax.ShapeDtypeStruct((BLOCK, 128), F32),
            jax.ShapeDtypeStruct((BLOCK, 1024), BF),
            jax.ShapeDtypeStruct((BLOCK, 128), F32),
            jax.ShapeDtypeStruct((HEADS, window, BLOCK), BF),
            jax.ShapeDtypeStruct((HEADS, BLOCK), F32),
        ],
        scratch_shapes=[
            pltpu.VMEM((128, BLOCK), F32),
            pltpu.VMEM((8, 1024, WIDTH), BF),
            pltpu.SemaphoreType.DMA((8,)),
        ],
        compiler_params=pltpu.CompilerParams(vmem_limit_bytes=48 * 1024 * 1024),
        cost_estimate=pl.CostEstimate(
            flops=6 << 30, bytes_accessed=12 << 20, transcendentals=3 << 20
        ),
    )(
        counts,
        left,
        right,
        latent_own,
        w_qkv,
        projected,
        projected,
        projected,
        w_out,
        readout_weight,
    )


def score_kernel(
    counts_ref,
    own_ref,
    near_ref,
    others_ref,
    target_ref,
    attended_ref,
    hidden_ref,
    stats_ref,
    w_out_ref,
    readout_ref,
    crps_ref,
    packed_ref,
    grad_ref,
    small_ref,
):
    members = 4
    fair_eps = (1.0 - alpha_fair) / members
    coefficient = (1.0 - fair_eps) / (members * (members - 1))
    valid = (iota((BLOCK, 1), 0) < counts_ref[1]).astype(F32)
    own = own_ref[...]
    forecasts = [own, near_ref[...], others_ref[0], others_ref[1]]
    target = target_ref[...]
    error = jnp.zeros_like(target)
    for forecast in forecasts:
        error += smooth_abs(forecast - target)
    spread = jnp.full_like(target, members * smooth_width**0.5)
    for first in range(members):
        for second in range(first + 1, members):
            spread += 2.0 * smooth_abs(forecasts[first] - forecasts[second])
    crps_ref[...] = valid * (error / members - 0.5 * coefficient * spread)
    pull = jnp.zeros_like(target)
    for other in forecasts[1:]:
        pull += smooth_sign(own - other)
    slope = (
        valid / 128 * (smooth_sign(own - target) / members - coefficient * pull)
    ).astype(BF)
    dhidden = dot_nt(slope, readout_ref[...]).astype(BF)
    dattended = dot_nt(dhidden, w_out_ref[...]).astype(BF)
    grad_ref[...] = dattended
    attended = attended_ref[...]
    product = dattended.astype(F32) * attended
    high = product.astype(BF)
    low = (product - high.astype(F32)).astype(BF)
    pick = (iota((1024, 128), 0) // HEAD_WIDTH + HEADS == iota((1024, 128), 1)).astype(BF)
    stats = stats_ref[...] + dot_nn(high, pick) + dot_nn(low, pick)
    first = stats.astype(BF)
    rest = stats - first.astype(F32)
    second = rest.astype(BF)
    third = (rest - second.astype(F32)).astype(BF)
    terms = jnp.zeros((BLOCK, 128), F32)
    for place, term in enumerate((first, second, third)):
        shift = (iota((128, 128), 0) + 32 * place == iota((128, 128), 1)) & (
            iota((128, 128), 0) < 32
        )
        terms += dot_nn(term, shift.astype(BF))
    packed_ref[:, :128] = slope
    packed_ref[:, 128:] = terms.astype(BF)
    small_ref[:, :128] = dot_tn(attended.astype(BF), slope).astype(BF)
    small_ref[:, 128:] = dot_tn(hidden_ref[...], slope).astype(BF)


def score(counts, own, near, others, target, attended, hidden, stats, w_out, readout_weight):
    vmem = pl.BlockSpec(memory_space=pltpu.VMEM)
    return pl.pallas_call(
        score_kernel,
        in_specs=[pl.BlockSpec(memory_space=pltpu.SMEM)] + [vmem] * 9,
        out_specs=[vmem] * 4,
        out_shape=[
            jax.ShapeDtypeStruct((BLOCK, 128), F32),
            jax.ShapeDtypeStruct((BLOCK, 256), BF),
            jax.ShapeDtypeStruct((BLOCK, 1024), BF),
            jax.ShapeDtypeStruct((1024, 256), BF),
        ],
        compiler_params=pltpu.CompilerParams(vmem_limit_bytes=12 * 1024 * 1024),
    )(counts, own, near, others, target, attended, hidden, stats, w_out, readout_weight)


def query_kernel(
    kcat_ref, vcat_ref, grad_ref, packed_ref, probs_ref, inverse_ref, dq_ref, dscores
):
    step = pl.program_id(0)
    window = kcat_ref.shape[0]
    value_fill = (spare_lane((window, PAIR)) < 3).astype(BF)
    low_q = iota((BLOCK, PAIR), 1) < HEAD_WIDTH
    low_k = iota((window, PAIR), 1) < HEAD_WIDTH
    g_fill = dot_nn(packed_ref[:, 128:], stat_spread(step, HEADS)).astype(BF)
    turned = []
    for pair in range(2):
        columns = slice(pair * PAIR, (pair + 1) * PAIR)
        g_pair = grad_ref[:, columns]
        v_pair = vcat_ref[:, columns]
        k_turned = kcat_ref[:, columns].T
        for half in range(2):
            slot = pair * 2 + half
            pick_q = low_q if half == 0 else ~low_q
            pick_k = low_k if half == 0 else ~low_k
            g_head = jnp.where(pick_q, g_pair, g_fill[:, columns])
            v_head = jnp.where(pick_k, v_pair, value_fill)
            change = dot_nt(v_head, g_head)
            dscores[slot] = (probs_ref[slot].astype(F32) * change).astype(BF)
            turned.append(k_turned[half * HEAD_WIDTH : (half + 1) * HEAD_WIDTH])
    for slot in range(4):
        scale = inverse_ref[pl.ds(step * 4 + slot, 1), :] * HEAD_WIDTH ** (-0.5)
        dquery = dot_nn(turned[slot], dscores[slot]) * scale
        dq_ref[slot * HEAD_WIDTH : (slot + 1) * HEAD_WIDTH] = dquery.astype(BF)


def query_grads(kcat, vcat, grad, packed, probs, inverse):
    part = lambda rows, first: pl.BlockSpec((rows, WIDTH), lambda j: (0, first + j))
    window = 2 * WIN + BLOCK
    return pl.pallas_call(
        query_kernel,
        grid=(4,),
        in_specs=[
            part(window, 0),
            part(window, 0),
            part(BLOCK, 0),
            pl.BlockSpec((BLOCK, 256), lambda j: (0, 0)),
            pl.BlockSpec((4, window, BLOCK), lambda j: (j, 0, 0)),
            pl.BlockSpec((HEADS, BLOCK), lambda j: (0, 0)),
        ],
        out_specs=pl.BlockSpec((WIDTH, BLOCK), lambda j: (j, 0)),
        out_shape=jax.ShapeDtypeStruct((1024, BLOCK), BF),
        scratch_shapes=[pltpu.VMEM((4, window, BLOCK), BF)],
        compiler_params=pltpu.CompilerParams(vmem_limit_bytes=16 * 1024 * 1024),
        cost_estimate=pl.CostEstimate(
            flops=6 << 30, bytes_accessed=5 << 20, transcendentals=3 << 20
        ),
    )(kcat, vcat, grad, packed, probs, inverse)


def key_kernel(
    counts_ref,
    q_ref,
    k_ref,
    v_ref,
    qhalo_ref,
    grad_ref,
    own_ref,
    left_ref,
    right_ref,
    w_out_ref,
    readout_ref,
    out_ref,
    probs,
    dscores,
    dhidden,
):
    step = pl.program_id(0)

    @pl.when(step == 0)
    def _():
        probs[...] = jnp.zeros_like(probs)
        dscores[...] = jnp.zeros_like(dscores)
        dhidden[:WIN] = dot_nt(left_ref[:, :128], readout_ref[...]).astype(BF)
        dhidden[WIN:] = dot_nt(right_ref[:, :128], readout_ref[...]).astype(BF)

    ghalo = dot_nt(dhidden[...], w_out_ref[...]).astype(BF)
    terms = jnp.concatenate(
        [left_ref[:, 128:], own_ref[:, 128:], right_ref[:, 128:]], axis=0
    )
    window = terms.shape[0]
    fill = key_fill([(counts_ref[1], BLOCK)])
    value_fill = (spare_lane(fill.shape) < 3).astype(BF)
    low_q = iota((window, PAIR), 1) < HEAD_WIDTH
    low_k = iota(fill.shape, 1) < HEAD_WIDTH
    ones = (spare_lane((window, WIDTH)) == 3).astype(F32)
    q_fill = (dot_nn(terms, stat_spread(step, 0)) + ones).astype(BF)
    g_fill = dot_nn(terms, stat_spread(step, HEADS)).astype(BF)
    turned = []
    for pair in range(2):
        columns = slice(pair * PAIR, (pair + 1) * PAIR)
        q_pair = jnp.concatenate(
            [qhalo_ref[:WIN, columns], q_ref[:, columns], qhalo_ref[WIN:, columns]], axis=0
        ) * jnp.asarray(HEAD_WIDTH ** (-0.5), BF)
        g_pair = jnp.concatenate(
            [ghalo[:WIN, columns], grad_ref[:, columns], ghalo[WIN:, columns]], axis=0
        )
        k_pair = k_ref[:, columns]
        v_pair = v_ref[:, columns]
        q_turned = q_pair.T
        g_turned = g_pair.T
        for half in range(2):
            slot = pair * 2 + half
            pick_q = low_q if half == 0 else ~low_q
            pick_k = low_k if half == 0 else ~low_k
            q_head = jnp.where(pick_q, q_pair, q_fill[:, columns])
            g_head = jnp.where(pick_q, g_pair, g_fill[:, columns])
            k_head = jnp.where(pick_k, k_pair, fill)
            v_head = jnp.where(pick_k, v_pair, value_fill)
            scores = dot_nt(q_head, k_head)
            change = dot_nt(g_head, v_head)
            for tile in range(2):
                rows = slice(tile * 128, tile * 128 + 640)
                lanes = slice(tile * 128, tile * 128 + 128)
                weight = keep_band(jnp.exp(scores[rows, lanes]), 0.0)
                moved = change[rows, lanes]
                start = tile * 128
                for piece, (low, high) in zip(weight, ((0, 128), (128, 512), (512, 640))):
                    place = slice(start + low, start + high)
                    probs[slot, place, lanes] = piece.astype(BF)
                    dscores[slot, place, lanes] = (piece * moved[low:high]).astype(BF)
            lanes = slice(half * HEAD_WIDTH, (half + 1) * HEAD_WIDTH)
            turned.append((q_turned[lanes], g_turned[lanes]))
    for slot in range(4):
        place = slice(slot * HEAD_WIDTH, (slot + 1) * HEAD_WIDTH)
        out_ref[0, place] = dot_nn(turned[slot][0], dscores[slot]).astype(BF)
        out_ref[1, place] = dot_nn(turned[slot][1], probs[slot]).astype(BF)


def key_grads(counts, projected, qhalo, grad, own, left, right, w_out, readout_weight):
    part = lambda rows, first: pl.BlockSpec((rows, WIDTH), lambda j: (0, first + j))
    whole = lambda *shape: pl.BlockSpec(shape, lambda j: (0, 0))
    window = 2 * WIN + BLOCK
    return pl.pallas_call(
        key_kernel,
        grid=(4,),
        in_specs=[
            pl.BlockSpec(memory_space=pltpu.SMEM),
            part(BLOCK, 0),
            part(BLOCK, 4),
            part(BLOCK, 8),
            part(2 * WIN, 0),
            part(BLOCK, 0),
            whole(BLOCK, 256),
            whole(BLOCK, 256),
            whole(BLOCK, 256),
            pl.BlockSpec((WIDTH, 1024), lambda j: (j, 0)),
            whole(1024, 128),
        ],
        out_specs=pl.BlockSpec((2, WIDTH, BLOCK), lambda j: (0, j, 0)),
        out_shape=jax.ShapeDtypeStruct((2, 1024, BLOCK), BF),
        scratch_shapes=[
            pltpu.VMEM((4, window, BLOCK), BF),
            pltpu.VMEM((4, window, BLOCK), BF),
            pltpu.VMEM((2 * WIN, 1024), BF),
        ],
        compiler_params=pltpu.CompilerParams(vmem_limit_bytes=56 * 1024 * 1024),
        cost_estimate=FREE,
    )(
        counts,
        projected,
        projected,
        projected,
        qhalo,
        grad,
        own,
        left,
        right,
        w_out,
        readout_weight,
    )


AXES = ("x_hi", "core", "y", "x_lo", "z")
MEMBER = ("x_hi", "core")
CELLS = ("y", "x_lo", "z")
CHIPS = ("x_hi", "y", "x_lo", "z")
SWAP = [(0, 1), (1, 0)]


def swap_core(values):
    return lax.ppermute(values, "core", SWAP)


def scatter(partial):
    columns = partial.shape[1]
    return lax.all_to_all(partial.reshape(64, 8, columns), CHIPS, split_axis=0, concat_axis=0)


def add_up(pieces):
    return jnp.sum(pieces.astype(F32), axis=0)


def per_device(latent, counts, w_qkv, w_out, readout_weight, target):
    latent_own = latent[0]
    cell_count = 32
    cell_index = lax.axis_index(CELLS)
    member_index = lax.axis_index(MEMBER)
    core = lax.axis_index("core")
    up = [(i, i + 1) for i in range(cell_count - 1)]
    down = [(i + 1, i) for i in range(cell_count - 1)]
    from_left = lax.ppermute(latent_own, CELLS, up)
    from_right = lax.ppermute(latent_own, CELLS, down)

    own_count = counts[cell_index]
    left_count = jnp.where(cell_index > 0, counts[jnp.maximum(cell_index - 1, 0)], 0)
    right_count = jnp.where(
        cell_index < cell_count - 1, counts[jnp.minimum(cell_index + 1, cell_count - 1)], 0
    )
    scalars = jnp.stack([left_count, own_count, right_count])

    projected, turned = project(latent_own, w_qkv)
    turned_other = swap_core(turned)
    normed_halo, kcat, vcat, attended, stats, hidden, forecast, probs, inverse = forward(
        scalars, from_left, from_right, latent_own, w_qkv, projected, w_out, readout_weight
    )
    near = lax.ppermute(forecast, "x_hi", SWAP)
    qhalo = halo_queries(normed_halo, w_qkv)
    near, qhalo = lax.optimization_barrier((near, qhalo))
    others = swap_core(jnp.stack([forecast, near]))
    crps_whole, packed, grad, small = score(
        scalars, forecast, near, others, target, attended, hidden, stats, w_out, readout_weight
    )
    crps = lax.dynamic_slice_in_dim(crps_whole, member_index * 32, 32, 1)
    packed_left = lax.ppermute(packed, CELLS, up)
    packed_right = lax.ppermute(packed, CELLS, down)

    dquery = query_grads(kcat, vcat, grad, packed, probs, inverse)
    dquery, packed_left, packed_right = lax.optimization_barrier(
        (dquery, packed_left, packed_right)
    )

    first_part = partial_sums(
        core, turned, turned_other, dquery, swap_core(dquery), (small, swap_core(small))
    )
    first_part, scalars = lax.optimization_barrier((first_part, scalars))
    first = scatter(first_part)
    pairs = key_grads(
        scalars,
        projected,
        qhalo,
        grad,
        packed,
        packed_left,
        packed_right,
        w_out,
        readout_weight,
    )
    pairs = pairs.reshape(2048, BLOCK)
    second_part = partial_sums(core, turned, turned_other, pairs, swap_core(pairs))
    second_part, first = lax.optimization_barrier((second_part, first))
    second = add_up(scatter(second_part))
    first = add_up(first)
    grad_out = lax.dot_general(
        first[:, 1024:1152],
        readout_weight.astype(F32),
        (((1,), (1,)), ((), ())),
        precision=lax.Precision.HIGHEST,
        preferred_element_type=F32,
    )
    grads = jnp.concatenate([first[:, :1024], second, grad_out, first[:, 1152:]], axis=1)
    return (crps, grads)


def solution(mesh):
    fine = jax.sharding.Mesh(mesh.devices.reshape(2, 2, 4, 2, 4), AXES)
    placed = (P(MEMBER, CELLS, None), P(), P(), P(), P(), P(CELLS, None))
    return jax.shard_map(
        per_device,
        mesh=fine,
        in_specs=placed,
        out_specs=(P(CELLS, MEMBER), P(MEMBER + CELLS, None)),
        check_vma=False,
    )
```

```python
import functools

import jax
import jax.numpy as jnp
import numpy as np
from jax import lax
from jax.experimental import pallas as pl
from jax.experimental.pallas import tpu as pltpu
from jax.sharding import PartitionSpec as P

HEADS = 16
WIN = 256
BLOCK = 256
WIDTH = 256
HEAD_WIDTH = 64
PAIR = 128
NEVER = -1e30

alpha_fair = 0.95
smooth_width = 0.0625

BF = jnp.bfloat16
F32 = jnp.float32


def smooth_abs(values):
    return jnp.sqrt(values * values + smooth_width)


def smooth_sign(values):
    return values * lax.rsqrt(values * values + smooth_width)


def layer_norm(latent_rows):
    values = latent_rows.astype(F32)
    center = values - jnp.mean(values, axis=-1, keepdims=True)
    spread = jnp.mean(center * center, axis=-1, keepdims=True)
    return (center * lax.rsqrt(spread + 1e-05)).astype(BF)


def dot_nn(left, right):
    return lax.dot_general(left, right, (((1,), (0,)), ((), ())), preferred_element_type=F32)


def dot_nt(left, right):
    return lax.dot_general(left, right, (((1,), (1,)), ((), ())), preferred_element_type=F32)


def dot_tn(left, right):
    return lax.dot_general(left, right, (((0,), (0,)), ((), ())), preferred_element_type=F32)


def iota(shape, axis):
    return lax.broadcasted_iota(jnp.int32, shape, axis)


FREE = pl.CostEstimate(flops=0, bytes_accessed=0, transcendentals=0)
HBM = pl.BlockSpec(memory_space=pltpu.HBM)


def in_hbm(values):
    return pltpu.with_memory_space_constraint(values, pltpu.HBM)


def fetches(weight_ref, buffer, arrived, width, first):
    return [
        pltpu.make_async_copy(
            weight_ref.at[:, pl.ds(first + place * width, width)],
            buffer.at[place],
            arrived.at[place],
        )
        for place in range(buffer.shape[0])
    ]


def fetch_one(weight_ref, buffer, arrived, width, first, place):
    start = pl.multiple_of(first + place * width, width)
    return pltpu.make_async_copy(
        weight_ref.at[:, pl.ds(start, width)], buffer.at[place], arrived.at[place]
    )


def project_kernel(latent_ref, weight_ref, projected_ref, turned_ref, normed, buffer, arrived):
    step = pl.program_id(0)

    @pl.when(step == 0)
    def _():
        for copy in fetches(weight_ref, buffer, arrived, 512, 0):
            copy.start()
        normed[...] = layer_norm(latent_ref[...])
        turned_ref[...] = normed[...].T

    fetch_one(weight_ref, buffer, arrived, 512, 0, step).wait()
    projected_ref[...] = dot_nn(normed[...], buffer[step]).astype(BF)


def project(latent_own, w_qkv):
    rows, width = latent_own.shape
    return pl.pallas_call(
        project_kernel,
        grid=(6,),
        in_specs=[pl.BlockSpec((rows, width), lambda j: (0, 0)), HBM],
        out_specs=[
            pl.BlockSpec((rows, 512), lambda j: (0, j)),
            pl.BlockSpec((width, rows), lambda j: (0, 0)),
        ],
        out_shape=[
            jax.ShapeDtypeStruct((rows, 3 * width), BF),
            jax.ShapeDtypeStruct((width, rows), BF),
        ],
        scratch_shapes=[
            pltpu.VMEM((rows, width), BF),
            pltpu.VMEM((6, width, 512), BF),
            pltpu.SemaphoreType.DMA((6,)),
        ],
        compiler_params=pltpu.CompilerParams(vmem_limit_bytes=16 * 1024 * 1024),
        cost_estimate=pl.CostEstimate(
            flops=2 * rows * width * width * 4, bytes_accessed=8 << 20, transcendentals=0
        ),
    )(latent_own, in_hbm(w_qkv))


def halo_query_kernel(normed_ref, weight_ref, out_ref, buffer, arrived):
    step = pl.program_id(0)

    @pl.when(step == 0)
    def _():
        for copy in fetches(weight_ref, buffer, arrived, 256, 0):
            copy.start()

    fetch_one(weight_ref, buffer, arrived, 256, 0, step).wait()
    out_ref[...] = dot_nn(normed_ref[...], buffer[step]).astype(BF)


def halo_queries(normed_halo, w_qkv):
    rows, width = normed_halo.shape
    return pl.pallas_call(
        halo_query_kernel,
        grid=(4,),
        in_specs=[pl.BlockSpec((rows, width), lambda j: (0, 0)), HBM],
        out_specs=pl.BlockSpec((rows, 256), lambda j: (0, j)),
        out_shape=jax.ShapeDtypeStruct((rows, width), BF),
        scratch_shapes=[
            pltpu.VMEM((4, width, 256), BF),
            pltpu.SemaphoreType.DMA((4,)),
        ],
        compiler_params=pltpu.CompilerParams(vmem_limit_bytes=12 * 1024 * 1024),
        cost_estimate=FREE,
    )(normed_halo, in_hbm(w_qkv))


def partial_kernel(
    core_ref, normed_ref, normed_other_ref, piece_ref, other_ref, small_ref, small_other_ref,
    out_ref,
):
    core = core_ref[0]
    for top in range(2):
        rows = slice(top * 256, (top + 1) * 256)
        own = normed_ref[top, core]
        near = normed_other_ref[top, core]
        for first in range(0, piece_ref.shape[0], 512):
            columns = slice(first, first + 512)
            out_ref[rows, columns] = (
                dot_nt(own, piece_ref[columns]) + dot_nt(near, other_ref[columns])
            ).astype(BF)
        if small_ref is not None:
            out_ref[rows, piece_ref.shape[0] :] = (
                small_ref[top, core].astype(F32) + small_other_ref[top, core].astype(F32)
            ).astype(BF)


def plain_partial_kernel(core_ref, normed_ref, normed_other_ref, piece_ref, other_ref, out_ref):
    partial_kernel(
        core_ref, normed_ref, normed_other_ref, piece_ref, other_ref, None, None, out_ref
    )


def partial_sums(core, turned, turned_other, piece, other, smalls=()):
    by_core = lambda values: values.reshape(2, 2, 256, 256)
    vmem = pl.BlockSpec(memory_space=pltpu.VMEM)
    columns = piece.shape[0] + 256 * (len(smalls) // 2)
    return pl.pallas_call(
        partial_kernel if smalls else plain_partial_kernel,
        in_specs=[pl.BlockSpec(memory_space=pltpu.SMEM)] + [vmem] * (4 + len(smalls)),
        out_specs=vmem,
        out_shape=jax.ShapeDtypeStruct((512, columns), BF),
        compiler_params=pltpu.CompilerParams(vmem_limit_bytes=12 * 1024 * 1024),
        cost_estimate=FREE,
    )(
        core.astype(jnp.int32).reshape(1),
        by_core(turned),
        by_core(turned_other),
        piece,
        other,
        *(by_core(small) for small in smalls),
    )


def spare_lane(shape):
    lane = iota(shape, len(shape) - 1)
    return lane % HEAD_WIDTH


def key_fill(count_pieces):
    fills = []
    for count, rows in count_pieces:
        spare = spare_lane((rows, PAIR))
        bias = jnp.where(iota((rows, PAIR), 0) < count, 0.0, NEVER)
        fills.append(
            jnp.where(spare < 3, 1.0, jnp.where(spare == 3, bias, 0.0)).astype(BF)
        )
    return jnp.concatenate(fills, axis=0)


def stat_spread(step, offset):
    shape = (128, WIDTH)
    lane = iota(shape, 1)
    head = step * 4 + 2 * (lane // PAIR) + jnp.where(lane % PAIR < HEAD_WIDTH, 1, 0)
    term = lane % HEAD_WIDTH
    chosen = (term < 3) & (iota(shape, 0) == term * 32 + offset + head)
    return jnp.where(chosen, -1.0, 0.0).astype(BF)


def keep_band(window, fill):
    shape = (128, 128)
    apart = iota(shape, 0) - iota(shape, 1)
    first = jnp.where(apart >= 0, window[:128], fill)
    last = jnp.where(apart <= 0, window[512:], fill)
    return first, window[128:512], last


def forward_kernel(
    counts_ref,
    left_ref,
    right_ref,
    latent_ref,
    weight_ref,
    q_ref,
    k_ref,
    v_ref,
    w_out_ref,
    readout_ref,
    normed_ref,
    kcat_ref,
    vcat_ref,
    attended_ref,
    stats_ref,
    hidden_ref,
    forecast_ref,
    probs,
    inverse_ref,
    stat_rows,
    buffer,
    arrived,
):
    step = pl.program_id(0)

    @pl.when(step == 0)
    def _():
        copies = fetches(weight_ref, buffer, arrived, WIDTH, 1024)
        for place in (0, 4, 1, 5, 2, 6, 3, 7):
            copies[place].start()
        normed_ref[:WIN] = layer_norm(left_ref[...])
        normed_ref[WIN:] = layer_norm(right_ref[...])

    fetch_one(weight_ref, buffer, arrived, WIDTH, 1024, step).wait()
    fetch_one(weight_ref, buffer, arrived, WIDTH, 1024, step + 4).wait()
    khalo = dot_nn(normed_ref[...], buffer[step]).astype(BF)
    kcat_ref[:WIN] = khalo[:WIN]
    kcat_ref[WIN : WIN + BLOCK] = k_ref[...]
    kcat_ref[WIN + BLOCK :] = khalo[WIN:]
    vhalo = dot_nn(normed_ref[...], buffer[step + 4]).astype(BF)
    vcat_ref[:WIN] = vhalo[:WIN]
    vcat_ref[WIN : WIN + BLOCK] = v_ref[...]
    vcat_ref[WIN + BLOCK :] = vhalo[WIN:]
    fill = key_fill([(counts_ref[0], WIN), (counts_ref[1], BLOCK), (counts_ref[2], WIN)])
    low_q = iota((BLOCK, PAIR), 1) < HEAD_WIDTH
    low_k = iota(fill.shape, 1) < HEAD_WIDTH
    query_fill = (spare_lane((BLOCK, PAIR)) == 3).astype(BF)
    scores, turned = [], []
    for pair in range(2):
        columns = slice(pair * PAIR, (pair + 1) * PAIR)
        q_pair = q_ref[:, columns] * jnp.asarray(HEAD_WIDTH ** (-0.5), BF)
        k_pair = kcat_ref[:, columns]
        turned.append(vcat_ref[:, columns].T)
        for half in range(2):
            if half == 0:
                q_head = jnp.where(low_q, q_pair, query_fill)
                k_head = jnp.where(low_k, k_pair, fill)
            else:
                q_head = jnp.where(low_q, query_fill, q_pair)
                k_head = jnp.where(low_k, fill, k_pair)
            scores.append(dot_nt(k_head, q_head))
    tops = []
    for slot in range(4):
        levels = []
        for tile in range(2):
            rows = slice(tile * 128, tile * 128 + 640)
            lanes = slice(tile * 128, tile * 128 + 128)
            first, middle, last = keep_band(scores[slot][rows, lanes], NEVER)
            top = jnp.maximum(
                jnp.max(middle, axis=0, keepdims=True),
                jnp.max(jnp.maximum(first, last), axis=0, keepdims=True),
            )
            start = tile * 128
            probs[slot, start : start + 128, lanes] = jnp.exp(first - top).astype(BF)
            probs[slot, start + 128 : start + 512, lanes] = jnp.exp(middle - top).astype(BF)
            probs[slot, start + 512 : start + 640, lanes] = jnp.exp(last - top).astype(BF)
            levels.append(top)
        probs[slot, :128, 128:] = jnp.zeros((128, 128), BF)
        probs[slot, 640:, :128] = jnp.zeros((128, 128), BF)
        tops.append(jnp.concatenate(levels, axis=1))
    ones = jnp.ones((16, fill.shape[0]), BF)
    for pair in range(2):
        halves = []
        for half in range(2):
            slot = pair * 2 + half
            lanes = slice(half * HEAD_WIDTH, (half + 1) * HEAD_WIDTH)
            values = jnp.concatenate([turned[pair][lanes], ones], axis=0)
            mixed = dot_nn(values, probs[slot])
            total = mixed[HEAD_WIDTH : HEAD_WIDTH + 1]
            inverse = 1.0 / total
            halves.append(mixed[:HEAD_WIDTH] * inverse)
            head = step * 4 + slot
            inverse_ref[pl.ds(head, 1), :] = inverse
            stat_rows[pl.ds(head, 1), :] = tops[slot] + jnp.log(total)
        start = pl.multiple_of(step * WIDTH + pair * PAIR, PAIR)
        attended_ref[:, pl.ds(start, PAIR)] = jnp.concatenate(halves, axis=0).T

    @pl.when(step == 3)
    def _():
        mixed = dot_nn(attended_ref[...].astype(BF), w_out_ref[...])
        hidden = (latent_ref[...].astype(F32) + mixed).astype(BF)
        hidden_ref[...] = hidden
        forecast_ref[...] = dot_nn(hidden, readout_ref[...])
        stat_rows[HEADS:] = jnp.zeros((128 - HEADS, BLOCK), F32)
        stats_ref[...] = stat_rows[...].T


def forward(counts, left, right, latent_own, w_qkv, projected, w_out, readout_weight):
    whole = lambda *shape: pl.BlockSpec(shape, lambda j: (0, 0))
    part = lambda rows, first: pl.BlockSpec((rows, WIDTH), lambda j: (0, first + j))
    window = 2 * WIN + BLOCK
    return pl.pallas_call(
        forward_kernel,
        grid=(4,),
        in_specs=[
            pl.BlockSpec(memory_space=pltpu.SMEM),
            whole(WIN, 1024),
            whole(WIN, 1024),
            whole(BLOCK, 1024),
            HBM,
            part(BLOCK, 0),
            part(BLOCK, 4),
            part(BLOCK, 8),
            whole(1024, 1024),
            whole(1024, 128),
        ],
        out_specs=[
            whole(2 * WIN, 1024),
            part(window, 0),
            part(window, 0),
            whole(BLOCK, 1024),
            whole(BLOCK, 128),
            whole(BLOCK, 1024),
            whole(BLOCK, 128),
            pl.BlockSpec((4, window, BLOCK), lambda j: (j, 0, 0)),
            whole(HEADS, BLOCK),
        ],
        out_shape=[
            jax.ShapeDtypeStruct((2 * WIN, 1024), BF),
            jax.ShapeDtypeStruct((window, 1024), BF),
            jax.ShapeDtypeStruct((window, 1024), BF),
            jax.ShapeDtypeStruct((BLOCK, 1024), F32),
            jax.ShapeDtypeStruct((BLOCK, 128), F32),
            jax.ShapeDtypeStruct((BLOCK, 1024), BF),
            jax.ShapeDtypeStruct((BLOCK, 128), F32),
            jax.ShapeDtypeStruct((HEADS, window, BLOCK), BF),
            jax.ShapeDtypeStruct((HEADS, BLOCK), F32),
        ],
        scratch_shapes=[
            pltpu.VMEM((128, BLOCK), F32),
            pltpu.VMEM((8, 1024, WIDTH), BF),
            pltpu.SemaphoreType.DMA((8,)),
        ],
        compiler_params=pltpu.CompilerParams(vmem_limit_bytes=30 * 1024 * 1024),
        cost_estimate=pl.CostEstimate(
            flops=6 << 30, bytes_accessed=12 << 20, transcendentals=3 << 20
        ),
    )(
        counts,
        left,
        right,
        latent_own,
        in_hbm(w_qkv),
        projected,
        projected,
        projected,
        w_out,
        readout_weight,
    )


def score_kernel(
    counts_ref,
    own_ref,
    near_ref,
    others_ref,
    target_ref,
    attended_ref,
    hidden_ref,
    stats_ref,
    w_out_ref,
    readout_ref,
    crps_ref,
    packed_ref,
    grad_ref,
    small_ref,
):
    members = 4
    fair_eps = (1.0 - alpha_fair) / members
    coefficient = (1.0 - fair_eps) / (members * (members - 1))
    valid = (iota((BLOCK, 1), 0) < counts_ref[1]).astype(F32)
    own = own_ref[...]
    forecasts = [own, near_ref[...], others_ref[0], others_ref[1]]
    target = target_ref[...]
    error = jnp.zeros_like(target)
    for forecast in forecasts:
        error += smooth_abs(forecast - target)
    spread = jnp.full_like(target, members * smooth_width**0.5)
    for first in range(members):
        for second in range(first + 1, members):
            spread += 2.0 * smooth_abs(forecasts[first] - forecasts[second])
    crps_ref[...] = valid * (error / members - 0.5 * coefficient * spread)
    pull = jnp.zeros_like(target)
    for other in forecasts[1:]:
        pull += smooth_sign(own - other)
    slope = (
        valid / 128 * (smooth_sign(own - target) / members - coefficient * pull)
    ).astype(BF)
    dhidden = dot_nt(slope, readout_ref[...]).astype(BF)
    dattended = dot_nt(dhidden, w_out_ref[...]).astype(BF)
    grad_ref[...] = dattended
    attended = attended_ref[...]
    product = dattended.astype(F32) * attended
    high = product.astype(BF)
    low = (product - high.astype(F32)).astype(BF)
    pick = (iota((1024, 128), 0) // HEAD_WIDTH + HEADS == iota((1024, 128), 1)).astype(BF)
    stats = stats_ref[...] + dot_nn(high, pick) + dot_nn(low, pick)
    first = stats.astype(BF)
    rest = stats - first.astype(F32)
    second = rest.astype(BF)
    third = (rest - second.astype(F32)).astype(BF)
    terms = jnp.zeros((BLOCK, 128), F32)
    for place, term in enumerate((first, second, third)):
        shift = (iota((128, 128), 0) + 32 * place == iota((128, 128), 1)) & (
            iota((128, 128), 0) < 32
        )
        terms += dot_nn(term, shift.astype(BF))
    packed_ref[:, :128] = slope
    packed_ref[:, 128:] = terms.astype(BF)
    small_ref[:, :128] = dot_tn(attended.astype(BF), slope).astype(BF)
    small_ref[:, 128:] = dot_tn(hidden_ref[...], slope).astype(BF)


def score(counts, own, near, others, target, attended, hidden, stats, w_out, readout_weight):
    vmem = pl.BlockSpec(memory_space=pltpu.VMEM)
    return pl.pallas_call(
        score_kernel,
        in_specs=[pl.BlockSpec(memory_space=pltpu.SMEM)] + [vmem] * 9,
        out_specs=[vmem] * 4,
        out_shape=[
            jax.ShapeDtypeStruct((BLOCK, 128), F32),
            jax.ShapeDtypeStruct((BLOCK, 256), BF),
            jax.ShapeDtypeStruct((BLOCK, 1024), BF),
            jax.ShapeDtypeStruct((1024, 256), BF),
        ],
        compiler_params=pltpu.CompilerParams(vmem_limit_bytes=12 * 1024 * 1024),
    )(counts, own, near, others, target, attended, hidden, stats, w_out, readout_weight)


def query_kernel(
    kcat_ref, vcat_ref, grad_ref, packed_ref, probs_ref, inverse_ref, dq_ref, dscores
):
    step = pl.program_id(0)
    window = kcat_ref.shape[0]
    value_fill = (spare_lane((window, PAIR)) < 3).astype(BF)
    low_q = iota((BLOCK, PAIR), 1) < HEAD_WIDTH
    low_k = iota((window, PAIR), 1) < HEAD_WIDTH
    g_fill = dot_nn(packed_ref[:, 128:], stat_spread(step, HEADS)).astype(BF)
    turned = []
    for pair in range(2):
        columns = slice(pair * PAIR, (pair + 1) * PAIR)
        g_pair = grad_ref[:, columns]
        v_pair = vcat_ref[:, columns]
        k_turned = kcat_ref[:, columns].T
        for half in range(2):
            slot = pair * 2 + half
            pick_q = low_q if half == 0 else ~low_q
            pick_k = low_k if half == 0 else ~low_k
            g_head = jnp.where(pick_q, g_pair, g_fill[:, columns])
            v_head = jnp.where(pick_k, v_pair, value_fill)
            change = dot_nt(v_head, g_head)
            dscores[slot] = (probs_ref[slot].astype(F32) * change).astype(BF)
            turned.append(k_turned[half * HEAD_WIDTH : (half + 1) * HEAD_WIDTH])
    for slot in range(4):
        scale = inverse_ref[pl.ds(step * 4 + slot, 1), :] * HEAD_WIDTH ** (-0.5)
        dquery = dot_nn(turned[slot], dscores[slot]) * scale
        dq_ref[slot * HEAD_WIDTH : (slot + 1) * HEAD_WIDTH] = dquery.astype(BF)


def query_grads(kcat, vcat, grad, packed, probs, inverse):
    part = lambda rows, first: pl.BlockSpec((rows, WIDTH), lambda j: (0, first + j))
    window = 2 * WIN + BLOCK
    return pl.pallas_call(
        query_kernel,
        grid=(4,),
        in_specs=[
            part(window, 0),
            part(window, 0),
            part(BLOCK, 0),
            pl.BlockSpec((BLOCK, 256), lambda j: (0, 0)),
            pl.BlockSpec((4, window, BLOCK), lambda j: (j, 0, 0)),
            pl.BlockSpec((HEADS, BLOCK), lambda j: (0, 0)),
        ],
        out_specs=pl.BlockSpec((WIDTH, BLOCK), lambda j: (j, 0)),
        out_shape=jax.ShapeDtypeStruct((1024, BLOCK), BF),
        scratch_shapes=[pltpu.VMEM((4, window, BLOCK), BF)],
        compiler_params=pltpu.CompilerParams(vmem_limit_bytes=16 * 1024 * 1024),
        cost_estimate=pl.CostEstimate(
            flops=6 << 30, bytes_accessed=5 << 20, transcendentals=3 << 20
        ),
    )(kcat, vcat, grad, packed, probs, inverse)


def key_kernel(
    counts_ref,
    q_ref,
    k_ref,
    v_ref,
    qhalo_ref,
    grad_ref,
    own_ref,
    left_ref,
    right_ref,
    w_out_ref,
    readout_ref,
    out_ref,
    probs,
    dscores,
    dhidden,
):
    step = pl.program_id(0)

    @pl.when(step == 0)
    def _():
        probs[...] = jnp.zeros_like(probs)
        dscores[...] = jnp.zeros_like(dscores)
        dhidden[:WIN] = dot_nt(left_ref[:, :128], readout_ref[...]).astype(BF)
        dhidden[WIN:] = dot_nt(right_ref[:, :128], readout_ref[...]).astype(BF)

    ghalo = dot_nt(dhidden[...], w_out_ref[...]).astype(BF)
    terms = jnp.concatenate(
        [left_ref[:, 128:], own_ref[:, 128:], right_ref[:, 128:]], axis=0
    )
    window = terms.shape[0]
    fill = key_fill([(counts_ref[1], BLOCK)])
    value_fill = (spare_lane(fill.shape) < 3).astype(BF)
    low_q = iota((window, PAIR), 1) < HEAD_WIDTH
    low_k = iota(fill.shape, 1) < HEAD_WIDTH
    ones = (spare_lane((window, WIDTH)) == 3).astype(F32)
    q_fill = (dot_nn(terms, stat_spread(step, 0)) + ones).astype(BF)
    g_fill = dot_nn(terms, stat_spread(step, HEADS)).astype(BF)
    turned = []
    for pair in range(2):
        columns = slice(pair * PAIR, (pair + 1) * PAIR)
        q_pair = jnp.concatenate(
            [qhalo_ref[:WIN, columns], q_ref[:, columns], qhalo_ref[WIN:, columns]], axis=0
        ) * jnp.asarray(HEAD_WIDTH ** (-0.5), BF)
        g_pair = jnp.concatenate(
            [ghalo[:WIN, columns], grad_ref[:, columns], ghalo[WIN:, columns]], axis=0
        )
        k_pair = k_ref[:, columns]
        v_pair = v_ref[:, columns]
        q_turned = q_pair.T
        g_turned = g_pair.T
        for half in range(2):
            slot = pair * 2 + half
            pick_q = low_q if half == 0 else ~low_q
            pick_k = low_k if half == 0 else ~low_k
            q_head = jnp.where(pick_q, q_pair, q_fill[:, columns])
            g_head = jnp.where(pick_q, g_pair, g_fill[:, columns])
            k_head = jnp.where(pick_k, k_pair, fill)
            v_head = jnp.where(pick_k, v_pair, value_fill)
            scores = dot_nt(q_head, k_head)
            change = dot_nt(g_head, v_head)
            for tile in range(2):
                rows = slice(tile * 128, tile * 128 + 640)
                lanes = slice(tile * 128, tile * 128 + 128)
                weight = keep_band(jnp.exp(scores[rows, lanes]), 0.0)
                moved = change[rows, lanes]
                start = tile * 128
                for piece, (low, high) in zip(weight, ((0, 128), (128, 512), (512, 640))):
                    place = slice(start + low, start + high)
                    probs[slot, place, lanes] = piece.astype(BF)
                    dscores[slot, place, lanes] = (piece * moved[low:high]).astype(BF)
            lanes = slice(half * HEAD_WIDTH, (half + 1) * HEAD_WIDTH)
            turned.append((q_turned[lanes], g_turned[lanes]))
    for slot in range(4):
        place = slice(slot * HEAD_WIDTH, (slot + 1) * HEAD_WIDTH)
        out_ref[0, place] = dot_nn(turned[slot][0], dscores[slot]).astype(BF)
        out_ref[1, place] = dot_nn(turned[slot][1], probs[slot]).astype(BF)


def key_grads(counts, projected, qhalo, grad, own, left, right, w_out, readout_weight):
    part = lambda rows, first: pl.BlockSpec((rows, WIDTH), lambda j: (0, first + j))
    whole = lambda *shape: pl.BlockSpec(shape, lambda j: (0, 0))
    window = 2 * WIN + BLOCK
    return pl.pallas_call(
        key_kernel,
        grid=(4,),
        in_specs=[
            pl.BlockSpec(memory_space=pltpu.SMEM),
            part(BLOCK, 0),
            part(BLOCK, 4),
            part(BLOCK, 8),
            part(2 * WIN, 0),
            part(BLOCK, 0),
            whole(BLOCK, 256),
            whole(BLOCK, 256),
            whole(BLOCK, 256),
            pl.BlockSpec((WIDTH, 1024), lambda j: (j, 0)),
            whole(1024, 128),
        ],
        out_specs=pl.BlockSpec((2, WIDTH, BLOCK), lambda j: (0, j, 0)),
        out_shape=jax.ShapeDtypeStruct((2, 1024, BLOCK), BF),
        scratch_shapes=[
            pltpu.VMEM((4, window, BLOCK), BF),
            pltpu.VMEM((4, window, BLOCK), BF),
            pltpu.VMEM((2 * WIN, 1024), BF),
        ],
        compiler_params=pltpu.CompilerParams(vmem_limit_bytes=18 * 1024 * 1024),
        cost_estimate=FREE,
    )(
        counts,
        projected,
        projected,
        projected,
        qhalo,
        grad,
        own,
        left,
        right,
        in_hbm(w_out),
        readout_weight,
    )


AXES = ("x_hi", "core", "y", "x_lo", "z")
MEMBER = ("x_hi", "core")
CELLS = ("y", "x_lo", "z")
CHIPS = ("x_hi", "y", "x_lo", "z")
SWAP = [(0, 1), (1, 0)]


def swap_core(values):
    return lax.ppermute(values, "core", SWAP)


def scatter(partial):
    columns = partial.shape[1]
    return lax.all_to_all(partial.reshape(64, 8, columns), CHIPS, split_axis=0, concat_axis=0)


def add_up(pieces):
    return jnp.sum(pieces.astype(F32), axis=0)


def per_device(latent, counts, w_qkv, w_out, readout_weight, target):
    latent_own = latent[0]
    cell_count = 32
    cell_index = lax.axis_index(CELLS)
    member_index = lax.axis_index(MEMBER)
    core = lax.axis_index("core")
    up = [(i, i + 1) for i in range(cell_count - 1)]
    down = [(i + 1, i) for i in range(cell_count - 1)]
    from_left = lax.ppermute(latent_own, CELLS, up)
    from_right = lax.ppermute(latent_own, CELLS, down)

    own_count = counts[cell_index]
    left_count = jnp.where(cell_index > 0, counts[jnp.maximum(cell_index - 1, 0)], 0)
    right_count = jnp.where(
        cell_index < cell_count - 1, counts[jnp.minimum(cell_index + 1, cell_count - 1)], 0
    )
    scalars = jnp.stack([left_count, own_count, right_count])

    projected, turned = project(latent_own, w_qkv)
    turned_other = swap_core(turned)
    normed_halo, kcat, vcat, attended, stats, hidden, forecast, probs, inverse = forward(
        scalars, from_left, from_right, latent_own, w_qkv, projected, w_out, readout_weight
    )
    near = lax.ppermute(forecast, "x_hi", SWAP)
    qhalo = halo_queries(normed_halo, w_qkv)
    near, qhalo = lax.optimization_barrier((near, qhalo))
    others = swap_core(jnp.stack([forecast, near]))
    crps_whole, packed, grad, small = score(
        scalars, forecast, near, others, target, attended, hidden, stats, w_out, readout_weight
    )
    crps = lax.dynamic_slice_in_dim(crps_whole, member_index * 32, 32, 1)
    packed_left = lax.ppermute(packed, CELLS, up)
    packed_right = lax.ppermute(packed, CELLS, down)

    dquery = query_grads(kcat, vcat, grad, packed, probs, inverse)
    dquery, packed_left, packed_right = lax.optimization_barrier(
        (dquery, packed_left, packed_right)
    )

    first_part = partial_sums(
        core, turned, turned_other, dquery, swap_core(dquery), (small, swap_core(small))
    )
    first_part, scalars = lax.optimization_barrier((first_part, scalars))
    first = scatter(first_part)
    pairs = key_grads(
        scalars,
        projected,
        qhalo,
        grad,
        packed,
        packed_left,
        packed_right,
        w_out,
        readout_weight,
    )
    pairs = pairs.reshape(2048, BLOCK)
    second_part = partial_sums(core, turned, turned_other, pairs, swap_core(pairs))
    second_part, first = lax.optimization_barrier((second_part, first))
    second = add_up(scatter(second_part))
    first = add_up(first)
    grad_out = lax.dot_general(
        first[:, 1024:1152],
        readout_weight.astype(F32),
        (((1,), (1,)), ((), ())),
        precision=lax.Precision.HIGHEST,
        preferred_element_type=F32,
    )
    grads = jnp.concatenate([first[:, :1024], second, grad_out, first[:, 1152:]], axis=1)
    return (crps, grads)


def solution(mesh):
    fine = jax.sharding.Mesh(mesh.devices.reshape(2, 2, 4, 2, 4), AXES)
    placed = (P(MEMBER, CELLS, None), P(), P(), P(), P(), P(CELLS, None))
    return jax.shard_map(
        per_device,
        mesh=fine,
        in_specs=placed,
        out_specs=(P(CELLS, MEMBER), P(MEMBER + CELLS, None)),
        check_vma=False,
    )
```

```python
import functools

import jax
import jax.numpy as jnp
import numpy as np
from jax import lax
from jax.experimental import pallas as pl
from jax.experimental.pallas import tpu as pltpu
from jax.sharding import PartitionSpec as P

HEADS = 16
WIN = 256
BLOCK = 256
WIDTH = 256
HEAD_WIDTH = 64
PAIR = 128
NEVER = -1e30

alpha_fair = 0.95
smooth_width = 0.0625

BF = jnp.bfloat16
F32 = jnp.float32


def smooth_abs(values):
    return jnp.sqrt(values * values + smooth_width)


def smooth_sign(values):
    return values * lax.rsqrt(values * values + smooth_width)


def layer_norm(latent_rows):
    values = latent_rows.astype(F32)
    center = values - jnp.mean(values, axis=-1, keepdims=True)
    spread = jnp.mean(center * center, axis=-1, keepdims=True)
    return (center * lax.rsqrt(spread + 1e-05)).astype(BF)


def dot_nn(left, right):
    return lax.dot_general(left, right, (((1,), (0,)), ((), ())), preferred_element_type=F32)


def dot_nt(left, right):
    return lax.dot_general(left, right, (((1,), (1,)), ((), ())), preferred_element_type=F32)


def dot_tn(left, right):
    return lax.dot_general(left, right, (((0,), (0,)), ((), ())), preferred_element_type=F32)


def iota(shape, axis):
    return lax.broadcasted_iota(jnp.int32, shape, axis)


FREE = pl.CostEstimate(flops=0, bytes_accessed=0, transcendentals=0)
HBM = pl.BlockSpec(memory_space=pltpu.HBM)


def in_hbm(values):
    return pltpu.with_memory_space_constraint(values, pltpu.HBM)


def in_vmem(values):
    return pltpu.with_memory_space_constraint(values, pltpu.VMEM)


def fetches(weight_ref, buffer, arrived, width, first):
    return [
        pltpu.make_async_copy(
            weight_ref.at[:, pl.ds(first + place * width, width)],
            buffer.at[place],
            arrived.at[place],
        )
        for place in range(buffer.shape[0])
    ]


def fetch_one(weight_ref, buffer, arrived, width, first, place):
    start = pl.multiple_of(first + place * width, width)
    return pltpu.make_async_copy(
        weight_ref.at[:, pl.ds(start, width)], buffer.at[place], arrived.at[place]
    )


def project_kernel(latent_ref, weight_ref, projected_ref, turned_ref, normed, buffer, arrived):
    step = pl.program_id(0)

    @pl.when(step == 0)
    def _():
        for copy in fetches(weight_ref, buffer, arrived, 512, 0):
            copy.start()
        normed[...] = layer_norm(latent_ref[...])
        turned_ref[...] = normed[...].T

    fetch_one(weight_ref, buffer, arrived, 512, 0, step).wait()
    projected_ref[...] = dot_nn(normed[...], buffer[step]).astype(BF)


def project(latent_own, w_qkv):
    rows, width = latent_own.shape
    return pl.pallas_call(
        project_kernel,
        grid=(6,),
        in_specs=[pl.BlockSpec((rows, width), lambda j: (0, 0)), HBM],
        out_specs=[
            pl.BlockSpec((rows, 512), lambda j: (0, j)),
            pl.BlockSpec((width, rows), lambda j: (0, 0)),
        ],
        out_shape=[
            jax.ShapeDtypeStruct((rows, 3 * width), BF),
            jax.ShapeDtypeStruct((width, rows), BF),
        ],
        scratch_shapes=[
            pltpu.VMEM((rows, width), BF),
            pltpu.VMEM((6, width, 512), BF),
            pltpu.SemaphoreType.DMA((6,)),
        ],
        compiler_params=pltpu.CompilerParams(vmem_limit_bytes=16 * 1024 * 1024),
        cost_estimate=pl.CostEstimate(
            flops=2 * rows * width * width * 4, bytes_accessed=8 << 20, transcendentals=0
        ),
    )(latent_own, in_hbm(w_qkv))


def halo_query_kernel(normed_ref, weight_ref, out_ref, buffer, arrived):
    step = pl.program_id(0)

    @pl.when(step == 0)
    def _():
        for copy in fetches(weight_ref, buffer, arrived, 256, 0):
            copy.start()

    fetch_one(weight_ref, buffer, arrived, 256, 0, step).wait()
    out_ref[...] = dot_nn(normed_ref[...], buffer[step]).astype(BF)


def halo_queries(normed_halo, w_qkv):
    rows, width = normed_halo.shape
    return pl.pallas_call(
        halo_query_kernel,
        grid=(4,),
        in_specs=[pl.BlockSpec((rows, width), lambda j: (0, 0)), HBM],
        out_specs=pl.BlockSpec((rows, 256), lambda j: (0, j)),
        out_shape=jax.ShapeDtypeStruct((rows, width), BF),
        scratch_shapes=[
            pltpu.VMEM((4, width, 256), BF),
            pltpu.SemaphoreType.DMA((4,)),
        ],
        compiler_params=pltpu.CompilerParams(vmem_limit_bytes=12 * 1024 * 1024),
        cost_estimate=FREE,
    )(normed_halo, in_hbm(w_qkv))


def partial_kernel(
    core_ref, normed_ref, normed_other_ref, piece_ref, other_ref, small_ref, small_other_ref,
    out_ref,
):
    core = core_ref[0]
    for top in range(2):
        rows = slice(top * 256, (top + 1) * 256)
        own = normed_ref[top, core]
        near = normed_other_ref[top, core]
        for first in range(0, piece_ref.shape[0], 512):
            columns = slice(first, first + 512)
            out_ref[rows, columns] = (
                dot_nt(own, piece_ref[columns]) + dot_nt(near, other_ref[columns])
            ).astype(BF)
        if small_ref is not None:
            out_ref[rows, piece_ref.shape[0] :] = (
                small_ref[top, core].astype(F32) + small_other_ref[top, core].astype(F32)
            ).astype(BF)


def plain_partial_kernel(core_ref, normed_ref, normed_other_ref, piece_ref, other_ref, out_ref):
    partial_kernel(
        core_ref, normed_ref, normed_other_ref, piece_ref, other_ref, None, None, out_ref
    )


def partial_sums(core, turned, turned_other, piece, other, smalls=()):
    by_core = lambda values: values.reshape(2, 2, 256, 256)
    vmem = pl.BlockSpec(memory_space=pltpu.VMEM)
    columns = piece.shape[0] + 256 * (len(smalls) // 2)
    return pl.pallas_call(
        partial_kernel if smalls else plain_partial_kernel,
        in_specs=[pl.BlockSpec(memory_space=pltpu.SMEM)] + [vmem] * (4 + len(smalls)),
        out_specs=vmem,
        out_shape=jax.ShapeDtypeStruct((512, columns), BF),
        compiler_params=pltpu.CompilerParams(vmem_limit_bytes=12 * 1024 * 1024),
        cost_estimate=FREE,
    )(
        core.astype(jnp.int32).reshape(1),
        in_vmem(by_core(turned)),
        in_vmem(by_core(turned_other)),
        in_vmem(piece),
        in_vmem(other),
        *(in_vmem(by_core(small)) for small in smalls),
    )


def spare_lane(shape):
    lane = iota(shape, len(shape) - 1)
    return lane % HEAD_WIDTH


def key_fill(count_pieces):
    fills = []
    for count, rows in count_pieces:
        spare = spare_lane((rows, PAIR))
        bias = jnp.where(iota((rows, PAIR), 0) < count, 0.0, NEVER)
        fills.append(
            jnp.where(spare < 3, 1.0, jnp.where(spare == 3, bias, 0.0)).astype(BF)
        )
    return jnp.concatenate(fills, axis=0)


def stat_spread(step, offset):
    shape = (128, WIDTH)
    lane = iota(shape, 1)
    head = step * 4 + 2 * (lane // PAIR) + jnp.where(lane % PAIR < HEAD_WIDTH, 1, 0)
    term = lane % HEAD_WIDTH
    chosen = (term < 3) & (iota(shape, 0) == term * 32 + offset + head)
    return jnp.where(chosen, -1.0, 0.0).astype(BF)


def keep_band(window, fill):
    shape = (128, 128)
    apart = iota(shape, 0) - iota(shape, 1)
    first = jnp.where(apart >= 0, window[:128], fill)
    last = jnp.where(apart <= 0, window[512:], fill)
    return first, window[128:512], last


def forward_kernel(
    counts_ref,
    left_ref,
    right_ref,
    latent_ref,
    weight_ref,
    q_ref,
    k_ref,
    v_ref,
    w_out_ref,
    readout_ref,
    normed_ref,
    kcat_ref,
    vcat_ref,
    attended_ref,
    stats_ref,
    hidden_ref,
    forecast_ref,
    probs,
    inverse_ref,
    stat_rows,
    buffer,
    arrived,
):
    step = pl.program_id(0)

    @pl.when(step == 0)
    def _():
        copies = fetches(weight_ref, buffer, arrived, WIDTH, 1024)
        for place in (0, 4, 1, 5, 2, 6, 3, 7):
            copies[place].start()
        normed_ref[:WIN] = layer_norm(left_ref[...])
        normed_ref[WIN:] = layer_norm(right_ref[...])

    fetch_one(weight_ref, buffer, arrived, WIDTH, 1024, step).wait()
    fetch_one(weight_ref, buffer, arrived, WIDTH, 1024, step + 4).wait()
    khalo = dot_nn(normed_ref[...], buffer[step]).astype(BF)
    kcat_ref[:WIN] = khalo[:WIN]
    kcat_ref[WIN : WIN + BLOCK] = k_ref[...]
    kcat_ref[WIN + BLOCK :] = khalo[WIN:]
    vhalo = dot_nn(normed_ref[...], buffer[step + 4]).astype(BF)
    vcat_ref[:WIN] = vhalo[:WIN]
    vcat_ref[WIN : WIN + BLOCK] = v_ref[...]
    vcat_ref[WIN + BLOCK :] = vhalo[WIN:]
    fill = key_fill([(counts_ref[0], WIN), (counts_ref[1], BLOCK), (counts_ref[2], WIN)])
    low_q = iota((BLOCK, PAIR), 1) < HEAD_WIDTH
    low_k = iota(fill.shape, 1) < HEAD_WIDTH
    query_fill = (spare_lane((BLOCK, PAIR)) == 3).astype(BF)
    scores, turned = [], []
    for pair in range(2):
        columns = slice(pair * PAIR, (pair + 1) * PAIR)
        q_pair = q_ref[:, columns] * jnp.asarray(HEAD_WIDTH ** (-0.5), BF)
        k_pair = kcat_ref[:, columns]
        turned.append(vcat_ref[:, columns].T)
        for half in range(2):
            if half == 0:
                q_head = jnp.where(low_q, q_pair, query_fill)
                k_head = jnp.where(low_k, k_pair, fill)
            else:
                q_head = jnp.where(low_q, query_fill, q_pair)
                k_head = jnp.where(low_k, fill, k_pair)
            scores.append(dot_nt(k_head, q_head))
    tops = []
    for slot in range(4):
        levels = []
        for tile in range(2):
            rows = slice(tile * 128, tile * 128 + 640)
            lanes = slice(tile * 128, tile * 128 + 128)
            first, middle, last = keep_band(scores[slot][rows, lanes], NEVER)
            top = jnp.maximum(
                jnp.max(middle, axis=0, keepdims=True),
                jnp.max(jnp.maximum(first, last), axis=0, keepdims=True),
            )
            start = tile * 128
            probs[slot, start : start + 128, lanes] = jnp.exp(first - top).astype(BF)
            probs[slot, start + 128 : start + 512, lanes] = jnp.exp(middle - top).astype(BF)
            probs[slot, start + 512 : start + 640, lanes] = jnp.exp(last - top).astype(BF)
            levels.append(top)
        probs[slot, :128, 128:] = jnp.zeros((128, 128), BF)
        probs[slot, 640:, :128] = jnp.zeros((128, 128), BF)
        tops.append(jnp.concatenate(levels, axis=1))
    ones = jnp.ones((16, fill.shape[0]), BF)
    for pair in range(2):
        halves = []
        for half in range(2):
            slot = pair * 2 + half
            lanes = slice(half * HEAD_WIDTH, (half + 1) * HEAD_WIDTH)
            values = jnp.concatenate([turned[pair][lanes], ones], axis=0)
            mixed = dot_nn(values, probs[slot])
            total = mixed[HEAD_WIDTH : HEAD_WIDTH + 1]
            inverse = 1.0 / total
            halves.append(mixed[:HEAD_WIDTH] * inverse)
            head = step * 4 + slot
            inverse_ref[pl.ds(head, 1), :] = inverse
            stat_rows[pl.ds(head, 1), :] = tops[slot] + jnp.log(total)
        start = pl.multiple_of(step * WIDTH + pair * PAIR, PAIR)
        attended_ref[:, pl.ds(start, PAIR)] = jnp.concatenate(halves, axis=0).T

    @pl.when(step == 3)
    def _():
        mixed = dot_nn(attended_ref[...].astype(BF), w_out_ref[...])
        hidden = (latent_ref[...].astype(F32) + mixed).astype(BF)
        hidden_ref[...] = hidden
        forecast_ref[...] = dot_nn(hidden, readout_ref[...])
        stat_rows[HEADS:] = jnp.zeros((128 - HEADS, BLOCK), F32)
        stats_ref[...] = stat_rows[...].T


def forward(counts, left, right, latent_own, w_qkv, projected, w_out, readout_weight):
    whole = lambda *shape: pl.BlockSpec(shape, lambda j: (0, 0))
    part = lambda rows, first: pl.BlockSpec((rows, WIDTH), lambda j: (0, first + j))
    window = 2 * WIN + BLOCK
    return pl.pallas_call(
        forward_kernel,
        grid=(4,),
        in_specs=[
            pl.BlockSpec(memory_space=pltpu.SMEM),
            whole(WIN, 1024),
            whole(WIN, 1024),
            whole(BLOCK, 1024),
            HBM,
            part(BLOCK, 0),
            part(BLOCK, 4),
            part(BLOCK, 8),
            whole(1024, 1024),
            whole(1024, 128),
        ],
        out_specs=[
            whole(2 * WIN, 1024),
            part(window, 0),
            part(window, 0),
            whole(BLOCK, 1024),
            whole(BLOCK, 128),
            whole(BLOCK, 1024),
            whole(BLOCK, 128),
            pl.BlockSpec((4, window, BLOCK), lambda j: (j, 0, 0)),
            whole(HEADS, BLOCK),
        ],
        out_shape=[
            jax.ShapeDtypeStruct((2 * WIN, 1024), BF),
            jax.ShapeDtypeStruct((window, 1024), BF),
            jax.ShapeDtypeStruct((window, 1024), BF),
            jax.ShapeDtypeStruct((BLOCK, 1024), F32),
            jax.ShapeDtypeStruct((BLOCK, 128), F32),
            jax.ShapeDtypeStruct((BLOCK, 1024), BF),
            jax.ShapeDtypeStruct((BLOCK, 128), F32),
            pltpu.HBM((HEADS, window, BLOCK), BF),
            jax.ShapeDtypeStruct((HEADS, BLOCK), F32),
        ],
        scratch_shapes=[
            pltpu.VMEM((128, BLOCK), F32),
            pltpu.VMEM((8, 1024, WIDTH), BF),
            pltpu.SemaphoreType.DMA((8,)),
        ],
        compiler_params=pltpu.CompilerParams(vmem_limit_bytes=30 * 1024 * 1024),
        cost_estimate=pl.CostEstimate(
            flops=6 << 30, bytes_accessed=12 << 20, transcendentals=3 << 20
        ),
    )(
        counts,
        left,
        right,
        latent_own,
        in_hbm(w_qkv),
        projected,
        projected,
        projected,
        w_out,
        readout_weight,
    )


def score_kernel(
    counts_ref,
    own_ref,
    near_ref,
    others_ref,
    target_ref,
    attended_ref,
    hidden_ref,
    stats_ref,
    w_out_ref,
    readout_ref,
    crps_ref,
    packed_ref,
    grad_ref,
    small_ref,
):
    members = 4
    fair_eps = (1.0 - alpha_fair) / members
    coefficient = (1.0 - fair_eps) / (members * (members - 1))
    valid = (iota((BLOCK, 1), 0) < counts_ref[1]).astype(F32)
    own = own_ref[...]
    forecasts = [own, near_ref[...], others_ref[0], others_ref[1]]
    target = target_ref[...]
    error = jnp.zeros_like(target)
    for forecast in forecasts:
        error += smooth_abs(forecast - target)
    spread = jnp.full_like(target, members * smooth_width**0.5)
    for first in range(members):
        for second in range(first + 1, members):
            spread += 2.0 * smooth_abs(forecasts[first] - forecasts[second])
    crps_ref[...] = valid * (error / members - 0.5 * coefficient * spread)
    pull = jnp.zeros_like(target)
    for other in forecasts[1:]:
        pull += smooth_sign(own - other)
    slope = (
        valid / 128 * (smooth_sign(own - target) / members - coefficient * pull)
    ).astype(BF)
    dhidden = dot_nt(slope, readout_ref[...]).astype(BF)
    dattended = dot_nt(dhidden, w_out_ref[...]).astype(BF)
    grad_ref[...] = dattended
    attended = attended_ref[...]
    product = dattended.astype(F32) * attended
    high = product.astype(BF)
    low = (product - high.astype(F32)).astype(BF)
    pick = (iota((1024, 128), 0) // HEAD_WIDTH + HEADS == iota((1024, 128), 1)).astype(BF)
    stats = stats_ref[...] + dot_nn(high, pick) + dot_nn(low, pick)
    first = stats.astype(BF)
    rest = stats - first.astype(F32)
    second = rest.astype(BF)
    third = (rest - second.astype(F32)).astype(BF)
    terms = jnp.zeros((BLOCK, 128), F32)
    for place, term in enumerate((first, second, third)):
        shift = (iota((128, 128), 0) + 32 * place == iota((128, 128), 1)) & (
            iota((128, 128), 0) < 32
        )
        terms += dot_nn(term, shift.astype(BF))
    packed_ref[:, :128] = slope
    packed_ref[:, 128:] = terms.astype(BF)
    small_ref[:, :128] = dot_tn(attended.astype(BF), slope).astype(BF)
    small_ref[:, 128:] = dot_tn(hidden_ref[...], slope).astype(BF)


def score(counts, own, near, others, target, attended, hidden, stats, w_out, readout_weight):
    vmem = pl.BlockSpec(memory_space=pltpu.VMEM)
    return pl.pallas_call(
        score_kernel,
        in_specs=[pl.BlockSpec(memory_space=pltpu.SMEM)] + [vmem] * 9,
        out_specs=[vmem] * 4,
        out_shape=[
            jax.ShapeDtypeStruct((BLOCK, 128), F32),
            pltpu.VMEM((BLOCK, 256), BF),
            pltpu.VMEM((BLOCK, 1024), BF),
            pltpu.VMEM((1024, 256), BF),
        ],
        compiler_params=pltpu.CompilerParams(vmem_limit_bytes=12 * 1024 * 1024),
    )(counts, own, near, others, target, attended, hidden, stats, w_out, readout_weight)


def query_kernel(
    kcat_ref, vcat_ref, grad_ref, packed_ref, probs_ref, inverse_ref, dq_ref, dscores
):
    step = pl.program_id(0)
    window = kcat_ref.shape[0]
    value_fill = (spare_lane((window, PAIR)) < 3).astype(BF)
    low_q = iota((BLOCK, PAIR), 1) < HEAD_WIDTH
    low_k = iota((window, PAIR), 1) < HEAD_WIDTH
    g_fill = dot_nn(packed_ref[:, 128:], stat_spread(step, HEADS)).astype(BF)
    turned = []
    for pair in range(2):
        columns = slice(pair * PAIR, (pair + 1) * PAIR)
        g_pair = grad_ref[:, columns]
        v_pair = vcat_ref[:, columns]
        k_turned = kcat_ref[:, columns].T
        for half in range(2):
            slot = pair * 2 + half
            pick_q = low_q if half == 0 else ~low_q
            pick_k = low_k if half == 0 else ~low_k
            g_head = jnp.where(pick_q, g_pair, g_fill[:, columns])
            v_head = jnp.where(pick_k, v_pair, value_fill)
            change = dot_nt(v_head, g_head)
            dscores[slot] = (probs_ref[slot].astype(F32) * change).astype(BF)
            turned.append(k_turned[half * HEAD_WIDTH : (half + 1) * HEAD_WIDTH])
    for slot in range(4):
        scale = inverse_ref[pl.ds(step * 4 + slot, 1), :] * HEAD_WIDTH ** (-0.5)
        dquery = dot_nn(turned[slot], dscores[slot]) * scale
        dq_ref[slot * HEAD_WIDTH : (slot + 1) * HEAD_WIDTH] = dquery.astype(BF)


def query_grads(kcat, vcat, grad, packed, probs, inverse):
    part = lambda rows, first: pl.BlockSpec((rows, WIDTH), lambda j: (0, first + j))
    window = 2 * WIN + BLOCK
    return pl.pallas_call(
        query_kernel,
        grid=(4,),
        in_specs=[
            part(window, 0),
            part(window, 0),
            part(BLOCK, 0),
            pl.BlockSpec((BLOCK, 256), lambda j: (0, 0)),
            pl.BlockSpec((4, window, BLOCK), lambda j: (j, 0, 0)),
            pl.BlockSpec((HEADS, BLOCK), lambda j: (0, 0)),
        ],
        out_specs=pl.BlockSpec((WIDTH, BLOCK), lambda j: (j, 0)),
        out_shape=pltpu.VMEM((1024, BLOCK), BF),
        scratch_shapes=[pltpu.VMEM((4, window, BLOCK), BF)],
        compiler_params=pltpu.CompilerParams(vmem_limit_bytes=16 * 1024 * 1024),
        cost_estimate=pl.CostEstimate(
            flops=6 << 30, bytes_accessed=5 << 20, transcendentals=3 << 20
        ),
    )(kcat, vcat, grad, packed, in_hbm(probs), inverse)


def key_kernel(
    counts_ref,
    q_ref,
    k_ref,
    v_ref,
    qhalo_ref,
    grad_ref,
    own_ref,
    left_ref,
    right_ref,
    w_out_ref,
    readout_ref,
    out_ref,
    probs,
    dscores,
    dhidden,
):
    step = pl.program_id(0)

    @pl.when(step == 0)
    def _():
        probs[...] = jnp.zeros_like(probs)
        dscores[...] = jnp.zeros_like(dscores)
        dhidden[:WIN] = dot_nt(left_ref[:, :128], readout_ref[...]).astype(BF)
        dhidden[WIN:] = dot_nt(right_ref[:, :128], readout_ref[...]).astype(BF)

    ghalo = dot_nt(dhidden[...], w_out_ref[...]).astype(BF)
    terms = jnp.concatenate(
        [left_ref[:, 128:], own_ref[:, 128:], right_ref[:, 128:]], axis=0
    )
    window = terms.shape[0]
    fill = key_fill([(counts_ref[1], BLOCK)])
    value_fill = (spare_lane(fill.shape) < 3).astype(BF)
    low_q = iota((window, PAIR), 1) < HEAD_WIDTH
    low_k = iota(fill.shape, 1) < HEAD_WIDTH
    ones = (spare_lane((window, WIDTH)) == 3).astype(F32)
    q_fill = (dot_nn(terms, stat_spread(step, 0)) + ones).astype(BF)
    g_fill = dot_nn(terms, stat_spread(step, HEADS)).astype(BF)
    turned = []
    for pair in range(2):
        columns = slice(pair * PAIR, (pair + 1) * PAIR)
        q_pair = jnp.concatenate(
            [qhalo_ref[:WIN, columns], q_ref[:, columns], qhalo_ref[WIN:, columns]], axis=0
        ) * jnp.asarray(HEAD_WIDTH ** (-0.5), BF)
        g_pair = jnp.concatenate(
            [ghalo[:WIN, columns], grad_ref[:, columns], ghalo[WIN:, columns]], axis=0
        )
        k_pair = k_ref[:, columns]
        v_pair = v_ref[:, columns]
        q_turned = q_pair.T
        g_turned = g_pair.T
        for half in range(2):
            slot = pair * 2 + half
            pick_q = low_q if half == 0 else ~low_q
            pick_k = low_k if half == 0 else ~low_k
            q_head = jnp.where(pick_q, q_pair, q_fill[:, columns])
            g_head = jnp.where(pick_q, g_pair, g_fill[:, columns])
            k_head = jnp.where(pick_k, k_pair, fill)
            v_head = jnp.where(pick_k, v_pair, value_fill)
            scores = dot_nt(q_head, k_head)
            change = dot_nt(g_head, v_head)
            for tile in range(2):
                rows = slice(tile * 128, tile * 128 + 640)
                lanes = slice(tile * 128, tile * 128 + 128)
                weight = keep_band(jnp.exp(scores[rows, lanes]), 0.0)
                moved = change[rows, lanes]
                start = tile * 128
                for piece, (low, high) in zip(weight, ((0, 128), (128, 512), (512, 640))):
                    place = slice(start + low, start + high)
                    probs[slot, place, lanes] = piece.astype(BF)
                    dscores[slot, place, lanes] = (piece * moved[low:high]).astype(BF)
            lanes = slice(half * HEAD_WIDTH, (half + 1) * HEAD_WIDTH)
            turned.append((q_turned[lanes], g_turned[lanes]))
    for slot in range(4):
        place = slice(slot * HEAD_WIDTH, (slot + 1) * HEAD_WIDTH)
        out_ref[0, place] = dot_nn(turned[slot][0], dscores[slot]).astype(BF)
        out_ref[1, place] = dot_nn(turned[slot][1], probs[slot]).astype(BF)


def key_grads(counts, projected, qhalo, grad, own, left, right, w_out, readout_weight):
    part = lambda rows, first: pl.BlockSpec((rows, WIDTH), lambda j: (0, first + j))
    whole = lambda *shape: pl.BlockSpec(shape, lambda j: (0, 0))
    window = 2 * WIN + BLOCK
    return pl.pallas_call(
        key_kernel,
        grid=(4,),
        in_specs=[
            pl.BlockSpec(memory_space=pltpu.SMEM),
            part(BLOCK, 0),
            part(BLOCK, 4),
            part(BLOCK, 8),
            part(2 * WIN, 0),
            part(BLOCK, 0),
            whole(BLOCK, 256),
            whole(BLOCK, 256),
            whole(BLOCK, 256),
            pl.BlockSpec((WIDTH, 1024), lambda j: (j, 0)),
            whole(1024, 128),
        ],
        out_specs=pl.BlockSpec((2, WIDTH, BLOCK), lambda j: (0, j, 0)),
        out_shape=pltpu.VMEM((2, 1024, BLOCK), BF),
        scratch_shapes=[
            pltpu.VMEM((4, window, BLOCK), BF),
            pltpu.VMEM((4, window, BLOCK), BF),
            pltpu.VMEM((2 * WIN, 1024), BF),
        ],
        compiler_params=pltpu.CompilerParams(vmem_limit_bytes=18 * 1024 * 1024),
        cost_estimate=FREE,
    )(
        counts,
        projected,
        projected,
        projected,
        qhalo,
        in_vmem(grad),
        own,
        in_vmem(left),
        in_vmem(right),
        in_hbm(w_out),
        readout_weight,
    )


AXES = ("x_hi", "core", "y", "x_lo", "z")
MEMBER = ("x_hi", "core")
CELLS = ("y", "x_lo", "z")
CHIPS = ("x_hi", "y", "x_lo", "z")
SWAP = [(0, 1), (1, 0)]


def swap_core(values):
    return lax.ppermute(values, "core", SWAP)


def scatter(partial):
    columns = partial.shape[1]
    return lax.all_to_all(partial.reshape(64, 8, columns), CHIPS, split_axis=0, concat_axis=0)


def add_up(pieces):
    return jnp.sum(pieces.astype(F32), axis=0)


def per_device(latent, counts, w_qkv, w_out, readout_weight, target):
    latent_own = latent[0]
    cell_count = 32
    cell_index = lax.axis_index(CELLS)
    member_index = lax.axis_index(MEMBER)
    core = lax.axis_index("core")
    up = [(i, i + 1) for i in range(cell_count - 1)]
    down = [(i + 1, i) for i in range(cell_count - 1)]
    from_left = lax.ppermute(latent_own, CELLS, up)
    from_right = lax.ppermute(latent_own, CELLS, down)

    own_count = counts[cell_index]
    left_count = jnp.where(cell_index > 0, counts[jnp.maximum(cell_index - 1, 0)], 0)
    right_count = jnp.where(
        cell_index < cell_count - 1, counts[jnp.minimum(cell_index + 1, cell_count - 1)], 0
    )
    scalars = jnp.stack([left_count, own_count, right_count])

    projected, turned = project(latent_own, w_qkv)
    turned_other = swap_core(turned)
    normed_halo, kcat, vcat, attended, stats, hidden, forecast, probs, inverse = forward(
        scalars, from_left, from_right, latent_own, w_qkv, projected, w_out, readout_weight
    )
    near = lax.ppermute(forecast, "x_hi", SWAP)
    qhalo = halo_queries(normed_halo, w_qkv)
    near, qhalo = lax.optimization_barrier((near, qhalo))
    others = swap_core(jnp.stack([forecast, near]))
    crps_whole, packed, grad, small = score(
        scalars, forecast, near, others, target, attended, hidden, stats, w_out, readout_weight
    )
    crps = lax.dynamic_slice_in_dim(crps_whole, member_index * 32, 32, 1)
    packed_left = lax.ppermute(packed, CELLS, up)
    packed_right = lax.ppermute(packed, CELLS, down)

    dquery = query_grads(kcat, vcat, grad, packed, probs, inverse)
    dquery, packed_left, packed_right = lax.optimization_barrier(
        (dquery, packed_left, packed_right)
    )

    first_part = partial_sums(
        core, turned, turned_other, dquery, swap_core(dquery), (small, swap_core(small))
    )
    first_part, scalars = lax.optimization_barrier((first_part, scalars))
    first = scatter(first_part)
    pairs = key_grads(
        scalars,
        projected,
        qhalo,
        grad,
        packed,
        packed_left,
        packed_right,
        w_out,
        readout_weight,
    )
    pairs = pairs.reshape(2048, BLOCK)
    second_part = partial_sums(core, turned, turned_other, pairs, swap_core(pairs))
    second_part, first = lax.optimization_barrier((second_part, first))
    second = add_up(scatter(second_part))
    first = add_up(first)
    grad_out = lax.dot_general(
        first[:, 1024:1152],
        readout_weight.astype(F32),
        (((1,), (1,)), ((), ())),
        precision=lax.Precision.HIGHEST,
        preferred_element_type=F32,
    )
    grads = jnp.concatenate([first[:, :1024], second, grad_out, first[:, 1152:]], axis=1)
    return (crps, grads)


def solution(mesh):
    fine = jax.sharding.Mesh(mesh.devices.reshape(2, 2, 4, 2, 4), AXES)
    placed = (P(MEMBER, CELLS, None), P(), P(), P(), P(), P(CELLS, None))
    return jax.shard_map(
        per_device,
        mesh=fine,
        in_specs=placed,
        out_specs=(P(CELLS, MEMBER), P(MEMBER + CELLS, None)),
        check_vma=False,
    )
```

```python
import functools

import jax
import jax.numpy as jnp
import numpy as np
from jax import lax
from jax.experimental import pallas as pl
from jax.experimental.pallas import tpu as pltpu
from jax.sharding import PartitionSpec as P

HEADS = 16
WIN = 256
BLOCK = 256
WIDTH = 256
HEAD_WIDTH = 64
PAIR = 128
NEVER = -1e30

alpha_fair = 0.95
smooth_width = 0.0625

BF = jnp.bfloat16
F32 = jnp.float32


def smooth_abs(values):
    return jnp.sqrt(values * values + smooth_width)


def smooth_sign(values):
    return values * lax.rsqrt(values * values + smooth_width)


def layer_norm(latent_rows):
    values = latent_rows.astype(F32)
    center = values - jnp.mean(values, axis=-1, keepdims=True)
    spread = jnp.mean(center * center, axis=-1, keepdims=True)
    return (center * lax.rsqrt(spread + 1e-05)).astype(BF)


def dot_nn(left, right):
    return lax.dot_general(left, right, (((1,), (0,)), ((), ())), preferred_element_type=F32)


def dot_nt(left, right):
    return lax.dot_general(left, right, (((1,), (1,)), ((), ())), preferred_element_type=F32)


def dot_tn(left, right):
    return lax.dot_general(left, right, (((0,), (0,)), ((), ())), preferred_element_type=F32)


def iota(shape, axis):
    return lax.broadcasted_iota(jnp.int32, shape, axis)


FREE = pl.CostEstimate(flops=0, bytes_accessed=0, transcendentals=0)
HBM = pl.BlockSpec(memory_space=pltpu.HBM)


def in_hbm(values):
    return pltpu.with_memory_space_constraint(values, pltpu.HBM)


def fetches(weight_ref, buffer, arrived, width, first):
    return [
        pltpu.make_async_copy(
            weight_ref.at[:, pl.ds(first + place * width, width)],
            buffer.at[place],
            arrived.at[place],
        )
        for place in range(buffer.shape[0])
    ]


def fetch_one(weight_ref, buffer, arrived, width, first, place):
    start = pl.multiple_of(first + place * width, width)
    return pltpu.make_async_copy(
        weight_ref.at[:, pl.ds(start, width)], buffer.at[place], arrived.at[place]
    )


def project_kernel(latent_ref, weight_ref, projected_ref, turned_ref, normed, buffer, arrived):
    step = pl.program_id(0)

    @pl.when(step == 0)
    def _():
        for copy in fetches(weight_ref, buffer, arrived, 512, 0):
            copy.start()
        normed[...] = layer_norm(latent_ref[...])
        turned_ref[...] = normed[...].T

    fetch_one(weight_ref, buffer, arrived, 512, 0, step).wait()
    projected_ref[...] = dot_nn(normed[...], buffer[step]).astype(BF)


def project(latent_own, w_qkv):
    rows, width = latent_own.shape
    return pl.pallas_call(
        project_kernel,
        grid=(6,),
        in_specs=[pl.BlockSpec((rows, width), lambda j: (0, 0)), HBM],
        out_specs=[
            pl.BlockSpec((rows, 512), lambda j: (0, j)),
            pl.BlockSpec((width, rows), lambda j: (0, 0)),
        ],
        out_shape=[
            jax.ShapeDtypeStruct((rows, 3 * width), BF),
            jax.ShapeDtypeStruct((width, rows), BF),
        ],
        scratch_shapes=[
            pltpu.VMEM((rows, width), BF),
            pltpu.VMEM((6, width, 512), BF),
            pltpu.SemaphoreType.DMA((6,)),
        ],
        compiler_params=pltpu.CompilerParams(vmem_limit_bytes=16 * 1024 * 1024),
        cost_estimate=pl.CostEstimate(
            flops=2 * rows * width * width * 4, bytes_accessed=8 << 20, transcendentals=0
        ),
    )(latent_own, in_hbm(w_qkv))


def halo_query_kernel(normed_ref, weight_ref, out_ref, buffer, arrived):
    step = pl.program_id(0)

    @pl.when(step == 0)
    def _():
        for copy in fetches(weight_ref, buffer, arrived, 256, 0):
            copy.start()

    fetch_one(weight_ref, buffer, arrived, 256, 0, step).wait()
    out_ref[...] = dot_nn(normed_ref[...], buffer[step]).astype(BF)


def halo_queries(normed_halo, w_qkv):
    rows, width = normed_halo.shape
    return pl.pallas_call(
        halo_query_kernel,
        grid=(4,),
        in_specs=[pl.BlockSpec((rows, width), lambda j: (0, 0)), HBM],
        out_specs=pl.BlockSpec((rows, 256), lambda j: (0, j)),
        out_shape=jax.ShapeDtypeStruct((rows, width), BF),
        scratch_shapes=[
            pltpu.VMEM((4, width, 256), BF),
            pltpu.SemaphoreType.DMA((4,)),
        ],
        compiler_params=pltpu.CompilerParams(vmem_limit_bytes=12 * 1024 * 1024),
        cost_estimate=FREE,
    )(normed_halo, in_hbm(w_qkv))


def partial_kernel(
    smalls, core_ref, normed_ref, normed_other_ref, piece_ref, other_ref, *refs
):
    small_refs, (out_ref, rows, pieces, others, sums, staged, arrived, left) = (
        refs[:smalls],
        refs[smalls:],
    )
    core = core_ref[0]
    chunks = piece_ref.shape[0] // 512
    sources = [
        (normed_ref.at[:, core], rows.at[0]),
        (normed_other_ref.at[:, core], rows.at[1]),
    ]
    for chunk in range(chunks):
        part = pl.ds(chunk * 512, 512)
        sources.append((piece_ref.at[part], pieces.at[chunk]))
        sources.append((other_ref.at[part], others.at[chunk]))
    for place, small_ref in enumerate(small_refs):
        sources.append((small_ref.at[:, core], sums.at[place]))
    copies = [
        pltpu.make_async_copy(source, target, arrived.at[place])
        for place, (source, target) in enumerate(sources)
    ]
    for copy in copies:
        copy.start()
    copies[0].wait()
    copies[1].wait()
    writes = []
    for chunk in range(chunks):
        copies[2 + 2 * chunk].wait()
        copies[3 + 2 * chunk].wait()
        for top in range(2):
            staged[chunk, top * 256 : (top + 1) * 256] = (
                dot_nt(rows[0, top], pieces[chunk]) + dot_nt(rows[1, top], others[chunk])
            ).astype(BF)
        writes.append(
            pltpu.make_async_copy(
                staged.at[chunk], out_ref.at[:, pl.ds(chunk * 512, 512)], left.at[chunk]
            )
        )
        writes[-1].start()
    if smalls:
        copies[-2].wait()
        copies[-1].wait()
        for top in range(2):
            staged[chunks, top * 256 : (top + 1) * 256, :256] = (
                sums[0, top].astype(F32) + sums[1, top].astype(F32)
            ).astype(BF)
        writes.append(
            pltpu.make_async_copy(
                staged.at[chunks, :, pl.ds(0, 256)],
                out_ref.at[:, pl.ds(chunks * 512, 256)],
                left.at[chunks],
            )
        )
        writes[-1].start()
    for write in writes:
        write.wait()


def partial_sums(core, turned, turned_other, piece, other, smalls=()):
    by_core = lambda values: values.reshape(2, 2, 256, 256)
    anywhere = pl.BlockSpec(memory_space=pl.ANY)
    chunks = piece.shape[0] // 512
    columns = piece.shape[0] + 256 * (len(smalls) // 2)
    return pl.pallas_call(
        functools.partial(partial_kernel, len(smalls)),
        in_specs=[pl.BlockSpec(memory_space=pltpu.SMEM)] + [anywhere] * (4 + len(smalls)),
        out_specs=anywhere,
        out_shape=jax.ShapeDtypeStruct((512, columns), BF),
        scratch_shapes=[
            pltpu.VMEM((2, 2, 256, 256), BF),
            pltpu.VMEM((chunks, 512, 256), BF),
            pltpu.VMEM((chunks, 512, 256), BF),
            pltpu.VMEM((2, 2, 256, 256), BF),
            pltpu.VMEM((chunks + 1, 512, 512), BF),
            pltpu.SemaphoreType.DMA((2 + 2 * chunks + len(smalls),)),
            pltpu.SemaphoreType.DMA((chunks + 1,)),
        ],
        compiler_params=pltpu.CompilerParams(vmem_limit_bytes=14 * 1024 * 1024),
        cost_estimate=FREE,
    )(
        core.astype(jnp.int32).reshape(1),
        by_core(turned),
        by_core(turned_other),
        piece,
        other,
        *(by_core(small) for small in smalls),
    )


def spare_lane(shape):
    lane = iota(shape, len(shape) - 1)
    return lane % HEAD_WIDTH


def key_fill(count_pieces):
    fills = []
    for count, rows in count_pieces:
        spare = spare_lane((rows, PAIR))
        bias = jnp.where(iota((rows, PAIR), 0) < count, 0.0, NEVER)
        fills.append(
            jnp.where(spare < 3, 1.0, jnp.where(spare == 3, bias, 0.0)).astype(BF)
        )
    return jnp.concatenate(fills, axis=0)


def stat_spread(step, offset):
    shape = (128, WIDTH)
    lane = iota(shape, 1)
    head = step * 4 + 2 * (lane // PAIR) + jnp.where(lane % PAIR < HEAD_WIDTH, 1, 0)
    term = lane % HEAD_WIDTH
    chosen = (term < 3) & (iota(shape, 0) == term * 32 + offset + head)
    return jnp.where(chosen, -1.0, 0.0).astype(BF)


def keep_band(window, fill):
    shape = (128, 128)
    apart = iota(shape, 0) - iota(shape, 1)
    first = jnp.where(apart >= 0, window[:128], fill)
    last = jnp.where(apart <= 0, window[512:], fill)
    return first, window[128:512], last


def forward_kernel(
    counts_ref,
    left_ref,
    right_ref,
    latent_ref,
    weight_ref,
    q_ref,
    k_ref,
    v_ref,
    w_out_ref,
    readout_ref,
    normed_ref,
    kcat_ref,
    vcat_ref,
    attended_ref,
    stats_ref,
    hidden_ref,
    forecast_ref,
    probs,
    inverse_ref,
    stat_rows,
    buffer,
    arrived,
):
    step = pl.program_id(0)

    @pl.when(step == 0)
    def _():
        copies = fetches(weight_ref, buffer, arrived, WIDTH, 1024)
        for place in (0, 4, 1, 5, 2, 6, 3, 7):
            copies[place].start()
        normed_ref[:WIN] = layer_norm(left_ref[...])
        normed_ref[WIN:] = layer_norm(right_ref[...])

    fetch_one(weight_ref, buffer, arrived, WIDTH, 1024, step).wait()
    fetch_one(weight_ref, buffer, arrived, WIDTH, 1024, step + 4).wait()
    khalo = dot_nn(normed_ref[...], buffer[step]).astype(BF)
    kcat_ref[:WIN] = khalo[:WIN]
    kcat_ref[WIN : WIN + BLOCK] = k_ref[...]
    kcat_ref[WIN + BLOCK :] = khalo[WIN:]
    vhalo = dot_nn(normed_ref[...], buffer[step + 4]).astype(BF)
    vcat_ref[:WIN] = vhalo[:WIN]
    vcat_ref[WIN : WIN + BLOCK] = v_ref[...]
    vcat_ref[WIN + BLOCK :] = vhalo[WIN:]
    fill = key_fill([(counts_ref[0], WIN), (counts_ref[1], BLOCK), (counts_ref[2], WIN)])
    low_q = iota((BLOCK, PAIR), 1) < HEAD_WIDTH
    low_k = iota(fill.shape, 1) < HEAD_WIDTH
    query_fill = (spare_lane((BLOCK, PAIR)) == 3).astype(BF)
    scores, turned = [], []
    for pair in range(2):
        columns = slice(pair * PAIR, (pair + 1) * PAIR)
        q_pair = q_ref[:, columns] * jnp.asarray(HEAD_WIDTH ** (-0.5), BF)
        k_pair = kcat_ref[:, columns]
        turned.append(vcat_ref[:, columns].T)
        for half in range(2):
            if half == 0:
                q_head = jnp.where(low_q, q_pair, query_fill)
                k_head = jnp.where(low_k, k_pair, fill)
            else:
                q_head = jnp.where(low_q, query_fill, q_pair)
                k_head = jnp.where(low_k, fill, k_pair)
            scores.append(dot_nt(k_head, q_head))
    tops = []
    for slot in range(4):
        levels = []
        for tile in range(2):
            rows = slice(tile * 128, tile * 128 + 640)
            lanes = slice(tile * 128, tile * 128 + 128)
            first, middle, last = keep_band(scores[slot][rows, lanes], NEVER)
            top = jnp.maximum(
                jnp.max(middle, axis=0, keepdims=True),
                jnp.max(jnp.maximum(first, last), axis=0, keepdims=True),
            )
            start = tile * 128
            probs[slot, start : start + 128, lanes] = jnp.exp(first - top).astype(BF)
            probs[slot, start + 128 : start + 512, lanes] = jnp.exp(middle - top).astype(BF)
            probs[slot, start + 512 : start + 640, lanes] = jnp.exp(last - top).astype(BF)
            levels.append(top)
        probs[slot, :128, 128:] = jnp.zeros((128, 128), BF)
        probs[slot, 640:, :128] = jnp.zeros((128, 128), BF)
        tops.append(jnp.concatenate(levels, axis=1))
    ones = jnp.ones((16, fill.shape[0]), BF)
    for pair in range(2):
        halves = []
        for half in range(2):
            slot = pair * 2 + half
            lanes = slice(half * HEAD_WIDTH, (half + 1) * HEAD_WIDTH)
            values = jnp.concatenate([turned[pair][lanes], ones], axis=0)
            mixed = dot_nn(values, probs[slot])
            total = mixed[HEAD_WIDTH : HEAD_WIDTH + 1]
            inverse = 1.0 / total
            halves.append(mixed[:HEAD_WIDTH] * inverse)
            head = step * 4 + slot
            inverse_ref[pl.ds(head, 1), :] = inverse
            stat_rows[pl.ds(head, 1), :] = tops[slot] + jnp.log(total)
        start = pl.multiple_of(step * WIDTH + pair * PAIR, PAIR)
        attended_ref[:, pl.ds(start, PAIR)] = jnp.concatenate(halves, axis=0).T

    @pl.when(step == 3)
    def _():
        mixed = dot_nn(attended_ref[...].astype(BF), w_out_ref[...])
        hidden = (latent_ref[...].astype(F32) + mixed).astype(BF)
        hidden_ref[...] = hidden
        forecast_ref[...] = dot_nn(hidden, readout_ref[...])
        stat_rows[HEADS:] = jnp.zeros((128 - HEADS, BLOCK), F32)
        stats_ref[...] = stat_rows[...].T


def forward(counts, left, right, latent_own, w_qkv, projected, w_out, readout_weight):
    whole = lambda *shape: pl.BlockSpec(shape, lambda j: (0, 0))
    part = lambda rows, first: pl.BlockSpec((rows, WIDTH), lambda j: (0, first + j))
    window = 2 * WIN + BLOCK
    return pl.pallas_call(
        forward_kernel,
        grid=(4,),
        in_specs=[
            pl.BlockSpec(memory_space=pltpu.SMEM),
            whole(WIN, 1024),
            whole(WIN, 1024),
            whole(BLOCK, 1024),
            HBM,
            part(BLOCK, 0),
            part(BLOCK, 4),
            part(BLOCK, 8),
            whole(1024, 1024),
            whole(1024, 128),
        ],
        out_specs=[
            whole(2 * WIN, 1024),
            part(window, 0),
            part(window, 0),
            whole(BLOCK, 1024),
            whole(BLOCK, 128),
            whole(BLOCK, 1024),
            whole(BLOCK, 128),
            pl.BlockSpec((4, window, BLOCK), lambda j: (j, 0, 0)),
            whole(HEADS, BLOCK),
        ],
        out_shape=[
            jax.ShapeDtypeStruct((2 * WIN, 1024), BF),
            jax.ShapeDtypeStruct((window, 1024), BF),
            jax.ShapeDtypeStruct((window, 1024), BF),
            jax.ShapeDtypeStruct((BLOCK, 1024), F32),
            jax.ShapeDtypeStruct((BLOCK, 128), F32),
            jax.ShapeDtypeStruct((BLOCK, 1024), BF),
            jax.ShapeDtypeStruct((BLOCK, 128), F32),
            jax.ShapeDtypeStruct((HEADS, window, BLOCK), BF),
            jax.ShapeDtypeStruct((HEADS, BLOCK), F32),
        ],
        scratch_shapes=[
            pltpu.VMEM((128, BLOCK), F32),
            pltpu.VMEM((8, 1024, WIDTH), BF),
            pltpu.SemaphoreType.DMA((8,)),
        ],
        compiler_params=pltpu.CompilerParams(vmem_limit_bytes=30 * 1024 * 1024),
        cost_estimate=pl.CostEstimate(
            flops=6 << 30, bytes_accessed=12 << 20, transcendentals=3 << 20
        ),
    )(
        counts,
        left,
        right,
        latent_own,
        in_hbm(w_qkv),
        projected,
        projected,
        projected,
        w_out,
        readout_weight,
    )


def score_kernel(
    counts_ref,
    own_ref,
    near_ref,
    others_ref,
    target_ref,
    attended_ref,
    hidden_ref,
    stats_ref,
    w_out_ref,
    readout_ref,
    crps_ref,
    packed_ref,
    grad_ref,
    small_ref,
):
    members = 4
    fair_eps = (1.0 - alpha_fair) / members
    coefficient = (1.0 - fair_eps) / (members * (members - 1))
    valid = (iota((BLOCK, 1), 0) < counts_ref[1]).astype(F32)
    own = own_ref[...]
    forecasts = [own, near_ref[...], others_ref[0], others_ref[1]]
    target = target_ref[...]
    error = jnp.zeros_like(target)
    for forecast in forecasts:
        error += smooth_abs(forecast - target)
    spread = jnp.full_like(target, members * smooth_width**0.5)
    for first in range(members):
        for second in range(first + 1, members):
            spread += 2.0 * smooth_abs(forecasts[first] - forecasts[second])
    crps_ref[...] = valid * (error / members - 0.5 * coefficient * spread)
    pull = jnp.zeros_like(target)
    for other in forecasts[1:]:
        pull += smooth_sign(own - other)
    slope = (
        valid / 128 * (smooth_sign(own - target) / members - coefficient * pull)
    ).astype(BF)
    dhidden = dot_nt(slope, readout_ref[...]).astype(BF)
    dattended = dot_nt(dhidden, w_out_ref[...]).astype(BF)
    grad_ref[...] = dattended
    attended = attended_ref[...]
    product = dattended.astype(F32) * attended
    high = product.astype(BF)
    low = (product - high.astype(F32)).astype(BF)
    pick = (iota((1024, 128), 0) // HEAD_WIDTH + HEADS == iota((1024, 128), 1)).astype(BF)
    stats = stats_ref[...] + dot_nn(high, pick) + dot_nn(low, pick)
    first = stats.astype(BF)
    rest = stats - first.astype(F32)
    second = rest.astype(BF)
    third = (rest - second.astype(F32)).astype(BF)
    terms = jnp.zeros((BLOCK, 128), F32)
    for place, term in enumerate((first, second, third)):
        shift = (iota((128, 128), 0) + 32 * place == iota((128, 128), 1)) & (
            iota((128, 128), 0) < 32
        )
        terms += dot_nn(term, shift.astype(BF))
    packed_ref[:, :128] = slope
    packed_ref[:, 128:] = terms.astype(BF)
    small_ref[:, :128] = dot_tn(attended.astype(BF), slope).astype(BF)
    small_ref[:, 128:] = dot_tn(hidden_ref[...], slope).astype(BF)


def score(counts, own, near, others, target, attended, hidden, stats, w_out, readout_weight):
    vmem = pl.BlockSpec(memory_space=pltpu.VMEM)
    return pl.pallas_call(
        score_kernel,
        in_specs=[pl.BlockSpec(memory_space=pltpu.SMEM)] + [vmem] * 9,
        out_specs=[vmem] * 4,
        out_shape=[
            jax.ShapeDtypeStruct((BLOCK, 128), F32),
            jax.ShapeDtypeStruct((BLOCK, 256), BF),
            jax.ShapeDtypeStruct((BLOCK, 1024), BF),
            jax.ShapeDtypeStruct((1024, 256), BF),
        ],
        compiler_params=pltpu.CompilerParams(vmem_limit_bytes=12 * 1024 * 1024),
    )(counts, own, near, others, target, attended, hidden, stats, w_out, readout_weight)


def query_kernel(
    kcat_ref, vcat_ref, grad_ref, packed_ref, probs_ref, inverse_ref, dq_ref, dscores
):
    step = pl.program_id(0)
    window = kcat_ref.shape[0]
    value_fill = (spare_lane((window, PAIR)) < 3).astype(BF)
    low_q = iota((BLOCK, PAIR), 1) < HEAD_WIDTH
    low_k = iota((window, PAIR), 1) < HEAD_WIDTH
    g_fill = dot_nn(packed_ref[:, 128:], stat_spread(step, HEADS)).astype(BF)
    turned = []
    for pair in range(2):
        columns = slice(pair * PAIR, (pair + 1) * PAIR)
        g_pair = grad_ref[:, columns]
        v_pair = vcat_ref[:, columns]
        k_turned = kcat_ref[:, columns].T
        for half in range(2):
            slot = pair * 2 + half
            pick_q = low_q if half == 0 else ~low_q
            pick_k = low_k if half == 0 else ~low_k
            g_head = jnp.where(pick_q, g_pair, g_fill[:, columns])
            v_head = jnp.where(pick_k, v_pair, value_fill)
            change = dot_nt(v_head, g_head)
            dscores[slot] = (probs_ref[slot].astype(F32) * change).astype(BF)
            turned.append(k_turned[half * HEAD_WIDTH : (half + 1) * HEAD_WIDTH])
    for slot in range(4):
        scale = inverse_ref[pl.ds(step * 4 + slot, 1), :] * HEAD_WIDTH ** (-0.5)
        dquery = dot_nn(turned[slot], dscores[slot]) * scale
        dq_ref[slot * HEAD_WIDTH : (slot + 1) * HEAD_WIDTH] = dquery.astype(BF)


def query_grads(kcat, vcat, grad, packed, probs, inverse):
    part = lambda rows, first: pl.BlockSpec((rows, WIDTH), lambda j: (0, first + j))
    window = 2 * WIN + BLOCK
    return pl.pallas_call(
        query_kernel,
        grid=(4,),
        in_specs=[
            part(window, 0),
            part(window, 0),
            part(BLOCK, 0),
            pl.BlockSpec((BLOCK, 256), lambda j: (0, 0)),
            pl.BlockSpec((4, window, BLOCK), lambda j: (j, 0, 0)),
            pl.BlockSpec((HEADS, BLOCK), lambda j: (0, 0)),
        ],
        out_specs=pl.BlockSpec((WIDTH, BLOCK), lambda j: (j, 0)),
        out_shape=jax.ShapeDtypeStruct((1024, BLOCK), BF),
        scratch_shapes=[pltpu.VMEM((4, window, BLOCK), BF)],
        compiler_params=pltpu.CompilerParams(vmem_limit_bytes=16 * 1024 * 1024),
        cost_estimate=pl.CostEstimate(
            flops=6 << 30, bytes_accessed=5 << 20, transcendentals=3 << 20
        ),
    )(kcat, vcat, grad, packed, probs, inverse)


def key_kernel(
    counts_ref,
    q_ref,
    k_ref,
    v_ref,
    qhalo_ref,
    grad_ref,
    own_ref,
    left_ref,
    right_ref,
    w_out_ref,
    readout_ref,
    out_ref,
    probs,
    dscores,
    dhidden,
):
    step = pl.program_id(0)

    @pl.when(step == 0)
    def _():
        probs[...] = jnp.zeros_like(probs)
        dscores[...] = jnp.zeros_like(dscores)
        dhidden[:WIN] = dot_nt(left_ref[:, :128], readout_ref[...]).astype(BF)
        dhidden[WIN:] = dot_nt(right_ref[:, :128], readout_ref[...]).astype(BF)

    ghalo = dot_nt(dhidden[...], w_out_ref[...]).astype(BF)
    terms = jnp.concatenate(
        [left_ref[:, 128:], own_ref[:, 128:], right_ref[:, 128:]], axis=0
    )
    window = terms.shape[0]
    fill = key_fill([(counts_ref[1], BLOCK)])
    value_fill = (spare_lane(fill.shape) < 3).astype(BF)
    low_q = iota((window, PAIR), 1) < HEAD_WIDTH
    low_k = iota(fill.shape, 1) < HEAD_WIDTH
    ones = (spare_lane((window, WIDTH)) == 3).astype(F32)
    q_fill = (dot_nn(terms, stat_spread(step, 0)) + ones).astype(BF)
    g_fill = dot_nn(terms, stat_spread(step, HEADS)).astype(BF)
    turned = []
    for pair in range(2):
        columns = slice(pair * PAIR, (pair + 1) * PAIR)
        q_pair = jnp.concatenate(
            [qhalo_ref[:WIN, columns], q_ref[:, columns], qhalo_ref[WIN:, columns]], axis=0
        ) * jnp.asarray(HEAD_WIDTH ** (-0.5), BF)
        g_pair = jnp.concatenate(
            [ghalo[:WIN, columns], grad_ref[:, columns], ghalo[WIN:, columns]], axis=0
        )
        k_pair = k_ref[:, columns]
        v_pair = v_ref[:, columns]
        q_turned = q_pair.T
        g_turned = g_pair.T
        for half in range(2):
            slot = pair * 2 + half
            pick_q = low_q if half == 0 else ~low_q
            pick_k = low_k if half == 0 else ~low_k
            q_head = jnp.where(pick_q, q_pair, q_fill[:, columns])
            g_head = jnp.where(pick_q, g_pair, g_fill[:, columns])
            k_head = jnp.where(pick_k, k_pair, fill)
            v_head = jnp.where(pick_k, v_pair, value_fill)
            scores = dot_nt(q_head, k_head)
            change = dot_nt(g_head, v_head)
            for tile in range(2):
                rows = slice(tile * 128, tile * 128 + 640)
                lanes = slice(tile * 128, tile * 128 + 128)
                weight = keep_band(jnp.exp(scores[rows, lanes]), 0.0)
                moved = change[rows, lanes]
                start = tile * 128
                for piece, (low, high) in zip(weight, ((0, 128), (128, 512), (512, 640))):
                    place = slice(start + low, start + high)
                    probs[slot, place, lanes] = piece.astype(BF)
                    dscores[slot, place, lanes] = (piece * moved[low:high]).astype(BF)
            lanes = slice(half * HEAD_WIDTH, (half + 1) * HEAD_WIDTH)
            turned.append((q_turned[lanes], g_turned[lanes]))
    for slot in range(4):
        place = slice(slot * HEAD_WIDTH, (slot + 1) * HEAD_WIDTH)
        out_ref[0, place] = dot_nn(turned[slot][0], dscores[slot]).astype(BF)
        out_ref[1, place] = dot_nn(turned[slot][1], probs[slot]).astype(BF)


def key_grads(counts, projected, qhalo, grad, own, left, right, w_out, readout_weight):
    part = lambda rows, first: pl.BlockSpec((rows, WIDTH), lambda j: (0, first + j))
    whole = lambda *shape: pl.BlockSpec(shape, lambda j: (0, 0))
    window = 2 * WIN + BLOCK
    return pl.pallas_call(
        key_kernel,
        grid=(4,),
        in_specs=[
            pl.BlockSpec(memory_space=pltpu.SMEM),
            part(BLOCK, 0),
            part(BLOCK, 4),
            part(BLOCK, 8),
            part(2 * WIN, 0),
            part(BLOCK, 0),
            whole(BLOCK, 256),
            whole(BLOCK, 256),
            whole(BLOCK, 256),
            pl.BlockSpec((WIDTH, 1024), lambda j: (j, 0)),
            whole(1024, 128),
        ],
        out_specs=pl.BlockSpec((2, WIDTH, BLOCK), lambda j: (0, j, 0)),
        out_shape=jax.ShapeDtypeStruct((2, 1024, BLOCK), BF),
        scratch_shapes=[
            pltpu.VMEM((4, window, BLOCK), BF),
            pltpu.VMEM((4, window, BLOCK), BF),
            pltpu.VMEM((2 * WIN, 1024), BF),
        ],
        compiler_params=pltpu.CompilerParams(vmem_limit_bytes=18 * 1024 * 1024),
        cost_estimate=FREE,
    )(
        counts,
        projected,
        projected,
        projected,
        qhalo,
        in_hbm(grad),
        own,
        in_hbm(left),
        in_hbm(right),
        in_hbm(w_out),
        readout_weight,
    )


AXES = ("x_hi", "core", "y", "x_lo", "z")
MEMBER = ("x_hi", "core")
CELLS = ("y", "x_lo", "z")
CHIPS = ("x_hi", "y", "x_lo", "z")
SWAP = [(0, 1), (1, 0)]


def swap_core(values):
    return lax.ppermute(values, "core", SWAP)


def scatter(partial):
    columns = partial.shape[1]
    return lax.all_to_all(partial.reshape(64, 8, columns), CHIPS, split_axis=0, concat_axis=0)


def add_up(pieces):
    return jnp.sum(pieces.astype(F32), axis=0)


def per_device(latent, counts, w_qkv, w_out, readout_weight, target):
    latent_own = latent[0]
    cell_count = 32
    cell_index = lax.axis_index(CELLS)
    member_index = lax.axis_index(MEMBER)
    core = lax.axis_index("core")
    up = [(i, i + 1) for i in range(cell_count - 1)]
    down = [(i + 1, i) for i in range(cell_count - 1)]
    from_left = lax.ppermute(latent_own, CELLS, up)
    from_right = lax.ppermute(latent_own, CELLS, down)

    own_count = counts[cell_index]
    left_count = jnp.where(cell_index > 0, counts[jnp.maximum(cell_index - 1, 0)], 0)
    right_count = jnp.where(
        cell_index < cell_count - 1, counts[jnp.minimum(cell_index + 1, cell_count - 1)], 0
    )
    scalars = jnp.stack([left_count, own_count, right_count])

    projected, turned = project(latent_own, w_qkv)
    turned_other = swap_core(turned)
    normed_halo, kcat, vcat, attended, stats, hidden, forecast, probs, inverse = forward(
        scalars, from_left, from_right, latent_own, w_qkv, projected, w_out, readout_weight
    )
    near = lax.ppermute(forecast, "x_hi", SWAP)
    qhalo = halo_queries(normed_halo, w_qkv)
    near, qhalo = lax.optimization_barrier((near, qhalo))
    others = swap_core(jnp.stack([forecast, near]))
    crps_whole, packed, grad, small = score(
        scalars, forecast, near, others, target, attended, hidden, stats, w_out, readout_weight
    )
    crps = lax.dynamic_slice_in_dim(crps_whole, member_index * 32, 32, 1)
    packed_left = lax.ppermute(packed, CELLS, up)
    packed_right = lax.ppermute(packed, CELLS, down)

    dquery = query_grads(kcat, vcat, grad, packed, probs, inverse)
    dquery, packed_left, packed_right = lax.optimization_barrier(
        (dquery, packed_left, packed_right)
    )

    first_part = partial_sums(
        core, turned, turned_other, dquery, swap_core(dquery), (small, swap_core(small))
    )
    first_part, scalars = lax.optimization_barrier((first_part, scalars))
    first = scatter(first_part)
    pairs = key_grads(
        scalars,
        projected,
        qhalo,
        grad,
        packed,
        packed_left,
        packed_right,
        w_out,
        readout_weight,
    )
    pairs = pairs.reshape(2048, BLOCK)
    second_part = partial_sums(core, turned, turned_other, pairs, swap_core(pairs))
    second_part, first = lax.optimization_barrier((second_part, first))
    second = add_up(scatter(second_part))
    first = add_up(first)
    grad_out = lax.dot_general(
        first[:, 1024:1152],
        readout_weight.astype(F32),
        (((1,), (1,)), ((), ())),
        precision=lax.Precision.HIGHEST,
        preferred_element_type=F32,
    )
    grads = jnp.concatenate([first[:, :1024], second, grad_out, first[:, 1152:]], axis=1)
    return (crps, grads)


def solution(mesh):
    fine = jax.sharding.Mesh(mesh.devices.reshape(2, 2, 4, 2, 4), AXES)
    placed = (P(MEMBER, CELLS, None), P(), P(), P(), P(), P(CELLS, None))
    return jax.shard_map(
        per_device,
        mesh=fine,
        in_specs=placed,
        out_specs=(P(CELLS, MEMBER), P(MEMBER + CELLS, None)),
        check_vma=False,
    )
```

```python
import functools

import jax
import jax.numpy as jnp
import numpy as np
from jax import lax
from jax.experimental import pallas as pl
from jax.experimental.pallas import tpu as pltpu
from jax.sharding import PartitionSpec as P

HEADS = 16
WIN = 256
BLOCK = 256
WIDTH = 256
HEAD_WIDTH = 64
PAIR = 128
NEVER = -1e30

alpha_fair = 0.95
smooth_width = 0.0625

BF = jnp.bfloat16
F32 = jnp.float32


def smooth_abs(values):
    return jnp.sqrt(values * values + smooth_width)


def smooth_sign(values):
    return values * lax.rsqrt(values * values + smooth_width)


def layer_norm(latent_rows):
    values = latent_rows.astype(F32)
    center = values - jnp.mean(values, axis=-1, keepdims=True)
    spread = jnp.mean(center * center, axis=-1, keepdims=True)
    return (center * lax.rsqrt(spread + 1e-05)).astype(BF)


def dot_nn(left, right):
    return lax.dot_general(left, right, (((1,), (0,)), ((), ())), preferred_element_type=F32)


def dot_nt(left, right):
    return lax.dot_general(left, right, (((1,), (1,)), ((), ())), preferred_element_type=F32)


def dot_tn(left, right):
    return lax.dot_general(left, right, (((0,), (0,)), ((), ())), preferred_element_type=F32)


def iota(shape, axis):
    return lax.broadcasted_iota(jnp.int32, shape, axis)


FREE = pl.CostEstimate(flops=0, bytes_accessed=0, transcendentals=0)
HBM = pl.BlockSpec(memory_space=pltpu.HBM)


def in_hbm(values):
    return pltpu.with_memory_space_constraint(values, pltpu.HBM)


def fetches(weight_ref, buffer, arrived, width, first):
    return [
        pltpu.make_async_copy(
            weight_ref.at[:, pl.ds(first + place * width, width)],
            buffer.at[place],
            arrived.at[place],
        )
        for place in range(buffer.shape[0])
    ]


def fetch_one(weight_ref, buffer, arrived, width, first, place):
    start = pl.multiple_of(first + place * width, width)
    return pltpu.make_async_copy(
        weight_ref.at[:, pl.ds(start, width)], buffer.at[place], arrived.at[place]
    )


def project_kernel(latent_ref, weight_ref, projected_ref, turned_ref, normed, buffer, arrived):
    step = pl.program_id(0)

    @pl.when(step == 0)
    def _():
        for copy in fetches(weight_ref, buffer, arrived, 512, 0):
            copy.start()
        normed[...] = layer_norm(latent_ref[...])
        turned_ref[...] = normed[...].T

    fetch_one(weight_ref, buffer, arrived, 512, 0, step).wait()
    projected_ref[...] = dot_nn(normed[...], buffer[step]).astype(BF)


def project(latent_own, w_qkv):
    rows, width = latent_own.shape
    return pl.pallas_call(
        project_kernel,
        grid=(6,),
        in_specs=[pl.BlockSpec((rows, width), lambda j: (0, 0)), HBM],
        out_specs=[
            pl.BlockSpec((rows, 512), lambda j: (0, j)),
            pl.BlockSpec((width, rows), lambda j: (0, 0)),
        ],
        out_shape=[
            jax.ShapeDtypeStruct((rows, 3 * width), BF),
            jax.ShapeDtypeStruct((width, rows), BF),
        ],
        scratch_shapes=[
            pltpu.VMEM((rows, width), BF),
            pltpu.VMEM((6, width, 512), BF),
            pltpu.SemaphoreType.DMA((6,)),
        ],
        compiler_params=pltpu.CompilerParams(vmem_limit_bytes=16 * 1024 * 1024),
        cost_estimate=pl.CostEstimate(
            flops=2 * rows * width * width * 4, bytes_accessed=8 << 20, transcendentals=0
        ),
    )(latent_own, in_hbm(w_qkv))


def halo_query_kernel(normed_ref, weight_ref, out_ref, buffer, arrived):
    step = pl.program_id(0)

    @pl.when(step == 0)
    def _():
        for copy in fetches(weight_ref, buffer, arrived, 256, 0):
            copy.start()

    fetch_one(weight_ref, buffer, arrived, 256, 0, step).wait()
    out_ref[...] = dot_nn(normed_ref[...], buffer[step]).astype(BF)


def halo_queries(normed_halo, w_qkv):
    rows, width = normed_halo.shape
    return pl.pallas_call(
        halo_query_kernel,
        grid=(4,),
        in_specs=[pl.BlockSpec((rows, width), lambda j: (0, 0)), HBM],
        out_specs=pl.BlockSpec((rows, 256), lambda j: (0, j)),
        out_shape=jax.ShapeDtypeStruct((rows, width), BF),
        scratch_shapes=[
            pltpu.VMEM((4, width, 256), BF),
            pltpu.SemaphoreType.DMA((4,)),
        ],
        compiler_params=pltpu.CompilerParams(vmem_limit_bytes=12 * 1024 * 1024),
        cost_estimate=FREE,
    )(normed_halo, in_hbm(w_qkv))


def partial_kernel(
    smalls, core_ref, normed_ref, normed_other_ref, piece_ref, other_ref, *refs
):
    small_refs, (out_ref, rows, pieces, others, sums, staged, arrived, left) = (
        refs[:smalls],
        refs[smalls:],
    )
    core = core_ref[0]
    chunks = piece_ref.shape[0] // 512
    sources = [
        (normed_ref.at[:, core], rows.at[0]),
        (normed_other_ref.at[:, core], rows.at[1]),
    ]
    for chunk in range(chunks):
        part = pl.ds(chunk * 512, 512)
        sources.append((piece_ref.at[part], pieces.at[chunk]))
        sources.append((other_ref.at[part], others.at[chunk]))
    for place, small_ref in enumerate(small_refs):
        sources.append((small_ref.at[:, core], sums.at[place]))
    copies = [
        pltpu.make_async_copy(source, target, arrived.at[place])
        for place, (source, target) in enumerate(sources)
    ]
    for copy in copies:
        copy.start()
    copies[0].wait()
    copies[1].wait()
    writes = []
    for chunk in range(chunks):
        copies[2 + 2 * chunk].wait()
        copies[3 + 2 * chunk].wait()
        for top in range(2):
            staged[chunk, top * 256 : (top + 1) * 256] = (
                dot_nt(rows[0, top], pieces[chunk]) + dot_nt(rows[1, top], others[chunk])
            ).astype(BF)
        writes.append(
            pltpu.make_async_copy(
                staged.at[chunk], out_ref.at[:, pl.ds(chunk * 512, 512)], left.at[chunk]
            )
        )
        writes[-1].start()
    if smalls:
        copies[-2].wait()
        copies[-1].wait()
        for top in range(2):
            staged[chunks, top * 256 : (top + 1) * 256, :256] = (
                sums[0, top].astype(F32) + sums[1, top].astype(F32)
            ).astype(BF)
        writes.append(
            pltpu.make_async_copy(
                staged.at[chunks, :, pl.ds(0, 256)],
                out_ref.at[:, pl.ds(chunks * 512, 256)],
                left.at[chunks],
            )
        )
        writes[-1].start()
    for write in writes:
        write.wait()


def partial_sums(core, turned, turned_other, piece, other, smalls=()):
    by_core = lambda values: values.reshape(2, 2, 256, 256)
    anywhere = pl.BlockSpec(memory_space=pl.ANY)
    chunks = piece.shape[0] // 512
    columns = piece.shape[0] + 256 * (len(smalls) // 2)
    return pl.pallas_call(
        functools.partial(partial_kernel, len(smalls)),
        in_specs=[pl.BlockSpec(memory_space=pltpu.SMEM)] + [anywhere] * (4 + len(smalls)),
        out_specs=anywhere,
        out_shape=jax.ShapeDtypeStruct((512, columns), BF),
        scratch_shapes=[
            pltpu.VMEM((2, 2, 256, 256), BF),
            pltpu.VMEM((chunks, 512, 256), BF),
            pltpu.VMEM((chunks, 512, 256), BF),
            pltpu.VMEM((2, 2, 256, 256), BF),
            pltpu.VMEM((chunks + 1, 512, 512), BF),
            pltpu.SemaphoreType.DMA((2 + 2 * chunks + len(smalls),)),
            pltpu.SemaphoreType.DMA((chunks + 1,)),
        ],
        compiler_params=pltpu.CompilerParams(vmem_limit_bytes=14 * 1024 * 1024),
        cost_estimate=FREE,
    )(
        core.astype(jnp.int32).reshape(1),
        by_core(turned),
        by_core(turned_other),
        piece,
        other,
        *(by_core(small) for small in smalls),
    )


def spare_lane(shape):
    lane = iota(shape, len(shape) - 1)
    return lane % HEAD_WIDTH


def key_fill(count_pieces):
    fills = []
    for count, rows in count_pieces:
        spare = spare_lane((rows, PAIR))
        bias = jnp.where(iota((rows, PAIR), 0) < count, 0.0, NEVER)
        fills.append(
            jnp.where(spare < 3, 1.0, jnp.where(spare == 3, bias, 0.0)).astype(BF)
        )
    return jnp.concatenate(fills, axis=0)


def stat_spread(step, offset):
    shape = (128, WIDTH)
    lane = iota(shape, 1)
    head = step * 4 + 2 * (lane // PAIR) + jnp.where(lane % PAIR < HEAD_WIDTH, 1, 0)
    term = lane % HEAD_WIDTH
    chosen = (term < 3) & (iota(shape, 0) == term * 32 + offset + head)
    return jnp.where(chosen, -1.0, 0.0).astype(BF)


def keep_band(window, fill):
    shape = (128, 128)
    apart = iota(shape, 0) - iota(shape, 1)
    first = jnp.where(apart >= 0, window[:128], fill)
    last = jnp.where(apart <= 0, window[512:], fill)
    return first, window[128:512], last


def forward_kernel(
    counts_ref,
    left_ref,
    right_ref,
    latent_ref,
    weight_ref,
    q_ref,
    k_ref,
    v_ref,
    w_out_ref,
    readout_ref,
    normed_ref,
    kcat_ref,
    vcat_ref,
    attended_ref,
    stats_ref,
    hidden_ref,
    forecast_ref,
    probs,
    inverse_ref,
    stat_rows,
    buffer,
    arrived,
):
    step = pl.program_id(0)

    @pl.when(step == 0)
    def _():
        copies = fetches(weight_ref, buffer, arrived, WIDTH, 1024)
        for place in (0, 4, 1, 5, 2, 6, 3, 7):
            copies[place].start()
        normed_ref[:WIN] = layer_norm(left_ref[...])
        normed_ref[WIN:] = layer_norm(right_ref[...])

    fetch_one(weight_ref, buffer, arrived, WIDTH, 1024, step).wait()
    fetch_one(weight_ref, buffer, arrived, WIDTH, 1024, step + 4).wait()
    khalo = dot_nn(normed_ref[...], buffer[step]).astype(BF)
    kcat_ref[:WIN] = khalo[:WIN]
    kcat_ref[WIN : WIN + BLOCK] = k_ref[...]
    kcat_ref[WIN + BLOCK :] = khalo[WIN:]
    vhalo = dot_nn(normed_ref[...], buffer[step + 4]).astype(BF)
    vcat_ref[:WIN] = vhalo[:WIN]
    vcat_ref[WIN : WIN + BLOCK] = v_ref[...]
    vcat_ref[WIN + BLOCK :] = vhalo[WIN:]
    fill = key_fill([(counts_ref[0], WIN), (counts_ref[1], BLOCK), (counts_ref[2], WIN)])
    low_q = iota((BLOCK, PAIR), 1) < HEAD_WIDTH
    low_k = iota(fill.shape, 1) < HEAD_WIDTH
    query_fill = (spare_lane((BLOCK, PAIR)) == 3).astype(BF)
    scores, turned = [], []
    for pair in range(2):
        columns = slice(pair * PAIR, (pair + 1) * PAIR)
        q_pair = q_ref[:, columns] * jnp.asarray(HEAD_WIDTH ** (-0.5), BF)
        k_pair = kcat_ref[:, columns]
        turned.append(vcat_ref[:, columns].T)
        for half in range(2):
            if half == 0:
                q_head = jnp.where(low_q, q_pair, query_fill)
                k_head = jnp.where(low_k, k_pair, fill)
            else:
                q_head = jnp.where(low_q, query_fill, q_pair)
                k_head = jnp.where(low_k, fill, k_pair)
            scores.append(dot_nt(k_head, q_head))
    tops = []
    for slot in range(4):
        levels = []
        for tile in range(2):
            rows = slice(tile * 128, tile * 128 + 640)
            lanes = slice(tile * 128, tile * 128 + 128)
            first, middle, last = keep_band(scores[slot][rows, lanes], NEVER)
            top = jnp.maximum(
                jnp.max(middle, axis=0, keepdims=True),
                jnp.max(jnp.maximum(first, last), axis=0, keepdims=True),
            )
            start = tile * 128
            probs[slot, start : start + 128, lanes] = jnp.exp(first - top).astype(BF)
            probs[slot, start + 128 : start + 512, lanes] = jnp.exp(middle - top).astype(BF)
            probs[slot, start + 512 : start + 640, lanes] = jnp.exp(last - top).astype(BF)
            levels.append(top)
        probs[slot, :128, 128:] = jnp.zeros((128, 128), BF)
        probs[slot, 640:, :128] = jnp.zeros((128, 128), BF)
        tops.append(jnp.concatenate(levels, axis=1))
    ones = jnp.ones((16, fill.shape[0]), BF)
    for pair in range(2):
        halves = []
        for half in range(2):
            slot = pair * 2 + half
            lanes = slice(half * HEAD_WIDTH, (half + 1) * HEAD_WIDTH)
            values = jnp.concatenate([turned[pair][lanes], ones], axis=0)
            mixed = dot_nn(values, probs[slot])
            total = mixed[HEAD_WIDTH : HEAD_WIDTH + 1]
            inverse = 1.0 / total
            halves.append(mixed[:HEAD_WIDTH] * inverse)
            head = step * 4 + slot
            inverse_ref[pl.ds(head, 1), :] = inverse
            stat_rows[pl.ds(head, 1), :] = tops[slot] + jnp.log(total)
        start = pl.multiple_of(step * WIDTH + pair * PAIR, PAIR)
        attended_ref[:, pl.ds(start, PAIR)] = jnp.concatenate(halves, axis=0).T

    @pl.when(step == 3)
    def _():
        mixed = dot_nn(attended_ref[...].astype(BF), w_out_ref[...])
        hidden = (latent_ref[...].astype(F32) + mixed).astype(BF)
        hidden_ref[...] = hidden
        forecast_ref[...] = dot_nn(hidden, readout_ref[...])
        stat_rows[HEADS:] = jnp.zeros((128 - HEADS, BLOCK), F32)
        stats_ref[...] = stat_rows[...].T


def forward(counts, left, right, latent_own, w_qkv, projected, w_out, readout_weight):
    whole = lambda *shape: pl.BlockSpec(shape, lambda j: (0, 0))
    part = lambda rows, first: pl.BlockSpec((rows, WIDTH), lambda j: (0, first + j))
    window = 2 * WIN + BLOCK
    return pl.pallas_call(
        forward_kernel,
        grid=(4,),
        in_specs=[
            pl.BlockSpec(memory_space=pltpu.SMEM),
            whole(WIN, 1024),
            whole(WIN, 1024),
            whole(BLOCK, 1024),
            HBM,
            part(BLOCK, 0),
            part(BLOCK, 4),
            part(BLOCK, 8),
            whole(1024, 1024),
            whole(1024, 128),
        ],
        out_specs=[
            whole(2 * WIN, 1024),
            part(window, 0),
            part(window, 0),
            whole(BLOCK, 1024),
            whole(BLOCK, 128),
            whole(BLOCK, 1024),
            whole(BLOCK, 128),
            pl.BlockSpec((4, window, BLOCK), lambda j: (j, 0, 0)),
            whole(HEADS, BLOCK),
        ],
        out_shape=[
            jax.ShapeDtypeStruct((2 * WIN, 1024), BF),
            jax.ShapeDtypeStruct((window, 1024), BF),
            jax.ShapeDtypeStruct((window, 1024), BF),
            jax.ShapeDtypeStruct((BLOCK, 1024), F32),
            jax.ShapeDtypeStruct((BLOCK, 128), F32),
            jax.ShapeDtypeStruct((BLOCK, 1024), BF),
            jax.ShapeDtypeStruct((BLOCK, 128), F32),
            jax.ShapeDtypeStruct((HEADS, window, BLOCK), BF),
            jax.ShapeDtypeStruct((HEADS, BLOCK), F32),
        ],
        scratch_shapes=[
            pltpu.VMEM((128, BLOCK), F32),
            pltpu.VMEM((8, 1024, WIDTH), BF),
            pltpu.SemaphoreType.DMA((8,)),
        ],
        compiler_params=pltpu.CompilerParams(vmem_limit_bytes=30 * 1024 * 1024),
        cost_estimate=pl.CostEstimate(
            flops=6 << 30, bytes_accessed=12 << 20, transcendentals=3 << 20
        ),
    )(
        counts,
        left,
        right,
        latent_own,
        in_hbm(w_qkv),
        projected,
        projected,
        projected,
        w_out,
        readout_weight,
    )


def score_kernel(
    counts_ref,
    own_ref,
    near_ref,
    others_ref,
    target_ref,
    attended_ref,
    hidden_ref,
    stats_ref,
    w_out_ref,
    readout_ref,
    crps_ref,
    packed_ref,
    grad_ref,
    small_ref,
):
    members = 4
    fair_eps = (1.0 - alpha_fair) / members
    coefficient = (1.0 - fair_eps) / (members * (members - 1))
    valid = (iota((BLOCK, 1), 0) < counts_ref[1]).astype(F32)
    own = own_ref[...]
    forecasts = [own, near_ref[...], others_ref[0], others_ref[1]]
    target = target_ref[...]
    error = jnp.zeros_like(target)
    for forecast in forecasts:
        error += smooth_abs(forecast - target)
    spread = jnp.full_like(target, members * smooth_width**0.5)
    for first in range(members):
        for second in range(first + 1, members):
            spread += 2.0 * smooth_abs(forecasts[first] - forecasts[second])
    crps_ref[...] = valid * (error / members - 0.5 * coefficient * spread)
    pull = jnp.zeros_like(target)
    for other in forecasts[1:]:
        pull += smooth_sign(own - other)
    slope = (
        valid / 128 * (smooth_sign(own - target) / members - coefficient * pull)
    ).astype(BF)
    dhidden = dot_nt(slope, readout_ref[...]).astype(BF)
    dattended = dot_nt(dhidden, w_out_ref[...]).astype(BF)
    grad_ref[...] = dattended
    attended = attended_ref[...]
    product = dattended.astype(F32) * attended
    high = product.astype(BF)
    low = (product - high.astype(F32)).astype(BF)
    pick = (iota((1024, 128), 0) // HEAD_WIDTH + HEADS == iota((1024, 128), 1)).astype(BF)
    stats = stats_ref[...] + dot_nn(high, pick) + dot_nn(low, pick)
    first = stats.astype(BF)
    rest = stats - first.astype(F32)
    second = rest.astype(BF)
    third = (rest - second.astype(F32)).astype(BF)
    terms = jnp.zeros((BLOCK, 128), F32)
    for place, term in enumerate((first, second, third)):
        shift = (iota((128, 128), 0) + 32 * place == iota((128, 128), 1)) & (
            iota((128, 128), 0) < 32
        )
        terms += dot_nn(term, shift.astype(BF))
    packed_ref[:, :128] = slope
    packed_ref[:, 128:] = terms.astype(BF)
    small_ref[:, :128] = dot_tn(attended.astype(BF), slope).astype(BF)
    small_ref[:, 128:] = dot_tn(hidden_ref[...], slope).astype(BF)


def score(counts, own, near, others, target, attended, hidden, stats, w_out, readout_weight):
    vmem = pl.BlockSpec(memory_space=pltpu.VMEM)
    return pl.pallas_call(
        score_kernel,
        in_specs=[pl.BlockSpec(memory_space=pltpu.SMEM)] + [vmem] * 9,
        out_specs=[vmem] * 4,
        out_shape=[
            pltpu.HBM((BLOCK, 128), F32),
            pltpu.HBM((BLOCK, 256), BF),
            jax.ShapeDtypeStruct((BLOCK, 1024), BF),
            jax.ShapeDtypeStruct((1024, 256), BF),
        ],
        compiler_params=pltpu.CompilerParams(vmem_limit_bytes=12 * 1024 * 1024),
    )(counts, own, near, others, target, attended, hidden, stats, w_out, readout_weight)


def query_kernel(
    kcat_ref, vcat_ref, grad_ref, packed_ref, probs_ref, inverse_ref, dq_ref, dscores
):
    step = pl.program_id(0)
    window = kcat_ref.shape[0]
    value_fill = (spare_lane((window, PAIR)) < 3).astype(BF)
    low_q = iota((BLOCK, PAIR), 1) < HEAD_WIDTH
    low_k = iota((window, PAIR), 1) < HEAD_WIDTH
    g_fill = dot_nn(packed_ref[:, 128:], stat_spread(step, HEADS)).astype(BF)
    turned = []
    for pair in range(2):
        columns = slice(pair * PAIR, (pair + 1) * PAIR)
        g_pair = grad_ref[:, columns]
        v_pair = vcat_ref[:, columns]
        k_turned = kcat_ref[:, columns].T
        for half in range(2):
            slot = pair * 2 + half
            pick_q = low_q if half == 0 else ~low_q
            pick_k = low_k if half == 0 else ~low_k
            g_head = jnp.where(pick_q, g_pair, g_fill[:, columns])
            v_head = jnp.where(pick_k, v_pair, value_fill)
            change = dot_nt(v_head, g_head)
            dscores[slot] = (probs_ref[slot].astype(F32) * change).astype(BF)
            turned.append(k_turned[half * HEAD_WIDTH : (half + 1) * HEAD_WIDTH])
    for slot in range(4):
        scale = inverse_ref[pl.ds(step * 4 + slot, 1), :] * HEAD_WIDTH ** (-0.5)
        dquery = dot_nn(turned[slot], dscores[slot]) * scale
        dq_ref[slot * HEAD_WIDTH : (slot + 1) * HEAD_WIDTH] = dquery.astype(BF)


def query_grads(kcat, vcat, grad, packed, probs, inverse):
    part = lambda rows, first: pl.BlockSpec((rows, WIDTH), lambda j: (0, first + j))
    window = 2 * WIN + BLOCK
    return pl.pallas_call(
        query_kernel,
        grid=(4,),
        in_specs=[
            part(window, 0),
            part(window, 0),
            part(BLOCK, 0),
            pl.BlockSpec((BLOCK, 256), lambda j: (0, 0)),
            pl.BlockSpec((4, window, BLOCK), lambda j: (j, 0, 0)),
            pl.BlockSpec((HEADS, BLOCK), lambda j: (0, 0)),
        ],
        out_specs=pl.BlockSpec((WIDTH, BLOCK), lambda j: (j, 0)),
        out_shape=jax.ShapeDtypeStruct((1024, BLOCK), BF),
        scratch_shapes=[pltpu.VMEM((4, window, BLOCK), BF)],
        compiler_params=pltpu.CompilerParams(vmem_limit_bytes=16 * 1024 * 1024),
        cost_estimate=pl.CostEstimate(
            flops=6 << 30, bytes_accessed=5 << 20, transcendentals=3 << 20
        ),
    )(kcat, vcat, grad, in_hbm(packed), probs, inverse)


def key_kernel(
    counts_ref,
    q_ref,
    k_ref,
    v_ref,
    qhalo_ref,
    grad_ref,
    own_ref,
    left_ref,
    right_ref,
    w_out_ref,
    readout_ref,
    out_ref,
    probs,
    dscores,
    dhidden,
):
    step = pl.program_id(0)

    @pl.when(step == 0)
    def _():
        probs[...] = jnp.zeros_like(probs)
        dscores[...] = jnp.zeros_like(dscores)
        dhidden[:WIN] = dot_nt(left_ref[:, :128], readout_ref[...]).astype(BF)
        dhidden[WIN:] = dot_nt(right_ref[:, :128], readout_ref[...]).astype(BF)

    ghalo = dot_nt(dhidden[...], w_out_ref[...]).astype(BF)
    terms = jnp.concatenate(
        [left_ref[:, 128:], own_ref[:, 128:], right_ref[:, 128:]], axis=0
    )
    window = terms.shape[0]
    fill = key_fill([(counts_ref[1], BLOCK)])
    value_fill = (spare_lane(fill.shape) < 3).astype(BF)
    low_q = iota((window, PAIR), 1) < HEAD_WIDTH
    low_k = iota(fill.shape, 1) < HEAD_WIDTH
    ones = (spare_lane((window, WIDTH)) == 3).astype(F32)
    q_fill = (dot_nn(terms, stat_spread(step, 0)) + ones).astype(BF)
    g_fill = dot_nn(terms, stat_spread(step, HEADS)).astype(BF)
    turned = []
    for pair in range(2):
        columns = slice(pair * PAIR, (pair + 1) * PAIR)
        q_pair = jnp.concatenate(
            [qhalo_ref[:WIN, columns], q_ref[:, columns], qhalo_ref[WIN:, columns]], axis=0
        ) * jnp.asarray(HEAD_WIDTH ** (-0.5), BF)
        g_pair = jnp.concatenate(
            [ghalo[:WIN, columns], grad_ref[:, columns], ghalo[WIN:, columns]], axis=0
        )
        k_pair = k_ref[:, columns]
        v_pair = v_ref[:, columns]
        q_turned = q_pair.T
        g_turned = g_pair.T
        for half in range(2):
            slot = pair * 2 + half
            pick_q = low_q if half == 0 else ~low_q
            pick_k = low_k if half == 0 else ~low_k
            q_head = jnp.where(pick_q, q_pair, q_fill[:, columns])
            g_head = jnp.where(pick_q, g_pair, g_fill[:, columns])
            k_head = jnp.where(pick_k, k_pair, fill)
            v_head = jnp.where(pick_k, v_pair, value_fill)
            scores = dot_nt(q_head, k_head)
            change = dot_nt(g_head, v_head)
            for tile in range(2):
                rows = slice(tile * 128, tile * 128 + 640)
                lanes = slice(tile * 128, tile * 128 + 128)
                weight = keep_band(jnp.exp(scores[rows, lanes]), 0.0)
                moved = change[rows, lanes]
                start = tile * 128
                for piece, (low, high) in zip(weight, ((0, 128), (128, 512), (512, 640))):
                    place = slice(start + low, start + high)
                    probs[slot, place, lanes] = piece.astype(BF)
                    dscores[slot, place, lanes] = (piece * moved[low:high]).astype(BF)
            lanes = slice(half * HEAD_WIDTH, (half + 1) * HEAD_WIDTH)
            turned.append((q_turned[lanes], g_turned[lanes]))
    for slot in range(4):
        place = slice(slot * HEAD_WIDTH, (slot + 1) * HEAD_WIDTH)
        out_ref[0, place] = dot_nn(turned[slot][0], dscores[slot]).astype(BF)
        out_ref[1, place] = dot_nn(turned[slot][1], probs[slot]).astype(BF)


def key_grads(counts, projected, qhalo, grad, own, left, right, w_out, readout_weight):
    part = lambda rows, first: pl.BlockSpec((rows, WIDTH), lambda j: (0, first + j))
    whole = lambda *shape: pl.BlockSpec(shape, lambda j: (0, 0))
    window = 2 * WIN + BLOCK
    return pl.pallas_call(
        key_kernel,
        grid=(4,),
        in_specs=[
            pl.BlockSpec(memory_space=pltpu.SMEM),
            part(BLOCK, 0),
            part(BLOCK, 4),
            part(BLOCK, 8),
            part(2 * WIN, 0),
            part(BLOCK, 0),
            whole(BLOCK, 256),
            whole(BLOCK, 256),
            whole(BLOCK, 256),
            pl.BlockSpec((WIDTH, 1024), lambda j: (j, 0)),
            whole(1024, 128),
        ],
        out_specs=pl.BlockSpec((2, WIDTH, BLOCK), lambda j: (0, j, 0)),
        out_shape=jax.ShapeDtypeStruct((2, 1024, BLOCK), BF),
        scratch_shapes=[
            pltpu.VMEM((4, window, BLOCK), BF),
            pltpu.VMEM((4, window, BLOCK), BF),
            pltpu.VMEM((2 * WIN, 1024), BF),
        ],
        compiler_params=pltpu.CompilerParams(vmem_limit_bytes=18 * 1024 * 1024),
        cost_estimate=FREE,
    )(
        counts,
        projected,
        projected,
        projected,
        qhalo,
        in_hbm(grad),
        in_hbm(own),
        in_hbm(left),
        in_hbm(right),
        in_hbm(w_out),
        readout_weight,
    )


AXES = ("x_hi", "core", "y", "x_lo", "z")
MEMBER = ("x_hi", "core")
CELLS = ("y", "x_lo", "z")
CHIPS = ("x_hi", "y", "x_lo", "z")
SWAP = [(0, 1), (1, 0)]


def swap_core(values):
    return lax.ppermute(values, "core", SWAP)


def scatter(partial):
    columns = partial.shape[1]
    return lax.all_to_all(partial.reshape(64, 8, columns), CHIPS, split_axis=0, concat_axis=0)


def add_up(pieces):
    return jnp.sum(pieces.astype(F32), axis=0)


def per_device(latent, counts, w_qkv, w_out, readout_weight, target):
    latent_own = latent[0]
    cell_count = 32
    cell_index = lax.axis_index(CELLS)
    member_index = lax.axis_index(MEMBER)
    core = lax.axis_index("core")
    up = [(i, i + 1) for i in range(cell_count - 1)]
    down = [(i + 1, i) for i in range(cell_count - 1)]
    from_left = lax.ppermute(latent_own, CELLS, up)
    from_right = lax.ppermute(latent_own, CELLS, down)

    own_count = counts[cell_index]
    left_count = jnp.where(cell_index > 0, counts[jnp.maximum(cell_index - 1, 0)], 0)
    right_count = jnp.where(
        cell_index < cell_count - 1, counts[jnp.minimum(cell_index + 1, cell_count - 1)], 0
    )
    scalars = jnp.stack([left_count, own_count, right_count])

    projected, turned = project(latent_own, w_qkv)
    turned_other = swap_core(turned)
    normed_halo, kcat, vcat, attended, stats, hidden, forecast, probs, inverse = forward(
        scalars, from_left, from_right, latent_own, w_qkv, projected, w_out, readout_weight
    )
    near = lax.ppermute(forecast, "x_hi", SWAP)
    qhalo = halo_queries(normed_halo, w_qkv)
    near, qhalo = lax.optimization_barrier((near, qhalo))
    others = swap_core(jnp.stack([forecast, near]))
    crps_whole, packed, grad, small = score(
        scalars, forecast, near, others, target, attended, hidden, stats, w_out, readout_weight
    )
    crps = lax.dynamic_slice_in_dim(crps_whole, member_index * 32, 32, 1)
    dquery = query_grads(kcat, vcat, grad, packed, probs, inverse)
    packed, dquery = lax.optimization_barrier((packed, dquery))
    packed_left = lax.ppermute(packed, CELLS, up)
    packed_right = lax.ppermute(packed, CELLS, down)

    first_part = partial_sums(
        core, turned, turned_other, dquery, swap_core(dquery), (small, swap_core(small))
    )
    first_part, scalars = lax.optimization_barrier((first_part, scalars))
    first = scatter(first_part)
    pairs = key_grads(
        scalars,
        projected,
        qhalo,
        grad,
        packed,
        packed_left,
        packed_right,
        w_out,
        readout_weight,
    )
    pairs = pairs.reshape(2048, BLOCK)
    second_part = partial_sums(core, turned, turned_other, pairs, swap_core(pairs))
    second_part, first = lax.optimization_barrier((second_part, first))
    second = add_up(scatter(second_part))
    first = add_up(first)
    grad_out = lax.dot_general(
        first[:, 1024:1152],
        readout_weight.astype(F32),
        (((1,), (1,)), ((), ())),
        precision=lax.Precision.HIGHEST,
        preferred_element_type=F32,
    )
    grads = jnp.concatenate([first[:, :1024], second, grad_out, first[:, 1152:]], axis=1)
    return (crps, grads)


def solution(mesh):
    fine = jax.sharding.Mesh(mesh.devices.reshape(2, 2, 4, 2, 4), AXES)
    placed = (P(MEMBER, CELLS, None), P(), P(), P(), P(), P(CELLS, None))
    return jax.shard_map(
        per_device,
        mesh=fine,
        in_specs=placed,
        out_specs=(P(CELLS, MEMBER), P(MEMBER + CELLS, None)),
        check_vma=False,
    )
```

```python
import functools

import jax
import jax.numpy as jnp
import numpy as np
from jax import lax
from jax.experimental import pallas as pl
from jax.experimental.pallas import tpu as pltpu
from jax.sharding import PartitionSpec as P

HEADS = 16
WIN = 256
BLOCK = 256
WIDTH = 256
HEAD_WIDTH = 64
PAIR = 128
NEVER = -1e30

alpha_fair = 0.95
smooth_width = 0.0625

BF = jnp.bfloat16
F32 = jnp.float32


def smooth_abs(values):
    return jnp.sqrt(values * values + smooth_width)


def smooth_sign(values):
    return values * lax.rsqrt(values * values + smooth_width)


def layer_norm(latent_rows):
    values = latent_rows.astype(F32)
    center = values - jnp.mean(values, axis=-1, keepdims=True)
    spread = jnp.mean(center * center, axis=-1, keepdims=True)
    return (center * lax.rsqrt(spread + 1e-05)).astype(BF)


def dot_nn(left, right):
    return lax.dot_general(left, right, (((1,), (0,)), ((), ())), preferred_element_type=F32)


def dot_nt(left, right):
    return lax.dot_general(left, right, (((1,), (1,)), ((), ())), preferred_element_type=F32)


def dot_tn(left, right):
    return lax.dot_general(left, right, (((0,), (0,)), ((), ())), preferred_element_type=F32)


def iota(shape, axis):
    return lax.broadcasted_iota(jnp.int32, shape, axis)


FREE = pl.CostEstimate(flops=0, bytes_accessed=0, transcendentals=0)
HBM = pl.BlockSpec(memory_space=pltpu.HBM)


def in_hbm(values):
    return pltpu.with_memory_space_constraint(values, pltpu.HBM)


def fetches(weight_ref, buffer, arrived, width, first):
    return [
        pltpu.make_async_copy(
            weight_ref.at[:, pl.ds(first + place * width, width)],
            buffer.at[place],
            arrived.at[place],
        )
        for place in range(buffer.shape[0])
    ]


def fetch_one(weight_ref, buffer, arrived, width, first, place):
    start = pl.multiple_of(first + place * width, width)
    return pltpu.make_async_copy(
        weight_ref.at[:, pl.ds(start, width)], buffer.at[place], arrived.at[place]
    )


def project_kernel(latent_ref, weight_ref, projected_ref, turned_ref, normed, buffer, arrived):
    step = pl.program_id(0)

    @pl.when(step == 0)
    def _():
        for copy in fetches(weight_ref, buffer, arrived, 512, 0):
            copy.start()
        normed[...] = layer_norm(latent_ref[...])
        turned_ref[...] = normed[...].T

    fetch_one(weight_ref, buffer, arrived, 512, 0, step).wait()
    projected_ref[...] = dot_nn(normed[...], buffer[step]).astype(BF)


def project(latent_own, w_qkv):
    rows, width = latent_own.shape
    return pl.pallas_call(
        project_kernel,
        grid=(6,),
        in_specs=[pl.BlockSpec((rows, width), lambda j: (0, 0)), HBM],
        out_specs=[
            pl.BlockSpec((rows, 512), lambda j: (0, j)),
            pl.BlockSpec((width, rows), lambda j: (0, 0)),
        ],
        out_shape=[
            jax.ShapeDtypeStruct((rows, 3 * width), BF),
            jax.ShapeDtypeStruct((width, rows), BF),
        ],
        scratch_shapes=[
            pltpu.VMEM((rows, width), BF),
            pltpu.VMEM((6, width, 512), BF),
            pltpu.SemaphoreType.DMA((6,)),
        ],
        compiler_params=pltpu.CompilerParams(vmem_limit_bytes=16 * 1024 * 1024),
        cost_estimate=pl.CostEstimate(
            flops=2 * rows * width * width * 4, bytes_accessed=8 << 20, transcendentals=0
        ),
    )(latent_own, in_hbm(w_qkv))


def halo_query_kernel(normed_ref, weight_ref, out_ref, buffer, arrived):
    step = pl.program_id(0)

    @pl.when(step == 0)
    def _():
        for copy in fetches(weight_ref, buffer, arrived, 256, 0):
            copy.start()

    fetch_one(weight_ref, buffer, arrived, 256, 0, step).wait()
    out_ref[...] = dot_nn(normed_ref[...], buffer[step]).astype(BF)


def halo_queries(normed_halo, w_qkv):
    rows, width = normed_halo.shape
    return pl.pallas_call(
        halo_query_kernel,
        grid=(4,),
        in_specs=[pl.BlockSpec((rows, width), lambda j: (0, 0)), HBM],
        out_specs=pl.BlockSpec((rows, 256), lambda j: (0, j)),
        out_shape=jax.ShapeDtypeStruct((rows, width), BF),
        scratch_shapes=[
            pltpu.VMEM((4, width, 256), BF),
            pltpu.SemaphoreType.DMA((4,)),
        ],
        compiler_params=pltpu.CompilerParams(vmem_limit_bytes=12 * 1024 * 1024),
        cost_estimate=FREE,
    )(normed_halo, in_hbm(w_qkv))


def partial_kernel(
    smalls, core_ref, normed_ref, normed_other_ref, piece_ref, other_ref, *refs
):
    small_refs, (out_ref, rows, pieces, others, sums, staged, arrived, left) = (
        refs[:smalls],
        refs[smalls:],
    )
    core = core_ref[0]
    chunks = piece_ref.shape[0] // 512
    sources = [
        (normed_ref.at[:, core], rows.at[0]),
        (normed_other_ref.at[:, core], rows.at[1]),
    ]
    for chunk in range(chunks):
        part = pl.ds(chunk * 512, 512)
        sources.append((piece_ref.at[part], pieces.at[chunk]))
        sources.append((other_ref.at[part], others.at[chunk]))
    for place, small_ref in enumerate(small_refs):
        sources.append((small_ref.at[:, core], sums.at[place]))
    copies = [
        pltpu.make_async_copy(source, target, arrived.at[place])
        for place, (source, target) in enumerate(sources)
    ]
    for copy in copies:
        copy.start()
    copies[0].wait()
    copies[1].wait()
    writes = []
    for chunk in range(chunks):
        copies[2 + 2 * chunk].wait()
        copies[3 + 2 * chunk].wait()
        for top in range(2):
            staged[chunk, top * 256 : (top + 1) * 256] = (
                dot_nt(rows[0, top], pieces[chunk]) + dot_nt(rows[1, top], others[chunk])
            ).astype(BF)
        writes.append(
            pltpu.make_async_copy(
                staged.at[chunk], out_ref.at[:, pl.ds(chunk * 512, 512)], left.at[chunk]
            )
        )
        writes[-1].start()
    if smalls:
        copies[-2].wait()
        copies[-1].wait()
        for top in range(2):
            staged[chunks, top * 256 : (top + 1) * 256, :256] = (
                sums[0, top].astype(F32) + sums[1, top].astype(F32)
            ).astype(BF)
        writes.append(
            pltpu.make_async_copy(
                staged.at[chunks, :, pl.ds(0, 256)],
                out_ref.at[:, pl.ds(chunks * 512, 256)],
                left.at[chunks],
            )
        )
        writes[-1].start()
    for write in writes:
        write.wait()


def partial_sums(core, turned, turned_other, piece, other, smalls=()):
    by_core = lambda values: values.reshape(2, 2, 256, 256)
    anywhere = pl.BlockSpec(memory_space=pl.ANY)
    chunks = piece.shape[0] // 512
    columns = piece.shape[0] + 256 * (len(smalls) // 2)
    return pl.pallas_call(
        functools.partial(partial_kernel, len(smalls)),
        in_specs=[pl.BlockSpec(memory_space=pltpu.SMEM)] + [anywhere] * (4 + len(smalls)),
        out_specs=anywhere,
        out_shape=jax.ShapeDtypeStruct((512, columns), BF),
        scratch_shapes=[
            pltpu.VMEM((2, 2, 256, 256), BF),
            pltpu.VMEM((chunks, 512, 256), BF),
            pltpu.VMEM((chunks, 512, 256), BF),
            pltpu.VMEM((2, 2, 256, 256), BF),
            pltpu.VMEM((chunks + 1, 512, 512), BF),
            pltpu.SemaphoreType.DMA((2 + 2 * chunks + len(smalls),)),
            pltpu.SemaphoreType.DMA((chunks + 1,)),
        ],
        compiler_params=pltpu.CompilerParams(vmem_limit_bytes=14 * 1024 * 1024),
        cost_estimate=FREE,
    )(
        core.astype(jnp.int32).reshape(1),
        by_core(turned),
        by_core(turned_other),
        piece,
        other,
        *(by_core(small) for small in smalls),
    )


def spare_lane(shape):
    lane = iota(shape, len(shape) - 1)
    return lane % HEAD_WIDTH


def key_fill(count_pieces):
    fills = []
    for count, rows in count_pieces:
        spare = spare_lane((rows, PAIR))
        bias = jnp.where(iota((rows, PAIR), 0) < count, 0.0, NEVER)
        fills.append(
            jnp.where(spare < 3, 1.0, jnp.where(spare == 3, bias, 0.0)).astype(BF)
        )
    return jnp.concatenate(fills, axis=0)


def stat_spread(step, offset):
    shape = (128, WIDTH)
    lane = iota(shape, 1)
    head = step * 4 + 2 * (lane // PAIR) + jnp.where(lane % PAIR < HEAD_WIDTH, 1, 0)
    term = lane % HEAD_WIDTH
    chosen = (term < 3) & (iota(shape, 0) == term * 32 + offset + head)
    return jnp.where(chosen, -1.0, 0.0).astype(BF)


def keep_band(window, fill):
    shape = (128, 128)
    apart = iota(shape, 0) - iota(shape, 1)
    first = jnp.where(apart >= 0, window[:128], fill)
    last = jnp.where(apart <= 0, window[512:], fill)
    return first, window[128:512], last


def forward_kernel(
    counts_ref,
    left_ref,
    right_ref,
    latent_ref,
    weight_ref,
    q_ref,
    k_ref,
    v_ref,
    w_out_ref,
    readout_ref,
    normed_ref,
    kcat_ref,
    vcat_ref,
    attended_ref,
    stats_ref,
    hidden_ref,
    forecast_ref,
    probs,
    inverse_ref,
    stat_rows,
    buffer,
    arrived,
):
    step = pl.program_id(0)

    @pl.when(step == 0)
    def _():
        copies = fetches(weight_ref, buffer, arrived, WIDTH, 1024)
        for place in (0, 4, 1, 5, 2, 6, 3, 7):
            copies[place].start()
        normed_ref[:WIN] = layer_norm(left_ref[...])
        normed_ref[WIN:] = layer_norm(right_ref[...])

    fetch_one(weight_ref, buffer, arrived, WIDTH, 1024, step).wait()
    fetch_one(weight_ref, buffer, arrived, WIDTH, 1024, step + 4).wait()
    khalo = dot_nn(normed_ref[...], buffer[step]).astype(BF)
    kcat_ref[:WIN] = khalo[:WIN]
    kcat_ref[WIN : WIN + BLOCK] = k_ref[...]
    kcat_ref[WIN + BLOCK :] = khalo[WIN:]
    vhalo = dot_nn(normed_ref[...], buffer[step + 4]).astype(BF)
    vcat_ref[:WIN] = vhalo[:WIN]
    vcat_ref[WIN : WIN + BLOCK] = v_ref[...]
    vcat_ref[WIN + BLOCK :] = vhalo[WIN:]
    fill = key_fill([(counts_ref[0], WIN), (counts_ref[1], BLOCK), (counts_ref[2], WIN)])
    low_q = iota((BLOCK, PAIR), 1) < HEAD_WIDTH
    low_k = iota(fill.shape, 1) < HEAD_WIDTH
    query_fill = (spare_lane((BLOCK, PAIR)) == 3).astype(BF)
    scores, turned = [], []
    for pair in range(2):
        columns = slice(pair * PAIR, (pair + 1) * PAIR)
        q_pair = q_ref[:, columns] * jnp.asarray(HEAD_WIDTH ** (-0.5), BF)
        k_pair = kcat_ref[:, columns]
        turned.append(vcat_ref[:, columns].T)
        for half in range(2):
            if half == 0:
                q_head = jnp.where(low_q, q_pair, query_fill)
                k_head = jnp.where(low_k, k_pair, fill)
            else:
                q_head = jnp.where(low_q, query_fill, q_pair)
                k_head = jnp.where(low_k, fill, k_pair)
            scores.append(dot_nt(k_head, q_head))
    tops = []
    for slot in range(4):
        levels = []
        for tile in range(2):
            rows = slice(tile * 128, tile * 128 + 640)
            lanes = slice(tile * 128, tile * 128 + 128)
            first, middle, last = keep_band(scores[slot][rows, lanes], NEVER)
            top = jnp.maximum(
                jnp.max(middle, axis=0, keepdims=True),
                jnp.max(jnp.maximum(first, last), axis=0, keepdims=True),
            )
            start = tile * 128
            probs[slot, start : start + 128, lanes] = jnp.exp(first - top).astype(BF)
            probs[slot, start + 128 : start + 512, lanes] = jnp.exp(middle - top).astype(BF)
            probs[slot, start + 512 : start + 640, lanes] = jnp.exp(last - top).astype(BF)
            levels.append(top)
        probs[slot, :128, 128:] = jnp.zeros((128, 128), BF)
        probs[slot, 640:, :128] = jnp.zeros((128, 128), BF)
        tops.append(jnp.concatenate(levels, axis=1))
    ones = jnp.ones((16, fill.shape[0]), BF)
    for pair in range(2):
        halves = []
        for half in range(2):
            slot = pair * 2 + half
            lanes = slice(half * HEAD_WIDTH, (half + 1) * HEAD_WIDTH)
            values = jnp.concatenate([turned[pair][lanes], ones], axis=0)
            mixed = dot_nn(values, probs[slot])
            total = mixed[HEAD_WIDTH : HEAD_WIDTH + 1]
            inverse = 1.0 / total
            halves.append(mixed[:HEAD_WIDTH] * inverse)
            head = step * 4 + slot
            inverse_ref[pl.ds(head, 1), :] = inverse
            stat_rows[pl.ds(head, 1), :] = tops[slot] + jnp.log(total)
        start = pl.multiple_of(step * WIDTH + pair * PAIR, PAIR)
        attended_ref[:, pl.ds(start, PAIR)] = jnp.concatenate(halves, axis=0).T

    @pl.when(step == 3)
    def _():
        mixed = dot_nn(attended_ref[...].astype(BF), w_out_ref[...])
        hidden = (latent_ref[...].astype(F32) + mixed).astype(BF)
        hidden_ref[...] = hidden
        forecast_ref[...] = dot_nn(hidden, readout_ref[...])
        stat_rows[HEADS:] = jnp.zeros((128 - HEADS, BLOCK), F32)
        stats_ref[...] = stat_rows[...].T


def forward(counts, left, right, latent_own, w_qkv, projected, w_out, readout_weight):
    whole = lambda *shape: pl.BlockSpec(shape, lambda j: (0, 0))
    part = lambda rows, first: pl.BlockSpec((rows, WIDTH), lambda j: (0, first + j))
    window = 2 * WIN + BLOCK
    return pl.pallas_call(
        forward_kernel,
        grid=(4,),
        in_specs=[
            pl.BlockSpec(memory_space=pltpu.SMEM),
            whole(WIN, 1024),
            whole(WIN, 1024),
            whole(BLOCK, 1024),
            HBM,
            part(BLOCK, 0),
            part(BLOCK, 4),
            part(BLOCK, 8),
            whole(1024, 1024),
            whole(1024, 128),
        ],
        out_specs=[
            whole(2 * WIN, 1024),
            part(window, 0),
            part(window, 0),
            whole(BLOCK, 1024),
            whole(BLOCK, 128),
            whole(BLOCK, 1024),
            whole(BLOCK, 128),
            pl.BlockSpec((4, window, BLOCK), lambda j: (j, 0, 0)),
            whole(HEADS, BLOCK),
        ],
        out_shape=[
            jax.ShapeDtypeStruct((2 * WIN, 1024), BF),
            jax.ShapeDtypeStruct((window, 1024), BF),
            jax.ShapeDtypeStruct((window, 1024), BF),
            jax.ShapeDtypeStruct((BLOCK, 1024), F32),
            jax.ShapeDtypeStruct((BLOCK, 128), F32),
            jax.ShapeDtypeStruct((BLOCK, 1024), BF),
            jax.ShapeDtypeStruct((BLOCK, 128), F32),
            jax.ShapeDtypeStruct((HEADS, window, BLOCK), BF),
            jax.ShapeDtypeStruct((HEADS, BLOCK), F32),
        ],
        scratch_shapes=[
            pltpu.VMEM((128, BLOCK), F32),
            pltpu.VMEM((8, 1024, WIDTH), BF),
            pltpu.SemaphoreType.DMA((8,)),
        ],
        compiler_params=pltpu.CompilerParams(vmem_limit_bytes=30 * 1024 * 1024),
        cost_estimate=pl.CostEstimate(
            flops=6 << 30, bytes_accessed=12 << 20, transcendentals=3 << 20
        ),
    )(
        counts,
        left,
        right,
        latent_own,
        in_hbm(w_qkv),
        projected,
        projected,
        projected,
        w_out,
        readout_weight,
    )


def score_kernel(
    counts_ref,
    own_ref,
    near_ref,
    others_ref,
    target_ref,
    attended_ref,
    hidden_ref,
    stats_ref,
    w_out_ref,
    readout_ref,
    crps_ref,
    packed_ref,
    grad_ref,
    small_ref,
):
    members = 4
    fair_eps = (1.0 - alpha_fair) / members
    coefficient = (1.0 - fair_eps) / (members * (members - 1))
    valid = (iota((BLOCK, 1), 0) < counts_ref[1]).astype(F32)
    own = own_ref[...]
    forecasts = [own, near_ref[...], others_ref[0], others_ref[1]]
    target = target_ref[...]
    error = jnp.zeros_like(target)
    for forecast in forecasts:
        error += smooth_abs(forecast - target)
    spread = jnp.full_like(target, members * smooth_width**0.5)
    for first in range(members):
        for second in range(first + 1, members):
            spread += 2.0 * smooth_abs(forecasts[first] - forecasts[second])
    crps_ref[...] = valid * (error / members - 0.5 * coefficient * spread)
    pull = jnp.zeros_like(target)
    for other in forecasts[1:]:
        pull += smooth_sign(own - other)
    slope = (
        valid / 128 * (smooth_sign(own - target) / members - coefficient * pull)
    ).astype(BF)
    dhidden = dot_nt(slope, readout_ref[...]).astype(BF)
    dattended = dot_nt(dhidden, w_out_ref[...]).astype(BF)
    grad_ref[...] = dattended
    attended = attended_ref[...]
    product = dattended.astype(F32) * attended
    high = product.astype(BF)
    low = (product - high.astype(F32)).astype(BF)
    pick = (iota((1024, 128), 0) // HEAD_WIDTH + HEADS == iota((1024, 128), 1)).astype(BF)
    stats = stats_ref[...] + dot_nn(high, pick) + dot_nn(low, pick)
    first = stats.astype(BF)
    rest = stats - first.astype(F32)
    second = rest.astype(BF)
    third = (rest - second.astype(F32)).astype(BF)
    terms = jnp.zeros((BLOCK, 128), F32)
    for place, term in enumerate((first, second, third)):
        shift = (iota((128, 128), 0) + 32 * place == iota((128, 128), 1)) & (
            iota((128, 128), 0) < 32
        )
        terms += dot_nn(term, shift.astype(BF))
    packed_ref[:, :128] = slope
    packed_ref[:, 128:] = terms.astype(BF)
    small_ref[:, :128] = dot_tn(attended.astype(BF), slope).astype(BF)
    small_ref[:, 128:] = dot_tn(hidden_ref[...], slope).astype(BF)


def score(counts, own, near, others, target, attended, hidden, stats, w_out, readout_weight):
    vmem = pl.BlockSpec(memory_space=pltpu.VMEM)
    return pl.pallas_call(
        score_kernel,
        in_specs=[pl.BlockSpec(memory_space=pltpu.SMEM)] + [vmem] * 9,
        out_specs=[vmem] * 4,
        out_shape=[
            pltpu.HBM((BLOCK, 128), F32),
            pltpu.HBM((BLOCK, 256), BF),
            jax.ShapeDtypeStruct((BLOCK, 1024), BF),
            jax.ShapeDtypeStruct((1024, 256), BF),
        ],
        compiler_params=pltpu.CompilerParams(vmem_limit_bytes=12 * 1024 * 1024),
    )(counts, own, near, others, target, attended, hidden, stats, w_out, readout_weight)


def query_kernel(
    kcat_ref, vcat_ref, grad_ref, packed_ref, probs_ref, inverse_ref, dq_ref, dscores
):
    step = pl.program_id(0)
    window = kcat_ref.shape[0]
    value_fill = (spare_lane((window, PAIR)) < 3).astype(BF)
    low_q = iota((BLOCK, PAIR), 1) < HEAD_WIDTH
    low_k = iota((window, PAIR), 1) < HEAD_WIDTH
    g_fill = dot_nn(packed_ref[:, 128:], stat_spread(step, HEADS)).astype(BF)
    turned = []
    for pair in range(2):
        columns = slice(pair * PAIR, (pair + 1) * PAIR)
        g_pair = grad_ref[:, columns]
        v_pair = vcat_ref[:, columns]
        k_turned = kcat_ref[:, columns].T
        for half in range(2):
            slot = pair * 2 + half
            pick_q = low_q if half == 0 else ~low_q
            pick_k = low_k if half == 0 else ~low_k
            g_head = jnp.where(pick_q, g_pair, g_fill[:, columns])
            v_head = jnp.where(pick_k, v_pair, value_fill)
            change = dot_nt(v_head, g_head)
            dscores[slot] = (probs_ref[slot].astype(F32) * change).astype(BF)
            turned.append(k_turned[half * HEAD_WIDTH : (half + 1) * HEAD_WIDTH])
    for slot in range(4):
        scale = inverse_ref[pl.ds(step * 4 + slot, 1), :] * HEAD_WIDTH ** (-0.5)
        dquery = dot_nn(turned[slot], dscores[slot]) * scale
        dq_ref[slot * HEAD_WIDTH : (slot + 1) * HEAD_WIDTH] = dquery.astype(BF)


def query_grads(kcat, vcat, grad, packed, probs, inverse):
    part = lambda rows, first: pl.BlockSpec((rows, WIDTH), lambda j: (0, first + j))
    window = 2 * WIN + BLOCK
    return pl.pallas_call(
        query_kernel,
        grid=(4,),
        in_specs=[
            part(window, 0),
            part(window, 0),
            part(BLOCK, 0),
            pl.BlockSpec((BLOCK, 256), lambda j: (0, 0)),
            pl.BlockSpec((4, window, BLOCK), lambda j: (j, 0, 0)),
            pl.BlockSpec((HEADS, BLOCK), lambda j: (0, 0)),
        ],
        out_specs=pl.BlockSpec((WIDTH, BLOCK), lambda j: (j, 0)),
        out_shape=jax.ShapeDtypeStruct((1024, BLOCK), BF),
        scratch_shapes=[pltpu.VMEM((4, window, BLOCK), BF)],
        compiler_params=pltpu.CompilerParams(vmem_limit_bytes=16 * 1024 * 1024),
        cost_estimate=pl.CostEstimate(
            flops=6 << 30, bytes_accessed=5 << 20, transcendentals=3 << 20
        ),
    )(kcat, vcat, grad, in_hbm(packed), probs, inverse)


def key_kernel(
    counts_ref,
    q_ref,
    k_ref,
    v_ref,
    qhalo_ref,
    grad_ref,
    own_ref,
    left_ref,
    right_ref,
    w_out_ref,
    readout_ref,
    out_ref,
    probs,
    dscores,
    dhidden,
):
    step = pl.program_id(0)

    @pl.when(step == 0)
    def _():
        probs[...] = jnp.zeros_like(probs)
        dscores[...] = jnp.zeros_like(dscores)
        dhidden[:WIN] = dot_nt(left_ref[:, :128], readout_ref[...]).astype(BF)
        dhidden[WIN:] = dot_nt(right_ref[:, :128], readout_ref[...]).astype(BF)

    ghalo = dot_nt(dhidden[...], w_out_ref[...]).astype(BF)
    terms = jnp.concatenate(
        [left_ref[:, 128:], own_ref[:, 128:], right_ref[:, 128:]], axis=0
    )
    window = terms.shape[0]
    fill = key_fill([(counts_ref[1], BLOCK)])
    value_fill = (spare_lane(fill.shape) < 3).astype(BF)
    low_q = iota((window, PAIR), 1) < HEAD_WIDTH
    low_k = iota(fill.shape, 1) < HEAD_WIDTH
    ones = (spare_lane((window, WIDTH)) == 3).astype(F32)
    q_fill = (dot_nn(terms, stat_spread(step, 0)) + ones).astype(BF)
    g_fill = dot_nn(terms, stat_spread(step, HEADS)).astype(BF)
    turned = []
    for pair in range(2):
        columns = slice(pair * PAIR, (pair + 1) * PAIR)
        q_pair = jnp.concatenate(
            [qhalo_ref[:WIN, columns], q_ref[:, columns], qhalo_ref[WIN:, columns]], axis=0
        ) * jnp.asarray(HEAD_WIDTH ** (-0.5), BF)
        g_pair = jnp.concatenate(
            [ghalo[:WIN, columns], grad_ref[:, columns], ghalo[WIN:, columns]], axis=0
        )
        k_pair = k_ref[:, columns]
        v_pair = v_ref[:, columns]
        q_turned = q_pair.T
        g_turned = g_pair.T
        for half in range(2):
            slot = pair * 2 + half
            pick_q = low_q if half == 0 else ~low_q
            pick_k = low_k if half == 0 else ~low_k
            q_head = jnp.where(pick_q, q_pair, q_fill[:, columns])
            g_head = jnp.where(pick_q, g_pair, g_fill[:, columns])
            k_head = jnp.where(pick_k, k_pair, fill)
            v_head = jnp.where(pick_k, v_pair, value_fill)
            scores = dot_nt(q_head, k_head)
            change = dot_nt(g_head, v_head)
            for tile in range(2):
                rows = slice(tile * 128, tile * 128 + 640)
                lanes = slice(tile * 128, tile * 128 + 128)
                weight = keep_band(jnp.exp(scores[rows, lanes]), 0.0)
                moved = change[rows, lanes]
                start = tile * 128
                for piece, (low, high) in zip(weight, ((0, 128), (128, 512), (512, 640))):
                    place = slice(start + low, start + high)
                    probs[slot, place, lanes] = piece.astype(BF)
                    dscores[slot, place, lanes] = (piece * moved[low:high]).astype(BF)
            lanes = slice(half * HEAD_WIDTH, (half + 1) * HEAD_WIDTH)
            turned.append((q_turned[lanes], g_turned[lanes]))
    for slot in range(4):
        place = slice(slot * HEAD_WIDTH, (slot + 1) * HEAD_WIDTH)
        out_ref[0, place] = dot_nn(turned[slot][0], dscores[slot]).astype(BF)
        out_ref[1, place] = dot_nn(turned[slot][1], probs[slot]).astype(BF)


def key_grads(counts, projected, qhalo, grad, own, left, right, w_out, readout_weight):
    part = lambda rows, first: pl.BlockSpec((rows, WIDTH), lambda j: (0, first + j))
    whole = lambda *shape: pl.BlockSpec(shape, lambda j: (0, 0))
    window = 2 * WIN + BLOCK
    return pl.pallas_call(
        key_kernel,
        grid=(4,),
        in_specs=[
            pl.BlockSpec(memory_space=pltpu.SMEM),
            part(BLOCK, 0),
            part(BLOCK, 4),
            part(BLOCK, 8),
            part(2 * WIN, 0),
            part(BLOCK, 0),
            whole(BLOCK, 256),
            whole(BLOCK, 256),
            whole(BLOCK, 256),
            pl.BlockSpec((WIDTH, 1024), lambda j: (j, 0)),
            whole(1024, 128),
        ],
        out_specs=pl.BlockSpec((2, WIDTH, BLOCK), lambda j: (0, j, 0)),
        out_shape=jax.ShapeDtypeStruct((2, 1024, BLOCK), BF),
        scratch_shapes=[
            pltpu.VMEM((4, window, BLOCK), BF),
            pltpu.VMEM((4, window, BLOCK), BF),
            pltpu.VMEM((2 * WIN, 1024), BF),
        ],
        compiler_params=pltpu.CompilerParams(vmem_limit_bytes=18 * 1024 * 1024),
        cost_estimate=FREE,
    )(
        counts,
        projected,
        projected,
        projected,
        qhalo,
        in_hbm(grad),
        in_hbm(own),
        in_hbm(left),
        in_hbm(right),
        in_hbm(w_out),
        readout_weight,
    )


AXES = ("x_hi", "core", "y", "x_lo", "z")
MEMBER = ("x_hi", "core")
CELLS = ("y", "x_lo", "z")
CHIPS = ("x_hi", "y", "x_lo", "z")
SWAP = [(0, 1), (1, 0)]


def swap_core(values):
    return lax.ppermute(values, "core", SWAP)


def scatter(partial):
    columns = partial.shape[1]
    return lax.all_to_all(partial.reshape(64, 8, columns), CHIPS, split_axis=0, concat_axis=0)


def add_up(pieces):
    return jnp.sum(pieces.astype(F32), axis=0)


def per_device(latent, counts, w_qkv, w_out, readout_weight, target):
    latent_own = latent[0]
    cell_count = 32
    cell_index = lax.axis_index(CELLS)
    member_index = lax.axis_index(MEMBER)
    core = lax.axis_index("core")
    up = [(i, i + 1) for i in range(cell_count - 1)]
    down = [(i + 1, i) for i in range(cell_count - 1)]
    from_left = lax.ppermute(latent_own, CELLS, up)
    from_right = lax.ppermute(latent_own, CELLS, down)

    own_count = counts[cell_index]
    left_count = jnp.where(cell_index > 0, counts[jnp.maximum(cell_index - 1, 0)], 0)
    right_count = jnp.where(
        cell_index < cell_count - 1, counts[jnp.minimum(cell_index + 1, cell_count - 1)], 0
    )
    scalars = jnp.stack([left_count, own_count, right_count])

    projected, turned = project(latent_own, w_qkv)
    turned_other = swap_core(turned)
    normed_halo, kcat, vcat, attended, stats, hidden, forecast, probs, inverse = forward(
        scalars, from_left, from_right, latent_own, w_qkv, projected, w_out, readout_weight
    )
    near = lax.ppermute(forecast, "x_hi", SWAP)
    qhalo = halo_queries(normed_halo, w_qkv)
    near, qhalo = lax.optimization_barrier((near, qhalo))
    others = swap_core(jnp.stack([forecast, near]))
    crps_whole, packed, grad, small = score(
        scalars, forecast, near, others, target, attended, hidden, stats, w_out, readout_weight
    )
    crps = lax.dynamic_slice_in_dim(crps_whole, member_index * 32, 32, 1)
    dquery = query_grads(kcat, vcat, grad, packed, probs, inverse)
    packed, dquery = lax.optimization_barrier((packed, dquery))
    packed_left = lax.ppermute(packed, CELLS, up)
    packed_right = lax.ppermute(packed, CELLS, down)

    dquery_other, packed_left, packed_right = lax.optimization_barrier(
        (swap_core(dquery), packed_left, packed_right)
    )
    first_part = partial_sums(
        core, turned, turned_other, dquery, dquery_other, (small, swap_core(small))
    )
    first_part, scalars = lax.optimization_barrier((first_part, scalars))
    first = scatter(first_part)
    pairs = key_grads(
        scalars,
        projected,
        qhalo,
        grad,
        packed,
        packed_left,
        packed_right,
        w_out,
        readout_weight,
    )
    pairs = pairs.reshape(2048, BLOCK)
    second_part = partial_sums(core, turned, turned_other, pairs, swap_core(pairs))
    second_part, first = lax.optimization_barrier((second_part, first))
    second = add_up(scatter(second_part))
    first = add_up(first)
    grad_out = lax.dot_general(
        first[:, 1024:1152],
        readout_weight.astype(F32),
        (((1,), (1,)), ((), ())),
        precision=lax.Precision.HIGHEST,
        preferred_element_type=F32,
    )
    grads = jnp.concatenate([first[:, :1024], second, grad_out, first[:, 1152:]], axis=1)
    return (crps, grads)


def solution(mesh):
    fine = jax.sharding.Mesh(mesh.devices.reshape(2, 2, 4, 2, 4), AXES)
    placed = (P(MEMBER, CELLS, None), P(), P(), P(), P(), P(CELLS, None))
    return jax.shard_map(
        per_device,
        mesh=fine,
        in_specs=placed,
        out_specs=(P(CELLS, MEMBER), P(MEMBER + CELLS, None)),
        check_vma=False,
    )
```

```python
import functools

import jax
import jax.numpy as jnp
import numpy as np
from jax import lax
from jax.experimental import pallas as pl
from jax.experimental.pallas import tpu as pltpu
from jax.sharding import PartitionSpec as P

HEADS = 16
WIN = 256
BLOCK = 256
WIDTH = 256
HEAD_WIDTH = 64
PAIR = 128
NEVER = -1e30

alpha_fair = 0.95
smooth_width = 0.0625

BF = jnp.bfloat16
F32 = jnp.float32


def smooth_abs(values):
    return jnp.sqrt(values * values + smooth_width)


def smooth_sign(values):
    return values * lax.rsqrt(values * values + smooth_width)


def layer_norm(latent_rows):
    values = latent_rows.astype(F32)
    center = values - jnp.mean(values, axis=-1, keepdims=True)
    spread = jnp.mean(center * center, axis=-1, keepdims=True)
    return (center * lax.rsqrt(spread + 1e-05)).astype(BF)


def dot_nn(left, right):
    return lax.dot_general(left, right, (((1,), (0,)), ((), ())), preferred_element_type=F32)


def dot_nt(left, right):
    return lax.dot_general(left, right, (((1,), (1,)), ((), ())), preferred_element_type=F32)


def dot_tn(left, right):
    return lax.dot_general(left, right, (((0,), (0,)), ((), ())), preferred_element_type=F32)


def iota(shape, axis):
    return lax.broadcasted_iota(jnp.int32, shape, axis)


FREE = pl.CostEstimate(flops=0, bytes_accessed=0, transcendentals=0)
HBM = pl.BlockSpec(memory_space=pltpu.HBM)


def in_hbm(values):
    return pltpu.with_memory_space_constraint(values, pltpu.HBM)


def fetches(weight_ref, buffer, arrived, width, first):
    return [
        pltpu.make_async_copy(
            weight_ref.at[:, pl.ds(first + place * width, width)],
            buffer.at[place],
            arrived.at[place],
        )
        for place in range(buffer.shape[0])
    ]


def fetch_one(weight_ref, buffer, arrived, width, first, place):
    start = pl.multiple_of(first + place * width, width)
    return pltpu.make_async_copy(
        weight_ref.at[:, pl.ds(start, width)], buffer.at[place], arrived.at[place]
    )


def project_kernel(latent_ref, weight_ref, projected_ref, turned_ref, normed, buffer, arrived):
    step = pl.program_id(0)

    @pl.when(step == 0)
    def _():
        for copy in fetches(weight_ref, buffer, arrived, 512, 0):
            copy.start()
        normed[...] = layer_norm(latent_ref[...])
        turned_ref[...] = normed[...].T

    fetch_one(weight_ref, buffer, arrived, 512, 0, step).wait()
    projected_ref[...] = dot_nn(normed[...], buffer[step]).astype(BF)


def project(latent_own, w_qkv):
    rows, width = latent_own.shape
    return pl.pallas_call(
        project_kernel,
        grid=(6,),
        in_specs=[pl.BlockSpec((rows, width), lambda j: (0, 0)), HBM],
        out_specs=[
            pl.BlockSpec((rows, 512), lambda j: (0, j)),
            pl.BlockSpec((width, rows), lambda j: (0, 0)),
        ],
        out_shape=[
            jax.ShapeDtypeStruct((rows, 3 * width), BF),
            jax.ShapeDtypeStruct((width, rows), BF),
        ],
        scratch_shapes=[
            pltpu.VMEM((rows, width), BF),
            pltpu.VMEM((6, width, 512), BF),
            pltpu.SemaphoreType.DMA((6,)),
        ],
        compiler_params=pltpu.CompilerParams(vmem_limit_bytes=16 * 1024 * 1024),
        cost_estimate=pl.CostEstimate(
            flops=2 * rows * width * width * 4, bytes_accessed=8 << 20, transcendentals=0
        ),
    )(latent_own, in_hbm(w_qkv))


def halo_query_kernel(normed_ref, weight_ref, out_ref, buffer, arrived):
    step = pl.program_id(0)

    @pl.when(step == 0)
    def _():
        for copy in fetches(weight_ref, buffer, arrived, 256, 0):
            copy.start()

    fetch_one(weight_ref, buffer, arrived, 256, 0, step).wait()
    out_ref[...] = dot_nn(normed_ref[...], buffer[step]).astype(BF)


def halo_queries(normed_halo, w_qkv):
    rows, width = normed_halo.shape
    return pl.pallas_call(
        halo_query_kernel,
        grid=(4,),
        in_specs=[pl.BlockSpec((rows, width), lambda j: (0, 0)), HBM],
        out_specs=pl.BlockSpec((rows, 256), lambda j: (0, j)),
        out_shape=jax.ShapeDtypeStruct((rows, width), BF),
        scratch_shapes=[
            pltpu.VMEM((4, width, 256), BF),
            pltpu.SemaphoreType.DMA((4,)),
        ],
        compiler_params=pltpu.CompilerParams(vmem_limit_bytes=12 * 1024 * 1024),
        cost_estimate=FREE,
    )(normed_halo, in_hbm(w_qkv))


def partial_kernel(
    smalls, core_ref, normed_ref, normed_other_ref, piece_ref, other_ref, *refs
):
    small_refs, (out_ref, rows, pieces, others, sums, staged, arrived, left) = (
        refs[:smalls],
        refs[smalls:],
    )
    core = core_ref[0]
    chunks = piece_ref.shape[0] // 512
    sources = [
        (normed_ref.at[:, core], rows.at[0]),
        (normed_other_ref.at[:, core], rows.at[1]),
    ]
    for chunk in range(chunks):
        part = pl.ds(chunk * 512, 512)
        sources.append((piece_ref.at[part], pieces.at[chunk]))
        sources.append((other_ref.at[part], others.at[chunk]))
    for place, small_ref in enumerate(small_refs):
        sources.append((small_ref.at[:, core], sums.at[place]))
    copies = [
        pltpu.make_async_copy(source, target, arrived.at[place])
        for place, (source, target) in enumerate(sources)
    ]
    for copy in copies:
        copy.start()
    copies[0].wait()
    copies[1].wait()
    writes = []
    for chunk in range(chunks):
        copies[2 + 2 * chunk].wait()
        copies[3 + 2 * chunk].wait()
        for top in range(2):
            staged[chunk, top * 256 : (top + 1) * 256] = (
                dot_nt(rows[0, top], pieces[chunk]) + dot_nt(rows[1, top], others[chunk])
            ).astype(BF)
        writes.append(
            pltpu.make_async_copy(
                staged.at[chunk], out_ref.at[:, pl.ds(chunk * 512, 512)], left.at[chunk]
            )
        )
        writes[-1].start()
    if smalls:
        copies[-2].wait()
        copies[-1].wait()
        for top in range(2):
            staged[chunks, top * 256 : (top + 1) * 256, :256] = (
                sums[0, top].astype(F32) + sums[1, top].astype(F32)
            ).astype(BF)
        writes.append(
            pltpu.make_async_copy(
                staged.at[chunks, :, pl.ds(0, 256)],
                out_ref.at[:, pl.ds(chunks * 512, 256)],
                left.at[chunks],
            )
        )
        writes[-1].start()
    for write in writes:
        write.wait()


def partial_sums(core, turned, turned_other, piece, other, smalls=()):
    by_core = lambda values: values.reshape(2, 2, 256, 256)
    anywhere = pl.BlockSpec(memory_space=pl.ANY)
    chunks = piece.shape[0] // 512
    columns = piece.shape[0] + 256 * (len(smalls) // 2)
    return pl.pallas_call(
        functools.partial(partial_kernel, len(smalls)),
        in_specs=[pl.BlockSpec(memory_space=pltpu.SMEM)] + [anywhere] * (4 + len(smalls)),
        out_specs=anywhere,
        out_shape=jax.ShapeDtypeStruct((512, columns), BF),
        scratch_shapes=[
            pltpu.VMEM((2, 2, 256, 256), BF),
            pltpu.VMEM((chunks, 512, 256), BF),
            pltpu.VMEM((chunks, 512, 256), BF),
            pltpu.VMEM((2, 2, 256, 256), BF),
            pltpu.VMEM((chunks + 1, 512, 512), BF),
            pltpu.SemaphoreType.DMA((2 + 2 * chunks + len(smalls),)),
            pltpu.SemaphoreType.DMA((chunks + 1,)),
        ],
        compiler_params=pltpu.CompilerParams(vmem_limit_bytes=14 * 1024 * 1024),
        cost_estimate=FREE,
    )(
        core.astype(jnp.int32).reshape(1),
        by_core(turned),
        by_core(turned_other),
        piece,
        other,
        *(by_core(small) for small in smalls),
    )


def spare_lane(shape):
    lane = iota(shape, len(shape) - 1)
    return lane % HEAD_WIDTH


def key_fill(count_pieces):
    fills = []
    for count, rows in count_pieces:
        spare = spare_lane((rows, PAIR))
        bias = jnp.where(iota((rows, PAIR), 0) < count, 0.0, NEVER)
        fills.append(
            jnp.where(spare < 3, 1.0, jnp.where(spare == 3, bias, 0.0)).astype(BF)
        )
    return jnp.concatenate(fills, axis=0)


def stat_spread(step, offset):
    shape = (128, WIDTH)
    lane = iota(shape, 1)
    head = step * 4 + 2 * (lane // PAIR) + jnp.where(lane % PAIR < HEAD_WIDTH, 1, 0)
    term = lane % HEAD_WIDTH
    chosen = (term < 3) & (iota(shape, 0) == term * 32 + offset + head)
    return jnp.where(chosen, -1.0, 0.0).astype(BF)


def keep_band(window, fill):
    shape = (128, 128)
    apart = iota(shape, 0) - iota(shape, 1)
    first = jnp.where(apart >= 0, window[:128], fill)
    last = jnp.where(apart <= 0, window[512:], fill)
    return first, window[128:512], last


def forward_kernel(
    counts_ref,
    left_ref,
    right_ref,
    latent_ref,
    weight_ref,
    q_ref,
    k_ref,
    v_ref,
    w_out_ref,
    readout_ref,
    normed_ref,
    kcat_ref,
    vcat_ref,
    attended_ref,
    stats_ref,
    hidden_ref,
    forecast_ref,
    probs,
    inverse_ref,
    stat_rows,
    buffer,
    arrived,
):
    step = pl.program_id(0)

    @pl.when(step == 0)
    def _():
        copies = fetches(weight_ref, buffer, arrived, WIDTH, 1024)
        for place in (0, 4, 1, 5, 2, 6, 3, 7):
            copies[place].start()
        normed_ref[:WIN] = layer_norm(left_ref[...])
        normed_ref[WIN:] = layer_norm(right_ref[...])

    fetch_one(weight_ref, buffer, arrived, WIDTH, 1024, step).wait()
    fetch_one(weight_ref, buffer, arrived, WIDTH, 1024, step + 4).wait()
    khalo = dot_nn(normed_ref[...], buffer[step]).astype(BF)
    kcat_ref[:WIN] = khalo[:WIN]
    kcat_ref[WIN : WIN + BLOCK] = k_ref[...]
    kcat_ref[WIN + BLOCK :] = khalo[WIN:]
    vhalo = dot_nn(normed_ref[...], buffer[step + 4]).astype(BF)
    vcat_ref[:WIN] = vhalo[:WIN]
    vcat_ref[WIN : WIN + BLOCK] = v_ref[...]
    vcat_ref[WIN + BLOCK :] = vhalo[WIN:]
    fill = key_fill([(counts_ref[0], WIN), (counts_ref[1], BLOCK), (counts_ref[2], WIN)])
    low_q = iota((BLOCK, PAIR), 1) < HEAD_WIDTH
    low_k = iota(fill.shape, 1) < HEAD_WIDTH
    query_fill = (spare_lane((BLOCK, PAIR)) == 3).astype(BF)
    scores, turned = [], []
    for pair in range(2):
        columns = slice(pair * PAIR, (pair + 1) * PAIR)
        q_pair = q_ref[:, columns] * jnp.asarray(HEAD_WIDTH ** (-0.5), BF)
        k_pair = kcat_ref[:, columns]
        turned.append(vcat_ref[:, columns].T)
        for half in range(2):
            if half == 0:
                q_head = jnp.where(low_q, q_pair, query_fill)
                k_head = jnp.where(low_k, k_pair, fill)
            else:
                q_head = jnp.where(low_q, query_fill, q_pair)
                k_head = jnp.where(low_k, fill, k_pair)
            scores.append(dot_nt(k_head, q_head))
    tops = []
    for slot in range(4):
        levels = []
        for tile in range(2):
            rows = slice(tile * 128, tile * 128 + 640)
            lanes = slice(tile * 128, tile * 128 + 128)
            first, middle, last = keep_band(scores[slot][rows, lanes], NEVER)
            top = jnp.maximum(
                jnp.max(middle, axis=0, keepdims=True),
                jnp.max(jnp.maximum(first, last), axis=0, keepdims=True),
            )
            start = tile * 128
            probs[slot, start : start + 128, lanes] = jnp.exp(first - top).astype(BF)
            probs[slot, start + 128 : start + 512, lanes] = jnp.exp(middle - top).astype(BF)
            probs[slot, start + 512 : start + 640, lanes] = jnp.exp(last - top).astype(BF)
            levels.append(top)
        probs[slot, :128, 128:] = jnp.zeros((128, 128), BF)
        probs[slot, 640:, :128] = jnp.zeros((128, 128), BF)
        tops.append(jnp.concatenate(levels, axis=1))
    ones = jnp.ones((16, fill.shape[0]), BF)
    for pair in range(2):
        halves = []
        for half in range(2):
            slot = pair * 2 + half
            lanes = slice(half * HEAD_WIDTH, (half + 1) * HEAD_WIDTH)
            values = jnp.concatenate([turned[pair][lanes], ones], axis=0)
            mixed = dot_nn(values, probs[slot])
            total = mixed[HEAD_WIDTH : HEAD_WIDTH + 1]
            inverse = 1.0 / total
            halves.append(mixed[:HEAD_WIDTH] * inverse)
            head = step * 4 + slot
            inverse_ref[pl.ds(head, 1), :] = inverse
            stat_rows[pl.ds(head, 1), :] = tops[slot] + jnp.log(total)
        start = pl.multiple_of(step * WIDTH + pair * PAIR, PAIR)
        attended_ref[:, pl.ds(start, PAIR)] = jnp.concatenate(halves, axis=0).T

    @pl.when(step == 3)
    def _():
        mixed = dot_nn(attended_ref[...].astype(BF), w_out_ref[...])
        hidden = (latent_ref[...].astype(F32) + mixed).astype(BF)
        hidden_ref[...] = hidden
        forecast_ref[...] = dot_nn(hidden, readout_ref[...])
        stat_rows[HEADS:] = jnp.zeros((128 - HEADS, BLOCK), F32)
        stats_ref[...] = stat_rows[...].T


def forward(counts, left, right, latent_own, w_qkv, projected, w_out, readout_weight):
    whole = lambda *shape: pl.BlockSpec(shape, lambda j: (0, 0))
    part = lambda rows, first: pl.BlockSpec((rows, WIDTH), lambda j: (0, first + j))
    window = 2 * WIN + BLOCK
    return pl.pallas_call(
        forward_kernel,
        grid=(4,),
        in_specs=[
            pl.BlockSpec(memory_space=pltpu.SMEM),
            whole(WIN, 1024),
            whole(WIN, 1024),
            whole(BLOCK, 1024),
            HBM,
            part(BLOCK, 0),
            part(BLOCK, 4),
            part(BLOCK, 8),
            whole(1024, 1024),
            whole(1024, 128),
        ],
        out_specs=[
            whole(2 * WIN, 1024),
            part(window, 0),
            part(window, 0),
            whole(BLOCK, 1024),
            whole(BLOCK, 128),
            whole(BLOCK, 1024),
            whole(BLOCK, 128),
            pl.BlockSpec((4, window, BLOCK), lambda j: (j, 0, 0)),
            whole(HEADS, BLOCK),
        ],
        out_shape=[
            jax.ShapeDtypeStruct((2 * WIN, 1024), BF),
            jax.ShapeDtypeStruct((window, 1024), BF),
            jax.ShapeDtypeStruct((window, 1024), BF),
            jax.ShapeDtypeStruct((BLOCK, 1024), F32),
            jax.ShapeDtypeStruct((BLOCK, 128), F32),
            jax.ShapeDtypeStruct((BLOCK, 1024), BF),
            jax.ShapeDtypeStruct((BLOCK, 128), F32),
            jax.ShapeDtypeStruct((HEADS, window, BLOCK), BF),
            jax.ShapeDtypeStruct((HEADS, BLOCK), F32),
        ],
        scratch_shapes=[
            pltpu.VMEM((128, BLOCK), F32),
            pltpu.VMEM((8, 1024, WIDTH), BF),
            pltpu.SemaphoreType.DMA((8,)),
        ],
        compiler_params=pltpu.CompilerParams(vmem_limit_bytes=30 * 1024 * 1024),
        cost_estimate=pl.CostEstimate(
            flops=6 << 30, bytes_accessed=12 << 20, transcendentals=3 << 20
        ),
    )(
        counts,
        left,
        right,
        latent_own,
        in_hbm(w_qkv),
        projected,
        projected,
        projected,
        w_out,
        readout_weight,
    )


def score_kernel(
    counts_ref,
    own_ref,
    near_ref,
    others_ref,
    target_ref,
    attended_ref,
    hidden_ref,
    stats_ref,
    w_out_ref,
    readout_ref,
    crps_ref,
    packed_ref,
    sent_ref,
    grad_ref,
    small_ref,
):
    members = 4
    fair_eps = (1.0 - alpha_fair) / members
    coefficient = (1.0 - fair_eps) / (members * (members - 1))
    valid = (iota((BLOCK, 1), 0) < counts_ref[1]).astype(F32)
    own = own_ref[...]
    forecasts = [own, near_ref[...], others_ref[0], others_ref[1]]
    target = target_ref[...]
    error = jnp.zeros_like(target)
    for forecast in forecasts:
        error += smooth_abs(forecast - target)
    spread = jnp.full_like(target, members * smooth_width**0.5)
    for first in range(members):
        for second in range(first + 1, members):
            spread += 2.0 * smooth_abs(forecasts[first] - forecasts[second])
    crps_ref[...] = valid * (error / members - 0.5 * coefficient * spread)
    pull = jnp.zeros_like(target)
    for other in forecasts[1:]:
        pull += smooth_sign(own - other)
    slope = (
        valid / 128 * (smooth_sign(own - target) / members - coefficient * pull)
    ).astype(BF)
    dhidden = dot_nt(slope, readout_ref[...]).astype(BF)
    dattended = dot_nt(dhidden, w_out_ref[...]).astype(BF)
    grad_ref[...] = dattended
    attended = attended_ref[...]
    product = dattended.astype(F32) * attended
    high = product.astype(BF)
    low = (product - high.astype(F32)).astype(BF)
    pick = (iota((1024, 128), 0) // HEAD_WIDTH + HEADS == iota((1024, 128), 1)).astype(BF)
    stats = stats_ref[...] + dot_nn(high, pick) + dot_nn(low, pick)
    first = stats.astype(BF)
    rest = stats - first.astype(F32)
    second = rest.astype(BF)
    third = (rest - second.astype(F32)).astype(BF)
    terms = jnp.zeros((BLOCK, 128), F32)
    for place, term in enumerate((first, second, third)):
        shift = (iota((128, 128), 0) + 32 * place == iota((128, 128), 1)) & (
            iota((128, 128), 0) < 32
        )
        terms += dot_nn(term, shift.astype(BF))
    packed_ref[:, :128] = slope
    packed_ref[:, 128:] = terms.astype(BF)
    sent_ref[...] = packed_ref[...]
    small_ref[:, :128] = dot_tn(attended.astype(BF), slope).astype(BF)
    small_ref[:, 128:] = dot_tn(hidden_ref[...], slope).astype(BF)


def score(counts, own, near, others, target, attended, hidden, stats, w_out, readout_weight):
    vmem = pl.BlockSpec(memory_space=pltpu.VMEM)
    return pl.pallas_call(
        score_kernel,
        in_specs=[pl.BlockSpec(memory_space=pltpu.SMEM)] + [vmem] * 9,
        out_specs=[vmem] * 5,
        out_shape=[
            pltpu.HBM((BLOCK, 128), F32),
            jax.ShapeDtypeStruct((BLOCK, 256), BF),
            pltpu.HBM((BLOCK, 256), BF),
            jax.ShapeDtypeStruct((BLOCK, 1024), BF),
            jax.ShapeDtypeStruct((1024, 256), BF),
        ],
        compiler_params=pltpu.CompilerParams(vmem_limit_bytes=12 * 1024 * 1024),
    )(counts, own, near, others, target, attended, hidden, stats, w_out, readout_weight)


def query_kernel(
    kcat_ref, vcat_ref, grad_ref, packed_ref, probs_ref, inverse_ref, dq_ref, dscores
):
    step = pl.program_id(0)
    window = kcat_ref.shape[0]
    value_fill = (spare_lane((window, PAIR)) < 3).astype(BF)
    low_q = iota((BLOCK, PAIR), 1) < HEAD_WIDTH
    low_k = iota((window, PAIR), 1) < HEAD_WIDTH
    g_fill = dot_nn(packed_ref[:, 128:], stat_spread(step, HEADS)).astype(BF)
    turned = []
    for pair in range(2):
        columns = slice(pair * PAIR, (pair + 1) * PAIR)
        g_pair = grad_ref[:, columns]
        v_pair = vcat_ref[:, columns]
        k_turned = kcat_ref[:, columns].T
        for half in range(2):
            slot = pair * 2 + half
            pick_q = low_q if half == 0 else ~low_q
            pick_k = low_k if half == 0 else ~low_k
            g_head = jnp.where(pick_q, g_pair, g_fill[:, columns])
            v_head = jnp.where(pick_k, v_pair, value_fill)
            change = dot_nt(v_head, g_head)
            dscores[slot] = (probs_ref[slot].astype(F32) * change).astype(BF)
            turned.append(k_turned[half * HEAD_WIDTH : (half + 1) * HEAD_WIDTH])
    for slot in range(4):
        scale = inverse_ref[pl.ds(step * 4 + slot, 1), :] * HEAD_WIDTH ** (-0.5)
        dquery = dot_nn(turned[slot], dscores[slot]) * scale
        dq_ref[slot * HEAD_WIDTH : (slot + 1) * HEAD_WIDTH] = dquery.astype(BF)


def query_grads(kcat, vcat, grad, packed, probs, inverse):
    part = lambda rows, first: pl.BlockSpec((rows, WIDTH), lambda j: (0, first + j))
    window = 2 * WIN + BLOCK
    return pl.pallas_call(
        query_kernel,
        grid=(4,),
        in_specs=[
            part(window, 0),
            part(window, 0),
            part(BLOCK, 0),
            pl.BlockSpec((BLOCK, 256), lambda j: (0, 0)),
            pl.BlockSpec((4, window, BLOCK), lambda j: (j, 0, 0)),
            pl.BlockSpec((HEADS, BLOCK), lambda j: (0, 0)),
        ],
        out_specs=pl.BlockSpec((WIDTH, BLOCK), lambda j: (j, 0)),
        out_shape=jax.ShapeDtypeStruct((1024, BLOCK), BF),
        scratch_shapes=[pltpu.VMEM((4, window, BLOCK), BF)],
        compiler_params=pltpu.CompilerParams(vmem_limit_bytes=16 * 1024 * 1024),
        cost_estimate=pl.CostEstimate(
            flops=6 << 30, bytes_accessed=5 << 20, transcendentals=3 << 20
        ),
    )(kcat, vcat, grad, packed, probs, inverse)


def key_kernel(
    counts_ref,
    q_ref,
    k_ref,
    v_ref,
    qhalo_ref,
    grad_ref,
    own_ref,
    left_ref,
    right_ref,
    w_out_ref,
    readout_ref,
    out_ref,
    probs,
    dscores,
    dhidden,
):
    step = pl.program_id(0)

    @pl.when(step == 0)
    def _():
        probs[...] = jnp.zeros_like(probs)
        dscores[...] = jnp.zeros_like(dscores)
        dhidden[:WIN] = dot_nt(left_ref[:, :128], readout_ref[...]).astype(BF)
        dhidden[WIN:] = dot_nt(right_ref[:, :128], readout_ref[...]).astype(BF)

    ghalo = dot_nt(dhidden[...], w_out_ref[...]).astype(BF)
    terms = jnp.concatenate(
        [left_ref[:, 128:], own_ref[:, 128:], right_ref[:, 128:]], axis=0
    )
    window = terms.shape[0]
    fill = key_fill([(counts_ref[1], BLOCK)])
    value_fill = (spare_lane(fill.shape) < 3).astype(BF)
    low_q = iota((window, PAIR), 1) < HEAD_WIDTH
    low_k = iota(fill.shape, 1) < HEAD_WIDTH
    ones = (spare_lane((window, WIDTH)) == 3).astype(F32)
    q_fill = (dot_nn(terms, stat_spread(step, 0)) + ones).astype(BF)
    g_fill = dot_nn(terms, stat_spread(step, HEADS)).astype(BF)
    turned = []
    for pair in range(2):
        columns = slice(pair * PAIR, (pair + 1) * PAIR)
        q_pair = jnp.concatenate(
            [qhalo_ref[:WIN, columns], q_ref[:, columns], qhalo_ref[WIN:, columns]], axis=0
        ) * jnp.asarray(HEAD_WIDTH ** (-0.5), BF)
        g_pair = jnp.concatenate(
            [ghalo[:WIN, columns], grad_ref[:, columns], ghalo[WIN:, columns]], axis=0
        )
        k_pair = k_ref[:, columns]
        v_pair = v_ref[:, columns]
        q_turned = q_pair.T
        g_turned = g_pair.T
        for half in range(2):
            slot = pair * 2 + half
            pick_q = low_q if half == 0 else ~low_q
            pick_k = low_k if half == 0 else ~low_k
            q_head = jnp.where(pick_q, q_pair, q_fill[:, columns])
            g_head = jnp.where(pick_q, g_pair, g_fill[:, columns])
            k_head = jnp.where(pick_k, k_pair, fill)
            v_head = jnp.where(pick_k, v_pair, value_fill)
            scores = dot_nt(q_head, k_head)
            change = dot_nt(g_head, v_head)
            for tile in range(2):
                rows = slice(tile * 128, tile * 128 + 640)
                lanes = slice(tile * 128, tile * 128 + 128)
                weight = keep_band(jnp.exp(scores[rows, lanes]), 0.0)
                moved = change[rows, lanes]
                start = tile * 128
                for piece, (low, high) in zip(weight, ((0, 128), (128, 512), (512, 640))):
                    place = slice(start + low, start + high)
                    probs[slot, place, lanes] = piece.astype(BF)
                    dscores[slot, place, lanes] = (piece * moved[low:high]).astype(BF)
            lanes = slice(half * HEAD_WIDTH, (half + 1) * HEAD_WIDTH)
            turned.append((q_turned[lanes], g_turned[lanes]))
    for slot in range(4):
        place = slice(slot * HEAD_WIDTH, (slot + 1) * HEAD_WIDTH)
        out_ref[0, place] = dot_nn(turned[slot][0], dscores[slot]).astype(BF)
        out_ref[1, place] = dot_nn(turned[slot][1], probs[slot]).astype(BF)


def key_grads(counts, projected, qhalo, grad, own, left, right, w_out, readout_weight):
    part = lambda rows, first: pl.BlockSpec((rows, WIDTH), lambda j: (0, first + j))
    whole = lambda *shape: pl.BlockSpec(shape, lambda j: (0, 0))
    window = 2 * WIN + BLOCK
    return pl.pallas_call(
        key_kernel,
        grid=(4,),
        in_specs=[
            pl.BlockSpec(memory_space=pltpu.SMEM),
            part(BLOCK, 0),
            part(BLOCK, 4),
            part(BLOCK, 8),
            part(2 * WIN, 0),
            part(BLOCK, 0),
            whole(BLOCK, 256),
            whole(BLOCK, 256),
            whole(BLOCK, 256),
            pl.BlockSpec((WIDTH, 1024), lambda j: (j, 0)),
            whole(1024, 128),
        ],
        out_specs=pl.BlockSpec((2, WIDTH, BLOCK), lambda j: (0, j, 0)),
        out_shape=jax.ShapeDtypeStruct((2, 1024, BLOCK), BF),
        scratch_shapes=[
            pltpu.VMEM((4, window, BLOCK), BF),
            pltpu.VMEM((4, window, BLOCK), BF),
            pltpu.VMEM((2 * WIN, 1024), BF),
        ],
        compiler_params=pltpu.CompilerParams(vmem_limit_bytes=18 * 1024 * 1024),
        cost_estimate=FREE,
    )(
        counts,
        projected,
        projected,
        projected,
        qhalo,
        in_hbm(grad),
        own,
        in_hbm(left),
        in_hbm(right),
        in_hbm(w_out),
        readout_weight,
    )


AXES = ("x_hi", "core", "y", "x_lo", "z")
MEMBER = ("x_hi", "core")
CELLS = ("y", "x_lo", "z")
CHIPS = ("x_hi", "y", "x_lo", "z")
SWAP = [(0, 1), (1, 0)]


def swap_core(values):
    return lax.ppermute(values, "core", SWAP)


def scatter(partial):
    columns = partial.shape[1]
    return lax.all_to_all(partial.reshape(64, 8, columns), CHIPS, split_axis=0, concat_axis=0)


def add_up(pieces):
    return jnp.sum(pieces.astype(F32), axis=0)


def per_device(latent, counts, w_qkv, w_out, readout_weight, target):
    latent_own = latent[0]
    cell_count = 32
    cell_index = lax.axis_index(CELLS)
    member_index = lax.axis_index(MEMBER)
    core = lax.axis_index("core")
    up = [(i, i + 1) for i in range(cell_count - 1)]
    down = [(i + 1, i) for i in range(cell_count - 1)]
    from_left = lax.ppermute(latent_own, CELLS, up)
    from_right = lax.ppermute(latent_own, CELLS, down)

    own_count = counts[cell_index]
    left_count = jnp.where(cell_index > 0, counts[jnp.maximum(cell_index - 1, 0)], 0)
    right_count = jnp.where(
        cell_index < cell_count - 1, counts[jnp.minimum(cell_index + 1, cell_count - 1)], 0
    )
    scalars = jnp.stack([left_count, own_count, right_count])

    projected, turned = project(latent_own, w_qkv)
    turned_other = swap_core(turned)
    normed_halo, kcat, vcat, attended, stats, hidden, forecast, probs, inverse = forward(
        scalars, from_left, from_right, latent_own, w_qkv, projected, w_out, readout_weight
    )
    near = lax.ppermute(forecast, "x_hi", SWAP)
    qhalo = halo_queries(normed_halo, w_qkv)
    near, qhalo = lax.optimization_barrier((near, qhalo))
    others = swap_core(jnp.stack([forecast, near]))
    crps_whole, packed, sent, grad, small = score(
        scalars, forecast, near, others, target, attended, hidden, stats, w_out, readout_weight
    )
    crps = lax.dynamic_slice_in_dim(crps_whole, member_index * 32, 32, 1)
    packed_left = lax.ppermute(sent, CELLS, up)
    packed_right = lax.ppermute(sent, CELLS, down)

    dquery = query_grads(kcat, vcat, grad, packed, probs, inverse)
    dquery, packed_left, packed_right = lax.optimization_barrier(
        (dquery, packed_left, packed_right)
    )

    first_part = partial_sums(
        core, turned, turned_other, dquery, swap_core(dquery), (small, swap_core(small))
    )
    first_part, scalars = lax.optimization_barrier((first_part, scalars))
    first = scatter(first_part)
    pairs = key_grads(
        scalars,
        projected,
        qhalo,
        grad,
        packed,
        packed_left,
        packed_right,
        w_out,
        readout_weight,
    )
    pairs = pairs.reshape(2048, BLOCK)
    second_part = partial_sums(core, turned, turned_other, pairs, swap_core(pairs))
    second_part, first = lax.optimization_barrier((second_part, first))
    second = add_up(scatter(second_part))
    first = add_up(first)
    grad_out = lax.dot_general(
        first[:, 1024:1152],
        readout_weight.astype(F32),
        (((1,), (1,)), ((), ())),
        precision=lax.Precision.HIGHEST,
        preferred_element_type=F32,
    )
    grads = jnp.concatenate([first[:, :1024], second, grad_out, first[:, 1152:]], axis=1)
    return (crps, grads)


def solution(mesh):
    fine = jax.sharding.Mesh(mesh.devices.reshape(2, 2, 4, 2, 4), AXES)
    placed = (P(MEMBER, CELLS, None), P(), P(), P(), P(), P(CELLS, None))
    return jax.shard_map(
        per_device,
        mesh=fine,
        in_specs=placed,
        out_specs=(P(CELLS, MEMBER), P(MEMBER + CELLS, None)),
        check_vma=False,
    )
```

```python
import functools

import jax
import jax.numpy as jnp
import numpy as np
from jax import lax
from jax.experimental import pallas as pl
from jax.experimental.pallas import tpu as pltpu
from jax.sharding import PartitionSpec as P

HEADS = 16
WIN = 256
BLOCK = 256
WIDTH = 256
HEAD_WIDTH = 64
PAIR = 128
NEVER = -1e30

alpha_fair = 0.95
smooth_width = 0.0625

BF = jnp.bfloat16
F32 = jnp.float32


def smooth_abs(values):
    return jnp.sqrt(values * values + smooth_width)


def smooth_sign(values):
    return values * lax.rsqrt(values * values + smooth_width)


def layer_norm(latent_rows):
    values = latent_rows.astype(F32)
    center = values - jnp.mean(values, axis=-1, keepdims=True)
    spread = jnp.mean(center * center, axis=-1, keepdims=True)
    return (center * lax.rsqrt(spread + 1e-05)).astype(BF)


def dot_nn(left, right):
    return lax.dot_general(left, right, (((1,), (0,)), ((), ())), preferred_element_type=F32)


def dot_nt(left, right):
    return lax.dot_general(left, right, (((1,), (1,)), ((), ())), preferred_element_type=F32)


def dot_tn(left, right):
    return lax.dot_general(left, right, (((0,), (0,)), ((), ())), preferred_element_type=F32)


def iota(shape, axis):
    return lax.broadcasted_iota(jnp.int32, shape, axis)


FREE = pl.CostEstimate(flops=0, bytes_accessed=0, transcendentals=0)
HBM = pl.BlockSpec(memory_space=pltpu.HBM)


def in_hbm(values):
    return pltpu.with_memory_space_constraint(values, pltpu.HBM)


def fetches(weight_ref, buffer, arrived, width, first):
    return [
        pltpu.make_async_copy(
            weight_ref.at[:, pl.ds(first + place * width, width)],
            buffer.at[place],
            arrived.at[place],
        )
        for place in range(buffer.shape[0])
    ]


def fetch_one(weight_ref, buffer, arrived, width, first, place):
    start = pl.multiple_of(first + place * width, width)
    return pltpu.make_async_copy(
        weight_ref.at[:, pl.ds(start, width)], buffer.at[place], arrived.at[place]
    )


def project_kernel(latent_ref, weight_ref, projected_ref, turned_ref, normed, buffer, arrived):
    step = pl.program_id(0)

    @pl.when(step == 0)
    def _():
        for copy in fetches(weight_ref, buffer, arrived, 512, 0):
            copy.start()
        normed[...] = layer_norm(latent_ref[...])
        turned_ref[...] = normed[...].T

    fetch_one(weight_ref, buffer, arrived, 512, 0, step).wait()
    projected_ref[...] = dot_nn(normed[...], buffer[step]).astype(BF)


def project(latent_own, w_qkv):
    rows, width = latent_own.shape
    return pl.pallas_call(
        project_kernel,
        grid=(6,),
        in_specs=[pl.BlockSpec((rows, width), lambda j: (0, 0)), HBM],
        out_specs=[
            pl.BlockSpec((rows, 512), lambda j: (0, j)),
            pl.BlockSpec((width, rows), lambda j: (0, 0)),
        ],
        out_shape=[
            jax.ShapeDtypeStruct((rows, 3 * width), BF),
            jax.ShapeDtypeStruct((width, rows), BF),
        ],
        scratch_shapes=[
            pltpu.VMEM((rows, width), BF),
            pltpu.VMEM((6, width, 512), BF),
            pltpu.SemaphoreType.DMA((6,)),
        ],
        compiler_params=pltpu.CompilerParams(vmem_limit_bytes=16 * 1024 * 1024),
        cost_estimate=pl.CostEstimate(
            flops=2 * rows * width * width * 4, bytes_accessed=8 << 20, transcendentals=0
        ),
    )(latent_own, in_hbm(w_qkv))


def halo_query_kernel(normed_ref, weight_ref, out_ref, buffer, arrived):
    step = pl.program_id(0)

    @pl.when(step == 0)
    def _():
        for copy in fetches(weight_ref, buffer, arrived, 256, 0):
            copy.start()

    fetch_one(weight_ref, buffer, arrived, 256, 0, step).wait()
    out_ref[...] = dot_nn(normed_ref[...], buffer[step]).astype(BF)


def halo_queries(normed_halo, w_qkv):
    rows, width = normed_halo.shape
    return pl.pallas_call(
        halo_query_kernel,
        grid=(4,),
        in_specs=[pl.BlockSpec((rows, width), lambda j: (0, 0)), HBM],
        out_specs=pl.BlockSpec((rows, 256), lambda j: (0, j)),
        out_shape=jax.ShapeDtypeStruct((rows, width), BF),
        scratch_shapes=[
            pltpu.VMEM((4, width, 256), BF),
            pltpu.SemaphoreType.DMA((4,)),
        ],
        compiler_params=pltpu.CompilerParams(vmem_limit_bytes=12 * 1024 * 1024),
        cost_estimate=FREE,
    )(normed_halo, in_hbm(w_qkv))


def partial_kernel(
    smalls, core_ref, normed_ref, normed_other_ref, piece_ref, other_ref, *refs
):
    small_refs, (out_ref, rows, pieces, others, sums, staged, arrived, left) = (
        refs[:smalls],
        refs[smalls:],
    )
    core = core_ref[0]
    chunks = piece_ref.shape[0] // 512
    sources = [
        (normed_ref.at[:, core], rows.at[0]),
        (normed_other_ref.at[:, core], rows.at[1]),
    ]
    for chunk in range(chunks):
        part = pl.ds(chunk * 512, 512)
        sources.append((piece_ref.at[part], pieces.at[chunk]))
        sources.append((other_ref.at[part], others.at[chunk]))
    for place, small_ref in enumerate(small_refs):
        sources.append((small_ref.at[:, core], sums.at[place]))
    copies = [
        pltpu.make_async_copy(source, target, arrived.at[place])
        for place, (source, target) in enumerate(sources)
    ]
    for copy in copies:
        copy.start()
    copies[0].wait()
    copies[1].wait()
    writes = []
    for chunk in range(chunks):
        copies[2 + 2 * chunk].wait()
        copies[3 + 2 * chunk].wait()
        for top in range(2):
            staged[chunk, top * 256 : (top + 1) * 256] = (
                dot_nt(rows[0, top], pieces[chunk]) + dot_nt(rows[1, top], others[chunk])
            ).astype(BF)
        writes.append(
            pltpu.make_async_copy(
                staged.at[chunk], out_ref.at[:, pl.ds(chunk * 512, 512)], left.at[chunk]
            )
        )
        writes[-1].start()
    if smalls:
        copies[-2].wait()
        copies[-1].wait()
        for top in range(2):
            staged[chunks, top * 256 : (top + 1) * 256, :256] = (
                sums[0, top].astype(F32) + sums[1, top].astype(F32)
            ).astype(BF)
        writes.append(
            pltpu.make_async_copy(
                staged.at[chunks, :, pl.ds(0, 256)],
                out_ref.at[:, pl.ds(chunks * 512, 256)],
                left.at[chunks],
            )
        )
        writes[-1].start()
    for write in writes:
        write.wait()


def partial_sums(core, turned, turned_other, piece, other, smalls=()):
    by_core = lambda values: values.reshape(2, 2, 256, 256)
    anywhere = pl.BlockSpec(memory_space=pl.ANY)
    chunks = piece.shape[0] // 512
    columns = piece.shape[0] + 256 * (len(smalls) // 2)
    return pl.pallas_call(
        functools.partial(partial_kernel, len(smalls)),
        in_specs=[pl.BlockSpec(memory_space=pltpu.SMEM)] + [anywhere] * (4 + len(smalls)),
        out_specs=anywhere,
        out_shape=jax.ShapeDtypeStruct((512, columns), BF),
        scratch_shapes=[
            pltpu.VMEM((2, 2, 256, 256), BF),
            pltpu.VMEM((chunks, 512, 256), BF),
            pltpu.VMEM((chunks, 512, 256), BF),
            pltpu.VMEM((2, 2, 256, 256), BF),
            pltpu.VMEM((chunks + 1, 512, 512), BF),
            pltpu.SemaphoreType.DMA((2 + 2 * chunks + len(smalls),)),
            pltpu.SemaphoreType.DMA((chunks + 1,)),
        ],
        compiler_params=pltpu.CompilerParams(vmem_limit_bytes=14 * 1024 * 1024),
        cost_estimate=FREE,
    )(
        core.astype(jnp.int32).reshape(1),
        by_core(turned),
        by_core(turned_other),
        piece,
        other,
        *(by_core(small) for small in smalls),
    )


def spare_lane(shape):
    lane = iota(shape, len(shape) - 1)
    return lane % HEAD_WIDTH


def key_fill(count_pieces):
    fills = []
    for count, rows in count_pieces:
        spare = spare_lane((rows, PAIR))
        bias = jnp.where(iota((rows, PAIR), 0) < count, 0.0, NEVER)
        fills.append(
            jnp.where(spare < 3, 1.0, jnp.where(spare == 3, bias, 0.0)).astype(BF)
        )
    return jnp.concatenate(fills, axis=0)


def stat_spread(step, offset):
    shape = (128, WIDTH)
    lane = iota(shape, 1)
    head = step * 4 + 2 * (lane // PAIR) + jnp.where(lane % PAIR < HEAD_WIDTH, 1, 0)
    term = lane % HEAD_WIDTH
    chosen = (term < 3) & (iota(shape, 0) == term * 32 + offset + head)
    return jnp.where(chosen, -1.0, 0.0).astype(BF)


def keep_band(window, fill):
    shape = (128, 128)
    apart = iota(shape, 0) - iota(shape, 1)
    first = jnp.where(apart >= 0, window[:128], fill)
    last = jnp.where(apart <= 0, window[512:], fill)
    return first, window[128:512], last


def forward_kernel(
    counts_ref,
    left_ref,
    right_ref,
    latent_ref,
    weight_ref,
    q_ref,
    k_ref,
    v_ref,
    w_out_ref,
    readout_ref,
    normed_ref,
    kcat_ref,
    vcat_ref,
    attended_ref,
    stats_ref,
    hidden_ref,
    forecast_ref,
    probs,
    inverse_ref,
    stat_rows,
    buffer,
    arrived,
):
    step = pl.program_id(0)

    @pl.when(step == 0)
    def _():
        copies = fetches(weight_ref, buffer, arrived, WIDTH, 1024)
        for place in (0, 4, 1, 5, 2, 6, 3, 7):
            copies[place].start()
        normed_ref[:WIN] = layer_norm(left_ref[...])
        normed_ref[WIN:] = layer_norm(right_ref[...])

    fetch_one(weight_ref, buffer, arrived, WIDTH, 1024, step).wait()
    fetch_one(weight_ref, buffer, arrived, WIDTH, 1024, step + 4).wait()
    khalo = dot_nn(normed_ref[...], buffer[step]).astype(BF)
    kcat_ref[:WIN] = khalo[:WIN]
    kcat_ref[WIN : WIN + BLOCK] = k_ref[...]
    kcat_ref[WIN + BLOCK :] = khalo[WIN:]
    vhalo = dot_nn(normed_ref[...], buffer[step + 4]).astype(BF)
    vcat_ref[:WIN] = vhalo[:WIN]
    vcat_ref[WIN : WIN + BLOCK] = v_ref[...]
    vcat_ref[WIN + BLOCK :] = vhalo[WIN:]
    fill = key_fill([(counts_ref[0], WIN), (counts_ref[1], BLOCK), (counts_ref[2], WIN)])
    low_q = iota((BLOCK, PAIR), 1) < HEAD_WIDTH
    low_k = iota(fill.shape, 1) < HEAD_WIDTH
    query_fill = (spare_lane((BLOCK, PAIR)) == 3).astype(BF)
    scores, turned = [], []
    for pair in range(2):
        columns = slice(pair * PAIR, (pair + 1) * PAIR)
        q_pair = q_ref[:, columns] * jnp.asarray(HEAD_WIDTH ** (-0.5), BF)
        k_pair = kcat_ref[:, columns]
        turned.append(vcat_ref[:, columns].T)
        for half in range(2):
            if half == 0:
                q_head = jnp.where(low_q, q_pair, query_fill)
                k_head = jnp.where(low_k, k_pair, fill)
            else:
                q_head = jnp.where(low_q, query_fill, q_pair)
                k_head = jnp.where(low_k, fill, k_pair)
            scores.append(dot_nt(k_head, q_head))
    tops = []
    for slot in range(4):
        levels = []
        for tile in range(2):
            rows = slice(tile * 128, tile * 128 + 640)
            lanes = slice(tile * 128, tile * 128 + 128)
            first, middle, last = keep_band(scores[slot][rows, lanes], NEVER)
            top = jnp.maximum(
                jnp.max(middle, axis=0, keepdims=True),
                jnp.max(jnp.maximum(first, last), axis=0, keepdims=True),
            )
            start = tile * 128
            probs[slot, start : start + 128, lanes] = jnp.exp(first - top).astype(BF)
            probs[slot, start + 128 : start + 512, lanes] = jnp.exp(middle - top).astype(BF)
            probs[slot, start + 512 : start + 640, lanes] = jnp.exp(last - top).astype(BF)
            levels.append(top)
        probs[slot, :128, 128:] = jnp.zeros((128, 128), BF)
        probs[slot, 640:, :128] = jnp.zeros((128, 128), BF)
        tops.append(jnp.concatenate(levels, axis=1))
    ones = jnp.ones((16, fill.shape[0]), BF)
    for pair in range(2):
        halves = []
        for half in range(2):
            slot = pair * 2 + half
            lanes = slice(half * HEAD_WIDTH, (half + 1) * HEAD_WIDTH)
            values = jnp.concatenate([turned[pair][lanes], ones], axis=0)
            mixed = dot_nn(values, probs[slot])
            total = mixed[HEAD_WIDTH : HEAD_WIDTH + 1]
            inverse = 1.0 / total
            halves.append(mixed[:HEAD_WIDTH] * inverse)
            head = step * 4 + slot
            inverse_ref[pl.ds(head, 1), :] = inverse
            stat_rows[pl.ds(head, 1), :] = tops[slot] + jnp.log(total)
        start = pl.multiple_of(step * WIDTH + pair * PAIR, PAIR)
        attended_ref[:, pl.ds(start, PAIR)] = jnp.concatenate(halves, axis=0).T

    @pl.when(step == 3)
    def _():
        mixed = dot_nn(attended_ref[...].astype(BF), w_out_ref[...])
        hidden = (latent_ref[...].astype(F32) + mixed).astype(BF)
        hidden_ref[...] = hidden
        forecast_ref[...] = dot_nn(hidden, readout_ref[...])
        stat_rows[HEADS:] = jnp.zeros((128 - HEADS, BLOCK), F32)
        stats_ref[...] = stat_rows[...].T


def forward(counts, left, right, latent_own, w_qkv, projected, w_out, readout_weight):
    whole = lambda *shape: pl.BlockSpec(shape, lambda j: (0, 0))
    part = lambda rows, first: pl.BlockSpec((rows, WIDTH), lambda j: (0, first + j))
    window = 2 * WIN + BLOCK
    return pl.pallas_call(
        forward_kernel,
        grid=(4,),
        in_specs=[
            pl.BlockSpec(memory_space=pltpu.SMEM),
            whole(WIN, 1024),
            whole(WIN, 1024),
            whole(BLOCK, 1024),
            HBM,
            part(BLOCK, 0),
            part(BLOCK, 4),
            part(BLOCK, 8),
            whole(1024, 1024),
            whole(1024, 128),
        ],
        out_specs=[
            whole(2 * WIN, 1024),
            part(window, 0),
            part(window, 0),
            whole(BLOCK, 1024),
            whole(BLOCK, 128),
            whole(BLOCK, 1024),
            whole(BLOCK, 128),
            pl.BlockSpec((4, window, BLOCK), lambda j: (j, 0, 0)),
            whole(HEADS, BLOCK),
        ],
        out_shape=[
            jax.ShapeDtypeStruct((2 * WIN, 1024), BF),
            jax.ShapeDtypeStruct((window, 1024), BF),
            jax.ShapeDtypeStruct((window, 1024), BF),
            jax.ShapeDtypeStruct((BLOCK, 1024), F32),
            jax.ShapeDtypeStruct((BLOCK, 128), F32),
            jax.ShapeDtypeStruct((BLOCK, 1024), BF),
            jax.ShapeDtypeStruct((BLOCK, 128), F32),
            jax.ShapeDtypeStruct((HEADS, window, BLOCK), BF),
            jax.ShapeDtypeStruct((HEADS, BLOCK), F32),
        ],
        scratch_shapes=[
            pltpu.VMEM((128, BLOCK), F32),
            pltpu.VMEM((8, 1024, WIDTH), BF),
            pltpu.SemaphoreType.DMA((8,)),
        ],
        compiler_params=pltpu.CompilerParams(vmem_limit_bytes=30 * 1024 * 1024),
        cost_estimate=pl.CostEstimate(
            flops=6 << 30, bytes_accessed=12 << 20, transcendentals=3 << 20
        ),
    )(
        counts,
        left,
        right,
        latent_own,
        in_hbm(w_qkv),
        projected,
        projected,
        projected,
        w_out,
        readout_weight,
    )


def crps_kernel(counts_ref, own_ref, near_ref, third_ref, fourth_ref, target_ref, crps_ref):
    members = 4
    fair_eps = (1.0 - alpha_fair) / members
    coefficient = (1.0 - fair_eps) / (members * (members - 1))
    valid = (iota((BLOCK, 1), 0) < counts_ref[1]).astype(F32)
    forecasts = [own_ref[...], near_ref[...], third_ref[...], fourth_ref[...]]
    target = target_ref[...]
    error = jnp.zeros_like(target)
    for forecast in forecasts:
        error += smooth_abs(forecast - target)
    spread = jnp.full_like(target, members * smooth_width**0.5)
    for first in range(members):
        for second in range(first + 1, members):
            spread += 2.0 * smooth_abs(forecasts[first] - forecasts[second])
    crps_ref[...] = valid * (error / members - 0.5 * coefficient * spread)


def crps_of(counts, own, near, third, fourth, target):
    vmem = pl.BlockSpec(memory_space=pltpu.VMEM)
    return pl.pallas_call(
        crps_kernel,
        in_specs=[pl.BlockSpec(memory_space=pltpu.SMEM)] + [vmem] * 5,
        out_specs=vmem,
        out_shape=jax.ShapeDtypeStruct((BLOCK, 128), F32),
        compiler_params=pltpu.CompilerParams(vmem_limit_bytes=8 * 1024 * 1024),
        cost_estimate=FREE,
    )(counts, own, near, third, fourth, target)


def score_kernel(
    counts_ref,
    own_ref,
    near_ref,
    third_ref,
    fourth_ref,
    target_ref,
    attended_ref,
    hidden_ref,
    stats_ref,
    w_out_ref,
    readout_ref,
    packed_ref,
    sent_ref,
    grad_ref,
    small_ref,
):
    members = 4
    fair_eps = (1.0 - alpha_fair) / members
    coefficient = (1.0 - fair_eps) / (members * (members - 1))
    valid = (iota((BLOCK, 1), 0) < counts_ref[1]).astype(F32)
    own = own_ref[...]
    target = target_ref[...]
    pull = jnp.zeros_like(target)
    for other in (near_ref[...], third_ref[...], fourth_ref[...]):
        pull += smooth_sign(own - other)
    slope = (
        valid / 128 * (smooth_sign(own - target) / members - coefficient * pull)
    ).astype(BF)
    dhidden = dot_nt(slope, readout_ref[...]).astype(BF)
    dattended = dot_nt(dhidden, w_out_ref[...]).astype(BF)
    grad_ref[...] = dattended
    attended = attended_ref[...]
    product = dattended.astype(F32) * attended
    high = product.astype(BF)
    low = (product - high.astype(F32)).astype(BF)
    pick = (iota((1024, 128), 0) // HEAD_WIDTH + HEADS == iota((1024, 128), 1)).astype(BF)
    stats = stats_ref[...] + dot_nn(high, pick) + dot_nn(low, pick)
    first = stats.astype(BF)
    rest = stats - first.astype(F32)
    second = rest.astype(BF)
    third = (rest - second.astype(F32)).astype(BF)
    terms = jnp.zeros((BLOCK, 128), F32)
    for place, term in enumerate((first, second, third)):
        shift = (iota((128, 128), 0) + 32 * place == iota((128, 128), 1)) & (
            iota((128, 128), 0) < 32
        )
        terms += dot_nn(term, shift.astype(BF))
    packed_ref[:, :128] = slope
    packed_ref[:, 128:] = terms.astype(BF)
    sent_ref[...] = packed_ref[...]
    small_ref[:, :128] = dot_tn(attended.astype(BF), slope).astype(BF)
    small_ref[:, 128:] = dot_tn(hidden_ref[...], slope).astype(BF)


def score(
    counts, own, near, third, fourth, target, attended, hidden, stats, w_out, readout_weight
):
    vmem = pl.BlockSpec(memory_space=pltpu.VMEM)
    return pl.pallas_call(
        score_kernel,
        in_specs=[pl.BlockSpec(memory_space=pltpu.SMEM)] + [vmem] * 10,
        out_specs=[vmem] * 4,
        out_shape=[
            jax.ShapeDtypeStruct((BLOCK, 256), BF),
            pltpu.HBM((BLOCK, 256), BF),
            jax.ShapeDtypeStruct((BLOCK, 1024), BF),
            jax.ShapeDtypeStruct((1024, 256), BF),
        ],
        compiler_params=pltpu.CompilerParams(vmem_limit_bytes=12 * 1024 * 1024),
    )(
        counts,
        own,
        near,
        third,
        fourth,
        target,
        attended,
        hidden,
        stats,
        w_out,
        readout_weight,
    )


def query_kernel(
    kcat_ref, vcat_ref, grad_ref, packed_ref, probs_ref, inverse_ref, dq_ref, dscores
):
    step = pl.program_id(0)
    window = kcat_ref.shape[0]
    value_fill = (spare_lane((window, PAIR)) < 3).astype(BF)
    low_q = iota((BLOCK, PAIR), 1) < HEAD_WIDTH
    low_k = iota((window, PAIR), 1) < HEAD_WIDTH
    g_fill = dot_nn(packed_ref[:, 128:], stat_spread(step, HEADS)).astype(BF)
    turned = []
    for pair in range(2):
        columns = slice(pair * PAIR, (pair + 1) * PAIR)
        g_pair = grad_ref[:, columns]
        v_pair = vcat_ref[:, columns]
        k_turned = kcat_ref[:, columns].T
        for half in range(2):
            slot = pair * 2 + half
            pick_q = low_q if half == 0 else ~low_q
            pick_k = low_k if half == 0 else ~low_k
            g_head = jnp.where(pick_q, g_pair, g_fill[:, columns])
            v_head = jnp.where(pick_k, v_pair, value_fill)
            change = dot_nt(v_head, g_head)
            dscores[slot] = (probs_ref[slot].astype(F32) * change).astype(BF)
            turned.append(k_turned[half * HEAD_WIDTH : (half + 1) * HEAD_WIDTH])
    for slot in range(4):
        scale = inverse_ref[pl.ds(step * 4 + slot, 1), :] * HEAD_WIDTH ** (-0.5)
        dquery = dot_nn(turned[slot], dscores[slot]) * scale
        dq_ref[slot * HEAD_WIDTH : (slot + 1) * HEAD_WIDTH] = dquery.astype(BF)


def query_grads(kcat, vcat, grad, packed, probs, inverse):
    part = lambda rows, first: pl.BlockSpec((rows, WIDTH), lambda j: (0, first + j))
    window = 2 * WIN + BLOCK
    return pl.pallas_call(
        query_kernel,
        grid=(4,),
        in_specs=[
            part(window, 0),
            part(window, 0),
            part(BLOCK, 0),
            pl.BlockSpec((BLOCK, 256), lambda j: (0, 0)),
            pl.BlockSpec((4, window, BLOCK), lambda j: (j, 0, 0)),
            pl.BlockSpec((HEADS, BLOCK), lambda j: (0, 0)),
        ],
        out_specs=pl.BlockSpec((WIDTH, BLOCK), lambda j: (j, 0)),
        out_shape=jax.ShapeDtypeStruct((1024, BLOCK), BF),
        scratch_shapes=[pltpu.VMEM((4, window, BLOCK), BF)],
        compiler_params=pltpu.CompilerParams(vmem_limit_bytes=16 * 1024 * 1024),
        cost_estimate=pl.CostEstimate(
            flops=6 << 30, bytes_accessed=5 << 20, transcendentals=3 << 20
        ),
    )(kcat, vcat, grad, packed, probs, inverse)


def key_kernel(
    counts_ref,
    q_ref,
    k_ref,
    v_ref,
    qhalo_ref,
    grad_ref,
    own_ref,
    left_ref,
    right_ref,
    w_out_ref,
    readout_ref,
    out_ref,
    probs,
    dscores,
    dhidden,
):
    step = pl.program_id(0)

    @pl.when(step == 0)
    def _():
        probs[...] = jnp.zeros_like(probs)
        dscores[...] = jnp.zeros_like(dscores)
        dhidden[:WIN] = dot_nt(left_ref[:, :128], readout_ref[...]).astype(BF)
        dhidden[WIN:] = dot_nt(right_ref[:, :128], readout_ref[...]).astype(BF)

    ghalo = dot_nt(dhidden[...], w_out_ref[...]).astype(BF)
    terms = jnp.concatenate(
        [left_ref[:, 128:], own_ref[:, 128:], right_ref[:, 128:]], axis=0
    )
    window = terms.shape[0]
    fill = key_fill([(counts_ref[1], BLOCK)])
    value_fill = (spare_lane(fill.shape) < 3).astype(BF)
    low_q = iota((window, PAIR), 1) < HEAD_WIDTH
    low_k = iota(fill.shape, 1) < HEAD_WIDTH
    ones = (spare_lane((window, WIDTH)) == 3).astype(F32)
    q_fill = (dot_nn(terms, stat_spread(step, 0)) + ones).astype(BF)
    g_fill = dot_nn(terms, stat_spread(step, HEADS)).astype(BF)
    turned = []
    for pair in range(2):
        columns = slice(pair * PAIR, (pair + 1) * PAIR)
        q_pair = jnp.concatenate(
            [qhalo_ref[:WIN, columns], q_ref[:, columns], qhalo_ref[WIN:, columns]], axis=0
        ) * jnp.asarray(HEAD_WIDTH ** (-0.5), BF)
        g_pair = jnp.concatenate(
            [ghalo[:WIN, columns], grad_ref[:, columns], ghalo[WIN:, columns]], axis=0
        )
        k_pair = k_ref[:, columns]
        v_pair = v_ref[:, columns]
        q_turned = q_pair.T
        g_turned = g_pair.T
        for half in range(2):
            slot = pair * 2 + half
            pick_q = low_q if half == 0 else ~low_q
            pick_k = low_k if half == 0 else ~low_k
            q_head = jnp.where(pick_q, q_pair, q_fill[:, columns])
            g_head = jnp.where(pick_q, g_pair, g_fill[:, columns])
            k_head = jnp.where(pick_k, k_pair, fill)
            v_head = jnp.where(pick_k, v_pair, value_fill)
            scores = dot_nt(q_head, k_head)
            change = dot_nt(g_head, v_head)
            for tile in range(2):
                rows = slice(tile * 128, tile * 128 + 640)
                lanes = slice(tile * 128, tile * 128 + 128)
                weight = keep_band(jnp.exp(scores[rows, lanes]), 0.0)
                moved = change[rows, lanes]
                start = tile * 128
                for piece, (low, high) in zip(weight, ((0, 128), (128, 512), (512, 640))):
                    place = slice(start + low, start + high)
                    probs[slot, place, lanes] = piece.astype(BF)
                    dscores[slot, place, lanes] = (piece * moved[low:high]).astype(BF)
            lanes = slice(half * HEAD_WIDTH, (half + 1) * HEAD_WIDTH)
            turned.append((q_turned[lanes], g_turned[lanes]))
    for slot in range(4):
        place = slice(slot * HEAD_WIDTH, (slot + 1) * HEAD_WIDTH)
        out_ref[0, place] = dot_nn(turned[slot][0], dscores[slot]).astype(BF)
        out_ref[1, place] = dot_nn(turned[slot][1], probs[slot]).astype(BF)


def key_grads(counts, projected, qhalo, grad, own, left, right, w_out, readout_weight):
    part = lambda rows, first: pl.BlockSpec((rows, WIDTH), lambda j: (0, first + j))
    whole = lambda *shape: pl.BlockSpec(shape, lambda j: (0, 0))
    window = 2 * WIN + BLOCK
    return pl.pallas_call(
        key_kernel,
        grid=(4,),
        in_specs=[
            pl.BlockSpec(memory_space=pltpu.SMEM),
            part(BLOCK, 0),
            part(BLOCK, 4),
            part(BLOCK, 8),
            part(2 * WIN, 0),
            part(BLOCK, 0),
            whole(BLOCK, 256),
            whole(BLOCK, 256),
            whole(BLOCK, 256),
            pl.BlockSpec((WIDTH, 1024), lambda j: (j, 0)),
            whole(1024, 128),
        ],
        out_specs=pl.BlockSpec((2, WIDTH, BLOCK), lambda j: (0, j, 0)),
        out_shape=jax.ShapeDtypeStruct((2, 1024, BLOCK), BF),
        scratch_shapes=[
            pltpu.VMEM((4, window, BLOCK), BF),
            pltpu.VMEM((4, window, BLOCK), BF),
            pltpu.VMEM((2 * WIN, 1024), BF),
        ],
        compiler_params=pltpu.CompilerParams(vmem_limit_bytes=18 * 1024 * 1024),
        cost_estimate=FREE,
    )(
        counts,
        projected,
        projected,
        projected,
        qhalo,
        in_hbm(grad),
        own,
        in_hbm(left),
        in_hbm(right),
        in_hbm(w_out),
        readout_weight,
    )


AXES = ("x_hi", "core", "y", "x_lo", "z")
MEMBER = ("x_hi", "core")
CELLS = ("y", "x_lo", "z")
CHIPS = ("x_hi", "y", "x_lo", "z")
SWAP = [(0, 1), (1, 0)]


def swap_core(values):
    return lax.ppermute(values, "core", SWAP)


def scatter(partial):
    columns = partial.shape[1]
    return lax.all_to_all(partial.reshape(64, 8, columns), CHIPS, split_axis=0, concat_axis=0)


def add_up(pieces):
    return jnp.sum(pieces.astype(F32), axis=0)


def per_device(latent, counts, w_qkv, w_out, readout_weight, target):
    latent_own = latent[0]
    cell_count = 32
    cell_index = lax.axis_index(CELLS)
    member_index = lax.axis_index(MEMBER)
    core = lax.axis_index("core")
    up = [(i, i + 1) for i in range(cell_count - 1)]
    down = [(i + 1, i) for i in range(cell_count - 1)]
    from_left = lax.ppermute(latent_own, CELLS, up)
    from_right = lax.ppermute(latent_own, CELLS, down)

    own_count = counts[cell_index]
    left_count = jnp.where(cell_index > 0, counts[jnp.maximum(cell_index - 1, 0)], 0)
    right_count = jnp.where(
        cell_index < cell_count - 1, counts[jnp.minimum(cell_index + 1, cell_count - 1)], 0
    )
    scalars = jnp.stack([left_count, own_count, right_count])

    projected, turned = project(latent_own, w_qkv)
    turned_other = swap_core(turned)
    normed_halo, kcat, vcat, attended, stats, hidden, forecast, probs, inverse = forward(
        scalars, from_left, from_right, latent_own, w_qkv, projected, w_out, readout_weight
    )
    near = lax.ppermute(forecast, "x_hi", SWAP)
    third = swap_core(forecast)
    qhalo = halo_queries(normed_halo, w_qkv)
    near, third, qhalo = lax.optimization_barrier((near, third, qhalo))
    fourth = swap_core(near)
    packed, sent, grad, small = score(
        scalars,
        forecast,
        near,
        third,
        fourth,
        target,
        attended,
        hidden,
        stats,
        w_out,
        readout_weight,
    )
    packed_left = lax.ppermute(sent, CELLS, up)
    packed_right = lax.ppermute(sent, CELLS, down)

    dquery = query_grads(kcat, vcat, grad, packed, probs, inverse)
    dquery, packed_left, packed_right = lax.optimization_barrier(
        (dquery, packed_left, packed_right)
    )

    first_part = partial_sums(
        core, turned, turned_other, dquery, swap_core(dquery), (small, swap_core(small))
    )
    first_part, scalars = lax.optimization_barrier((first_part, scalars))
    first = scatter(first_part)
    pairs = key_grads(
        scalars,
        projected,
        qhalo,
        grad,
        packed,
        packed_left,
        packed_right,
        w_out,
        readout_weight,
    )
    pairs = pairs.reshape(2048, BLOCK)
    second_part = partial_sums(core, turned, turned_other, pairs, swap_core(pairs))
    second_part, first = lax.optimization_barrier((second_part, first))
    second_part, late_near = lax.optimization_barrier((second_part, near))
    second = add_up(scatter(second_part))
    crps_whole = crps_of(scalars, forecast, late_near, third, fourth, target)
    crps = lax.dynamic_slice_in_dim(crps_whole, member_index * 32, 32, 1)
    first = add_up(first)
    grad_out = lax.dot_general(
        first[:, 1024:1152],
        readout_weight.astype(F32),
        (((1,), (1,)), ((), ())),
        precision=lax.Precision.HIGHEST,
        preferred_element_type=F32,
    )
    grads = jnp.concatenate([first[:, :1024], second, grad_out, first[:, 1152:]], axis=1)
    return (crps, grads)


def solution(mesh):
    fine = jax.sharding.Mesh(mesh.devices.reshape(2, 2, 4, 2, 4), AXES)
    placed = (P(MEMBER, CELLS, None), P(), P(), P(), P(), P(CELLS, None))
    return jax.shard_map(
        per_device,
        mesh=fine,
        in_specs=placed,
        out_specs=(P(CELLS, MEMBER), P(MEMBER + CELLS, None)),
        check_vma=False,
    )
```

```python
import functools

import jax
import jax.numpy as jnp
import numpy as np
from jax import lax
from jax.experimental import pallas as pl
from jax.experimental.pallas import tpu as pltpu
from jax.sharding import PartitionSpec as P

HEADS = 16
WIN = 256
BLOCK = 256
WIDTH = 256
HEAD_WIDTH = 64
PAIR = 128
NEVER = -1e30

alpha_fair = 0.95
smooth_width = 0.0625

BF = jnp.bfloat16
F32 = jnp.float32


def smooth_abs(values):
    return jnp.sqrt(values * values + smooth_width)


def smooth_sign(values):
    return values * lax.rsqrt(values * values + smooth_width)


def layer_norm(latent_rows):
    values = latent_rows.astype(F32)
    center = values - jnp.mean(values, axis=-1, keepdims=True)
    spread = jnp.mean(center * center, axis=-1, keepdims=True)
    return (center * lax.rsqrt(spread + 1e-05)).astype(BF)


def dot_nn(left, right):
    return lax.dot_general(left, right, (((1,), (0,)), ((), ())), preferred_element_type=F32)


def dot_nt(left, right):
    return lax.dot_general(left, right, (((1,), (1,)), ((), ())), preferred_element_type=F32)


def dot_tn(left, right):
    return lax.dot_general(left, right, (((0,), (0,)), ((), ())), preferred_element_type=F32)


def iota(shape, axis):
    return lax.broadcasted_iota(jnp.int32, shape, axis)


FREE = pl.CostEstimate(flops=0, bytes_accessed=0, transcendentals=0)
HBM = pl.BlockSpec(memory_space=pltpu.HBM)


def in_hbm(values):
    return pltpu.with_memory_space_constraint(values, pltpu.HBM)


def fetches(weight_ref, buffer, arrived, width, first):
    return [
        pltpu.make_async_copy(
            weight_ref.at[:, pl.ds(first + place * width, width)],
            buffer.at[place],
            arrived.at[place],
        )
        for place in range(buffer.shape[0])
    ]


def fetch_one(weight_ref, buffer, arrived, width, first, place):
    start = pl.multiple_of(first + place * width, width)
    return pltpu.make_async_copy(
        weight_ref.at[:, pl.ds(start, width)], buffer.at[place], arrived.at[place]
    )


def project_kernel(latent_ref, weight_ref, projected_ref, turned_ref, normed, buffer, arrived):
    step = pl.program_id(0)

    @pl.when(step == 0)
    def _():
        for copy in fetches(weight_ref, buffer, arrived, 512, 0):
            copy.start()
        normed[...] = layer_norm(latent_ref[...])
        turned_ref[...] = normed[...].T

    fetch_one(weight_ref, buffer, arrived, 512, 0, step).wait()
    projected_ref[...] = dot_nn(normed[...], buffer[step]).astype(BF)


def project(latent_own, w_qkv):
    rows, width = latent_own.shape
    return pl.pallas_call(
        project_kernel,
        grid=(6,),
        in_specs=[pl.BlockSpec((rows, width), lambda j: (0, 0)), HBM],
        out_specs=[
            pl.BlockSpec((rows, 512), lambda j: (0, j)),
            pl.BlockSpec((width, rows), lambda j: (0, 0)),
        ],
        out_shape=[
            jax.ShapeDtypeStruct((rows, 3 * width), BF),
            jax.ShapeDtypeStruct((width, rows), BF),
        ],
        scratch_shapes=[
            pltpu.VMEM((rows, width), BF),
            pltpu.VMEM((6, width, 512), BF),
            pltpu.SemaphoreType.DMA((6,)),
        ],
        compiler_params=pltpu.CompilerParams(vmem_limit_bytes=16 * 1024 * 1024),
        cost_estimate=pl.CostEstimate(
            flops=2 * rows * width * width * 4, bytes_accessed=8 << 20, transcendentals=0
        ),
    )(latent_own, in_hbm(w_qkv))


def halo_query_kernel(normed_ref, weight_ref, out_ref, buffer, arrived):
    step = pl.program_id(0)

    @pl.when(step == 0)
    def _():
        for copy in fetches(weight_ref, buffer, arrived, 256, 0):
            copy.start()

    fetch_one(weight_ref, buffer, arrived, 256, 0, step).wait()
    out_ref[...] = dot_nn(normed_ref[...], buffer[step]).astype(BF)


def halo_queries(normed_halo, w_qkv):
    rows, width = normed_halo.shape
    return pl.pallas_call(
        halo_query_kernel,
        grid=(4,),
        in_specs=[pl.BlockSpec((rows, width), lambda j: (0, 0)), HBM],
        out_specs=pl.BlockSpec((rows, 256), lambda j: (0, j)),
        out_shape=jax.ShapeDtypeStruct((rows, width), BF),
        scratch_shapes=[
            pltpu.VMEM((4, width, 256), BF),
            pltpu.SemaphoreType.DMA((4,)),
        ],
        compiler_params=pltpu.CompilerParams(vmem_limit_bytes=12 * 1024 * 1024),
        cost_estimate=FREE,
    )(normed_halo, in_hbm(w_qkv))


def partial_kernel(
    smalls, core_ref, normed_ref, normed_other_ref, piece_ref, other_ref, *refs
):
    small_refs, (out_ref, rows, pieces, others, sums, staged, arrived, left) = (
        refs[:smalls],
        refs[smalls:],
    )
    core = core_ref[0]
    chunks = piece_ref.shape[0] // 512
    sources = [
        (normed_ref.at[:, core], rows.at[0]),
        (normed_other_ref.at[:, core], rows.at[1]),
    ]
    for chunk in range(chunks):
        part = pl.ds(chunk * 512, 512)
        sources.append((piece_ref.at[part], pieces.at[chunk]))
        sources.append((other_ref.at[part], others.at[chunk]))
    for place, small_ref in enumerate(small_refs):
        sources.append((small_ref.at[:, core], sums.at[place]))
    copies = [
        pltpu.make_async_copy(source, target, arrived.at[place])
        for place, (source, target) in enumerate(sources)
    ]
    for copy in copies:
        copy.start()
    copies[0].wait()
    copies[1].wait()
    writes = []
    for chunk in range(chunks):
        copies[2 + 2 * chunk].wait()
        copies[3 + 2 * chunk].wait()
        for top in range(2):
            staged[chunk, top * 256 : (top + 1) * 256] = (
                dot_nt(rows[0, top], pieces[chunk]) + dot_nt(rows[1, top], others[chunk])
            ).astype(BF)
        writes.append(
            pltpu.make_async_copy(
                staged.at[chunk], out_ref.at[:, pl.ds(chunk * 512, 512)], left.at[chunk]
            )
        )
        writes[-1].start()
    if smalls:
        copies[-2].wait()
        copies[-1].wait()
        for top in range(2):
            staged[chunks, top * 256 : (top + 1) * 256, :256] = (
                sums[0, top].astype(F32) + sums[1, top].astype(F32)
            ).astype(BF)
        writes.append(
            pltpu.make_async_copy(
                staged.at[chunks, :, pl.ds(0, 256)],
                out_ref.at[:, pl.ds(chunks * 512, 256)],
                left.at[chunks],
            )
        )
        writes[-1].start()
    for write in writes:
        write.wait()


def partial_sums(core, turned, turned_other, piece, other, smalls=()):
    by_core = lambda values: values.reshape(2, 2, 256, 256)
    anywhere = pl.BlockSpec(memory_space=pl.ANY)
    chunks = piece.shape[0] // 512
    columns = piece.shape[0] + 256 * (len(smalls) // 2)
    return pl.pallas_call(
        functools.partial(partial_kernel, len(smalls)),
        in_specs=[pl.BlockSpec(memory_space=pltpu.SMEM)] + [anywhere] * (4 + len(smalls)),
        out_specs=anywhere,
        out_shape=jax.ShapeDtypeStruct((512, columns), BF),
        scratch_shapes=[
            pltpu.VMEM((2, 2, 256, 256), BF),
            pltpu.VMEM((chunks, 512, 256), BF),
            pltpu.VMEM((chunks, 512, 256), BF),
            pltpu.VMEM((2, 2, 256, 256), BF),
            pltpu.VMEM((chunks + 1, 512, 512), BF),
            pltpu.SemaphoreType.DMA((2 + 2 * chunks + len(smalls),)),
            pltpu.SemaphoreType.DMA((chunks + 1,)),
        ],
        compiler_params=pltpu.CompilerParams(vmem_limit_bytes=14 * 1024 * 1024),
        cost_estimate=FREE,
    )(
        core.astype(jnp.int32).reshape(1),
        by_core(turned),
        by_core(turned_other),
        piece,
        other,
        *(by_core(small) for small in smalls),
    )


def spare_lane(shape):
    lane = iota(shape, len(shape) - 1)
    return lane % HEAD_WIDTH


def key_fill(count_pieces):
    fills = []
    for count, rows in count_pieces:
        spare = spare_lane((rows, PAIR))
        bias = jnp.where(iota((rows, PAIR), 0) < count, 0.0, NEVER)
        fills.append(
            jnp.where(spare < 3, 1.0, jnp.where(spare == 3, bias, 0.0)).astype(BF)
        )
    return jnp.concatenate(fills, axis=0)


def stat_spread(step, offset):
    shape = (128, WIDTH)
    lane = iota(shape, 1)
    head = step * 4 + 2 * (lane // PAIR) + jnp.where(lane % PAIR < HEAD_WIDTH, 1, 0)
    term = lane % HEAD_WIDTH
    chosen = (term < 3) & (iota(shape, 0) == term * 32 + offset + head)
    return jnp.where(chosen, -1.0, 0.0).astype(BF)


def keep_band(window, fill):
    shape = (128, 128)
    apart = iota(shape, 0) - iota(shape, 1)
    first = jnp.where(apart >= 0, window[:128], fill)
    last = jnp.where(apart <= 0, window[512:], fill)
    return first, window[128:512], last


def forward_kernel(
    counts_ref,
    left_ref,
    right_ref,
    latent_ref,
    weight_ref,
    q_ref,
    k_ref,
    v_ref,
    w_out_ref,
    readout_ref,
    normed_ref,
    kcat_ref,
    vcat_ref,
    attended_ref,
    stats_ref,
    hidden_ref,
    forecast_ref,
    probs,
    inverse_ref,
    stat_rows,
    buffer,
    arrived,
):
    step = pl.program_id(0)

    @pl.when(step == 0)
    def _():
        copies = fetches(weight_ref, buffer, arrived, WIDTH, 1024)
        for place in (0, 4, 1, 5, 2, 6, 3, 7):
            copies[place].start()
        normed_ref[:WIN] = layer_norm(left_ref[...])
        normed_ref[WIN:] = layer_norm(right_ref[...])

    fetch_one(weight_ref, buffer, arrived, WIDTH, 1024, step).wait()
    fetch_one(weight_ref, buffer, arrived, WIDTH, 1024, step + 4).wait()
    khalo = dot_nn(normed_ref[...], buffer[step]).astype(BF)
    kcat_ref[:WIN] = khalo[:WIN]
    kcat_ref[WIN : WIN + BLOCK] = k_ref[...]
    kcat_ref[WIN + BLOCK :] = khalo[WIN:]
    vhalo = dot_nn(normed_ref[...], buffer[step + 4]).astype(BF)
    vcat_ref[:WIN] = vhalo[:WIN]
    vcat_ref[WIN : WIN + BLOCK] = v_ref[...]
    vcat_ref[WIN + BLOCK :] = vhalo[WIN:]
    fill = key_fill([(counts_ref[0], WIN), (counts_ref[1], BLOCK), (counts_ref[2], WIN)])
    low_q = iota((BLOCK, PAIR), 1) < HEAD_WIDTH
    low_k = iota(fill.shape, 1) < HEAD_WIDTH
    query_fill = (spare_lane((BLOCK, PAIR)) == 3).astype(BF)
    scores, turned = [], []
    for pair in range(2):
        columns = slice(pair * PAIR, (pair + 1) * PAIR)
        q_pair = q_ref[:, columns] * jnp.asarray(HEAD_WIDTH ** (-0.5), BF)
        k_pair = kcat_ref[:, columns]
        turned.append(vcat_ref[:, columns].T)
        for half in range(2):
            if half == 0:
                q_head = jnp.where(low_q, q_pair, query_fill)
                k_head = jnp.where(low_k, k_pair, fill)
            else:
                q_head = jnp.where(low_q, query_fill, q_pair)
                k_head = jnp.where(low_k, fill, k_pair)
            scores.append(dot_nt(k_head, q_head))
    tops = []
    for slot in range(4):
        levels = []
        for tile in range(2):
            rows = slice(tile * 128, tile * 128 + 640)
            lanes = slice(tile * 128, tile * 128 + 128)
            first, middle, last = keep_band(scores[slot][rows, lanes], NEVER)
            top = jnp.maximum(
                jnp.max(middle, axis=0, keepdims=True),
                jnp.max(jnp.maximum(first, last), axis=0, keepdims=True),
            )
            start = tile * 128
            probs[slot, start : start + 128, lanes] = jnp.exp(first - top).astype(BF)
            probs[slot, start + 128 : start + 512, lanes] = jnp.exp(middle - top).astype(BF)
            probs[slot, start + 512 : start + 640, lanes] = jnp.exp(last - top).astype(BF)
            levels.append(top)
        probs[slot, :128, 128:] = jnp.zeros((128, 128), BF)
        probs[slot, 640:, :128] = jnp.zeros((128, 128), BF)
        tops.append(jnp.concatenate(levels, axis=1))
    ones = jnp.ones((16, fill.shape[0]), BF)
    for pair in range(2):
        halves = []
        for half in range(2):
            slot = pair * 2 + half
            lanes = slice(half * HEAD_WIDTH, (half + 1) * HEAD_WIDTH)
            values = jnp.concatenate([turned[pair][lanes], ones], axis=0)
            mixed = dot_nn(values, probs[slot])
            total = mixed[HEAD_WIDTH : HEAD_WIDTH + 1]
            inverse = 1.0 / total
            halves.append(mixed[:HEAD_WIDTH] * inverse)
            head = step * 4 + slot
            inverse_ref[pl.ds(head, 1), :] = inverse
            stat_rows[pl.ds(head, 1), :] = tops[slot] + jnp.log(total)
        start = pl.multiple_of(step * WIDTH + pair * PAIR, PAIR)
        attended_ref[:, pl.ds(start, PAIR)] = jnp.concatenate(halves, axis=0).T

    @pl.when(step == 3)
    def _():
        mixed = dot_nn(attended_ref[...].astype(BF), w_out_ref[...])
        hidden = (latent_ref[...].astype(F32) + mixed).astype(BF)
        hidden_ref[...] = hidden
        forecast_ref[...] = dot_nn(hidden, readout_ref[...])
        stat_rows[HEADS:] = jnp.zeros((128 - HEADS, BLOCK), F32)
        stats_ref[...] = stat_rows[...].T


def forward(counts, left, right, latent_own, w_qkv, projected, w_out, readout_weight):
    whole = lambda *shape: pl.BlockSpec(shape, lambda j: (0, 0))
    part = lambda rows, first: pl.BlockSpec((rows, WIDTH), lambda j: (0, first + j))
    window = 2 * WIN + BLOCK
    return pl.pallas_call(
        forward_kernel,
        grid=(4,),
        in_specs=[
            pl.BlockSpec(memory_space=pltpu.SMEM),
            whole(WIN, 1024),
            whole(WIN, 1024),
            whole(BLOCK, 1024),
            HBM,
            part(BLOCK, 0),
            part(BLOCK, 4),
            part(BLOCK, 8),
            whole(1024, 1024),
            whole(1024, 128),
        ],
        out_specs=[
            whole(2 * WIN, 1024),
            part(window, 0),
            part(window, 0),
            whole(BLOCK, 1024),
            whole(BLOCK, 128),
            whole(BLOCK, 1024),
            whole(BLOCK, 128),
            pl.BlockSpec((4, window, BLOCK), lambda j: (j, 0, 0)),
            whole(HEADS, BLOCK),
        ],
        out_shape=[
            jax.ShapeDtypeStruct((2 * WIN, 1024), BF),
            jax.ShapeDtypeStruct((window, 1024), BF),
            jax.ShapeDtypeStruct((window, 1024), BF),
            jax.ShapeDtypeStruct((BLOCK, 1024), F32),
            jax.ShapeDtypeStruct((BLOCK, 128), F32),
            jax.ShapeDtypeStruct((BLOCK, 1024), BF),
            jax.ShapeDtypeStruct((BLOCK, 128), F32),
            jax.ShapeDtypeStruct((HEADS, window, BLOCK), BF),
            jax.ShapeDtypeStruct((HEADS, BLOCK), F32),
        ],
        scratch_shapes=[
            pltpu.VMEM((128, BLOCK), F32),
            pltpu.VMEM((8, 1024, WIDTH), BF),
            pltpu.SemaphoreType.DMA((8,)),
        ],
        compiler_params=pltpu.CompilerParams(vmem_limit_bytes=30 * 1024 * 1024),
        cost_estimate=pl.CostEstimate(
            flops=6 << 30, bytes_accessed=12 << 20, transcendentals=3 << 20
        ),
    )(
        counts,
        left,
        right,
        latent_own,
        in_hbm(w_qkv),
        projected,
        projected,
        projected,
        w_out,
        readout_weight,
    )


def score_kernel(
    counts_ref,
    own_ref,
    near_ref,
    others_ref,
    target_ref,
    attended_ref,
    hidden_ref,
    stats_ref,
    w_out_ref,
    readout_ref,
    crps_ref,
    packed_ref,
    sent_ref,
    grad_ref,
    small_ref,
):
    members = 4
    fair_eps = (1.0 - alpha_fair) / members
    coefficient = (1.0 - fair_eps) / (members * (members - 1))
    valid = (iota((BLOCK, 1), 0) < counts_ref[1]).astype(F32)
    own = own_ref[...]
    forecasts = [own, near_ref[...], others_ref[0], others_ref[1]]
    target = target_ref[...]
    error = jnp.zeros_like(target)
    for forecast in forecasts:
        error += smooth_abs(forecast - target)
    spread = jnp.full_like(target, members * smooth_width**0.5)
    for first in range(members):
        for second in range(first + 1, members):
            spread += 2.0 * smooth_abs(forecasts[first] - forecasts[second])
    crps_ref[...] = valid * (error / members - 0.5 * coefficient * spread)
    pull = jnp.zeros_like(target)
    for other in forecasts[1:]:
        pull += smooth_sign(own - other)
    slope = (
        valid / 128 * (smooth_sign(own - target) / members - coefficient * pull)
    ).astype(BF)
    dhidden = dot_nt(slope, readout_ref[...]).astype(BF)
    dattended = dot_nt(dhidden, w_out_ref[...]).astype(BF)
    grad_ref[...] = dattended
    attended = attended_ref[...]
    product = dattended.astype(F32) * attended
    high = product.astype(BF)
    low = (product - high.astype(F32)).astype(BF)
    pick = (iota((1024, 128), 0) // HEAD_WIDTH + HEADS == iota((1024, 128), 1)).astype(BF)
    stats = stats_ref[...] + dot_nn(high, pick) + dot_nn(low, pick)
    first = stats.astype(BF)
    rest = stats - first.astype(F32)
    second = rest.astype(BF)
    third = (rest - second.astype(F32)).astype(BF)
    terms = jnp.zeros((BLOCK, 128), F32)
    for place, term in enumerate((first, second, third)):
        shift = (iota((128, 128), 0) + 32 * place == iota((128, 128), 1)) & (
            iota((128, 128), 0) < 32
        )
        terms += dot_nn(term, shift.astype(BF))
    packed_ref[:, :128] = slope
    packed_ref[:, 128:] = terms.astype(BF)
    sent_ref[...] = packed_ref[...]
    small_ref[:, :128] = dot_tn(attended.astype(BF), slope).astype(BF)
    small_ref[:, 128:] = dot_tn(hidden_ref[...], slope).astype(BF)


def score(counts, own, near, others, target, attended, hidden, stats, w_out, readout_weight):
    vmem = pl.BlockSpec(memory_space=pltpu.VMEM)
    return pl.pallas_call(
        score_kernel,
        in_specs=[pl.BlockSpec(memory_space=pltpu.SMEM)] + [vmem] * 9,
        out_specs=[vmem] * 5,
        out_shape=[
            pltpu.HBM((BLOCK, 128), F32),
            jax.ShapeDtypeStruct((BLOCK, 256), BF),
            pltpu.HBM((BLOCK, 256), BF),
            jax.ShapeDtypeStruct((BLOCK, 1024), BF),
            jax.ShapeDtypeStruct((1024, 256), BF),
        ],
        compiler_params=pltpu.CompilerParams(vmem_limit_bytes=12 * 1024 * 1024),
    )(counts, own, near, others, target, attended, hidden, stats, w_out, readout_weight)


def query_kernel(
    kcat_ref, vcat_ref, grad_ref, packed_ref, probs_ref, inverse_ref, dq_ref, dscores
):
    step = pl.program_id(0)
    window = kcat_ref.shape[0]
    value_fill = (spare_lane((window, PAIR)) < 3).astype(BF)
    low_q = iota((BLOCK, PAIR), 1) < HEAD_WIDTH
    low_k = iota((window, PAIR), 1) < HEAD_WIDTH
    g_fill = dot_nn(packed_ref[:, 128:], stat_spread(step, HEADS)).astype(BF)
    turned = []
    for pair in range(2):
        columns = slice(pair * PAIR, (pair + 1) * PAIR)
        g_pair = grad_ref[:, columns]
        v_pair = vcat_ref[:, columns]
        k_turned = kcat_ref[:, columns].T
        for half in range(2):
            slot = pair * 2 + half
            pick_q = low_q if half == 0 else ~low_q
            pick_k = low_k if half == 0 else ~low_k
            g_head = jnp.where(pick_q, g_pair, g_fill[:, columns])
            v_head = jnp.where(pick_k, v_pair, value_fill)
            change = dot_nt(v_head, g_head)
            dscores[slot] = (probs_ref[slot].astype(F32) * change).astype(BF)
            turned.append(k_turned[half * HEAD_WIDTH : (half + 1) * HEAD_WIDTH])
    for slot in range(4):
        scale = inverse_ref[pl.ds(step * 4 + slot, 1), :] * HEAD_WIDTH ** (-0.5)
        dquery = dot_nn(turned[slot], dscores[slot]) * scale
        dq_ref[slot * HEAD_WIDTH : (slot + 1) * HEAD_WIDTH] = dquery.astype(BF)


def query_grads(kcat, vcat, grad, packed, probs, inverse):
    part = lambda rows, first: pl.BlockSpec((rows, WIDTH), lambda j: (0, first + j))
    window = 2 * WIN + BLOCK
    return pl.pallas_call(
        query_kernel,
        grid=(4,),
        in_specs=[
            part(window, 0),
            part(window, 0),
            part(BLOCK, 0),
            pl.BlockSpec((BLOCK, 256), lambda j: (0, 0)),
            pl.BlockSpec((4, window, BLOCK), lambda j: (j, 0, 0)),
            pl.BlockSpec((HEADS, BLOCK), lambda j: (0, 0)),
        ],
        out_specs=pl.BlockSpec((WIDTH, BLOCK), lambda j: (j, 0)),
        out_shape=jax.ShapeDtypeStruct((1024, BLOCK), BF),
        scratch_shapes=[pltpu.VMEM((4, window, BLOCK), BF)],
        compiler_params=pltpu.CompilerParams(vmem_limit_bytes=16 * 1024 * 1024),
        cost_estimate=pl.CostEstimate(
            flops=6 << 30, bytes_accessed=5 << 20, transcendentals=3 << 20
        ),
    )(kcat, vcat, grad, packed, probs, inverse)


def key_kernel(
    counts_ref,
    q_ref,
    k_ref,
    v_ref,
    qhalo_ref,
    grad_ref,
    own_ref,
    left_ref,
    right_ref,
    w_out_ref,
    readout_ref,
    out_ref,
    probs,
    dscores,
    dhidden,
    sides,
    arrived,
):
    step = pl.program_id(0)

    @pl.when(step == 0)
    def _():
        copies = [
            pltpu.make_async_copy(side_ref, sides.at[place], arrived.at[place])
            for place, side_ref in enumerate((left_ref, right_ref))
        ]
        for copy in copies:
            copy.start()
        for slot in range(4):
            for held in (probs, dscores):
                held[slot, :128, 128:] = jnp.zeros((128, 128), BF)
                held[slot, 640:, :128] = jnp.zeros((128, 128), BF)
        for place, copy in enumerate(copies):
            copy.wait()
            rows = slice(place * WIN, (place + 1) * WIN)
            dhidden[rows] = dot_nt(sides[place, :, :128], readout_ref[...]).astype(BF)

    ghalo = dot_nt(dhidden[...], w_out_ref[...]).astype(BF)
    terms = jnp.concatenate(
        [sides[0, :, 128:], own_ref[:, 128:], sides[1, :, 128:]], axis=0
    )
    window = terms.shape[0]
    fill = key_fill([(counts_ref[1], BLOCK)])
    value_fill = (spare_lane(fill.shape) < 3).astype(BF)
    low_q = iota((window, PAIR), 1) < HEAD_WIDTH
    low_k = iota(fill.shape, 1) < HEAD_WIDTH
    ones = (spare_lane((window, WIDTH)) == 3).astype(F32)
    q_fill = (dot_nn(terms, stat_spread(step, 0)) + ones).astype(BF)
    g_fill = dot_nn(terms, stat_spread(step, HEADS)).astype(BF)
    turned = []
    for pair in range(2):
        columns = slice(pair * PAIR, (pair + 1) * PAIR)
        q_pair = jnp.concatenate(
            [qhalo_ref[:WIN, columns], q_ref[:, columns], qhalo_ref[WIN:, columns]], axis=0
        ) * jnp.asarray(HEAD_WIDTH ** (-0.5), BF)
        g_pair = jnp.concatenate(
            [ghalo[:WIN, columns], grad_ref[:, columns], ghalo[WIN:, columns]], axis=0
        )
        k_pair = k_ref[:, columns]
        v_pair = v_ref[:, columns]
        q_turned = q_pair.T
        g_turned = g_pair.T
        for half in range(2):
            slot = pair * 2 + half
            pick_q = low_q if half == 0 else ~low_q
            pick_k = low_k if half == 0 else ~low_k
            q_head = jnp.where(pick_q, q_pair, q_fill[:, columns])
            g_head = jnp.where(pick_q, g_pair, g_fill[:, columns])
            k_head = jnp.where(pick_k, k_pair, fill)
            v_head = jnp.where(pick_k, v_pair, value_fill)
            scores = dot_nt(q_head, k_head)
            change = dot_nt(g_head, v_head)
            for tile in range(2):
                rows = slice(tile * 128, tile * 128 + 640)
                lanes = slice(tile * 128, tile * 128 + 128)
                weight = keep_band(jnp.exp(scores[rows, lanes]), 0.0)
                moved = change[rows, lanes]
                start = tile * 128
                for piece, (low, high) in zip(weight, ((0, 128), (128, 512), (512, 640))):
                    place = slice(start + low, start + high)
                    probs[slot, place, lanes] = piece.astype(BF)
                    dscores[slot, place, lanes] = (piece * moved[low:high]).astype(BF)
            lanes = slice(half * HEAD_WIDTH, (half + 1) * HEAD_WIDTH)
            turned.append((q_turned[lanes], g_turned[lanes]))
    for slot in range(4):
        place = slice(slot * HEAD_WIDTH, (slot + 1) * HEAD_WIDTH)
        out_ref[0, place] = dot_nn(turned[slot][0], dscores[slot]).astype(BF)
        out_ref[1, place] = dot_nn(turned[slot][1], probs[slot]).astype(BF)


def key_grads(counts, projected, qhalo, grad, own, left, right, w_out, readout_weight):
    part = lambda rows, first: pl.BlockSpec((rows, WIDTH), lambda j: (0, first + j))
    whole = lambda *shape: pl.BlockSpec(shape, lambda j: (0, 0))
    window = 2 * WIN + BLOCK
    return pl.pallas_call(
        key_kernel,
        grid=(4,),
        in_specs=[
            pl.BlockSpec(memory_space=pltpu.SMEM),
            part(BLOCK, 0),
            part(BLOCK, 4),
            part(BLOCK, 8),
            part(2 * WIN, 0),
            part(BLOCK, 0),
            whole(BLOCK, 256),
            pl.BlockSpec(memory_space=pl.ANY),
            pl.BlockSpec(memory_space=pl.ANY),
            pl.BlockSpec((WIDTH, 1024), lambda j: (j, 0)),
            whole(1024, 128),
        ],
        out_specs=pl.BlockSpec((2, WIDTH, BLOCK), lambda j: (0, j, 0)),
        out_shape=jax.ShapeDtypeStruct((2, 1024, BLOCK), BF),
        scratch_shapes=[
            pltpu.VMEM((4, window, BLOCK), BF),
            pltpu.VMEM((4, window, BLOCK), BF),
            pltpu.VMEM((2 * WIN, 1024), BF),
            pltpu.VMEM((2, WIN, 256), BF),
            pltpu.SemaphoreType.DMA((2,)),
        ],
        compiler_params=pltpu.CompilerParams(vmem_limit_bytes=18 * 1024 * 1024),
        cost_estimate=FREE,
    )(
        counts,
        projected,
        projected,
        projected,
        qhalo,
        in_hbm(grad),
        own,
        left,
        right,
        in_hbm(w_out),
        readout_weight,
    )


AXES = ("x_hi", "core", "y", "x_lo", "z")
MEMBER = ("x_hi", "core")
CELLS = ("y", "x_lo", "z")
CHIPS = ("x_hi", "y", "x_lo", "z")
SWAP = [(0, 1), (1, 0)]


def swap_core(values):
    return lax.ppermute(values, "core", SWAP)


def scatter(partial):
    columns = partial.shape[1]
    return lax.all_to_all(partial.reshape(64, 8, columns), CHIPS, split_axis=0, concat_axis=0)


def add_up(pieces):
    return jnp.sum(pieces.astype(F32), axis=0)


def per_device(latent, counts, w_qkv, w_out, readout_weight, target):
    latent_own = latent[0]
    cell_count = 32
    cell_index = lax.axis_index(CELLS)
    member_index = lax.axis_index(MEMBER)
    core = lax.axis_index("core")
    up = [(i, i + 1) for i in range(cell_count - 1)]
    down = [(i + 1, i) for i in range(cell_count - 1)]
    from_left = lax.ppermute(latent_own, CELLS, up)
    from_right = lax.ppermute(latent_own, CELLS, down)

    own_count = counts[cell_index]
    left_count = jnp.where(cell_index > 0, counts[jnp.maximum(cell_index - 1, 0)], 0)
    right_count = jnp.where(
        cell_index < cell_count - 1, counts[jnp.minimum(cell_index + 1, cell_count - 1)], 0
    )
    scalars = jnp.stack([left_count, own_count, right_count])

    projected, turned = project(latent_own, w_qkv)
    turned_other = swap_core(turned)
    normed_halo, kcat, vcat, attended, stats, hidden, forecast, probs, inverse = forward(
        scalars, from_left, from_right, latent_own, w_qkv, projected, w_out, readout_weight
    )
    near = lax.ppermute(forecast, "x_hi", SWAP)
    qhalo = halo_queries(normed_halo, w_qkv)
    near, qhalo = lax.optimization_barrier((near, qhalo))
    others = swap_core(jnp.stack([forecast, near]))
    crps_whole, packed, sent, grad, small = score(
        scalars, forecast, near, others, target, attended, hidden, stats, w_out, readout_weight
    )
    crps = lax.dynamic_slice_in_dim(crps_whole, member_index * 32, 32, 1)
    packed_left = lax.ppermute(sent, CELLS, up)
    packed_right = lax.ppermute(sent, CELLS, down)

    dquery = query_grads(kcat, vcat, grad, packed, probs, inverse)
    dquery, packed_left, packed_right = lax.optimization_barrier(
        (dquery, packed_left, packed_right)
    )

    first_part = partial_sums(
        core, turned, turned_other, dquery, swap_core(dquery), (small, swap_core(small))
    )
    first_part, scalars = lax.optimization_barrier((first_part, scalars))
    first = scatter(first_part)
    pairs = key_grads(
        scalars,
        projected,
        qhalo,
        grad,
        packed,
        packed_left,
        packed_right,
        w_out,
        readout_weight,
    )
    pairs = pairs.reshape(2048, BLOCK)
    second_part = partial_sums(core, turned, turned_other, pairs, swap_core(pairs))
    second_part, first = lax.optimization_barrier((second_part, first))
    second = add_up(scatter(second_part))
    first = add_up(first)
    grad_out = lax.dot_general(
        first[:, 1024:1152],
        readout_weight.astype(F32),
        (((1,), (1,)), ((), ())),
        precision=lax.Precision.HIGHEST,
        preferred_element_type=F32,
    )
    grads = jnp.concatenate([first[:, :1024], second, grad_out, first[:, 1152:]], axis=1)
    return (crps, grads)


def solution(mesh):
    fine = jax.sharding.Mesh(mesh.devices.reshape(2, 2, 4, 2, 4), AXES)
    placed = (P(MEMBER, CELLS, None), P(), P(), P(), P(), P(CELLS, None))
    return jax.shard_map(
        per_device,
        mesh=fine,
        in_specs=placed,
        out_specs=(P(CELLS, MEMBER), P(MEMBER + CELLS, None)),
        check_vma=False,
    )
```

```python
import functools

import jax
import jax.numpy as jnp
import numpy as np
from jax import lax
from jax.experimental import pallas as pl
from jax.experimental.pallas import tpu as pltpu
from jax.sharding import PartitionSpec as P

HEADS = 16
WIN = 256
BLOCK = 256
WIDTH = 256
HEAD_WIDTH = 64
PAIR = 128
NEVER = -1e30

alpha_fair = 0.95
smooth_width = 0.0625

BF = jnp.bfloat16
F32 = jnp.float32


def smooth_abs(values):
    return jnp.sqrt(values * values + smooth_width)


def smooth_sign(values):
    return values * lax.rsqrt(values * values + smooth_width)


def layer_norm(latent_rows):
    values = latent_rows.astype(F32)
    center = values - jnp.mean(values, axis=-1, keepdims=True)
    spread = jnp.mean(center * center, axis=-1, keepdims=True)
    return (center * lax.rsqrt(spread + 1e-05)).astype(BF)


def dot_nn(left, right):
    return lax.dot_general(left, right, (((1,), (0,)), ((), ())), preferred_element_type=F32)


def dot_nt(left, right):
    return lax.dot_general(left, right, (((1,), (1,)), ((), ())), preferred_element_type=F32)


def dot_tn(left, right):
    return lax.dot_general(left, right, (((0,), (0,)), ((), ())), preferred_element_type=F32)


def iota(shape, axis):
    return lax.broadcasted_iota(jnp.int32, shape, axis)


FREE = pl.CostEstimate(flops=0, bytes_accessed=0, transcendentals=0)
HBM = pl.BlockSpec(memory_space=pltpu.HBM)


def in_hbm(values):
    return pltpu.with_memory_space_constraint(values, pltpu.HBM)


def fetches(weight_ref, buffer, arrived, width, first):
    return [
        pltpu.make_async_copy(
            weight_ref.at[:, pl.ds(first + place * width, width)],
            buffer.at[place],
            arrived.at[place],
        )
        for place in range(buffer.shape[0])
    ]


def fetch_one(weight_ref, buffer, arrived, width, first, place):
    start = pl.multiple_of(first + place * width, width)
    return pltpu.make_async_copy(
        weight_ref.at[:, pl.ds(start, width)], buffer.at[place], arrived.at[place]
    )


def project_kernel(latent_ref, weight_ref, projected_ref, turned_ref, normed, buffer, arrived):
    step = pl.program_id(0)

    @pl.when(step == 0)
    def _():
        for copy in fetches(weight_ref, buffer, arrived, 512, 0):
            copy.start()
        normed[...] = layer_norm(latent_ref[...])
        turned_ref[...] = normed[...].T

    fetch_one(weight_ref, buffer, arrived, 512, 0, step).wait()
    projected_ref[...] = dot_nn(normed[...], buffer[step]).astype(BF)


def project(latent_own, w_qkv):
    rows, width = latent_own.shape
    return pl.pallas_call(
        project_kernel,
        grid=(6,),
        in_specs=[pl.BlockSpec((rows, width), lambda j: (0, 0)), HBM],
        out_specs=[
            pl.BlockSpec((rows, 512), lambda j: (0, j)),
            pl.BlockSpec((width, rows), lambda j: (0, 0)),
        ],
        out_shape=[
            jax.ShapeDtypeStruct((rows, 3 * width), BF),
            jax.ShapeDtypeStruct((width, rows), BF),
        ],
        scratch_shapes=[
            pltpu.VMEM((rows, width), BF),
            pltpu.VMEM((6, width, 512), BF),
            pltpu.SemaphoreType.DMA((6,)),
        ],
        compiler_params=pltpu.CompilerParams(vmem_limit_bytes=16 * 1024 * 1024),
        cost_estimate=pl.CostEstimate(
            flops=2 * rows * width * width * 4, bytes_accessed=8 << 20, transcendentals=0
        ),
    )(latent_own, in_hbm(w_qkv))


def halo_query_kernel(normed_ref, weight_ref, out_ref, buffer, arrived):
    step = pl.program_id(0)

    @pl.when(step == 0)
    def _():
        for copy in fetches(weight_ref, buffer, arrived, 256, 0):
            copy.start()

    fetch_one(weight_ref, buffer, arrived, 256, 0, step).wait()
    out_ref[...] = dot_nn(normed_ref[...], buffer[step]).astype(BF)


def halo_queries(normed_halo, w_qkv):
    rows, width = normed_halo.shape
    return pl.pallas_call(
        halo_query_kernel,
        grid=(4,),
        in_specs=[pl.BlockSpec((rows, width), lambda j: (0, 0)), HBM],
        out_specs=pl.BlockSpec((rows, 256), lambda j: (0, j)),
        out_shape=jax.ShapeDtypeStruct((rows, width), BF),
        scratch_shapes=[
            pltpu.VMEM((4, width, 256), BF),
            pltpu.SemaphoreType.DMA((4,)),
        ],
        compiler_params=pltpu.CompilerParams(vmem_limit_bytes=12 * 1024 * 1024),
        cost_estimate=FREE,
    )(normed_halo, in_hbm(w_qkv))


def partial_kernel(
    smalls, passed, core_ref, normed_ref, normed_other_ref, piece_ref, other_ref, *refs
):
    small_refs, side_refs, out_ref = refs[:smalls], refs[smalls : smalls + passed], None
    refs = refs[smalls + passed :]
    if passed:
        out_ref, sides_ref, rows, pieces, others, sums, staged, arrived, left, moved = refs
    else:
        out_ref, rows, pieces, others, sums, staged, arrived, left, moved = refs
    core = core_ref[0]
    chunks = piece_ref.shape[0] // 512
    sources = [
        (normed_ref.at[:, core], rows.at[0]),
        (normed_other_ref.at[:, core], rows.at[1]),
    ]
    for chunk in range(chunks):
        part = pl.ds(chunk * 512, 512)
        sources.append((piece_ref.at[part], pieces.at[chunk]))
        sources.append((other_ref.at[part], others.at[chunk]))
    for place, small_ref in enumerate(small_refs):
        sources.append((small_ref.at[:, core], sums.at[place]))
    copies = [
        pltpu.make_async_copy(source, target, arrived.at[place])
        for place, (source, target) in enumerate(sources)
    ]
    for copy in copies:
        copy.start()
    writes = []
    for place, side_ref in enumerate(side_refs):
        writes.append(pltpu.make_async_copy(side_ref, sides_ref.at[place], moved.at[place]))
        writes[-1].start()
    copies[0].wait()
    copies[1].wait()
    for chunk in range(chunks):
        copies[2 + 2 * chunk].wait()
        copies[3 + 2 * chunk].wait()
        for top in range(2):
            staged[chunk, top * 256 : (top + 1) * 256] = (
                dot_nt(rows[0, top], pieces[chunk]) + dot_nt(rows[1, top], others[chunk])
            ).astype(BF)
        writes.append(
            pltpu.make_async_copy(
                staged.at[chunk], out_ref.at[:, pl.ds(chunk * 512, 512)], left.at[chunk]
            )
        )
        writes[-1].start()
    if smalls:
        copies[-2].wait()
        copies[-1].wait()
        for top in range(2):
            staged[chunks, top * 256 : (top + 1) * 256, :256] = (
                sums[0, top].astype(F32) + sums[1, top].astype(F32)
            ).astype(BF)
        writes.append(
            pltpu.make_async_copy(
                staged.at[chunks, :, pl.ds(0, 256)],
                out_ref.at[:, pl.ds(chunks * 512, 256)],
                left.at[chunks],
            )
        )
        writes[-1].start()
    for write in writes:
        write.wait()


def partial_sums(core, turned, turned_other, piece, other, smalls=(), sides=()):
    by_core = lambda values: values.reshape(2, 2, 256, 256)
    anywhere = pl.BlockSpec(memory_space=pl.ANY)
    chunks = piece.shape[0] // 512
    columns = piece.shape[0] + 256 * (len(smalls) // 2)
    return pl.pallas_call(
        functools.partial(partial_kernel, len(smalls), len(sides)),
        in_specs=[pl.BlockSpec(memory_space=pltpu.SMEM)]
        + [anywhere] * (4 + len(smalls) + len(sides)),
        out_specs=[anywhere, HBM] if sides else anywhere,
        out_shape=(
            [jax.ShapeDtypeStruct((512, columns), BF), pltpu.HBM((2, WIN, 256), BF)]
            if sides
            else jax.ShapeDtypeStruct((512, columns), BF)
        ),
        scratch_shapes=[
            pltpu.VMEM((2, 2, 256, 256), BF),
            pltpu.VMEM((chunks, 512, 256), BF),
            pltpu.VMEM((chunks, 512, 256), BF),
            pltpu.VMEM((2, 2, 256, 256), BF),
            pltpu.VMEM((chunks + 1, 512, 512), BF),
            pltpu.SemaphoreType.DMA((2 + 2 * chunks + len(smalls),)),
            pltpu.SemaphoreType.DMA((chunks + 1,)),
            pltpu.SemaphoreType.DMA((2,)),
        ],
        compiler_params=pltpu.CompilerParams(vmem_limit_bytes=14 * 1024 * 1024),
        cost_estimate=FREE,
    )(
        core.astype(jnp.int32).reshape(1),
        by_core(turned),
        by_core(turned_other),
        piece,
        other,
        *(by_core(small) for small in smalls),
        *sides,
    )


def spare_lane(shape):
    lane = iota(shape, len(shape) - 1)
    return lane % HEAD_WIDTH


def key_fill(count_pieces):
    fills = []
    for count, rows in count_pieces:
        spare = spare_lane((rows, PAIR))
        bias = jnp.where(iota((rows, PAIR), 0) < count, 0.0, NEVER)
        fills.append(
            jnp.where(spare < 3, 1.0, jnp.where(spare == 3, bias, 0.0)).astype(BF)
        )
    return jnp.concatenate(fills, axis=0)


def stat_spread(step, offset):
    shape = (128, WIDTH)
    lane = iota(shape, 1)
    head = step * 4 + 2 * (lane // PAIR) + jnp.where(lane % PAIR < HEAD_WIDTH, 1, 0)
    term = lane % HEAD_WIDTH
    chosen = (term < 3) & (iota(shape, 0) == term * 32 + offset + head)
    return jnp.where(chosen, -1.0, 0.0).astype(BF)


def keep_band(window, fill):
    shape = (128, 128)
    apart = iota(shape, 0) - iota(shape, 1)
    first = jnp.where(apart >= 0, window[:128], fill)
    last = jnp.where(apart <= 0, window[512:], fill)
    return first, window[128:512], last


def forward_kernel(
    counts_ref,
    left_ref,
    right_ref,
    latent_ref,
    weight_ref,
    q_ref,
    k_ref,
    v_ref,
    w_out_ref,
    readout_ref,
    normed_ref,
    kcat_ref,
    vcat_ref,
    attended_ref,
    stats_ref,
    hidden_ref,
    forecast_ref,
    probs,
    inverse_ref,
    stat_rows,
    buffer,
    arrived,
):
    step = pl.program_id(0)

    @pl.when(step == 0)
    def _():
        copies = fetches(weight_ref, buffer, arrived, WIDTH, 1024)
        for place in (0, 4, 1, 5, 2, 6, 3, 7):
            copies[place].start()
        normed_ref[:WIN] = layer_norm(left_ref[...])
        normed_ref[WIN:] = layer_norm(right_ref[...])

    fetch_one(weight_ref, buffer, arrived, WIDTH, 1024, step).wait()
    fetch_one(weight_ref, buffer, arrived, WIDTH, 1024, step + 4).wait()
    khalo = dot_nn(normed_ref[...], buffer[step]).astype(BF)
    kcat_ref[:WIN] = khalo[:WIN]
    kcat_ref[WIN : WIN + BLOCK] = k_ref[...]
    kcat_ref[WIN + BLOCK :] = khalo[WIN:]
    vhalo = dot_nn(normed_ref[...], buffer[step + 4]).astype(BF)
    vcat_ref[:WIN] = vhalo[:WIN]
    vcat_ref[WIN : WIN + BLOCK] = v_ref[...]
    vcat_ref[WIN + BLOCK :] = vhalo[WIN:]
    fill = key_fill([(counts_ref[0], WIN), (counts_ref[1], BLOCK), (counts_ref[2], WIN)])
    low_q = iota((BLOCK, PAIR), 1) < HEAD_WIDTH
    low_k = iota(fill.shape, 1) < HEAD_WIDTH
    query_fill = (spare_lane((BLOCK, PAIR)) == 3).astype(BF)
    scores, turned = [], []
    for pair in range(2):
        columns = slice(pair * PAIR, (pair + 1) * PAIR)
        q_pair = q_ref[:, columns] * jnp.asarray(HEAD_WIDTH ** (-0.5), BF)
        k_pair = kcat_ref[:, columns]
        turned.append(vcat_ref[:, columns].T)
        for half in range(2):
            if half == 0:
                q_head = jnp.where(low_q, q_pair, query_fill)
                k_head = jnp.where(low_k, k_pair, fill)
            else:
                q_head = jnp.where(low_q, query_fill, q_pair)
                k_head = jnp.where(low_k, fill, k_pair)
            scores.append(dot_nt(k_head, q_head))
    tops = []
    for slot in range(4):
        levels = []
        for tile in range(2):
            rows = slice(tile * 128, tile * 128 + 640)
            lanes = slice(tile * 128, tile * 128 + 128)
            first, middle, last = keep_band(scores[slot][rows, lanes], NEVER)
            top = jnp.maximum(
                jnp.max(middle, axis=0, keepdims=True),
                jnp.max(jnp.maximum(first, last), axis=0, keepdims=True),
            )
            start = tile * 128
            probs[slot, start : start + 128, lanes] = jnp.exp(first - top).astype(BF)
            probs[slot, start + 128 : start + 512, lanes] = jnp.exp(middle - top).astype(BF)
            probs[slot, start + 512 : start + 640, lanes] = jnp.exp(last - top).astype(BF)
            levels.append(top)
        probs[slot, :128, 128:] = jnp.zeros((128, 128), BF)
        probs[slot, 640:, :128] = jnp.zeros((128, 128), BF)
        tops.append(jnp.concatenate(levels, axis=1))
    ones = jnp.ones((16, fill.shape[0]), BF)
    for pair in range(2):
        halves = []
        for half in range(2):
            slot = pair * 2 + half
            lanes = slice(half * HEAD_WIDTH, (half + 1) * HEAD_WIDTH)
            values = jnp.concatenate([turned[pair][lanes], ones], axis=0)
            mixed = dot_nn(values, probs[slot])
            total = mixed[HEAD_WIDTH : HEAD_WIDTH + 1]
            inverse = 1.0 / total
            halves.append(mixed[:HEAD_WIDTH] * inverse)
            head = step * 4 + slot
            inverse_ref[pl.ds(head, 1), :] = inverse
            stat_rows[pl.ds(head, 1), :] = tops[slot] + jnp.log(total)
        start = pl.multiple_of(step * WIDTH + pair * PAIR, PAIR)
        attended_ref[:, pl.ds(start, PAIR)] = jnp.concatenate(halves, axis=0).T

    @pl.when(step == 3)
    def _():
        mixed = dot_nn(attended_ref[...].astype(BF), w_out_ref[...])
        hidden = (latent_ref[...].astype(F32) + mixed).astype(BF)
        hidden_ref[...] = hidden
        forecast_ref[...] = dot_nn(hidden, readout_ref[...])
        stat_rows[HEADS:] = jnp.zeros((128 - HEADS, BLOCK), F32)
        stats_ref[...] = stat_rows[...].T


def forward(counts, left, right, latent_own, w_qkv, projected, w_out, readout_weight):
    whole = lambda *shape: pl.BlockSpec(shape, lambda j: (0, 0))
    part = lambda rows, first: pl.BlockSpec((rows, WIDTH), lambda j: (0, first + j))
    window = 2 * WIN + BLOCK
    return pl.pallas_call(
        forward_kernel,
        grid=(4,),
        in_specs=[
            pl.BlockSpec(memory_space=pltpu.SMEM),
            whole(WIN, 1024),
            whole(WIN, 1024),
            whole(BLOCK, 1024),
            HBM,
            part(BLOCK, 0),
            part(BLOCK, 4),
            part(BLOCK, 8),
            whole(1024, 1024),
            whole(1024, 128),
        ],
        out_specs=[
            whole(2 * WIN, 1024),
            part(window, 0),
            part(window, 0),
            whole(BLOCK, 1024),
            whole(BLOCK, 128),
            whole(BLOCK, 1024),
            whole(BLOCK, 128),
            pl.BlockSpec((4, window, BLOCK), lambda j: (j, 0, 0)),
            whole(HEADS, BLOCK),
        ],
        out_shape=[
            jax.ShapeDtypeStruct((2 * WIN, 1024), BF),
            jax.ShapeDtypeStruct((window, 1024), BF),
            jax.ShapeDtypeStruct((window, 1024), BF),
            jax.ShapeDtypeStruct((BLOCK, 1024), F32),
            jax.ShapeDtypeStruct((BLOCK, 128), F32),
            jax.ShapeDtypeStruct((BLOCK, 1024), BF),
            jax.ShapeDtypeStruct((BLOCK, 128), F32),
            jax.ShapeDtypeStruct((HEADS, window, BLOCK), BF),
            jax.ShapeDtypeStruct((HEADS, BLOCK), F32),
        ],
        scratch_shapes=[
            pltpu.VMEM((128, BLOCK), F32),
            pltpu.VMEM((8, 1024, WIDTH), BF),
            pltpu.SemaphoreType.DMA((8,)),
        ],
        compiler_params=pltpu.CompilerParams(vmem_limit_bytes=30 * 1024 * 1024),
        cost_estimate=pl.CostEstimate(
            flops=6 << 30, bytes_accessed=12 << 20, transcendentals=3 << 20
        ),
    )(
        counts,
        left,
        right,
        latent_own,
        in_hbm(w_qkv),
        projected,
        projected,
        projected,
        w_out,
        readout_weight,
    )


def score_kernel(
    counts_ref,
    own_ref,
    near_ref,
    others_ref,
    target_ref,
    attended_ref,
    hidden_ref,
    stats_ref,
    w_out_ref,
    readout_ref,
    crps_ref,
    packed_ref,
    sent_ref,
    grad_ref,
    small_ref,
):
    members = 4
    fair_eps = (1.0 - alpha_fair) / members
    coefficient = (1.0 - fair_eps) / (members * (members - 1))
    valid = (iota((BLOCK, 1), 0) < counts_ref[1]).astype(F32)
    own = own_ref[...]
    forecasts = [own, near_ref[...], others_ref[0], others_ref[1]]
    target = target_ref[...]
    error = jnp.zeros_like(target)
    for forecast in forecasts:
        error += smooth_abs(forecast - target)
    spread = jnp.full_like(target, members * smooth_width**0.5)
    for first in range(members):
        for second in range(first + 1, members):
            spread += 2.0 * smooth_abs(forecasts[first] - forecasts[second])
    crps_ref[...] = valid * (error / members - 0.5 * coefficient * spread)
    pull = jnp.zeros_like(target)
    for other in forecasts[1:]:
        pull += smooth_sign(own - other)
    slope = (
        valid / 128 * (smooth_sign(own - target) / members - coefficient * pull)
    ).astype(BF)
    dhidden = dot_nt(slope, readout_ref[...]).astype(BF)
    dattended = dot_nt(dhidden, w_out_ref[...]).astype(BF)
    grad_ref[...] = dattended
    attended = attended_ref[...]
    product = dattended.astype(F32) * attended
    high = product.astype(BF)
    low = (product - high.astype(F32)).astype(BF)
    pick = (iota((1024, 128), 0) // HEAD_WIDTH + HEADS == iota((1024, 128), 1)).astype(BF)
    stats = stats_ref[...] + dot_nn(high, pick) + dot_nn(low, pick)
    first = stats.astype(BF)
    rest = stats - first.astype(F32)
    second = rest.astype(BF)
    third = (rest - second.astype(F32)).astype(BF)
    terms = jnp.zeros((BLOCK, 128), F32)
    for place, term in enumerate((first, second, third)):
        shift = (iota((128, 128), 0) + 32 * place == iota((128, 128), 1)) & (
            iota((128, 128), 0) < 32
        )
        terms += dot_nn(term, shift.astype(BF))
    packed_ref[:, :128] = slope
    packed_ref[:, 128:] = terms.astype(BF)
    sent_ref[...] = packed_ref[...]
    small_ref[:, :128] = dot_tn(attended.astype(BF), slope).astype(BF)
    small_ref[:, 128:] = dot_tn(hidden_ref[...], slope).astype(BF)


def score(counts, own, near, others, target, attended, hidden, stats, w_out, readout_weight):
    vmem = pl.BlockSpec(memory_space=pltpu.VMEM)
    return pl.pallas_call(
        score_kernel,
        in_specs=[pl.BlockSpec(memory_space=pltpu.SMEM)] + [vmem] * 9,
        out_specs=[vmem] * 5,
        out_shape=[
            pltpu.HBM((BLOCK, 128), F32),
            jax.ShapeDtypeStruct((BLOCK, 256), BF),
            pltpu.HBM((BLOCK, 256), BF),
            jax.ShapeDtypeStruct((BLOCK, 1024), BF),
            jax.ShapeDtypeStruct((1024, 256), BF),
        ],
        compiler_params=pltpu.CompilerParams(vmem_limit_bytes=12 * 1024 * 1024),
    )(counts, own, near, others, target, attended, hidden, stats, w_out, readout_weight)


def query_kernel(
    kcat_ref, vcat_ref, grad_ref, packed_ref, probs_ref, inverse_ref, dq_ref, dscores
):
    step = pl.program_id(0)
    window = kcat_ref.shape[0]
    value_fill = (spare_lane((window, PAIR)) < 3).astype(BF)
    low_q = iota((BLOCK, PAIR), 1) < HEAD_WIDTH
    low_k = iota((window, PAIR), 1) < HEAD_WIDTH
    g_fill = dot_nn(packed_ref[:, 128:], stat_spread(step, HEADS)).astype(BF)
    turned = []
    for pair in range(2):
        columns = slice(pair * PAIR, (pair + 1) * PAIR)
        g_pair = grad_ref[:, columns]
        v_pair = vcat_ref[:, columns]
        k_turned = kcat_ref[:, columns].T
        for half in range(2):
            slot = pair * 2 + half
            pick_q = low_q if half == 0 else ~low_q
            pick_k = low_k if half == 0 else ~low_k
            g_head = jnp.where(pick_q, g_pair, g_fill[:, columns])
            v_head = jnp.where(pick_k, v_pair, value_fill)
            change = dot_nt(v_head, g_head)
            dscores[slot] = (probs_ref[slot].astype(F32) * change).astype(BF)
            turned.append(k_turned[half * HEAD_WIDTH : (half + 1) * HEAD_WIDTH])
    for slot in range(4):
        scale = inverse_ref[pl.ds(step * 4 + slot, 1), :] * HEAD_WIDTH ** (-0.5)
        dquery = dot_nn(turned[slot], dscores[slot]) * scale
        dq_ref[slot * HEAD_WIDTH : (slot + 1) * HEAD_WIDTH] = dquery.astype(BF)


def query_grads(kcat, vcat, grad, packed, probs, inverse):
    part = lambda rows, first: pl.BlockSpec((rows, WIDTH), lambda j: (0, first + j))
    window = 2 * WIN + BLOCK
    return pl.pallas_call(
        query_kernel,
        grid=(4,),
        in_specs=[
            part(window, 0),
            part(window, 0),
            part(BLOCK, 0),
            pl.BlockSpec((BLOCK, 256), lambda j: (0, 0)),
            pl.BlockSpec((4, window, BLOCK), lambda j: (j, 0, 0)),
            pl.BlockSpec((HEADS, BLOCK), lambda j: (0, 0)),
        ],
        out_specs=pl.BlockSpec((WIDTH, BLOCK), lambda j: (j, 0)),
        out_shape=jax.ShapeDtypeStruct((1024, BLOCK), BF),
        scratch_shapes=[pltpu.VMEM((4, window, BLOCK), BF)],
        compiler_params=pltpu.CompilerParams(vmem_limit_bytes=16 * 1024 * 1024),
        cost_estimate=pl.CostEstimate(
            flops=6 << 30, bytes_accessed=5 << 20, transcendentals=3 << 20
        ),
    )(kcat, vcat, grad, packed, probs, inverse)


def key_kernel(
    counts_ref,
    q_ref,
    k_ref,
    v_ref,
    qhalo_ref,
    grad_ref,
    own_ref,
    sides_ref,
    w_out_ref,
    readout_ref,
    out_ref,
    probs,
    dscores,
    dhidden,
):
    step = pl.program_id(0)

    @pl.when(step == 0)
    def _():
        for slot in range(4):
            for held in (probs, dscores):
                held[slot, :128, 128:] = jnp.zeros((128, 128), BF)
                held[slot, 640:, :128] = jnp.zeros((128, 128), BF)
        dhidden[:WIN] = dot_nt(sides_ref[0, :, :128], readout_ref[...]).astype(BF)
        dhidden[WIN:] = dot_nt(sides_ref[1, :, :128], readout_ref[...]).astype(BF)

    ghalo = dot_nt(dhidden[...], w_out_ref[...]).astype(BF)
    terms = jnp.concatenate(
        [sides_ref[0, :, 128:], own_ref[:, 128:], sides_ref[1, :, 128:]], axis=0
    )
    window = terms.shape[0]
    fill = key_fill([(counts_ref[1], BLOCK)])
    value_fill = (spare_lane(fill.shape) < 3).astype(BF)
    low_q = iota((window, PAIR), 1) < HEAD_WIDTH
    low_k = iota(fill.shape, 1) < HEAD_WIDTH
    ones = (spare_lane((window, WIDTH)) == 3).astype(F32)
    q_fill = (dot_nn(terms, stat_spread(step, 0)) + ones).astype(BF)
    g_fill = dot_nn(terms, stat_spread(step, HEADS)).astype(BF)
    turned = []
    for pair in range(2):
        columns = slice(pair * PAIR, (pair + 1) * PAIR)
        q_pair = jnp.concatenate(
            [qhalo_ref[:WIN, columns], q_ref[:, columns], qhalo_ref[WIN:, columns]], axis=0
        ) * jnp.asarray(HEAD_WIDTH ** (-0.5), BF)
        g_pair = jnp.concatenate(
            [ghalo[:WIN, columns], grad_ref[:, columns], ghalo[WIN:, columns]], axis=0
        )
        k_pair = k_ref[:, columns]
        v_pair = v_ref[:, columns]
        q_turned = q_pair.T
        g_turned = g_pair.T
        for half in range(2):
            slot = pair * 2 + half
            pick_q = low_q if half == 0 else ~low_q
            pick_k = low_k if half == 0 else ~low_k
            q_head = jnp.where(pick_q, q_pair, q_fill[:, columns])
            g_head = jnp.where(pick_q, g_pair, g_fill[:, columns])
            k_head = jnp.where(pick_k, k_pair, fill)
            v_head = jnp.where(pick_k, v_pair, value_fill)
            scores = dot_nt(q_head, k_head)
            change = dot_nt(g_head, v_head)
            for tile in range(2):
                rows = slice(tile * 128, tile * 128 + 640)
                lanes = slice(tile * 128, tile * 128 + 128)
                weight = keep_band(jnp.exp(scores[rows, lanes]), 0.0)
                moved = change[rows, lanes]
                start = tile * 128
                for piece, (low, high) in zip(weight, ((0, 128), (128, 512), (512, 640))):
                    place = slice(start + low, start + high)
                    probs[slot, place, lanes] = piece.astype(BF)
                    dscores[slot, place, lanes] = (piece * moved[low:high]).astype(BF)
            lanes = slice(half * HEAD_WIDTH, (half + 1) * HEAD_WIDTH)
            turned.append((q_turned[lanes], g_turned[lanes]))
    for slot in range(4):
        place = slice(slot * HEAD_WIDTH, (slot + 1) * HEAD_WIDTH)
        out_ref[0, place] = dot_nn(turned[slot][0], dscores[slot]).astype(BF)
        out_ref[1, place] = dot_nn(turned[slot][1], probs[slot]).astype(BF)


def key_grads(counts, projected, qhalo, grad, own, sides, w_out, readout_weight):
    part = lambda rows, first: pl.BlockSpec((rows, WIDTH), lambda j: (0, first + j))
    whole = lambda *shape: pl.BlockSpec(shape, lambda j: (0, 0))
    window = 2 * WIN + BLOCK
    return pl.pallas_call(
        key_kernel,
        grid=(4,),
        in_specs=[
            pl.BlockSpec(memory_space=pltpu.SMEM),
            part(BLOCK, 0),
            part(BLOCK, 4),
            part(BLOCK, 8),
            part(2 * WIN, 0),
            part(BLOCK, 0),
            whole(BLOCK, 256),
            pl.BlockSpec((2, WIN, 256), lambda j: (0, 0, 0)),
            pl.BlockSpec((WIDTH, 1024), lambda j: (j, 0)),
            whole(1024, 128),
        ],
        out_specs=pl.BlockSpec((2, WIDTH, BLOCK), lambda j: (0, j, 0)),
        out_shape=jax.ShapeDtypeStruct((2, 1024, BLOCK), BF),
        scratch_shapes=[
            pltpu.VMEM((4, window, BLOCK), BF),
            pltpu.VMEM((4, window, BLOCK), BF),
            pltpu.VMEM((2 * WIN, 1024), BF),
        ],
        compiler_params=pltpu.CompilerParams(vmem_limit_bytes=18 * 1024 * 1024),
        cost_estimate=FREE,
    )(
        counts,
        projected,
        projected,
        projected,
        qhalo,
        in_hbm(grad),
        own,
        in_hbm(sides),
        in_hbm(w_out),
        readout_weight,
    )


AXES = ("x_hi", "core", "y", "x_lo", "z")
MEMBER = ("x_hi", "core")
CELLS = ("y", "x_lo", "z")
CHIPS = ("x_hi", "y", "x_lo", "z")
SWAP = [(0, 1), (1, 0)]


def swap_core(values):
    return lax.ppermute(values, "core", SWAP)


def scatter(partial):
    columns = partial.shape[1]
    return lax.all_to_all(partial.reshape(64, 8, columns), CHIPS, split_axis=0, concat_axis=0)


def add_up(pieces):
    return jnp.sum(pieces.astype(F32), axis=0)


def per_device(latent, counts, w_qkv, w_out, readout_weight, target):
    latent_own = latent[0]
    cell_count = 32
    cell_index = lax.axis_index(CELLS)
    member_index = lax.axis_index(MEMBER)
    core = lax.axis_index("core")
    up = [(i, i + 1) for i in range(cell_count - 1)]
    down = [(i + 1, i) for i in range(cell_count - 1)]
    from_left = lax.ppermute(latent_own, CELLS, up)
    from_right = lax.ppermute(latent_own, CELLS, down)

    own_count = counts[cell_index]
    left_count = jnp.where(cell_index > 0, counts[jnp.maximum(cell_index - 1, 0)], 0)
    right_count = jnp.where(
        cell_index < cell_count - 1, counts[jnp.minimum(cell_index + 1, cell_count - 1)], 0
    )
    scalars = jnp.stack([left_count, own_count, right_count])

    projected, turned = project(latent_own, w_qkv)
    turned_other = swap_core(turned)
    normed_halo, kcat, vcat, attended, stats, hidden, forecast, probs, inverse = forward(
        scalars, from_left, from_right, latent_own, w_qkv, projected, w_out, readout_weight
    )
    near = lax.ppermute(forecast, "x_hi", SWAP)
    qhalo = halo_queries(normed_halo, w_qkv)
    near, qhalo = lax.optimization_barrier((near, qhalo))
    others = swap_core(jnp.stack([forecast, near]))
    crps_whole, packed, sent, grad, small = score(
        scalars, forecast, near, others, target, attended, hidden, stats, w_out, readout_weight
    )
    crps = lax.dynamic_slice_in_dim(crps_whole, member_index * 32, 32, 1)
    packed_left = lax.ppermute(sent, CELLS, up)
    packed_right = lax.ppermute(sent, CELLS, down)

    dquery = query_grads(kcat, vcat, grad, packed, probs, inverse)
    dquery, packed_left, packed_right = lax.optimization_barrier(
        (dquery, packed_left, packed_right)
    )

    first_part, sides = partial_sums(
        core,
        turned,
        turned_other,
        dquery,
        swap_core(dquery),
        (small, swap_core(small)),
        (packed_left, packed_right),
    )
    first_part, scalars = lax.optimization_barrier((first_part, scalars))
    first = scatter(first_part)
    pairs = key_grads(
        scalars,
        projected,
        qhalo,
        grad,
        packed,
        sides,
        w_out,
        readout_weight,
    )
    pairs = pairs.reshape(2048, BLOCK)
    second_part = partial_sums(core, turned, turned_other, pairs, swap_core(pairs))
    second_part, first = lax.optimization_barrier((second_part, first))
    second = add_up(scatter(second_part))
    first = add_up(first)
    grad_out = lax.dot_general(
        first[:, 1024:1152],
        readout_weight.astype(F32),
        (((1,), (1,)), ((), ())),
        precision=lax.Precision.HIGHEST,
        preferred_element_type=F32,
    )
    grads = jnp.concatenate([first[:, :1024], second, grad_out, first[:, 1152:]], axis=1)
    return (crps, grads)


def solution(mesh):
    fine = jax.sharding.Mesh(mesh.devices.reshape(2, 2, 4, 2, 4), AXES)
    placed = (P(MEMBER, CELLS, None), P(), P(), P(), P(), P(CELLS, None))
    return jax.shard_map(
        per_device,
        mesh=fine,
        in_specs=placed,
        out_specs=(P(CELLS, MEMBER), P(MEMBER + CELLS, None)),
        check_vma=False,
    )
```

```python
import functools

import jax
import jax.numpy as jnp
import numpy as np
from jax import lax
from jax.experimental import pallas as pl
from jax.experimental.pallas import tpu as pltpu
from jax.sharding import PartitionSpec as P

HEADS = 16
WIN = 256
BLOCK = 256
WIDTH = 256
HEAD_WIDTH = 64
PAIR = 128
NEVER = -1e30

alpha_fair = 0.95
smooth_width = 0.0625

BF = jnp.bfloat16
F32 = jnp.float32


def smooth_abs(values):
    return jnp.sqrt(values * values + smooth_width)


def smooth_sign(values):
    return values * lax.rsqrt(values * values + smooth_width)


def layer_norm(latent_rows):
    values = latent_rows.astype(F32)
    center = values - jnp.mean(values, axis=-1, keepdims=True)
    spread = jnp.mean(center * center, axis=-1, keepdims=True)
    return (center * lax.rsqrt(spread + 1e-05)).astype(BF)


def dot_nn(left, right):
    return lax.dot_general(left, right, (((1,), (0,)), ((), ())), preferred_element_type=F32)


def dot_nt(left, right):
    return lax.dot_general(left, right, (((1,), (1,)), ((), ())), preferred_element_type=F32)


def dot_tn(left, right):
    return lax.dot_general(left, right, (((0,), (0,)), ((), ())), preferred_element_type=F32)


def iota(shape, axis):
    return lax.broadcasted_iota(jnp.int32, shape, axis)


FREE = pl.CostEstimate(flops=0, bytes_accessed=0, transcendentals=0)
HBM = pl.BlockSpec(memory_space=pltpu.HBM)


def in_hbm(values):
    return pltpu.with_memory_space_constraint(values, pltpu.HBM)


def fetches(weight_ref, buffer, arrived, width, first):
    return [
        pltpu.make_async_copy(
            weight_ref.at[:, pl.ds(first + place * width, width)],
            buffer.at[place],
            arrived.at[place],
        )
        for place in range(buffer.shape[0])
    ]


def fetch_one(weight_ref, buffer, arrived, width, first, place):
    start = pl.multiple_of(first + place * width, width)
    return pltpu.make_async_copy(
        weight_ref.at[:, pl.ds(start, width)], buffer.at[place], arrived.at[place]
    )


def project_kernel(latent_ref, weight_ref, projected_ref, turned_ref, normed, buffer, arrived):
    step = pl.program_id(0)

    @pl.when(step == 0)
    def _():
        for copy in fetches(weight_ref, buffer, arrived, 512, 0):
            copy.start()
        normed[...] = layer_norm(latent_ref[...])
        turned_ref[...] = normed[...].T

    fetch_one(weight_ref, buffer, arrived, 512, 0, step).wait()
    projected_ref[...] = dot_nn(normed[...], buffer[step]).astype(BF)


def project(latent_own, w_qkv):
    rows, width = latent_own.shape
    return pl.pallas_call(
        project_kernel,
        grid=(6,),
        in_specs=[pl.BlockSpec((rows, width), lambda j: (0, 0)), HBM],
        out_specs=[
            pl.BlockSpec((rows, 512), lambda j: (0, j)),
            pl.BlockSpec((width, rows), lambda j: (0, 0)),
        ],
        out_shape=[
            jax.ShapeDtypeStruct((rows, 3 * width), BF),
            jax.ShapeDtypeStruct((width, rows), BF),
        ],
        scratch_shapes=[
            pltpu.VMEM((rows, width), BF),
            pltpu.VMEM((6, width, 512), BF),
            pltpu.SemaphoreType.DMA((6,)),
        ],
        compiler_params=pltpu.CompilerParams(vmem_limit_bytes=16 * 1024 * 1024),
        cost_estimate=pl.CostEstimate(
            flops=2 * rows * width * width * 4, bytes_accessed=8 << 20, transcendentals=0
        ),
    )(latent_own, in_hbm(w_qkv))


def halo_query_kernel(normed_ref, weight_ref, out_ref, buffer, arrived):
    step = pl.program_id(0)

    @pl.when(step == 0)
    def _():
        for copy in fetches(weight_ref, buffer, arrived, 256, 0):
            copy.start()

    fetch_one(weight_ref, buffer, arrived, 256, 0, step).wait()
    out_ref[...] = dot_nn(normed_ref[...], buffer[step]).astype(BF)


def halo_queries(normed_halo, w_qkv):
    rows, width = normed_halo.shape
    return pl.pallas_call(
        halo_query_kernel,
        grid=(4,),
        in_specs=[pl.BlockSpec((rows, width), lambda j: (0, 0)), HBM],
        out_specs=pl.BlockSpec((rows, 256), lambda j: (0, j)),
        out_shape=jax.ShapeDtypeStruct((rows, width), BF),
        scratch_shapes=[
            pltpu.VMEM((4, width, 256), BF),
            pltpu.SemaphoreType.DMA((4,)),
        ],
        compiler_params=pltpu.CompilerParams(vmem_limit_bytes=12 * 1024 * 1024),
        cost_estimate=FREE,
    )(normed_halo, in_hbm(w_qkv))


def partial_kernel(
    smalls, core_ref, normed_ref, normed_other_ref, piece_ref, other_ref, *refs
):
    small_refs, (out_ref, rows, pieces, others, sums, staged, arrived, left) = (
        refs[:smalls],
        refs[smalls:],
    )
    core = core_ref[0]
    chunks = piece_ref.shape[0] // 512
    sources = [
        (normed_ref.at[:, core], rows.at[0]),
        (normed_other_ref.at[:, core], rows.at[1]),
    ]
    for chunk in range(chunks):
        part = pl.ds(chunk * 512, 512)
        sources.append((piece_ref.at[part], pieces.at[chunk]))
        sources.append((other_ref.at[part], others.at[chunk]))
    for place, small_ref in enumerate(small_refs):
        sources.append((small_ref.at[:, core], sums.at[place]))
    copies = [
        pltpu.make_async_copy(source, target, arrived.at[place])
        for place, (source, target) in enumerate(sources)
    ]
    for copy in copies:
        copy.start()
    copies[0].wait()
    copies[1].wait()
    writes = []
    for chunk in range(chunks):
        copies[2 + 2 * chunk].wait()
        copies[3 + 2 * chunk].wait()
        for top in range(2):
            staged[chunk, top * 256 : (top + 1) * 256] = (
                dot_nt(rows[0, top], pieces[chunk]) + dot_nt(rows[1, top], others[chunk])
            ).astype(BF)
        writes.append(
            pltpu.make_async_copy(
                staged.at[chunk], out_ref.at[:, pl.ds(chunk * 512, 512)], left.at[chunk]
            )
        )
        writes[-1].start()
    if smalls:
        copies[-2].wait()
        copies[-1].wait()
        for top in range(2):
            staged[chunks, top * 256 : (top + 1) * 256, :256] = (
                sums[0, top].astype(F32) + sums[1, top].astype(F32)
            ).astype(BF)
        writes.append(
            pltpu.make_async_copy(
                staged.at[chunks, :, pl.ds(0, 256)],
                out_ref.at[:, pl.ds(chunks * 512, 256)],
                left.at[chunks],
            )
        )
        writes[-1].start()
    for write in writes:
        write.wait()


def partial_sums(core, turned, turned_other, piece, other, smalls=()):
    by_core = lambda values: values.reshape(2, 2, 256, 256)
    anywhere = pl.BlockSpec(memory_space=pl.ANY)
    chunks = piece.shape[0] // 512
    columns = piece.shape[0] + 256 * (len(smalls) // 2)
    return pl.pallas_call(
        functools.partial(partial_kernel, len(smalls)),
        in_specs=[pl.BlockSpec(memory_space=pltpu.SMEM)] + [anywhere] * (4 + len(smalls)),
        out_specs=anywhere,
        out_shape=jax.ShapeDtypeStruct((512, columns), BF),
        scratch_shapes=[
            pltpu.VMEM((2, 2, 256, 256), BF),
            pltpu.VMEM((chunks, 512, 256), BF),
            pltpu.VMEM((chunks, 512, 256), BF),
            pltpu.VMEM((2, 2, 256, 256), BF),
            pltpu.VMEM((chunks + 1, 512, 512), BF),
            pltpu.SemaphoreType.DMA((2 + 2 * chunks + len(smalls),)),
            pltpu.SemaphoreType.DMA((chunks + 1,)),
        ],
        compiler_params=pltpu.CompilerParams(vmem_limit_bytes=14 * 1024 * 1024),
        cost_estimate=FREE,
    )(
        core.astype(jnp.int32).reshape(1),
        by_core(turned),
        by_core(turned_other),
        piece,
        other,
        *(by_core(small) for small in smalls),
    )


def spare_lane(shape):
    lane = iota(shape, len(shape) - 1)
    return lane % HEAD_WIDTH


def key_fill(count_pieces):
    fills = []
    for count, rows in count_pieces:
        spare = spare_lane((rows, PAIR))
        bias = jnp.where(iota((rows, PAIR), 0) < count, 0.0, NEVER)
        fills.append(
            jnp.where(spare < 3, 1.0, jnp.where(spare == 3, bias, 0.0)).astype(BF)
        )
    return jnp.concatenate(fills, axis=0)


def stat_spread(step, offset):
    shape = (128, WIDTH)
    lane = iota(shape, 1)
    head = step * 4 + 2 * (lane // PAIR) + jnp.where(lane % PAIR < HEAD_WIDTH, 1, 0)
    term = lane % HEAD_WIDTH
    chosen = (term < 3) & (iota(shape, 0) == term * 32 + offset + head)
    return jnp.where(chosen, -1.0, 0.0).astype(BF)


def keep_band(window, fill):
    shape = (128, 128)
    apart = iota(shape, 0) - iota(shape, 1)
    first = jnp.where(apart >= 0, window[:128], fill)
    last = jnp.where(apart <= 0, window[-128:], fill)
    return first, window[128:-128], last


def own_kernel(counts_ref, q_ref, k_ref, v_ref, probs, mixed_ref, top_ref, total_ref):
    step = pl.program_id(0)
    fill = key_fill([(counts_ref[1], BLOCK)])
    low = iota((BLOCK, PAIR), 1) < HEAD_WIDTH
    query_fill = (spare_lane((BLOCK, PAIR)) == 3).astype(BF)
    ones = jnp.ones((16, BLOCK), BF)
    scores, turned = [], []
    for pair in range(2):
        columns = slice(pair * PAIR, (pair + 1) * PAIR)
        q_pair = q_ref[:, columns] * jnp.asarray(HEAD_WIDTH ** (-0.5), BF)
        k_pair = k_ref[:, columns]
        turned.append(v_ref[:, columns].T)
        for half in range(2):
            pick = low if half == 0 else ~low
            scores.append(
                dot_nt(jnp.where(pick, k_pair, fill), jnp.where(pick, q_pair, query_fill))
            )
    for slot in range(4):
        top = jnp.max(scores[slot], axis=0, keepdims=True)
        probs[slot] = jnp.exp(scores[slot] - top).astype(BF)
        top_ref[pl.ds(step * 4 + slot, 1), :] = top
    for slot in range(4):
        lanes = slice(slot % 2 * HEAD_WIDTH, (slot % 2 + 1) * HEAD_WIDTH)
        values = jnp.concatenate([turned[slot // 2][lanes], ones], axis=0)
        mixed = dot_nn(values, probs[slot])
        mixed_ref[slot * HEAD_WIDTH : (slot + 1) * HEAD_WIDTH] = mixed[:HEAD_WIDTH]
        total_ref[pl.ds(step * 4 + slot, 1), :] = mixed[HEAD_WIDTH : HEAD_WIDTH + 1]


def own_part(counts, projected):
    part = lambda rows, first: pl.BlockSpec((rows, WIDTH), lambda j: (0, first + j))
    whole = pl.BlockSpec((HEADS, BLOCK), lambda j: (0, 0))
    return pl.pallas_call(
        own_kernel,
        grid=(4,),
        in_specs=[
            pl.BlockSpec(memory_space=pltpu.SMEM),
            part(BLOCK, 0),
            part(BLOCK, 4),
            part(BLOCK, 8),
        ],
        out_specs=[
            pl.BlockSpec((4, BLOCK, BLOCK), lambda j: (j, 0, 0)),
            pl.BlockSpec((WIDTH, BLOCK), lambda j: (j, 0)),
            whole,
            whole,
        ],
        out_shape=[
            jax.ShapeDtypeStruct((HEADS, BLOCK, BLOCK), BF),
            jax.ShapeDtypeStruct((1024, BLOCK), F32),
            jax.ShapeDtypeStruct((HEADS, BLOCK), F32),
            jax.ShapeDtypeStruct((HEADS, BLOCK), F32),
        ],
        compiler_params=pltpu.CompilerParams(vmem_limit_bytes=14 * 1024 * 1024),
        cost_estimate=pl.CostEstimate(
            flops=1 << 30, bytes_accessed=4 << 20, transcendentals=1 << 20
        ),
    )(counts, projected, projected, projected)


def forward_kernel(
    counts_ref,
    left_ref,
    right_ref,
    latent_ref,
    weight_ref,
    q_ref,
    own_mixed_ref,
    own_top_ref,
    own_total_ref,
    w_out_ref,
    readout_ref,
    normed_ref,
    khalo_ref,
    vhalo_ref,
    attended_ref,
    stats_ref,
    hidden_ref,
    forecast_ref,
    probs,
    inverse_ref,
    own_inverse_ref,
    stat_rows,
    buffer,
    arrived,
):
    step = pl.program_id(0)

    @pl.when(step == 0)
    def _():
        copies = fetches(weight_ref, buffer, arrived, WIDTH, 1024)
        for place in (0, 4, 1, 5, 2, 6, 3, 7):
            copies[place].start()
        normed_ref[:WIN] = layer_norm(left_ref[...])
        normed_ref[WIN:] = layer_norm(right_ref[...])

    fetch_one(weight_ref, buffer, arrived, WIDTH, 1024, step).wait()
    fetch_one(weight_ref, buffer, arrived, WIDTH, 1024, step + 4).wait()
    khalo_ref[...] = dot_nn(normed_ref[...], buffer[step]).astype(BF)
    vhalo_ref[...] = dot_nn(normed_ref[...], buffer[step + 4]).astype(BF)
    fill = key_fill([(counts_ref[0], WIN), (counts_ref[2], WIN)])
    low_q = iota((BLOCK, PAIR), 1) < HEAD_WIDTH
    low_k = iota(fill.shape, 1) < HEAD_WIDTH
    query_fill = (spare_lane((BLOCK, PAIR)) == 3).astype(BF)
    scores, turned = [], []
    for pair in range(2):
        columns = slice(pair * PAIR, (pair + 1) * PAIR)
        q_pair = q_ref[:, columns] * jnp.asarray(HEAD_WIDTH ** (-0.5), BF)
        k_pair = khalo_ref[:, columns]
        turned.append(vhalo_ref[:, columns].T)
        for half in range(2):
            if half == 0:
                q_head = jnp.where(low_q, q_pair, query_fill)
                k_head = jnp.where(low_k, k_pair, fill)
            else:
                q_head = jnp.where(low_q, query_fill, q_pair)
                k_head = jnp.where(low_k, fill, k_pair)
            scores.append(dot_nt(k_head, q_head))
    tops = []
    for slot in range(4):
        levels = []
        for tile in range(2):
            rows = slice(tile * 128, tile * 128 + 384)
            lanes = slice(tile * 128, tile * 128 + 128)
            first, middle, last = keep_band(scores[slot][rows, lanes], NEVER)
            top = jnp.maximum(
                jnp.max(middle, axis=0, keepdims=True),
                jnp.max(jnp.maximum(first, last), axis=0, keepdims=True),
            )
            top = jnp.maximum(top, own_top_ref[pl.ds(step * 4 + slot, 1), :][:, lanes])
            start = tile * 128
            probs[slot, start : start + 128, lanes] = jnp.exp(first - top).astype(BF)
            probs[slot, start + 128 : start + 256, lanes] = jnp.exp(middle - top).astype(BF)
            probs[slot, start + 256 : start + 384, lanes] = jnp.exp(last - top).astype(BF)
            levels.append(top)
        probs[slot, :128, 128:] = jnp.zeros((128, 128), BF)
        probs[slot, 384:, :128] = jnp.zeros((128, 128), BF)
        tops.append(jnp.concatenate(levels, axis=1))
    ones = jnp.ones((16, fill.shape[0]), BF)
    for pair in range(2):
        halves = []
        for half in range(2):
            slot = pair * 2 + half
            lanes = slice(half * HEAD_WIDTH, (half + 1) * HEAD_WIDTH)
            values = jnp.concatenate([turned[pair][lanes], ones], axis=0)
            mixed = dot_nn(values, probs[slot])
            head = step * 4 + slot
            fade = jnp.exp(own_top_ref[pl.ds(head, 1), :] - tops[slot])
            total = mixed[HEAD_WIDTH : HEAD_WIDTH + 1]
            total += own_total_ref[pl.ds(head, 1), :] * fade
            inverse = 1.0 / total
            own_inverse = fade * inverse
            own_mixed = own_mixed_ref[slot * HEAD_WIDTH : (slot + 1) * HEAD_WIDTH]
            halves.append(mixed[:HEAD_WIDTH] * inverse + own_mixed * own_inverse)
            own_inverse_ref[pl.ds(head, 1), :] = own_inverse
            inverse_ref[pl.ds(head, 1), :] = inverse
            stat_rows[pl.ds(head, 1), :] = tops[slot] + jnp.log(total)
        start = pl.multiple_of(step * WIDTH + pair * PAIR, PAIR)
        attended_ref[:, pl.ds(start, PAIR)] = jnp.concatenate(halves, axis=0).T

    @pl.when(step == 3)
    def _():
        mixed = dot_nn(attended_ref[...].astype(BF), w_out_ref[...])
        hidden = (latent_ref[...].astype(F32) + mixed).astype(BF)
        hidden_ref[...] = hidden
        forecast_ref[...] = dot_nn(hidden, readout_ref[...])
        stat_rows[HEADS:] = jnp.zeros((128 - HEADS, BLOCK), F32)
        stats_ref[...] = stat_rows[...].T


def forward(counts, left, right, latent_own, w_qkv, projected, own, w_out, readout_weight):
    whole = lambda *shape: pl.BlockSpec(shape, lambda j: (0, 0))
    part = lambda rows, first: pl.BlockSpec((rows, WIDTH), lambda j: (0, first + j))
    window = 2 * WIN + BLOCK
    return pl.pallas_call(
        forward_kernel,
        grid=(4,),
        in_specs=[
            pl.BlockSpec(memory_space=pltpu.SMEM),
            whole(WIN, 1024),
            whole(WIN, 1024),
            whole(BLOCK, 1024),
            HBM,
            part(BLOCK, 0),
            pl.BlockSpec((WIDTH, BLOCK), lambda j: (j, 0)),
            whole(HEADS, BLOCK),
            whole(HEADS, BLOCK),
            whole(1024, 1024),
            whole(1024, 128),
        ],
        out_specs=[
            whole(2 * WIN, 1024),
            part(2 * WIN, 0),
            part(2 * WIN, 0),
            whole(BLOCK, 1024),
            whole(BLOCK, 128),
            whole(BLOCK, 1024),
            whole(BLOCK, 128),
            pl.BlockSpec((4, 2 * WIN, BLOCK), lambda j: (j, 0, 0)),
            whole(HEADS, BLOCK),
            whole(HEADS, BLOCK),
        ],
        out_shape=[
            jax.ShapeDtypeStruct((2 * WIN, 1024), BF),
            jax.ShapeDtypeStruct((2 * WIN, 1024), BF),
            jax.ShapeDtypeStruct((2 * WIN, 1024), BF),
            jax.ShapeDtypeStruct((BLOCK, 1024), F32),
            jax.ShapeDtypeStruct((BLOCK, 128), F32),
            jax.ShapeDtypeStruct((BLOCK, 1024), BF),
            jax.ShapeDtypeStruct((BLOCK, 128), F32),
            jax.ShapeDtypeStruct((HEADS, 2 * WIN, BLOCK), BF),
            jax.ShapeDtypeStruct((HEADS, BLOCK), F32),
            jax.ShapeDtypeStruct((HEADS, BLOCK), F32),
        ],
        scratch_shapes=[
            pltpu.VMEM((128, BLOCK), F32),
            pltpu.VMEM((8, 1024, WIDTH), BF),
            pltpu.SemaphoreType.DMA((8,)),
        ],
        compiler_params=pltpu.CompilerParams(vmem_limit_bytes=30 * 1024 * 1024),
        cost_estimate=pl.CostEstimate(
            flops=6 << 30, bytes_accessed=12 << 20, transcendentals=3 << 20
        ),
    )(
        counts,
        left,
        right,
        latent_own,
        in_hbm(w_qkv),
        projected,
        *own,
        w_out,
        readout_weight,
    )


def score_kernel(
    counts_ref,
    own_ref,
    near_ref,
    others_ref,
    target_ref,
    attended_ref,
    hidden_ref,
    stats_ref,
    w_out_ref,
    readout_ref,
    crps_ref,
    packed_ref,
    sent_ref,
    grad_ref,
    small_ref,
):
    members = 4
    fair_eps = (1.0 - alpha_fair) / members
    coefficient = (1.0 - fair_eps) / (members * (members - 1))
    valid = (iota((BLOCK, 1), 0) < counts_ref[1]).astype(F32)
    own = own_ref[...]
    forecasts = [own, near_ref[...], others_ref[0], others_ref[1]]
    target = target_ref[...]
    error = jnp.zeros_like(target)
    for forecast in forecasts:
        error += smooth_abs(forecast - target)
    spread = jnp.full_like(target, members * smooth_width**0.5)
    for first in range(members):
        for second in range(first + 1, members):
            spread += 2.0 * smooth_abs(forecasts[first] - forecasts[second])
    crps_ref[...] = valid * (error / members - 0.5 * coefficient * spread)
    pull = jnp.zeros_like(target)
    for other in forecasts[1:]:
        pull += smooth_sign(own - other)
    slope = (
        valid / 128 * (smooth_sign(own - target) / members - coefficient * pull)
    ).astype(BF)
    dhidden = dot_nt(slope, readout_ref[...]).astype(BF)
    dattended = dot_nt(dhidden, w_out_ref[...]).astype(BF)
    grad_ref[...] = dattended
    attended = attended_ref[...]
    product = dattended.astype(F32) * attended
    high = product.astype(BF)
    low = (product - high.astype(F32)).astype(BF)
    pick = (iota((1024, 128), 0) // HEAD_WIDTH + HEADS == iota((1024, 128), 1)).astype(BF)
    stats = stats_ref[...] + dot_nn(high, pick) + dot_nn(low, pick)
    first = stats.astype(BF)
    rest = stats - first.astype(F32)
    second = rest.astype(BF)
    third = (rest - second.astype(F32)).astype(BF)
    terms = jnp.zeros((BLOCK, 128), F32)
    for place, term in enumerate((first, second, third)):
        shift = (iota((128, 128), 0) + 32 * place == iota((128, 128), 1)) & (
            iota((128, 128), 0) < 32
        )
        terms += dot_nn(term, shift.astype(BF))
    packed_ref[:, :128] = slope
    packed_ref[:, 128:] = terms.astype(BF)
    sent_ref[...] = packed_ref[...]
    small_ref[:, :128] = dot_tn(attended.astype(BF), slope).astype(BF)
    small_ref[:, 128:] = dot_tn(hidden_ref[...], slope).astype(BF)


def score(counts, own, near, others, target, attended, hidden, stats, w_out, readout_weight):
    vmem = pl.BlockSpec(memory_space=pltpu.VMEM)
    return pl.pallas_call(
        score_kernel,
        in_specs=[pl.BlockSpec(memory_space=pltpu.SMEM)] + [vmem] * 9,
        out_specs=[vmem] * 5,
        out_shape=[
            pltpu.HBM((BLOCK, 128), F32),
            jax.ShapeDtypeStruct((BLOCK, 256), BF),
            pltpu.HBM((BLOCK, 256), BF),
            jax.ShapeDtypeStruct((BLOCK, 1024), BF),
            jax.ShapeDtypeStruct((1024, 256), BF),
        ],
        compiler_params=pltpu.CompilerParams(vmem_limit_bytes=12 * 1024 * 1024),
    )(counts, own, near, others, target, attended, hidden, stats, w_out, readout_weight)


def query_kernel(
    k_ref,
    v_ref,
    khalo_ref,
    vhalo_ref,
    grad_ref,
    packed_ref,
    probs_ref,
    own_probs_ref,
    inverse_ref,
    own_inverse_ref,
    dq_ref,
    dscores,
    own_dscores,
):
    step = pl.program_id(0)
    low_q = iota((BLOCK, PAIR), 1) < HEAD_WIDTH
    low_k = iota((2 * WIN, PAIR), 1) < HEAD_WIDTH
    own_fill = (spare_lane((BLOCK, PAIR)) < 3).astype(BF)
    halo_fill = (spare_lane((2 * WIN, PAIR)) < 3).astype(BF)
    g_fill = dot_nn(packed_ref[:, 128:], stat_spread(step, HEADS)).astype(BF)
    turned = []
    for pair in range(2):
        columns = slice(pair * PAIR, (pair + 1) * PAIR)
        g_pair = grad_ref[:, columns]
        own_turned = k_ref[:, columns].T
        halo_turned = khalo_ref[:, columns].T
        for half in range(2):
            slot = pair * 2 + half
            pick_q = low_q if half == 0 else ~low_q
            pick_k = low_k if half == 0 else ~low_k
            g_head = jnp.where(pick_q, g_pair, g_fill[:, columns])
            own_change = dot_nt(jnp.where(pick_q, v_ref[:, columns], own_fill), g_head)
            own_dscores[slot] = (own_probs_ref[slot].astype(F32) * own_change).astype(BF)
            change = dot_nt(jnp.where(pick_k, vhalo_ref[:, columns], halo_fill), g_head)
            dscores[slot] = (probs_ref[slot].astype(F32) * change).astype(BF)
            lanes = slice(half * HEAD_WIDTH, (half + 1) * HEAD_WIDTH)
            turned.append((own_turned[lanes], halo_turned[lanes]))
    for slot in range(4):
        row = pl.ds(step * 4 + slot, 1)
        dquery = dot_nn(turned[slot][0], own_dscores[slot]) * own_inverse_ref[row, :]
        dquery += dot_nn(turned[slot][1], dscores[slot]) * inverse_ref[row, :]
        dq_ref[slot * HEAD_WIDTH : (slot + 1) * HEAD_WIDTH] = (
            dquery * HEAD_WIDTH ** (-0.5)
        ).astype(BF)


def query_grads(projected, khalo, vhalo, grad, packed, probs, own_probs, inverse, own_inverse):
    part = lambda rows, first: pl.BlockSpec((rows, WIDTH), lambda j: (0, first + j))
    heads = lambda rows: pl.BlockSpec((4, rows, BLOCK), lambda j: (j, 0, 0))
    whole = pl.BlockSpec((HEADS, BLOCK), lambda j: (0, 0))
    return pl.pallas_call(
        query_kernel,
        grid=(4,),
        in_specs=[
            part(BLOCK, 4),
            part(BLOCK, 8),
            part(2 * WIN, 0),
            part(2 * WIN, 0),
            part(BLOCK, 0),
            pl.BlockSpec((BLOCK, 256), lambda j: (0, 0)),
            heads(2 * WIN),
            heads(BLOCK),
            whole,
            whole,
        ],
        out_specs=pl.BlockSpec((WIDTH, BLOCK), lambda j: (j, 0)),
        out_shape=jax.ShapeDtypeStruct((1024, BLOCK), BF),
        scratch_shapes=[
            pltpu.VMEM((4, 2 * WIN, BLOCK), BF),
            pltpu.VMEM((4, BLOCK, BLOCK), BF),
        ],
        compiler_params=pltpu.CompilerParams(vmem_limit_bytes=16 * 1024 * 1024),
        cost_estimate=pl.CostEstimate(
            flops=6 << 30, bytes_accessed=5 << 20, transcendentals=3 << 20
        ),
    )(
        projected,
        projected,
        khalo,
        vhalo,
        grad,
        packed,
        probs,
        own_probs,
        inverse,
        own_inverse,
    )


def key_kernel(
    counts_ref,
    q_ref,
    k_ref,
    v_ref,
    qhalo_ref,
    grad_ref,
    own_ref,
    left_ref,
    right_ref,
    w_out_ref,
    readout_ref,
    out_ref,
    probs,
    dscores,
    dhidden,
):
    step = pl.program_id(0)

    @pl.when(step == 0)
    def _():
        probs[...] = jnp.zeros_like(probs)
        dscores[...] = jnp.zeros_like(dscores)
        dhidden[:WIN] = dot_nt(left_ref[:, :128], readout_ref[...]).astype(BF)
        dhidden[WIN:] = dot_nt(right_ref[:, :128], readout_ref[...]).astype(BF)

    ghalo = dot_nt(dhidden[...], w_out_ref[...]).astype(BF)
    terms = jnp.concatenate(
        [left_ref[:, 128:], own_ref[:, 128:], right_ref[:, 128:]], axis=0
    )
    window = terms.shape[0]
    fill = key_fill([(counts_ref[1], BLOCK)])
    value_fill = (spare_lane(fill.shape) < 3).astype(BF)
    low_q = iota((window, PAIR), 1) < HEAD_WIDTH
    low_k = iota(fill.shape, 1) < HEAD_WIDTH
    ones = (spare_lane((window, WIDTH)) == 3).astype(F32)
    q_fill = (dot_nn(terms, stat_spread(step, 0)) + ones).astype(BF)
    g_fill = dot_nn(terms, stat_spread(step, HEADS)).astype(BF)
    turned = []
    for pair in range(2):
        columns = slice(pair * PAIR, (pair + 1) * PAIR)
        q_pair = jnp.concatenate(
            [qhalo_ref[:WIN, columns], q_ref[:, columns], qhalo_ref[WIN:, columns]], axis=0
        ) * jnp.asarray(HEAD_WIDTH ** (-0.5), BF)
        g_pair = jnp.concatenate(
            [ghalo[:WIN, columns], grad_ref[:, columns], ghalo[WIN:, columns]], axis=0
        )
        k_pair = k_ref[:, columns]
        v_pair = v_ref[:, columns]
        q_turned = q_pair.T
        g_turned = g_pair.T
        for half in range(2):
            slot = pair * 2 + half
            pick_q = low_q if half == 0 else ~low_q
            pick_k = low_k if half == 0 else ~low_k
            q_head = jnp.where(pick_q, q_pair, q_fill[:, columns])
            g_head = jnp.where(pick_q, g_pair, g_fill[:, columns])
            k_head = jnp.where(pick_k, k_pair, fill)
            v_head = jnp.where(pick_k, v_pair, value_fill)
            scores = dot_nt(q_head, k_head)
            change = dot_nt(g_head, v_head)
            for tile in range(2):
                rows = slice(tile * 128, tile * 128 + 640)
                lanes = slice(tile * 128, tile * 128 + 128)
                weight = keep_band(jnp.exp(scores[rows, lanes]), 0.0)
                moved = change[rows, lanes]
                start = tile * 128
                for piece, (low, high) in zip(weight, ((0, 128), (128, 512), (512, 640))):
                    place = slice(start + low, start + high)
                    probs[slot, place, lanes] = piece.astype(BF)
                    dscores[slot, place, lanes] = (piece * moved[low:high]).astype(BF)
            lanes = slice(half * HEAD_WIDTH, (half + 1) * HEAD_WIDTH)
            turned.append((q_turned[lanes], g_turned[lanes]))
    for slot in range(4):
        place = slice(slot * HEAD_WIDTH, (slot + 1) * HEAD_WIDTH)
        out_ref[0, place] = dot_nn(turned[slot][0], dscores[slot]).astype(BF)
        out_ref[1, place] = dot_nn(turned[slot][1], probs[slot]).astype(BF)


def key_grads(counts, projected, qhalo, grad, own, left, right, w_out, readout_weight):
    part = lambda rows, first: pl.BlockSpec((rows, WIDTH), lambda j: (0, first + j))
    whole = lambda *shape: pl.BlockSpec(shape, lambda j: (0, 0))
    window = 2 * WIN + BLOCK
    return pl.pallas_call(
        key_kernel,
        grid=(4,),
        in_specs=[
            pl.BlockSpec(memory_space=pltpu.SMEM),
            part(BLOCK, 0),
            part(BLOCK, 4),
            part(BLOCK, 8),
            part(2 * WIN, 0),
            part(BLOCK, 0),
            whole(BLOCK, 256),
            whole(BLOCK, 256),
            whole(BLOCK, 256),
            pl.BlockSpec((WIDTH, 1024), lambda j: (j, 0)),
            whole(1024, 128),
        ],
        out_specs=pl.BlockSpec((2, WIDTH, BLOCK), lambda j: (0, j, 0)),
        out_shape=jax.ShapeDtypeStruct((2, 1024, BLOCK), BF),
        scratch_shapes=[
            pltpu.VMEM((4, window, BLOCK), BF),
            pltpu.VMEM((4, window, BLOCK), BF),
            pltpu.VMEM((2 * WIN, 1024), BF),
        ],
        compiler_params=pltpu.CompilerParams(vmem_limit_bytes=18 * 1024 * 1024),
        cost_estimate=FREE,
    )(
        counts,
        projected,
        projected,
        projected,
        qhalo,
        in_hbm(grad),
        own,
        in_hbm(left),
        in_hbm(right),
        in_hbm(w_out),
        readout_weight,
    )


AXES = ("x_hi", "core", "y", "x_lo", "z")
MEMBER = ("x_hi", "core")
CELLS = ("y", "x_lo", "z")
CHIPS = ("x_hi", "y", "x_lo", "z")
SWAP = [(0, 1), (1, 0)]


def swap_core(values):
    return lax.ppermute(values, "core", SWAP)


def scatter(partial):
    columns = partial.shape[1]
    return lax.all_to_all(partial.reshape(64, 8, columns), CHIPS, split_axis=0, concat_axis=0)


def add_up(pieces):
    return jnp.sum(pieces.astype(F32), axis=0)


def per_device(latent, counts, w_qkv, w_out, readout_weight, target):
    latent_own = latent[0]
    cell_count = 32
    cell_index = lax.axis_index(CELLS)
    member_index = lax.axis_index(MEMBER)
    core = lax.axis_index("core")
    up = [(i, i + 1) for i in range(cell_count - 1)]
    down = [(i + 1, i) for i in range(cell_count - 1)]
    from_left = lax.ppermute(latent_own, CELLS, up)
    from_right = lax.ppermute(latent_own, CELLS, down)

    own_count = counts[cell_index]
    left_count = jnp.where(cell_index > 0, counts[jnp.maximum(cell_index - 1, 0)], 0)
    right_count = jnp.where(
        cell_index < cell_count - 1, counts[jnp.minimum(cell_index + 1, cell_count - 1)], 0
    )
    scalars = jnp.stack([left_count, own_count, right_count])

    projected, turned = project(latent_own, w_qkv)
    turned_other = swap_core(turned)
    own_probs, *own = own_part(scalars, projected)
    (
        normed_halo,
        khalo,
        vhalo,
        attended,
        stats,
        hidden,
        forecast,
        probs,
        inverse,
        own_inverse,
    ) = forward(
        scalars, from_left, from_right, latent_own, w_qkv, projected, own, w_out, readout_weight
    )
    near = lax.ppermute(forecast, "x_hi", SWAP)
    qhalo = halo_queries(normed_halo, w_qkv)
    near, qhalo = lax.optimization_barrier((near, qhalo))
    others = swap_core(jnp.stack([forecast, near]))
    crps_whole, packed, sent, grad, small = score(
        scalars, forecast, near, others, target, attended, hidden, stats, w_out, readout_weight
    )
    crps = lax.dynamic_slice_in_dim(crps_whole, member_index * 32, 32, 1)
    packed_left = lax.ppermute(sent, CELLS, up)
    packed_right = lax.ppermute(sent, CELLS, down)

    dquery = query_grads(
        projected, khalo, vhalo, grad, packed, probs, own_probs, inverse, own_inverse
    )
    dquery, packed_left, packed_right = lax.optimization_barrier(
        (dquery, packed_left, packed_right)
    )

    first_part = partial_sums(
        core, turned, turned_other, dquery, swap_core(dquery), (small, swap_core(small))
    )
    first_part, scalars = lax.optimization_barrier((first_part, scalars))
    first = scatter(first_part)
    pairs = key_grads(
        scalars,
        projected,
        qhalo,
        grad,
        packed,
        packed_left,
        packed_right,
        w_out,
        readout_weight,
    )
    pairs = pairs.reshape(2048, BLOCK)
    second_part = partial_sums(core, turned, turned_other, pairs, swap_core(pairs))
    second_part, first = lax.optimization_barrier((second_part, first))
    second = add_up(scatter(second_part))
    first = add_up(first)
    grad_out = lax.dot_general(
        first[:, 1024:1152],
        readout_weight.astype(F32),
        (((1,), (1,)), ((), ())),
        precision=lax.Precision.HIGHEST,
        preferred_element_type=F32,
    )
    grads = jnp.concatenate([first[:, :1024], second, grad_out, first[:, 1152:]], axis=1)
    return (crps, grads)


def solution(mesh):
    fine = jax.sharding.Mesh(mesh.devices.reshape(2, 2, 4, 2, 4), AXES)
    placed = (P(MEMBER, CELLS, None), P(), P(), P(), P(), P(CELLS, None))
    return jax.shard_map(
        per_device,
        mesh=fine,
        in_specs=placed,
        out_specs=(P(CELLS, MEMBER), P(MEMBER + CELLS, None)),
        check_vma=False,
    )
```

```python
import functools

import jax
import jax.numpy as jnp
import numpy as np
from jax import lax
from jax.experimental import pallas as pl
from jax.experimental.pallas import tpu as pltpu
from jax.sharding import PartitionSpec as P

HEADS = 16
WIN = 256
BLOCK = 256
WIDTH = 256
HEAD_WIDTH = 64
PAIR = 128
NEVER = -1e30

alpha_fair = 0.95
smooth_width = 0.0625

BF = jnp.bfloat16
F32 = jnp.float32


def smooth_abs(values):
    return jnp.sqrt(values * values + smooth_width)


def smooth_sign(values):
    return values * lax.rsqrt(values * values + smooth_width)


def layer_norm(latent_rows):
    values = latent_rows.astype(F32)
    center = values - jnp.mean(values, axis=-1, keepdims=True)
    spread = jnp.mean(center * center, axis=-1, keepdims=True)
    return (center * lax.rsqrt(spread + 1e-05)).astype(BF)


def dot_nn(left, right):
    return lax.dot_general(left, right, (((1,), (0,)), ((), ())), preferred_element_type=F32)


def dot_nt(left, right):
    return lax.dot_general(left, right, (((1,), (1,)), ((), ())), preferred_element_type=F32)


def dot_tn(left, right):
    return lax.dot_general(left, right, (((0,), (0,)), ((), ())), preferred_element_type=F32)


def iota(shape, axis):
    return lax.broadcasted_iota(jnp.int32, shape, axis)


FREE = pl.CostEstimate(flops=0, bytes_accessed=0, transcendentals=0)
HBM = pl.BlockSpec(memory_space=pltpu.HBM)


def in_hbm(values):
    return pltpu.with_memory_space_constraint(values, pltpu.HBM)


def fetches(weight_ref, buffer, arrived, width, first):
    return [
        pltpu.make_async_copy(
            weight_ref.at[:, pl.ds(first + place * width, width)],
            buffer.at[place],
            arrived.at[place],
        )
        for place in range(buffer.shape[0])
    ]


def fetch_one(weight_ref, buffer, arrived, width, first, place):
    start = pl.multiple_of(first + place * width, width)
    return pltpu.make_async_copy(
        weight_ref.at[:, pl.ds(start, width)], buffer.at[place], arrived.at[place]
    )


def project_kernel(latent_ref, weight_ref, projected_ref, turned_ref, normed, buffer, arrived):
    step = pl.program_id(0)

    @pl.when(step == 0)
    def _():
        for copy in fetches(weight_ref, buffer, arrived, 512, 0):
            copy.start()
        normed[...] = layer_norm(latent_ref[...])
        turned_ref[...] = normed[...].T

    fetch_one(weight_ref, buffer, arrived, 512, 0, step).wait()
    projected_ref[...] = dot_nn(normed[...], buffer[step]).astype(BF)


def project(latent_own, w_qkv):
    rows, width = latent_own.shape
    return pl.pallas_call(
        project_kernel,
        grid=(6,),
        in_specs=[pl.BlockSpec((rows, width), lambda j: (0, 0)), HBM],
        out_specs=[
            pl.BlockSpec((rows, 512), lambda j: (0, j)),
            pl.BlockSpec((width, rows), lambda j: (0, 0)),
        ],
        out_shape=[
            jax.ShapeDtypeStruct((rows, 3 * width), BF),
            jax.ShapeDtypeStruct((width, rows), BF),
        ],
        scratch_shapes=[
            pltpu.VMEM((rows, width), BF),
            pltpu.VMEM((6, width, 512), BF),
            pltpu.SemaphoreType.DMA((6,)),
        ],
        compiler_params=pltpu.CompilerParams(vmem_limit_bytes=16 * 1024 * 1024),
        cost_estimate=pl.CostEstimate(
            flops=2 * rows * width * width * 4, bytes_accessed=8 << 20, transcendentals=0
        ),
    )(latent_own, in_hbm(w_qkv))


def halo_query_kernel(normed_ref, weight_ref, out_ref, buffer, arrived):
    step = pl.program_id(0)

    @pl.when(step == 0)
    def _():
        for copy in fetches(weight_ref, buffer, arrived, 256, 0):
            copy.start()

    fetch_one(weight_ref, buffer, arrived, 256, 0, step).wait()
    out_ref[...] = dot_nn(normed_ref[...], buffer[step]).astype(BF)


def halo_queries(normed_halo, w_qkv):
    rows, width = normed_halo.shape
    return pl.pallas_call(
        halo_query_kernel,
        grid=(4,),
        in_specs=[pl.BlockSpec((rows, width), lambda j: (0, 0)), HBM],
        out_specs=pl.BlockSpec((rows, 256), lambda j: (0, j)),
        out_shape=jax.ShapeDtypeStruct((rows, width), BF),
        scratch_shapes=[
            pltpu.VMEM((4, width, 256), BF),
            pltpu.SemaphoreType.DMA((4,)),
        ],
        compiler_params=pltpu.CompilerParams(vmem_limit_bytes=12 * 1024 * 1024),
        cost_estimate=FREE,
    )(normed_halo, in_hbm(w_qkv))


def partial_kernel(
    smalls, core_ref, normed_ref, normed_other_ref, piece_ref, other_ref, *refs
):
    small_refs, (out_ref, rows, pieces, others, sums, staged, arrived, left) = (
        refs[:smalls],
        refs[smalls:],
    )
    core = core_ref[0]
    chunks = piece_ref.shape[0] // 512
    sources = [
        (normed_ref.at[:, core], rows.at[0]),
        (normed_other_ref.at[:, core], rows.at[1]),
    ]
    for chunk in range(chunks):
        part = pl.ds(chunk * 512, 512)
        sources.append((piece_ref.at[part], pieces.at[chunk]))
        sources.append((other_ref.at[part], others.at[chunk]))
    for place, small_ref in enumerate(small_refs):
        sources.append((small_ref.at[:, core], sums.at[place]))
    copies = [
        pltpu.make_async_copy(source, target, arrived.at[place])
        for place, (source, target) in enumerate(sources)
    ]
    for copy in copies:
        copy.start()
    copies[0].wait()
    copies[1].wait()
    writes = []
    for chunk in range(chunks):
        copies[2 + 2 * chunk].wait()
        copies[3 + 2 * chunk].wait()
        for top in range(2):
            staged[chunk, top * 256 : (top + 1) * 256] = (
                dot_nt(rows[0, top], pieces[chunk]) + dot_nt(rows[1, top], others[chunk])
            ).astype(BF)
        writes.append(
            pltpu.make_async_copy(
                staged.at[chunk], out_ref.at[:, pl.ds(chunk * 512, 512)], left.at[chunk]
            )
        )
        writes[-1].start()
    if smalls:
        copies[-2].wait()
        copies[-1].wait()
        for top in range(2):
            staged[chunks, top * 256 : (top + 1) * 256, :256] = (
                sums[0, top].astype(F32) + sums[1, top].astype(F32)
            ).astype(BF)
        writes.append(
            pltpu.make_async_copy(
                staged.at[chunks, :, pl.ds(0, 256)],
                out_ref.at[:, pl.ds(chunks * 512, 256)],
                left.at[chunks],
            )
        )
        writes[-1].start()
    for write in writes:
        write.wait()


def partial_sums(core, turned, turned_other, piece, other, smalls=()):
    by_core = lambda values: values.reshape(2, 2, 256, 256)
    anywhere = pl.BlockSpec(memory_space=pl.ANY)
    chunks = piece.shape[0] // 512
    columns = piece.shape[0] + 256 * (len(smalls) // 2)
    return pl.pallas_call(
        functools.partial(partial_kernel, len(smalls)),
        in_specs=[pl.BlockSpec(memory_space=pltpu.SMEM)] + [anywhere] * (4 + len(smalls)),
        out_specs=anywhere,
        out_shape=jax.ShapeDtypeStruct((512, columns), BF),
        scratch_shapes=[
            pltpu.VMEM((2, 2, 256, 256), BF),
            pltpu.VMEM((chunks, 512, 256), BF),
            pltpu.VMEM((chunks, 512, 256), BF),
            pltpu.VMEM((2, 2, 256, 256), BF),
            pltpu.VMEM((chunks + 1, 512, 512), BF),
            pltpu.SemaphoreType.DMA((2 + 2 * chunks + len(smalls),)),
            pltpu.SemaphoreType.DMA((chunks + 1,)),
        ],
        compiler_params=pltpu.CompilerParams(vmem_limit_bytes=14 * 1024 * 1024),
        cost_estimate=FREE,
    )(
        core.astype(jnp.int32).reshape(1),
        by_core(turned),
        by_core(turned_other),
        piece,
        other,
        *(by_core(small) for small in smalls),
    )


def spare_lane(shape):
    lane = iota(shape, len(shape) - 1)
    return lane % HEAD_WIDTH


def key_fill(count_pieces):
    fills = []
    for count, rows in count_pieces:
        spare = spare_lane((rows, PAIR))
        bias = jnp.where(iota((rows, PAIR), 0) < count, 0.0, NEVER)
        fills.append(
            jnp.where(spare < 3, 1.0, jnp.where(spare == 3, bias, 0.0)).astype(BF)
        )
    return jnp.concatenate(fills, axis=0)


def stat_spread(step, offset):
    shape = (128, WIDTH)
    lane = iota(shape, 1)
    head = step * 4 + 2 * (lane // PAIR) + jnp.where(lane % PAIR < HEAD_WIDTH, 1, 0)
    term = lane % HEAD_WIDTH
    chosen = (term < 3) & (iota(shape, 0) == term * 32 + offset + head)
    return jnp.where(chosen, -1.0, 0.0).astype(BF)


def keep_band(window, fill):
    shape = (128, 128)
    apart = iota(shape, 0) - iota(shape, 1)
    first = jnp.where(apart >= 0, window[:128], fill)
    last = jnp.where(apart <= 0, window[-128:], fill)
    return first, window[128:-128], last


def own_kernel(counts_ref, q_ref, k_ref, v_ref, probs, mixed_ref, top_ref, total_ref):
    step = pl.program_id(0)
    fill = key_fill([(counts_ref[1], BLOCK)])
    low = iota((BLOCK, PAIR), 1) < HEAD_WIDTH
    query_fill = (spare_lane((BLOCK, PAIR)) == 3).astype(BF)
    ones = jnp.ones((16, BLOCK), BF)
    scores, turned = [], []
    for pair in range(2):
        columns = slice(pair * PAIR, (pair + 1) * PAIR)
        q_pair = q_ref[:, columns] * jnp.asarray(HEAD_WIDTH ** (-0.5), BF)
        k_pair = k_ref[:, columns]
        turned.append(v_ref[:, columns].T)
        for half in range(2):
            pick = low if half == 0 else ~low
            scores.append(
                dot_nt(jnp.where(pick, k_pair, fill), jnp.where(pick, q_pair, query_fill))
            )
    for slot in range(4):
        top = jnp.max(scores[slot], axis=0, keepdims=True)
        probs[slot] = jnp.exp(scores[slot] - top).astype(BF)
        top_ref[pl.ds(step * 4 + slot, 1), :] = top
    for slot in range(4):
        lanes = slice(slot % 2 * HEAD_WIDTH, (slot % 2 + 1) * HEAD_WIDTH)
        values = jnp.concatenate([turned[slot // 2][lanes], ones], axis=0)
        mixed = dot_nn(values, probs[slot])
        mixed_ref[slot * HEAD_WIDTH : (slot + 1) * HEAD_WIDTH] = mixed[:HEAD_WIDTH]
        total_ref[pl.ds(step * 4 + slot, 1), :] = mixed[HEAD_WIDTH : HEAD_WIDTH + 1]


def own_part(counts, projected):
    part = lambda rows, first: pl.BlockSpec((rows, WIDTH), lambda j: (0, first + j))
    whole = pl.BlockSpec((HEADS, BLOCK), lambda j: (0, 0))
    return pl.pallas_call(
        own_kernel,
        grid=(4,),
        in_specs=[
            pl.BlockSpec(memory_space=pltpu.SMEM),
            part(BLOCK, 0),
            part(BLOCK, 4),
            part(BLOCK, 8),
        ],
        out_specs=[
            pl.BlockSpec((4, BLOCK, BLOCK), lambda j: (j, 0, 0)),
            pl.BlockSpec((WIDTH, BLOCK), lambda j: (j, 0)),
            whole,
            whole,
        ],
        out_shape=[
            jax.ShapeDtypeStruct((HEADS, BLOCK, BLOCK), BF),
            jax.ShapeDtypeStruct((1024, BLOCK), F32),
            jax.ShapeDtypeStruct((HEADS, BLOCK), F32),
            jax.ShapeDtypeStruct((HEADS, BLOCK), F32),
        ],
        compiler_params=pltpu.CompilerParams(vmem_limit_bytes=14 * 1024 * 1024),
        cost_estimate=pl.CostEstimate(
            flops=1 << 30, bytes_accessed=4 << 20, transcendentals=1 << 20
        ),
    )(counts, projected, projected, projected)


def forward_kernel(
    counts_ref,
    left_ref,
    right_ref,
    latent_ref,
    weight_ref,
    q_ref,
    own_mixed_ref,
    own_top_ref,
    own_total_ref,
    w_out_ref,
    readout_ref,
    normed_ref,
    khalo_ref,
    vhalo_ref,
    attended_ref,
    stats_ref,
    hidden_ref,
    forecast_ref,
    probs,
    inverse_ref,
    own_inverse_ref,
    stat_rows,
    buffer,
    arrived,
):
    step = pl.program_id(0)

    @pl.when(step == 0)
    def _():
        copies = fetches(weight_ref, buffer, arrived, WIDTH, 1024)
        for place in (0, 4, 1, 5, 2, 6, 3, 7):
            copies[place].start()
        normed_ref[:WIN] = layer_norm(left_ref[...])
        normed_ref[WIN:] = layer_norm(right_ref[...])

    fetch_one(weight_ref, buffer, arrived, WIDTH, 1024, step).wait()
    fetch_one(weight_ref, buffer, arrived, WIDTH, 1024, step + 4).wait()
    khalo_ref[...] = dot_nn(normed_ref[...], buffer[step]).astype(BF)
    vhalo_ref[...] = dot_nn(normed_ref[...], buffer[step + 4]).astype(BF)
    fill = key_fill([(counts_ref[0], WIN), (counts_ref[2], WIN)])
    low_q = iota((BLOCK, PAIR), 1) < HEAD_WIDTH
    low_k = iota(fill.shape, 1) < HEAD_WIDTH
    query_fill = (spare_lane((BLOCK, PAIR)) == 3).astype(BF)
    scores, turned = [], []
    for pair in range(2):
        columns = slice(pair * PAIR, (pair + 1) * PAIR)
        q_pair = q_ref[:, columns] * jnp.asarray(HEAD_WIDTH ** (-0.5), BF)
        k_pair = khalo_ref[:, columns]
        turned.append(vhalo_ref[:, columns].T)
        for half in range(2):
            if half == 0:
                q_head = jnp.where(low_q, q_pair, query_fill)
                k_head = jnp.where(low_k, k_pair, fill)
            else:
                q_head = jnp.where(low_q, query_fill, q_pair)
                k_head = jnp.where(low_k, fill, k_pair)
            scores.append(dot_nt(k_head, q_head))
    tops = []
    for slot in range(4):
        levels = []
        for tile in range(2):
            rows = slice(tile * 128, tile * 128 + 384)
            lanes = slice(tile * 128, tile * 128 + 128)
            first, middle, last = keep_band(scores[slot][rows, lanes], NEVER)
            top = jnp.maximum(
                jnp.max(middle, axis=0, keepdims=True),
                jnp.max(jnp.maximum(first, last), axis=0, keepdims=True),
            )
            top = jnp.maximum(top, own_top_ref[pl.ds(step * 4 + slot, 1), :][:, lanes])
            start = tile * 128
            probs[slot, start : start + 128, lanes] = jnp.exp(first - top).astype(BF)
            probs[slot, start + 128 : start + 256, lanes] = jnp.exp(middle - top).astype(BF)
            probs[slot, start + 256 : start + 384, lanes] = jnp.exp(last - top).astype(BF)
            levels.append(top)
        probs[slot, :128, 128:] = jnp.zeros((128, 128), BF)
        probs[slot, 384:, :128] = jnp.zeros((128, 128), BF)
        tops.append(jnp.concatenate(levels, axis=1))
    ones = jnp.ones((16, fill.shape[0]), BF)
    for pair in range(2):
        halves = []
        for half in range(2):
            slot = pair * 2 + half
            lanes = slice(half * HEAD_WIDTH, (half + 1) * HEAD_WIDTH)
            values = jnp.concatenate([turned[pair][lanes], ones], axis=0)
            mixed = dot_nn(values, probs[slot])
            head = step * 4 + slot
            fade = jnp.exp(own_top_ref[pl.ds(head, 1), :] - tops[slot])
            total = mixed[HEAD_WIDTH : HEAD_WIDTH + 1]
            total += own_total_ref[pl.ds(head, 1), :] * fade
            inverse = 1.0 / total
            own_inverse = fade * inverse
            own_mixed = own_mixed_ref[slot * HEAD_WIDTH : (slot + 1) * HEAD_WIDTH]
            halves.append(mixed[:HEAD_WIDTH] * inverse + own_mixed * own_inverse)
            own_inverse_ref[pl.ds(head, 1), :] = own_inverse
            inverse_ref[pl.ds(head, 1), :] = inverse
            stat_rows[pl.ds(head, 1), :] = tops[slot] + jnp.log(total)
        start = pl.multiple_of(step * WIDTH + pair * PAIR, PAIR)
        attended_ref[:, pl.ds(start, PAIR)] = jnp.concatenate(halves, axis=0).T

    @pl.when(step == 3)
    def _():
        mixed = dot_nn(attended_ref[...].astype(BF), w_out_ref[...])
        hidden = (latent_ref[...].astype(F32) + mixed).astype(BF)
        hidden_ref[...] = hidden
        forecast_ref[...] = dot_nn(hidden, readout_ref[...])
        stat_rows[HEADS:] = jnp.zeros((128 - HEADS, BLOCK), F32)
        stats_ref[...] = stat_rows[...].T


def forward(counts, left, right, latent_own, w_qkv, projected, own, w_out, readout_weight):
    whole = lambda *shape: pl.BlockSpec(shape, lambda j: (0, 0))
    part = lambda rows, first: pl.BlockSpec((rows, WIDTH), lambda j: (0, first + j))
    window = 2 * WIN + BLOCK
    return pl.pallas_call(
        forward_kernel,
        grid=(4,),
        in_specs=[
            pl.BlockSpec(memory_space=pltpu.SMEM),
            whole(WIN, 1024),
            whole(WIN, 1024),
            whole(BLOCK, 1024),
            HBM,
            part(BLOCK, 0),
            pl.BlockSpec((WIDTH, BLOCK), lambda j: (j, 0)),
            whole(HEADS, BLOCK),
            whole(HEADS, BLOCK),
            whole(1024, 1024),
            whole(1024, 128),
        ],
        out_specs=[
            whole(2 * WIN, 1024),
            part(2 * WIN, 0),
            part(2 * WIN, 0),
            whole(BLOCK, 1024),
            whole(BLOCK, 128),
            whole(BLOCK, 1024),
            whole(BLOCK, 128),
            pl.BlockSpec((4, 2 * WIN, BLOCK), lambda j: (j, 0, 0)),
            whole(HEADS, BLOCK),
            whole(HEADS, BLOCK),
        ],
        out_shape=[
            jax.ShapeDtypeStruct((2 * WIN, 1024), BF),
            jax.ShapeDtypeStruct((2 * WIN, 1024), BF),
            jax.ShapeDtypeStruct((2 * WIN, 1024), BF),
            jax.ShapeDtypeStruct((BLOCK, 1024), F32),
            jax.ShapeDtypeStruct((BLOCK, 128), F32),
            jax.ShapeDtypeStruct((BLOCK, 1024), BF),
            jax.ShapeDtypeStruct((BLOCK, 128), F32),
            jax.ShapeDtypeStruct((HEADS, 2 * WIN, BLOCK), BF),
            jax.ShapeDtypeStruct((HEADS, BLOCK), F32),
            jax.ShapeDtypeStruct((HEADS, BLOCK), F32),
        ],
        scratch_shapes=[
            pltpu.VMEM((128, BLOCK), F32),
            pltpu.VMEM((8, 1024, WIDTH), BF),
            pltpu.SemaphoreType.DMA((8,)),
        ],
        compiler_params=pltpu.CompilerParams(vmem_limit_bytes=30 * 1024 * 1024),
        cost_estimate=pl.CostEstimate(
            flops=6 << 30, bytes_accessed=12 << 20, transcendentals=3 << 20
        ),
    )(
        counts,
        left,
        right,
        latent_own,
        in_hbm(w_qkv),
        projected,
        *own,
        w_out,
        readout_weight,
    )


def crps_kernel(counts_ref, own_ref, near_ref, others_ref, target_ref, crps_ref):
    members = 4
    fair_eps = (1.0 - alpha_fair) / members
    coefficient = (1.0 - fair_eps) / (members * (members - 1))
    valid = (iota((BLOCK, 1), 0) < counts_ref[1]).astype(F32)
    forecasts = [own_ref[...], near_ref[...], others_ref[0], others_ref[1]]
    target = target_ref[...]
    error = jnp.zeros_like(target)
    for forecast in forecasts:
        error += smooth_abs(forecast - target)
    spread = jnp.full_like(target, members * smooth_width**0.5)
    for first in range(members):
        for second in range(first + 1, members):
            spread += 2.0 * smooth_abs(forecasts[first] - forecasts[second])
    crps_ref[...] = valid * (error / members - 0.5 * coefficient * spread)


def crps_of(counts, own, near, others, target):
    vmem = pl.BlockSpec(memory_space=pltpu.VMEM)
    return pl.pallas_call(
        crps_kernel,
        in_specs=[pl.BlockSpec(memory_space=pltpu.SMEM)] + [vmem] * 4,
        out_specs=vmem,
        out_shape=jax.ShapeDtypeStruct((BLOCK, 128), F32),
        compiler_params=pltpu.CompilerParams(vmem_limit_bytes=8 * 1024 * 1024),
        cost_estimate=FREE,
    )(counts, own, near, others, in_hbm(target))


def score_kernel(
    counts_ref,
    own_ref,
    near_ref,
    others_ref,
    target_ref,
    attended_ref,
    hidden_ref,
    stats_ref,
    w_out_ref,
    readout_ref,
    packed_ref,
    sent_ref,
    grad_ref,
    small_ref,
):
    members = 4
    fair_eps = (1.0 - alpha_fair) / members
    coefficient = (1.0 - fair_eps) / (members * (members - 1))
    valid = (iota((BLOCK, 1), 0) < counts_ref[1]).astype(F32)
    own = own_ref[...]
    target = target_ref[...]
    pull = jnp.zeros_like(target)
    for other in (near_ref[...], others_ref[0], others_ref[1]):
        pull += smooth_sign(own - other)
    slope = (
        valid / 128 * (smooth_sign(own - target) / members - coefficient * pull)
    ).astype(BF)
    dhidden = dot_nt(slope, readout_ref[...]).astype(BF)
    dattended = dot_nt(dhidden, w_out_ref[...]).astype(BF)
    grad_ref[...] = dattended
    attended = attended_ref[...]
    product = dattended.astype(F32) * attended
    high = product.astype(BF)
    low = (product - high.astype(F32)).astype(BF)
    pick = (iota((1024, 128), 0) // HEAD_WIDTH + HEADS == iota((1024, 128), 1)).astype(BF)
    stats = stats_ref[...] + dot_nn(high, pick) + dot_nn(low, pick)
    first = stats.astype(BF)
    rest = stats - first.astype(F32)
    second = rest.astype(BF)
    third = (rest - second.astype(F32)).astype(BF)
    terms = jnp.zeros((BLOCK, 128), F32)
    for place, term in enumerate((first, second, third)):
        shift = (iota((128, 128), 0) + 32 * place == iota((128, 128), 1)) & (
            iota((128, 128), 0) < 32
        )
        terms += dot_nn(term, shift.astype(BF))
    packed_ref[:, :128] = slope
    packed_ref[:, 128:] = terms.astype(BF)
    sent_ref[...] = packed_ref[...]
    small_ref[:, :128] = dot_tn(attended.astype(BF), slope).astype(BF)
    small_ref[:, 128:] = dot_tn(hidden_ref[...], slope).astype(BF)


def score(counts, own, near, others, target, attended, hidden, stats, w_out, readout_weight):
    vmem = pl.BlockSpec(memory_space=pltpu.VMEM)
    return pl.pallas_call(
        score_kernel,
        in_specs=[pl.BlockSpec(memory_space=pltpu.SMEM)] + [vmem] * 9,
        out_specs=[vmem] * 4,
        out_shape=[
            jax.ShapeDtypeStruct((BLOCK, 256), BF),
            pltpu.HBM((BLOCK, 256), BF),
            jax.ShapeDtypeStruct((BLOCK, 1024), BF),
            jax.ShapeDtypeStruct((1024, 256), BF),
        ],
        compiler_params=pltpu.CompilerParams(vmem_limit_bytes=12 * 1024 * 1024),
    )(counts, own, near, others, target, attended, hidden, stats, w_out, readout_weight)


def query_kernel(
    k_ref,
    v_ref,
    khalo_ref,
    vhalo_ref,
    grad_ref,
    packed_ref,
    probs_ref,
    own_probs_ref,
    inverse_ref,
    own_inverse_ref,
    dq_ref,
    dscores,
    own_dscores,
):
    step = pl.program_id(0)
    low_q = iota((BLOCK, PAIR), 1) < HEAD_WIDTH
    low_k = iota((2 * WIN, PAIR), 1) < HEAD_WIDTH
    own_fill = (spare_lane((BLOCK, PAIR)) < 3).astype(BF)
    halo_fill = (spare_lane((2 * WIN, PAIR)) < 3).astype(BF)
    g_fill = dot_nn(packed_ref[:, 128:], stat_spread(step, HEADS)).astype(BF)
    turned = []
    for pair in range(2):
        columns = slice(pair * PAIR, (pair + 1) * PAIR)
        g_pair = grad_ref[:, columns]
        own_turned = k_ref[:, columns].T
        halo_turned = khalo_ref[:, columns].T
        for half in range(2):
            slot = pair * 2 + half
            pick_q = low_q if half == 0 else ~low_q
            pick_k = low_k if half == 0 else ~low_k
            g_head = jnp.where(pick_q, g_pair, g_fill[:, columns])
            own_change = dot_nt(jnp.where(pick_q, v_ref[:, columns], own_fill), g_head)
            own_dscores[slot] = (own_probs_ref[slot].astype(F32) * own_change).astype(BF)
            change = dot_nt(jnp.where(pick_k, vhalo_ref[:, columns], halo_fill), g_head)
            dscores[slot] = (probs_ref[slot].astype(F32) * change).astype(BF)
            lanes = slice(half * HEAD_WIDTH, (half + 1) * HEAD_WIDTH)
            turned.append((own_turned[lanes], halo_turned[lanes]))
    for slot in range(4):
        row = pl.ds(step * 4 + slot, 1)
        dquery = dot_nn(turned[slot][0], own_dscores[slot]) * own_inverse_ref[row, :]
        dquery += dot_nn(turned[slot][1], dscores[slot]) * inverse_ref[row, :]
        dq_ref[slot * HEAD_WIDTH : (slot + 1) * HEAD_WIDTH] = (
            dquery * HEAD_WIDTH ** (-0.5)
        ).astype(BF)


def query_grads(projected, khalo, vhalo, grad, packed, probs, own_probs, inverse, own_inverse):
    part = lambda rows, first: pl.BlockSpec((rows, WIDTH), lambda j: (0, first + j))
    heads = lambda rows: pl.BlockSpec((4, rows, BLOCK), lambda j: (j, 0, 0))
    whole = pl.BlockSpec((HEADS, BLOCK), lambda j: (0, 0))
    return pl.pallas_call(
        query_kernel,
        grid=(4,),
        in_specs=[
            part(BLOCK, 4),
            part(BLOCK, 8),
            part(2 * WIN, 0),
            part(2 * WIN, 0),
            part(BLOCK, 0),
            pl.BlockSpec((BLOCK, 256), lambda j: (0, 0)),
            heads(2 * WIN),
            heads(BLOCK),
            whole,
            whole,
        ],
        out_specs=pl.BlockSpec((WIDTH, BLOCK), lambda j: (j, 0)),
        out_shape=jax.ShapeDtypeStruct((1024, BLOCK), BF),
        scratch_shapes=[
            pltpu.VMEM((4, 2 * WIN, BLOCK), BF),
            pltpu.VMEM((4, BLOCK, BLOCK), BF),
        ],
        compiler_params=pltpu.CompilerParams(vmem_limit_bytes=16 * 1024 * 1024),
        cost_estimate=pl.CostEstimate(
            flops=6 << 30, bytes_accessed=5 << 20, transcendentals=3 << 20
        ),
    )(
        projected,
        projected,
        khalo,
        vhalo,
        grad,
        packed,
        probs,
        own_probs,
        inverse,
        own_inverse,
    )


def key_kernel(
    counts_ref,
    q_ref,
    k_ref,
    v_ref,
    qhalo_ref,
    grad_ref,
    own_ref,
    left_ref,
    right_ref,
    w_out_ref,
    readout_ref,
    out_ref,
    probs,
    dscores,
    dhidden,
):
    step = pl.program_id(0)

    @pl.when(step == 0)
    def _():
        for slot in range(4):
            for held in (probs, dscores):
                held[slot, :128, 128:] = jnp.zeros((128, 128), BF)
                held[slot, 640:, :128] = jnp.zeros((128, 128), BF)
        dhidden[:WIN] = dot_nt(left_ref[:, :128], readout_ref[...]).astype(BF)
        dhidden[WIN:] = dot_nt(right_ref[:, :128], readout_ref[...]).astype(BF)

    ghalo = dot_nt(dhidden[...], w_out_ref[...]).astype(BF)
    terms = jnp.concatenate(
        [left_ref[:, 128:], own_ref[:, 128:], right_ref[:, 128:]], axis=0
    )
    window = terms.shape[0]
    fill = key_fill([(counts_ref[1], BLOCK)])
    value_fill = (spare_lane(fill.shape) < 3).astype(BF)
    low_q = iota((window, PAIR), 1) < HEAD_WIDTH
    low_k = iota(fill.shape, 1) < HEAD_WIDTH
    ones = (spare_lane((window, WIDTH)) == 3).astype(F32)
    q_fill = (dot_nn(terms, stat_spread(step, 0)) + ones).astype(BF)
    g_fill = dot_nn(terms, stat_spread(step, HEADS)).astype(BF)
    turned = []
    for pair in range(2):
        columns = slice(pair * PAIR, (pair + 1) * PAIR)
        q_pair = jnp.concatenate(
            [qhalo_ref[:WIN, columns], q_ref[:, columns], qhalo_ref[WIN:, columns]], axis=0
        ) * jnp.asarray(HEAD_WIDTH ** (-0.5), BF)
        g_pair = jnp.concatenate(
            [ghalo[:WIN, columns], grad_ref[:, columns], ghalo[WIN:, columns]], axis=0
        )
        k_pair = k_ref[:, columns]
        v_pair = v_ref[:, columns]
        q_turned = q_pair.T
        g_turned = g_pair.T
        for half in range(2):
            slot = pair * 2 + half
            pick_q = low_q if half == 0 else ~low_q
            pick_k = low_k if half == 0 else ~low_k
            q_head = jnp.where(pick_q, q_pair, q_fill[:, columns])
            g_head = jnp.where(pick_q, g_pair, g_fill[:, columns])
            k_head = jnp.where(pick_k, k_pair, fill)
            v_head = jnp.where(pick_k, v_pair, value_fill)
            scores = dot_nt(q_head, k_head)
            change = dot_nt(g_head, v_head)
            for tile in range(2):
                rows = slice(tile * 128, tile * 128 + 640)
                lanes = slice(tile * 128, tile * 128 + 128)
                weight = keep_band(jnp.exp(scores[rows, lanes]), 0.0)
                moved = change[rows, lanes]
                start = tile * 128
                for piece, (low, high) in zip(weight, ((0, 128), (128, 512), (512, 640))):
                    place = slice(start + low, start + high)
                    probs[slot, place, lanes] = piece.astype(BF)
                    dscores[slot, place, lanes] = (piece * moved[low:high]).astype(BF)
            lanes = slice(half * HEAD_WIDTH, (half + 1) * HEAD_WIDTH)
            turned.append((q_turned[lanes], g_turned[lanes]))
    for slot in range(4):
        place = slice(slot * HEAD_WIDTH, (slot + 1) * HEAD_WIDTH)
        out_ref[0, place] = dot_nn(turned[slot][0], dscores[slot]).astype(BF)
        out_ref[1, place] = dot_nn(turned[slot][1], probs[slot]).astype(BF)


def key_grads(counts, projected, qhalo, grad, own, left, right, w_out, readout_weight):
    part = lambda rows, first: pl.BlockSpec((rows, WIDTH), lambda j: (0, first + j))
    whole = lambda *shape: pl.BlockSpec(shape, lambda j: (0, 0))
    window = 2 * WIN + BLOCK
    return pl.pallas_call(
        key_kernel,
        grid=(4,),
        in_specs=[
            pl.BlockSpec(memory_space=pltpu.SMEM),
            part(BLOCK, 0),
            part(BLOCK, 4),
            part(BLOCK, 8),
            part(2 * WIN, 0),
            part(BLOCK, 0),
            whole(BLOCK, 256),
            whole(BLOCK, 256),
            whole(BLOCK, 256),
            pl.BlockSpec((WIDTH, 1024), lambda j: (j, 0)),
            whole(1024, 128),
        ],
        out_specs=pl.BlockSpec((2, WIDTH, BLOCK), lambda j: (0, j, 0)),
        out_shape=jax.ShapeDtypeStruct((2, 1024, BLOCK), BF),
        scratch_shapes=[
            pltpu.VMEM((4, window, BLOCK), BF),
            pltpu.VMEM((4, window, BLOCK), BF),
            pltpu.VMEM((2 * WIN, 1024), BF),
        ],
        compiler_params=pltpu.CompilerParams(vmem_limit_bytes=18 * 1024 * 1024),
        cost_estimate=FREE,
    )(
        counts,
        projected,
        projected,
        projected,
        qhalo,
        in_hbm(grad),
        in_hbm(own),
        in_hbm(left),
        in_hbm(right),
        in_hbm(w_out),
        readout_weight,
    )


AXES = ("x_hi", "core", "y", "x_lo", "z")
MEMBER = ("x_hi", "core")
CELLS = ("y", "x_lo", "z")
CHIPS = ("x_hi", "y", "x_lo", "z")
SWAP = [(0, 1), (1, 0)]


def swap_core(values):
    return lax.ppermute(values, "core", SWAP)


def scatter(partial):
    columns = partial.shape[1]
    return lax.all_to_all(partial.reshape(64, 8, columns), CHIPS, split_axis=0, concat_axis=0)


def add_up(pieces):
    return jnp.sum(pieces.astype(F32), axis=0)


def per_device(latent, counts, w_qkv, w_out, readout_weight, target):
    latent_own = latent[0]
    cell_count = 32
    cell_index = lax.axis_index(CELLS)
    member_index = lax.axis_index(MEMBER)
    core = lax.axis_index("core")
    up = [(i, i + 1) for i in range(cell_count - 1)]
    down = [(i + 1, i) for i in range(cell_count - 1)]
    from_left = lax.ppermute(latent_own, CELLS, up)
    from_right = lax.ppermute(latent_own, CELLS, down)

    own_count = counts[cell_index]
    left_count = jnp.where(cell_index > 0, counts[jnp.maximum(cell_index - 1, 0)], 0)
    right_count = jnp.where(
        cell_index < cell_count - 1, counts[jnp.minimum(cell_index + 1, cell_count - 1)], 0
    )
    scalars = jnp.stack([left_count, own_count, right_count])

    projected, turned = project(latent_own, w_qkv)
    turned_other = swap_core(turned)
    own_probs, *own = own_part(scalars, projected)
    (
        normed_halo,
        khalo,
        vhalo,
        attended,
        stats,
        hidden,
        forecast,
        probs,
        inverse,
        own_inverse,
    ) = forward(
        scalars, from_left, from_right, latent_own, w_qkv, projected, own, w_out, readout_weight
    )
    near = lax.ppermute(forecast, "x_hi", SWAP)
    qhalo = halo_queries(normed_halo, w_qkv)
    near, qhalo = lax.optimization_barrier((near, qhalo))
    others = swap_core(jnp.stack([forecast, near]))
    packed, sent, grad, small = score(
        scalars, forecast, near, others, target, attended, hidden, stats, w_out, readout_weight
    )
    packed_left = lax.ppermute(sent, CELLS, up)
    packed_right = lax.ppermute(sent, CELLS, down)

    dquery = query_grads(
        projected, khalo, vhalo, grad, packed, probs, own_probs, inverse, own_inverse
    )
    dquery, packed_left, packed_right = lax.optimization_barrier(
        (dquery, packed_left, packed_right)
    )

    first_part = partial_sums(
        core, turned, turned_other, dquery, swap_core(dquery), (small, swap_core(small))
    )
    first_part, scalars = lax.optimization_barrier((first_part, scalars))
    first = scatter(first_part)
    pairs = key_grads(
        scalars,
        projected,
        qhalo,
        grad,
        sent,
        packed_left,
        packed_right,
        w_out,
        readout_weight,
    )
    pairs = pairs.reshape(2048, BLOCK)
    second_part = partial_sums(core, turned, turned_other, pairs, swap_core(pairs))
    second_part, first = lax.optimization_barrier((second_part, first))
    second_part, late_near = lax.optimization_barrier((second_part, near))
    second = add_up(scatter(second_part))
    crps_whole = crps_of(scalars, forecast, late_near, others, target)
    crps = lax.dynamic_slice_in_dim(crps_whole, member_index * 32, 32, 1)
    first = add_up(first)
    grad_out = lax.dot_general(
        first[:, 1024:1152],
        readout_weight.astype(F32),
        (((1,), (1,)), ((), ())),
        precision=lax.Precision.HIGHEST,
        preferred_element_type=F32,
    )
    grads = jnp.concatenate([first[:, :1024], second, grad_out, first[:, 1152:]], axis=1)
    return (crps, grads)


def solution(mesh):
    fine = jax.sharding.Mesh(mesh.devices.reshape(2, 2, 4, 2, 4), AXES)
    placed = (P(MEMBER, CELLS, None), P(), P(), P(), P(), P(CELLS, None))
    return jax.shard_map(
        per_device,
        mesh=fine,
        in_specs=placed,
        out_specs=(P(CELLS, MEMBER), P(MEMBER + CELLS, None)),
        check_vma=False,
    )
```

```python
import functools

import jax
import jax.numpy as jnp
import numpy as np
from jax import lax
from jax.experimental import pallas as pl
from jax.experimental.pallas import tpu as pltpu
from jax.sharding import PartitionSpec as P

HEADS = 16
WIN = 256
BLOCK = 256
WIDTH = 256
HEAD_WIDTH = 64
PAIR = 128
NEVER = -1e30

alpha_fair = 0.95
smooth_width = 0.0625

BF = jnp.bfloat16
F32 = jnp.float32


def smooth_abs(values):
    return jnp.sqrt(values * values + smooth_width)


def smooth_sign(values):
    return values * lax.rsqrt(values * values + smooth_width)


def layer_norm(latent_rows):
    values = latent_rows.astype(F32)
    center = values - jnp.mean(values, axis=-1, keepdims=True)
    spread = jnp.mean(center * center, axis=-1, keepdims=True)
    return (center * lax.rsqrt(spread + 1e-05)).astype(BF)


def dot_nn(left, right):
    return lax.dot_general(left, right, (((1,), (0,)), ((), ())), preferred_element_type=F32)


def dot_nt(left, right):
    return lax.dot_general(left, right, (((1,), (1,)), ((), ())), preferred_element_type=F32)


def dot_tn(left, right):
    return lax.dot_general(left, right, (((0,), (0,)), ((), ())), preferred_element_type=F32)


def iota(shape, axis):
    return lax.broadcasted_iota(jnp.int32, shape, axis)


FREE = pl.CostEstimate(flops=0, bytes_accessed=0, transcendentals=0)
HBM = pl.BlockSpec(memory_space=pltpu.HBM)


def in_hbm(values):
    return pltpu.with_memory_space_constraint(values, pltpu.HBM)


def fetches(weight_ref, buffer, arrived, width, first):
    return [
        pltpu.make_async_copy(
            weight_ref.at[:, pl.ds(first + place * width, width)],
            buffer.at[place],
            arrived.at[place],
        )
        for place in range(buffer.shape[0])
    ]


def fetch_one(weight_ref, buffer, arrived, width, first, place):
    start = pl.multiple_of(first + place * width, width)
    return pltpu.make_async_copy(
        weight_ref.at[:, pl.ds(start, width)], buffer.at[place], arrived.at[place]
    )


def project_kernel(latent_ref, weight_ref, projected_ref, turned_ref, normed, buffer, arrived):
    step = pl.program_id(0)

    @pl.when(step == 0)
    def _():
        for copy in fetches(weight_ref, buffer, arrived, 512, 0):
            copy.start()
        normed[...] = layer_norm(latent_ref[...])
        turned_ref[...] = normed[...].T

    fetch_one(weight_ref, buffer, arrived, 512, 0, step).wait()
    projected_ref[...] = dot_nn(normed[...], buffer[step]).astype(BF)


def project(latent_own, w_qkv):
    rows, width = latent_own.shape
    return pl.pallas_call(
        project_kernel,
        grid=(6,),
        in_specs=[pl.BlockSpec((rows, width), lambda j: (0, 0)), HBM],
        out_specs=[
            pl.BlockSpec((rows, 512), lambda j: (0, j)),
            pl.BlockSpec((width, rows), lambda j: (0, 0)),
        ],
        out_shape=[
            jax.ShapeDtypeStruct((rows, 3 * width), BF),
            jax.ShapeDtypeStruct((width, rows), BF),
        ],
        scratch_shapes=[
            pltpu.VMEM((rows, width), BF),
            pltpu.VMEM((6, width, 512), BF),
            pltpu.SemaphoreType.DMA((6,)),
        ],
        compiler_params=pltpu.CompilerParams(vmem_limit_bytes=16 * 1024 * 1024),
        cost_estimate=pl.CostEstimate(
            flops=2 * rows * width * width * 4, bytes_accessed=8 << 20, transcendentals=0
        ),
    )(latent_own, in_hbm(w_qkv))


def halo_query_kernel(normed_ref, weight_ref, out_ref, buffer, arrived):
    step = pl.program_id(0)

    @pl.when(step == 0)
    def _():
        for copy in fetches(weight_ref, buffer, arrived, 256, 0):
            copy.start()

    fetch_one(weight_ref, buffer, arrived, 256, 0, step).wait()
    out_ref[...] = dot_nn(normed_ref[...], buffer[step]).astype(BF)


def halo_queries(normed_halo, w_qkv):
    rows, width = normed_halo.shape
    return pl.pallas_call(
        halo_query_kernel,
        grid=(4,),
        in_specs=[pl.BlockSpec((rows, width), lambda j: (0, 0)), HBM],
        out_specs=pl.BlockSpec((rows, 256), lambda j: (0, j)),
        out_shape=jax.ShapeDtypeStruct((rows, width), BF),
        scratch_shapes=[
            pltpu.VMEM((4, width, 256), BF),
            pltpu.SemaphoreType.DMA((4,)),
        ],
        compiler_params=pltpu.CompilerParams(vmem_limit_bytes=12 * 1024 * 1024),
        cost_estimate=FREE,
    )(normed_halo, in_hbm(w_qkv))


def partial_kernel(
    smalls, core_ref, normed_ref, normed_other_ref, piece_ref, other_ref, *refs
):
    small_refs, (out_ref, rows, pieces, others, sums, staged, arrived, left) = (
        refs[:smalls],
        refs[smalls:],
    )
    core = core_ref[0]
    chunks = piece_ref.shape[0] // 512
    sources = [
        (normed_ref.at[:, core], rows.at[0]),
        (normed_other_ref.at[:, core], rows.at[1]),
    ]
    for chunk in range(chunks):
        part = pl.ds(chunk * 512, 512)
        sources.append((piece_ref.at[part], pieces.at[chunk]))
        sources.append((other_ref.at[part], others.at[chunk]))
    for place, small_ref in enumerate(small_refs):
        sources.append((small_ref.at[:, core], sums.at[place]))
    copies = [
        pltpu.make_async_copy(source, target, arrived.at[place])
        for place, (source, target) in enumerate(sources)
    ]
    for copy in copies:
        copy.start()
    copies[0].wait()
    copies[1].wait()
    writes = []
    for chunk in range(chunks):
        copies[2 + 2 * chunk].wait()
        copies[3 + 2 * chunk].wait()
        for top in range(2):
            staged[chunk, top * 256 : (top + 1) * 256] = (
                dot_nt(rows[0, top], pieces[chunk]) + dot_nt(rows[1, top], others[chunk])
            ).astype(BF)
        writes.append(
            pltpu.make_async_copy(
                staged.at[chunk], out_ref.at[:, pl.ds(chunk * 512, 512)], left.at[chunk]
            )
        )
        writes[-1].start()
    if smalls:
        copies[-2].wait()
        copies[-1].wait()
        for top in range(2):
            staged[chunks, top * 256 : (top + 1) * 256, :256] = (
                sums[0, top].astype(F32) + sums[1, top].astype(F32)
            ).astype(BF)
        writes.append(
            pltpu.make_async_copy(
                staged.at[chunks, :, pl.ds(0, 256)],
                out_ref.at[:, pl.ds(chunks * 512, 256)],
                left.at[chunks],
            )
        )
        writes[-1].start()
    for write in writes:
        write.wait()


def partial_sums(core, turned, turned_other, piece, other, smalls=()):
    by_core = lambda values: values.reshape(2, 2, 256, 256)
    anywhere = pl.BlockSpec(memory_space=pl.ANY)
    chunks = piece.shape[0] // 512
    columns = piece.shape[0] + 256 * (len(smalls) // 2)
    return pl.pallas_call(
        functools.partial(partial_kernel, len(smalls)),
        in_specs=[pl.BlockSpec(memory_space=pltpu.SMEM)] + [anywhere] * (4 + len(smalls)),
        out_specs=anywhere,
        out_shape=jax.ShapeDtypeStruct((512, columns), BF),
        scratch_shapes=[
            pltpu.VMEM((2, 2, 256, 256), BF),
            pltpu.VMEM((chunks, 512, 256), BF),
            pltpu.VMEM((chunks, 512, 256), BF),
            pltpu.VMEM((2, 2, 256, 256), BF),
            pltpu.VMEM((chunks + 1, 512, 512), BF),
            pltpu.SemaphoreType.DMA((2 + 2 * chunks + len(smalls),)),
            pltpu.SemaphoreType.DMA((chunks + 1,)),
        ],
        compiler_params=pltpu.CompilerParams(vmem_limit_bytes=14 * 1024 * 1024),
        cost_estimate=FREE,
    )(
        core.astype(jnp.int32).reshape(1),
        by_core(turned),
        by_core(turned_other),
        piece,
        other,
        *(by_core(small) for small in smalls),
    )


def spare_lane(shape):
    lane = iota(shape, len(shape) - 1)
    return lane % HEAD_WIDTH


def key_fill(count_pieces):
    fills = []
    for count, rows in count_pieces:
        spare = spare_lane((rows, PAIR))
        bias = jnp.where(iota((rows, PAIR), 0) < count, 0.0, NEVER)
        fills.append(
            jnp.where(spare < 3, 1.0, jnp.where(spare == 3, bias, 0.0)).astype(BF)
        )
    return jnp.concatenate(fills, axis=0)


def stat_spread(step, offset):
    shape = (128, WIDTH)
    lane = iota(shape, 1)
    head = step * 4 + 2 * (lane // PAIR) + jnp.where(lane % PAIR < HEAD_WIDTH, 1, 0)
    term = lane % HEAD_WIDTH
    chosen = (term < 3) & (iota(shape, 0) == term * 32 + offset + head)
    return jnp.where(chosen, -1.0, 0.0).astype(BF)


def keep_band(window, fill):
    shape = (128, 128)
    apart = iota(shape, 0) - iota(shape, 1)
    first = jnp.where(apart >= 0, window[:128], fill)
    last = jnp.where(apart <= 0, window[-128:], fill)
    return first, window[128:-128], last


def own_kernel(counts_ref, q_ref, k_ref, v_ref, probs, mixed_ref, top_ref, total_ref):
    step = pl.program_id(0)
    fill = key_fill([(counts_ref[1], BLOCK)])
    low = iota((BLOCK, PAIR), 1) < HEAD_WIDTH
    query_fill = (spare_lane((BLOCK, PAIR)) == 3).astype(BF)
    ones = jnp.ones((16, BLOCK), BF)
    scores, turned = [], []
    for pair in range(2):
        columns = slice(pair * PAIR, (pair + 1) * PAIR)
        q_pair = q_ref[:, columns] * jnp.asarray(HEAD_WIDTH ** (-0.5), BF)
        k_pair = k_ref[:, columns]
        turned.append(v_ref[:, columns].T)
        for half in range(2):
            pick = low if half == 0 else ~low
            scores.append(
                dot_nt(jnp.where(pick, k_pair, fill), jnp.where(pick, q_pair, query_fill))
            )
    for slot in range(4):
        top = jnp.max(scores[slot], axis=0, keepdims=True)
        probs[slot] = jnp.exp(scores[slot] - top).astype(BF)
        top_ref[pl.ds(step * 4 + slot, 1), :] = top
    for slot in range(4):
        lanes = slice(slot % 2 * HEAD_WIDTH, (slot % 2 + 1) * HEAD_WIDTH)
        values = jnp.concatenate([turned[slot // 2][lanes], ones], axis=0)
        mixed = dot_nn(values, probs[slot])
        mixed_ref[slot * HEAD_WIDTH : (slot + 1) * HEAD_WIDTH] = mixed[:HEAD_WIDTH]
        total_ref[pl.ds(step * 4 + slot, 1), :] = mixed[HEAD_WIDTH : HEAD_WIDTH + 1]


def own_part(counts, projected):
    part = lambda rows, first: pl.BlockSpec((rows, WIDTH), lambda j: (0, first + j))
    whole = pl.BlockSpec((HEADS, BLOCK), lambda j: (0, 0))
    return pl.pallas_call(
        own_kernel,
        grid=(4,),
        in_specs=[
            pl.BlockSpec(memory_space=pltpu.SMEM),
            part(BLOCK, 0),
            part(BLOCK, 4),
            part(BLOCK, 8),
        ],
        out_specs=[
            pl.BlockSpec((4, BLOCK, BLOCK), lambda j: (j, 0, 0)),
            pl.BlockSpec((WIDTH, BLOCK), lambda j: (j, 0)),
            whole,
            whole,
        ],
        out_shape=[
            jax.ShapeDtypeStruct((HEADS, BLOCK, BLOCK), BF),
            jax.ShapeDtypeStruct((1024, BLOCK), F32),
            jax.ShapeDtypeStruct((HEADS, BLOCK), F32),
            jax.ShapeDtypeStruct((HEADS, BLOCK), F32),
        ],
        compiler_params=pltpu.CompilerParams(vmem_limit_bytes=14 * 1024 * 1024),
        cost_estimate=pl.CostEstimate(
            flops=1 << 30, bytes_accessed=4 << 20, transcendentals=1 << 20
        ),
    )(counts, projected, projected, projected)


def forward_kernel(
    counts_ref,
    left_ref,
    right_ref,
    latent_ref,
    weight_ref,
    q_ref,
    own_mixed_ref,
    own_top_ref,
    own_total_ref,
    w_out_ref,
    readout_ref,
    normed_ref,
    khalo_ref,
    vhalo_ref,
    attended_ref,
    stats_ref,
    hidden_ref,
    forecast_ref,
    probs,
    inverse_ref,
    own_inverse_ref,
    stat_rows,
    buffer,
    arrived,
):
    step = pl.program_id(0)

    @pl.when(step == 0)
    def _():
        copies = fetches(weight_ref, buffer, arrived, WIDTH, 1024)
        for place in (0, 4, 1, 5, 2, 6, 3, 7):
            copies[place].start()
        normed_ref[:WIN] = layer_norm(left_ref[...])
        normed_ref[WIN:] = layer_norm(right_ref[...])

    fetch_one(weight_ref, buffer, arrived, WIDTH, 1024, step).wait()
    fetch_one(weight_ref, buffer, arrived, WIDTH, 1024, step + 4).wait()
    khalo_ref[...] = dot_nn(normed_ref[...], buffer[step]).astype(BF)
    vhalo_ref[...] = dot_nn(normed_ref[...], buffer[step + 4]).astype(BF)
    fill = key_fill([(counts_ref[0], WIN), (counts_ref[2], WIN)])
    low_q = iota((BLOCK, PAIR), 1) < HEAD_WIDTH
    low_k = iota(fill.shape, 1) < HEAD_WIDTH
    query_fill = (spare_lane((BLOCK, PAIR)) == 3).astype(BF)
    scores, turned = [], []
    for pair in range(2):
        columns = slice(pair * PAIR, (pair + 1) * PAIR)
        q_pair = q_ref[:, columns] * jnp.asarray(HEAD_WIDTH ** (-0.5), BF)
        k_pair = khalo_ref[:, columns]
        turned.append(vhalo_ref[:, columns].T)
        for half in range(2):
            if half == 0:
                q_head = jnp.where(low_q, q_pair, query_fill)
                k_head = jnp.where(low_k, k_pair, fill)
            else:
                q_head = jnp.where(low_q, query_fill, q_pair)
                k_head = jnp.where(low_k, fill, k_pair)
            scores.append(dot_nt(k_head, q_head))
    tops = []
    for slot in range(4):
        levels = []
        for tile in range(2):
            rows = slice(tile * 128, tile * 128 + 384)
            lanes = slice(tile * 128, tile * 128 + 128)
            first, middle, last = keep_band(scores[slot][rows, lanes], NEVER)
            top = jnp.maximum(
                jnp.max(middle, axis=0, keepdims=True),
                jnp.max(jnp.maximum(first, last), axis=0, keepdims=True),
            )
            top = jnp.maximum(top, own_top_ref[pl.ds(step * 4 + slot, 1), :][:, lanes])
            start = tile * 128
            probs[slot, start : start + 128, lanes] = jnp.exp(first - top).astype(BF)
            probs[slot, start + 128 : start + 256, lanes] = jnp.exp(middle - top).astype(BF)
            probs[slot, start + 256 : start + 384, lanes] = jnp.exp(last - top).astype(BF)
            levels.append(top)
        probs[slot, :128, 128:] = jnp.zeros((128, 128), BF)
        probs[slot, 384:, :128] = jnp.zeros((128, 128), BF)
        tops.append(jnp.concatenate(levels, axis=1))
    ones = jnp.ones((16, fill.shape[0]), BF)
    for pair in range(2):
        halves = []
        for half in range(2):
            slot = pair * 2 + half
            lanes = slice(half * HEAD_WIDTH, (half + 1) * HEAD_WIDTH)
            values = jnp.concatenate([turned[pair][lanes], ones], axis=0)
            mixed = dot_nn(values, probs[slot])
            head = step * 4 + slot
            fade = jnp.exp(own_top_ref[pl.ds(head, 1), :] - tops[slot])
            total = mixed[HEAD_WIDTH : HEAD_WIDTH + 1]
            total += own_total_ref[pl.ds(head, 1), :] * fade
            inverse = 1.0 / total
            own_inverse = fade * inverse
            own_mixed = own_mixed_ref[slot * HEAD_WIDTH : (slot + 1) * HEAD_WIDTH]
            halves.append(mixed[:HEAD_WIDTH] * inverse + own_mixed * own_inverse)
            own_inverse_ref[pl.ds(head, 1), :] = own_inverse
            inverse_ref[pl.ds(head, 1), :] = inverse
            stat_rows[pl.ds(head, 1), :] = tops[slot] + jnp.log(total)
        start = pl.multiple_of(step * WIDTH + pair * PAIR, PAIR)
        attended_ref[:, pl.ds(start, PAIR)] = jnp.concatenate(halves, axis=0).T

    @pl.when(step == 3)
    def _():
        mixed = dot_nn(attended_ref[...].astype(BF), w_out_ref[...])
        hidden = (latent_ref[...].astype(F32) + mixed).astype(BF)
        hidden_ref[...] = hidden
        forecast_ref[...] = dot_nn(hidden, readout_ref[...])
        stat_rows[HEADS:] = jnp.zeros((128 - HEADS, BLOCK), F32)
        stats_ref[...] = stat_rows[...].T


def forward(counts, left, right, latent_own, w_qkv, projected, own, w_out, readout_weight):
    whole = lambda *shape: pl.BlockSpec(shape, lambda j: (0, 0))
    part = lambda rows, first: pl.BlockSpec((rows, WIDTH), lambda j: (0, first + j))
    window = 2 * WIN + BLOCK
    return pl.pallas_call(
        forward_kernel,
        grid=(4,),
        in_specs=[
            pl.BlockSpec(memory_space=pltpu.SMEM),
            whole(WIN, 1024),
            whole(WIN, 1024),
            whole(BLOCK, 1024),
            HBM,
            part(BLOCK, 0),
            pl.BlockSpec((WIDTH, BLOCK), lambda j: (j, 0)),
            whole(HEADS, BLOCK),
            whole(HEADS, BLOCK),
            whole(1024, 1024),
            whole(1024, 128),
        ],
        out_specs=[
            whole(2 * WIN, 1024),
            part(2 * WIN, 0),
            part(2 * WIN, 0),
            whole(BLOCK, 1024),
            whole(BLOCK, 128),
            whole(BLOCK, 1024),
            whole(BLOCK, 128),
            pl.BlockSpec((4, 2 * WIN, BLOCK), lambda j: (j, 0, 0)),
            whole(HEADS, BLOCK),
            whole(HEADS, BLOCK),
        ],
        out_shape=[
            jax.ShapeDtypeStruct((2 * WIN, 1024), BF),
            jax.ShapeDtypeStruct((2 * WIN, 1024), BF),
            jax.ShapeDtypeStruct((2 * WIN, 1024), BF),
            jax.ShapeDtypeStruct((BLOCK, 1024), F32),
            jax.ShapeDtypeStruct((BLOCK, 128), F32),
            jax.ShapeDtypeStruct((BLOCK, 1024), BF),
            jax.ShapeDtypeStruct((BLOCK, 128), F32),
            jax.ShapeDtypeStruct((HEADS, 2 * WIN, BLOCK), BF),
            jax.ShapeDtypeStruct((HEADS, BLOCK), F32),
            jax.ShapeDtypeStruct((HEADS, BLOCK), F32),
        ],
        scratch_shapes=[
            pltpu.VMEM((128, BLOCK), F32),
            pltpu.VMEM((8, 1024, WIDTH), BF),
            pltpu.SemaphoreType.DMA((8,)),
        ],
        compiler_params=pltpu.CompilerParams(vmem_limit_bytes=30 * 1024 * 1024),
        cost_estimate=pl.CostEstimate(
            flops=6 << 30, bytes_accessed=12 << 20, transcendentals=3 << 20
        ),
    )(
        counts,
        left,
        right,
        latent_own,
        in_hbm(w_qkv),
        projected,
        *own,
        w_out,
        readout_weight,
    )


def crps_kernel(counts_ref, own_ref, near_ref, others_ref, target_ref, crps_ref):
    members = 4
    fair_eps = (1.0 - alpha_fair) / members
    coefficient = (1.0 - fair_eps) / (members * (members - 1))
    valid = (iota((BLOCK, 1), 0) < counts_ref[1]).astype(F32)
    forecasts = [own_ref[...], near_ref[...], others_ref[0], others_ref[1]]
    target = target_ref[...]
    error = jnp.zeros_like(target)
    for forecast in forecasts:
        error += smooth_abs(forecast - target)
    spread = jnp.full_like(target, members * smooth_width**0.5)
    for first in range(members):
        for second in range(first + 1, members):
            spread += 2.0 * smooth_abs(forecasts[first] - forecasts[second])
    crps_ref[...] = valid * (error / members - 0.5 * coefficient * spread)


def crps_of(counts, own, near, others, target):
    vmem = pl.BlockSpec(memory_space=pltpu.VMEM)
    return pl.pallas_call(
        crps_kernel,
        in_specs=[pl.BlockSpec(memory_space=pltpu.SMEM)] + [vmem] * 4,
        out_specs=vmem,
        out_shape=jax.ShapeDtypeStruct((BLOCK, 128), F32),
        compiler_params=pltpu.CompilerParams(vmem_limit_bytes=8 * 1024 * 1024),
        cost_estimate=FREE,
    )(counts, own, near, others, in_hbm(target))


def score_kernel(
    counts_ref,
    own_ref,
    near_ref,
    others_ref,
    target_ref,
    attended_ref,
    hidden_ref,
    stats_ref,
    w_out_ref,
    readout_ref,
    packed_ref,
    sent_ref,
    grad_ref,
    small_ref,
):
    members = 4
    fair_eps = (1.0 - alpha_fair) / members
    coefficient = (1.0 - fair_eps) / (members * (members - 1))
    valid = (iota((BLOCK, 1), 0) < counts_ref[1]).astype(F32)
    own = own_ref[...]
    target = target_ref[...]
    pull = jnp.zeros_like(target)
    for other in (near_ref[...], others_ref[0], others_ref[1]):
        pull += smooth_sign(own - other)
    slope = (
        valid / 128 * (smooth_sign(own - target) / members - coefficient * pull)
    ).astype(BF)
    dhidden = dot_nt(slope, readout_ref[...]).astype(BF)
    dattended = dot_nt(dhidden, w_out_ref[...]).astype(BF)
    grad_ref[...] = dattended
    attended = attended_ref[...]
    product = dattended.astype(F32) * attended
    high = product.astype(BF)
    low = (product - high.astype(F32)).astype(BF)
    pick = (iota((1024, 128), 0) // HEAD_WIDTH + HEADS == iota((1024, 128), 1)).astype(BF)
    stats = stats_ref[...] + dot_nn(high, pick) + dot_nn(low, pick)
    first = stats.astype(BF)
    rest = stats - first.astype(F32)
    second = rest.astype(BF)
    third = (rest - second.astype(F32)).astype(BF)
    terms = jnp.zeros((BLOCK, 128), F32)
    for place, term in enumerate((first, second, third)):
        shift = (iota((128, 128), 0) + 32 * place == iota((128, 128), 1)) & (
            iota((128, 128), 0) < 32
        )
        terms += dot_nn(term, shift.astype(BF))
    packed_ref[:, :128] = slope
    packed_ref[:, 128:] = terms.astype(BF)
    sent_ref[...] = packed_ref[...]
    small_ref[:, :128] = dot_tn(attended.astype(BF), slope).astype(BF)
    small_ref[:, 128:] = dot_tn(hidden_ref[...], slope).astype(BF)


def score(counts, own, near, others, target, attended, hidden, stats, w_out, readout_weight):
    vmem = pl.BlockSpec(memory_space=pltpu.VMEM)
    return pl.pallas_call(
        score_kernel,
        in_specs=[pl.BlockSpec(memory_space=pltpu.SMEM)] + [vmem] * 9,
        out_specs=[vmem] * 4,
        out_shape=[
            jax.ShapeDtypeStruct((BLOCK, 256), BF),
            pltpu.HBM((BLOCK, 256), BF),
            jax.ShapeDtypeStruct((BLOCK, 1024), BF),
            jax.ShapeDtypeStruct((1024, 256), BF),
        ],
        compiler_params=pltpu.CompilerParams(vmem_limit_bytes=12 * 1024 * 1024),
    )(counts, own, near, others, target, attended, hidden, stats, w_out, readout_weight)


def query_kernel(
    k_ref,
    v_ref,
    khalo_ref,
    vhalo_ref,
    grad_ref,
    packed_ref,
    probs_ref,
    own_probs_ref,
    inverse_ref,
    own_inverse_ref,
    dq_ref,
    dscores,
    own_dscores,
):
    step = pl.program_id(0)
    low_q = iota((BLOCK, PAIR), 1) < HEAD_WIDTH
    low_k = iota((2 * WIN, PAIR), 1) < HEAD_WIDTH
    own_fill = (spare_lane((BLOCK, PAIR)) < 3).astype(BF)
    halo_fill = (spare_lane((2 * WIN, PAIR)) < 3).astype(BF)
    g_fill = dot_nn(packed_ref[:, 128:], stat_spread(step, HEADS)).astype(BF)
    turned = []
    for pair in range(2):
        columns = slice(pair * PAIR, (pair + 1) * PAIR)
        g_pair = grad_ref[:, columns]
        own_turned = k_ref[:, columns].T
        halo_turned = khalo_ref[:, columns].T
        for half in range(2):
            slot = pair * 2 + half
            pick_q = low_q if half == 0 else ~low_q
            pick_k = low_k if half == 0 else ~low_k
            g_head = jnp.where(pick_q, g_pair, g_fill[:, columns])
            own_change = dot_nt(jnp.where(pick_q, v_ref[:, columns], own_fill), g_head)
            own_dscores[slot] = (own_probs_ref[slot].astype(F32) * own_change).astype(BF)
            change = dot_nt(jnp.where(pick_k, vhalo_ref[:, columns], halo_fill), g_head)
            dscores[slot] = (probs_ref[slot].astype(F32) * change).astype(BF)
            lanes = slice(half * HEAD_WIDTH, (half + 1) * HEAD_WIDTH)
            turned.append((own_turned[lanes], halo_turned[lanes]))
    for slot in range(4):
        row = pl.ds(step * 4 + slot, 1)
        dquery = dot_nn(turned[slot][0], own_dscores[slot]) * own_inverse_ref[row, :]
        dquery += dot_nn(turned[slot][1], dscores[slot]) * inverse_ref[row, :]
        dq_ref[slot * HEAD_WIDTH : (slot + 1) * HEAD_WIDTH] = (
            dquery * HEAD_WIDTH ** (-0.5)
        ).astype(BF)


def query_grads(projected, khalo, vhalo, grad, packed, probs, own_probs, inverse, own_inverse):
    part = lambda rows, first: pl.BlockSpec((rows, WIDTH), lambda j: (0, first + j))
    heads = lambda rows: pl.BlockSpec((4, rows, BLOCK), lambda j: (j, 0, 0))
    whole = pl.BlockSpec((HEADS, BLOCK), lambda j: (0, 0))
    return pl.pallas_call(
        query_kernel,
        grid=(4,),
        in_specs=[
            part(BLOCK, 4),
            part(BLOCK, 8),
            part(2 * WIN, 0),
            part(2 * WIN, 0),
            part(BLOCK, 0),
            pl.BlockSpec((BLOCK, 256), lambda j: (0, 0)),
            heads(2 * WIN),
            heads(BLOCK),
            whole,
            whole,
        ],
        out_specs=pl.BlockSpec((WIDTH, BLOCK), lambda j: (j, 0)),
        out_shape=jax.ShapeDtypeStruct((1024, BLOCK), BF),
        scratch_shapes=[
            pltpu.VMEM((4, 2 * WIN, BLOCK), BF),
            pltpu.VMEM((4, BLOCK, BLOCK), BF),
        ],
        compiler_params=pltpu.CompilerParams(vmem_limit_bytes=16 * 1024 * 1024),
        cost_estimate=pl.CostEstimate(
            flops=6 << 30, bytes_accessed=5 << 20, transcendentals=3 << 20
        ),
    )(
        projected,
        projected,
        khalo,
        vhalo,
        grad,
        packed,
        probs,
        own_probs,
        inverse,
        own_inverse,
    )


def key_kernel(
    counts_ref,
    q_ref,
    k_ref,
    v_ref,
    qhalo_ref,
    grad_ref,
    own_ref,
    sides_ref,
    w_out_ref,
    readout_ref,
    out_ref,
    probs,
    dscores,
    dhidden,
):
    step = pl.program_id(0)

    @pl.when(step == 0)
    def _():
        for slot in range(4):
            for held in (probs, dscores):
                held[slot, :128, 128:] = jnp.zeros((128, 128), BF)
                held[slot, 640:, :128] = jnp.zeros((128, 128), BF)
        dhidden[:WIN] = dot_nt(sides_ref[0, :, :128], readout_ref[...]).astype(BF)
        dhidden[WIN:] = dot_nt(sides_ref[1, :, :128], readout_ref[...]).astype(BF)

    ghalo = dot_nt(dhidden[...], w_out_ref[...]).astype(BF)
    terms = jnp.concatenate(
        [sides_ref[0, :, 128:], own_ref[:, 128:], sides_ref[1, :, 128:]], axis=0
    )
    window = terms.shape[0]
    fill = key_fill([(counts_ref[1], BLOCK)])
    value_fill = (spare_lane(fill.shape) < 3).astype(BF)
    low_q = iota((window, PAIR), 1) < HEAD_WIDTH
    low_k = iota(fill.shape, 1) < HEAD_WIDTH
    ones = (spare_lane((window, WIDTH)) == 3).astype(F32)
    q_fill = (dot_nn(terms, stat_spread(step, 0)) + ones).astype(BF)
    g_fill = dot_nn(terms, stat_spread(step, HEADS)).astype(BF)
    turned = []
    for pair in range(2):
        columns = slice(pair * PAIR, (pair + 1) * PAIR)
        q_pair = jnp.concatenate(
            [qhalo_ref[:WIN, columns], q_ref[:, columns], qhalo_ref[WIN:, columns]], axis=0
        ) * jnp.asarray(HEAD_WIDTH ** (-0.5), BF)
        g_pair = jnp.concatenate(
            [ghalo[:WIN, columns], grad_ref[:, columns], ghalo[WIN:, columns]], axis=0
        )
        k_pair = k_ref[:, columns]
        v_pair = v_ref[:, columns]
        q_turned = q_pair.T
        g_turned = g_pair.T
        for half in range(2):
            slot = pair * 2 + half
            pick_q = low_q if half == 0 else ~low_q
            pick_k = low_k if half == 0 else ~low_k
            q_head = jnp.where(pick_q, q_pair, q_fill[:, columns])
            g_head = jnp.where(pick_q, g_pair, g_fill[:, columns])
            k_head = jnp.where(pick_k, k_pair, fill)
            v_head = jnp.where(pick_k, v_pair, value_fill)
            scores = dot_nt(q_head, k_head)
            change = dot_nt(g_head, v_head)
            for tile in range(2):
                rows = slice(tile * 128, tile * 128 + 640)
                lanes = slice(tile * 128, tile * 128 + 128)
                weight = keep_band(jnp.exp(scores[rows, lanes]), 0.0)
                moved = change[rows, lanes]
                start = tile * 128
                for piece, (low, high) in zip(weight, ((0, 128), (128, 512), (512, 640))):
                    place = slice(start + low, start + high)
                    probs[slot, place, lanes] = piece.astype(BF)
                    dscores[slot, place, lanes] = (piece * moved[low:high]).astype(BF)
            lanes = slice(half * HEAD_WIDTH, (half + 1) * HEAD_WIDTH)
            turned.append((q_turned[lanes], g_turned[lanes]))
    for slot in range(4):
        place = slice(slot * HEAD_WIDTH, (slot + 1) * HEAD_WIDTH)
        out_ref[0, place] = dot_nn(turned[slot][0], dscores[slot]).astype(BF)
        out_ref[1, place] = dot_nn(turned[slot][1], probs[slot]).astype(BF)


def key_grads(counts, projected, qhalo, grad, own, sides, w_out, readout_weight):
    part = lambda rows, first: pl.BlockSpec((rows, WIDTH), lambda j: (0, first + j))
    whole = lambda *shape: pl.BlockSpec(shape, lambda j: (0, 0))
    window = 2 * WIN + BLOCK
    return pl.pallas_call(
        key_kernel,
        grid=(4,),
        in_specs=[
            pl.BlockSpec(memory_space=pltpu.SMEM),
            part(BLOCK, 0),
            part(BLOCK, 4),
            part(BLOCK, 8),
            part(2 * WIN, 0),
            part(BLOCK, 0),
            whole(BLOCK, 256),
            pl.BlockSpec((2, WIN, 256), lambda j: (0, 0, 0)),
            pl.BlockSpec((WIDTH, 1024), lambda j: (j, 0)),
            whole(1024, 128),
        ],
        out_specs=pl.BlockSpec((2, WIDTH, BLOCK), lambda j: (0, j, 0)),
        out_shape=jax.ShapeDtypeStruct((2, 1024, BLOCK), BF),
        scratch_shapes=[
            pltpu.VMEM((4, window, BLOCK), BF),
            pltpu.VMEM((4, window, BLOCK), BF),
            pltpu.VMEM((2 * WIN, 1024), BF),
        ],
        compiler_params=pltpu.CompilerParams(vmem_limit_bytes=18 * 1024 * 1024),
        cost_estimate=FREE,
    )(
        counts,
        projected,
        projected,
        projected,
        qhalo,
        in_hbm(grad),
        in_hbm(own),
        in_hbm(sides),
        in_hbm(w_out),
        readout_weight,
    )


AXES = ("x_hi", "core", "y", "x_lo", "z")
MEMBER = ("x_hi", "core")
CELLS = ("y", "x_lo", "z")
CHIPS = ("x_hi", "y", "x_lo", "z")
SWAP = [(0, 1), (1, 0)]


def swap_core(values):
    return lax.ppermute(values, "core", SWAP)


def scatter(partial):
    columns = partial.shape[1]
    return lax.all_to_all(partial.reshape(64, 8, columns), CHIPS, split_axis=0, concat_axis=0)


def add_up(pieces):
    return jnp.sum(pieces.astype(F32), axis=0)


def per_device(latent, counts, w_qkv, w_out, readout_weight, target):
    latent_own = latent[0]
    cell_count = 32
    cell_index = lax.axis_index(CELLS)
    member_index = lax.axis_index(MEMBER)
    core = lax.axis_index("core")
    up = [(i, i + 1) for i in range(cell_count - 1)]
    down = [(i + 1, i) for i in range(cell_count - 1)]
    from_left = lax.ppermute(latent_own, CELLS, up)
    from_right = lax.ppermute(latent_own, CELLS, down)

    own_count = counts[cell_index]
    left_count = jnp.where(cell_index > 0, counts[jnp.maximum(cell_index - 1, 0)], 0)
    right_count = jnp.where(
        cell_index < cell_count - 1, counts[jnp.minimum(cell_index + 1, cell_count - 1)], 0
    )
    scalars = jnp.stack([left_count, own_count, right_count])

    projected, turned = project(latent_own, w_qkv)
    turned_other = swap_core(turned)
    own_probs, *own = own_part(scalars, projected)
    (
        normed_halo,
        khalo,
        vhalo,
        attended,
        stats,
        hidden,
        forecast,
        probs,
        inverse,
        own_inverse,
    ) = forward(
        scalars, from_left, from_right, latent_own, w_qkv, projected, own, w_out, readout_weight
    )
    near = lax.ppermute(forecast, "x_hi", SWAP)
    qhalo = halo_queries(normed_halo, w_qkv)
    near, qhalo = lax.optimization_barrier((near, qhalo))
    others = swap_core(jnp.stack([forecast, near]))
    packed, sent, grad, small = score(
        scalars, forecast, near, others, target, attended, hidden, stats, w_out, readout_weight
    )
    packed_left = lax.ppermute(sent, CELLS, up)
    packed_right = lax.ppermute(sent, CELLS, down)

    dquery = query_grads(
        projected, khalo, vhalo, grad, packed, probs, own_probs, inverse, own_inverse
    )
    dquery, packed_left, packed_right = lax.optimization_barrier(
        (dquery, packed_left, packed_right)
    )
    sides = jnp.stack([packed_left, packed_right])

    first_part = partial_sums(
        core, turned, turned_other, dquery, swap_core(dquery), (small, swap_core(small))
    )
    first_part, scalars = lax.optimization_barrier((first_part, scalars))
    first = scatter(first_part)
    pairs = key_grads(
        scalars,
        projected,
        qhalo,
        grad,
        sent,
        sides,
        w_out,
        readout_weight,
    )
    pairs = pairs.reshape(2048, BLOCK)
    second_part = partial_sums(core, turned, turned_other, pairs, swap_core(pairs))
    second_part, first = lax.optimization_barrier((second_part, first))
    second_part, late_near = lax.optimization_barrier((second_part, near))
    second = add_up(scatter(second_part))
    crps_whole = crps_of(scalars, forecast, late_near, others, target)
    crps = lax.dynamic_slice_in_dim(crps_whole, member_index * 32, 32, 1)
    first = add_up(first)
    grad_out = lax.dot_general(
        first[:, 1024:1152],
        readout_weight.astype(F32),
        (((1,), (1,)), ((), ())),
        precision=lax.Precision.HIGHEST,
        preferred_element_type=F32,
    )
    grads = jnp.concatenate([first[:, :1024], second, grad_out, first[:, 1152:]], axis=1)
    return (crps, grads)


def solution(mesh):
    fine = jax.sharding.Mesh(mesh.devices.reshape(2, 2, 4, 2, 4), AXES)
    placed = (P(MEMBER, CELLS, None), P(), P(), P(), P(), P(CELLS, None))
    return jax.shard_map(
        per_device,
        mesh=fine,
        in_specs=placed,
        out_specs=(P(CELLS, MEMBER), P(MEMBER + CELLS, None)),
        check_vma=False,
    )
```

```python
import functools

import jax
import jax.numpy as jnp
import numpy as np
from jax import lax
from jax.experimental import pallas as pl
from jax.experimental.pallas import tpu as pltpu
from jax.sharding import PartitionSpec as P

HEADS = 16
WIN = 256
BLOCK = 256
WIDTH = 256
HEAD_WIDTH = 64
PAIR = 128
NEVER = -1e30

alpha_fair = 0.95
smooth_width = 0.0625

BF = jnp.bfloat16
F32 = jnp.float32


def smooth_abs(values):
    return jnp.sqrt(values * values + smooth_width)


def smooth_sign(values):
    return values * lax.rsqrt(values * values + smooth_width)


def layer_norm(latent_rows):
    values = latent_rows.astype(F32)
    center = values - jnp.mean(values, axis=-1, keepdims=True)
    spread = jnp.mean(center * center, axis=-1, keepdims=True)
    return (center * lax.rsqrt(spread + 1e-05)).astype(BF)


def dot_nn(left, right):
    return lax.dot_general(left, right, (((1,), (0,)), ((), ())), preferred_element_type=F32)


def dot_nt(left, right):
    return lax.dot_general(left, right, (((1,), (1,)), ((), ())), preferred_element_type=F32)


def dot_tn(left, right):
    return lax.dot_general(left, right, (((0,), (0,)), ((), ())), preferred_element_type=F32)


def iota(shape, axis):
    return lax.broadcasted_iota(jnp.int32, shape, axis)


FREE = pl.CostEstimate(flops=0, bytes_accessed=0, transcendentals=0)
HBM = pl.BlockSpec(memory_space=pltpu.HBM)


def in_hbm(values):
    return pltpu.with_memory_space_constraint(values, pltpu.HBM)


def fetches(weight_ref, buffer, arrived, width, first):
    return [
        pltpu.make_async_copy(
            weight_ref.at[:, pl.ds(first + place * width, width)],
            buffer.at[place],
            arrived.at[place],
        )
        for place in range(buffer.shape[0])
    ]


def fetch_one(weight_ref, buffer, arrived, width, first, place):
    start = pl.multiple_of(first + place * width, width)
    return pltpu.make_async_copy(
        weight_ref.at[:, pl.ds(start, width)], buffer.at[place], arrived.at[place]
    )


def project_kernel(latent_ref, weight_ref, projected_ref, turned_ref, normed, buffer, arrived):
    step = pl.program_id(0)

    @pl.when(step == 0)
    def _():
        for copy in fetches(weight_ref, buffer, arrived, 512, 0):
            copy.start()
        normed[...] = layer_norm(latent_ref[...])
        turned_ref[...] = normed[...].T

    fetch_one(weight_ref, buffer, arrived, 512, 0, step).wait()
    projected_ref[...] = dot_nn(normed[...], buffer[step]).astype(BF)


def project(latent_own, w_qkv):
    rows, width = latent_own.shape
    return pl.pallas_call(
        project_kernel,
        grid=(6,),
        in_specs=[pl.BlockSpec((rows, width), lambda j: (0, 0)), HBM],
        out_specs=[
            pl.BlockSpec((rows, 512), lambda j: (0, j)),
            pl.BlockSpec((width, rows), lambda j: (0, 0)),
        ],
        out_shape=[
            jax.ShapeDtypeStruct((rows, 3 * width), BF),
            jax.ShapeDtypeStruct((width, rows), BF),
        ],
        scratch_shapes=[
            pltpu.VMEM((rows, width), BF),
            pltpu.VMEM((6, width, 512), BF),
            pltpu.SemaphoreType.DMA((6,)),
        ],
        compiler_params=pltpu.CompilerParams(vmem_limit_bytes=16 * 1024 * 1024),
        cost_estimate=pl.CostEstimate(
            flops=2 * rows * width * width * 4, bytes_accessed=8 << 20, transcendentals=0
        ),
    )(latent_own, in_hbm(w_qkv))


def halo_query_kernel(normed_ref, weight_ref, out_ref, buffer, arrived):
    step = pl.program_id(0)

    @pl.when(step == 0)
    def _():
        for copy in fetches(weight_ref, buffer, arrived, 256, 0):
            copy.start()

    fetch_one(weight_ref, buffer, arrived, 256, 0, step).wait()
    out_ref[...] = dot_nn(normed_ref[...], buffer[step]).astype(BF)


def halo_queries(normed_halo, w_qkv):
    rows, width = normed_halo.shape
    return pl.pallas_call(
        halo_query_kernel,
        grid=(4,),
        in_specs=[pl.BlockSpec((rows, width), lambda j: (0, 0)), HBM],
        out_specs=pl.BlockSpec((rows, 256), lambda j: (0, j)),
        out_shape=jax.ShapeDtypeStruct((rows, width), BF),
        scratch_shapes=[
            pltpu.VMEM((4, width, 256), BF),
            pltpu.SemaphoreType.DMA((4,)),
        ],
        compiler_params=pltpu.CompilerParams(vmem_limit_bytes=12 * 1024 * 1024),
        cost_estimate=FREE,
    )(normed_halo, in_hbm(w_qkv))


def partial_kernel(
    smalls, core_ref, normed_ref, normed_other_ref, piece_ref, other_ref, *refs
):
    small_refs, (out_ref, rows, pieces, others, sums, staged, arrived, left) = (
        refs[:smalls],
        refs[smalls:],
    )
    core = core_ref[0]
    chunks = piece_ref.shape[0] // 512
    sources = [
        (normed_ref.at[:, core], rows.at[0]),
        (normed_other_ref.at[:, core], rows.at[1]),
    ]
    for chunk in range(chunks):
        part = pl.ds(chunk * 512, 512)
        sources.append((piece_ref.at[part], pieces.at[chunk]))
        sources.append((other_ref.at[part], others.at[chunk]))
    for place, small_ref in enumerate(small_refs):
        sources.append((small_ref.at[:, core], sums.at[place]))
    copies = [
        pltpu.make_async_copy(source, target, arrived.at[place])
        for place, (source, target) in enumerate(sources)
    ]
    for copy in copies:
        copy.start()
    copies[0].wait()
    copies[1].wait()
    writes = []
    for chunk in range(chunks):
        copies[2 + 2 * chunk].wait()
        copies[3 + 2 * chunk].wait()
        for top in range(2):
            staged[chunk, top * 256 : (top + 1) * 256] = (
                dot_nt(rows[0, top], pieces[chunk]) + dot_nt(rows[1, top], others[chunk])
            ).astype(BF)
        writes.append(
            pltpu.make_async_copy(
                staged.at[chunk], out_ref.at[:, pl.ds(chunk * 512, 512)], left.at[chunk]
            )
        )
        writes[-1].start()
    if smalls:
        copies[-2].wait()
        copies[-1].wait()
        for top in range(2):
            staged[chunks, top * 256 : (top + 1) * 256, :256] = (
                sums[0, top].astype(F32) + sums[1, top].astype(F32)
            ).astype(BF)
        writes.append(
            pltpu.make_async_copy(
                staged.at[chunks, :, pl.ds(0, 256)],
                out_ref.at[:, pl.ds(chunks * 512, 256)],
                left.at[chunks],
            )
        )
        writes[-1].start()
    for write in writes:
        write.wait()


def partial_sums(core, turned, turned_other, piece, other, smalls=()):
    by_core = lambda values: values.reshape(2, 2, 256, 256)
    anywhere = pl.BlockSpec(memory_space=pl.ANY)
    chunks = piece.shape[0] // 512
    columns = piece.shape[0] + 256 * (len(smalls) // 2)
    return pl.pallas_call(
        functools.partial(partial_kernel, len(smalls)),
        in_specs=[pl.BlockSpec(memory_space=pltpu.SMEM)] + [anywhere] * (4 + len(smalls)),
        out_specs=anywhere,
        out_shape=jax.ShapeDtypeStruct((512, columns), BF),
        scratch_shapes=[
            pltpu.VMEM((2, 2, 256, 256), BF),
            pltpu.VMEM((chunks, 512, 256), BF),
            pltpu.VMEM((chunks, 512, 256), BF),
            pltpu.VMEM((2, 2, 256, 256), BF),
            pltpu.VMEM((chunks + 1, 512, 512), BF),
            pltpu.SemaphoreType.DMA((2 + 2 * chunks + len(smalls),)),
            pltpu.SemaphoreType.DMA((chunks + 1,)),
        ],
        compiler_params=pltpu.CompilerParams(vmem_limit_bytes=14 * 1024 * 1024),
        cost_estimate=FREE,
    )(
        core.astype(jnp.int32).reshape(1),
        by_core(turned),
        by_core(turned_other),
        piece,
        other,
        *(by_core(small) for small in smalls),
    )


def spare_lane(shape):
    lane = iota(shape, len(shape) - 1)
    return lane % HEAD_WIDTH


def key_fill(count_pieces):
    fills = []
    for count, rows in count_pieces:
        spare = spare_lane((rows, PAIR))
        bias = jnp.where(iota((rows, PAIR), 0) < count, 0.0, NEVER)
        fills.append(
            jnp.where(spare < 3, 1.0, jnp.where(spare == 3, bias, 0.0)).astype(BF)
        )
    return jnp.concatenate(fills, axis=0)


def stat_spread(step, offset):
    shape = (128, WIDTH)
    lane = iota(shape, 1)
    head = step * 4 + 2 * (lane // PAIR) + jnp.where(lane % PAIR < HEAD_WIDTH, 1, 0)
    term = lane % HEAD_WIDTH
    chosen = (term < 3) & (iota(shape, 0) == term * 32 + offset + head)
    return jnp.where(chosen, -1.0, 0.0).astype(BF)


def keep_band(window, fill):
    shape = (128, 128)
    apart = iota(shape, 0) - iota(shape, 1)
    first = jnp.where(apart >= 0, window[:128], fill)
    last = jnp.where(apart <= 0, window[-128:], fill)
    return first, window[128:-128], last


def own_kernel(counts_ref, q_ref, k_ref, v_ref, probs, mixed_ref, top_ref, total_ref):
    step = pl.program_id(0)
    fill = key_fill([(counts_ref[1], BLOCK)])
    low = iota((BLOCK, PAIR), 1) < HEAD_WIDTH
    query_fill = (spare_lane((BLOCK, PAIR)) == 3).astype(BF)
    ones = jnp.ones((16, BLOCK), BF)
    scores, turned = [], []
    for pair in range(2):
        columns = slice(pair * PAIR, (pair + 1) * PAIR)
        q_pair = q_ref[:, columns] * jnp.asarray(HEAD_WIDTH ** (-0.5), BF)
        k_pair = k_ref[:, columns]
        turned.append(v_ref[:, columns].T)
        for half in range(2):
            pick = low if half == 0 else ~low
            scores.append(
                dot_nt(jnp.where(pick, k_pair, fill), jnp.where(pick, q_pair, query_fill))
            )
    for slot in range(4):
        top = jnp.max(scores[slot], axis=0, keepdims=True)
        probs[slot] = jnp.exp(scores[slot] - top).astype(BF)
        top_ref[pl.ds(step * 4 + slot, 1), :] = top
    for slot in range(4):
        lanes = slice(slot % 2 * HEAD_WIDTH, (slot % 2 + 1) * HEAD_WIDTH)
        values = jnp.concatenate([turned[slot // 2][lanes], ones], axis=0)
        mixed = dot_nn(values, probs[slot])
        mixed_ref[slot * HEAD_WIDTH : (slot + 1) * HEAD_WIDTH] = mixed[:HEAD_WIDTH]
        total_ref[pl.ds(step * 4 + slot, 1), :] = mixed[HEAD_WIDTH : HEAD_WIDTH + 1]


def own_part(counts, projected):
    part = lambda rows, first: pl.BlockSpec((rows, WIDTH), lambda j: (0, first + j))
    whole = pl.BlockSpec((HEADS, BLOCK), lambda j: (0, 0))
    return pl.pallas_call(
        own_kernel,
        grid=(4,),
        in_specs=[
            pl.BlockSpec(memory_space=pltpu.SMEM),
            part(BLOCK, 0),
            part(BLOCK, 4),
            part(BLOCK, 8),
        ],
        out_specs=[
            pl.BlockSpec((4, BLOCK, BLOCK), lambda j: (j, 0, 0)),
            pl.BlockSpec((WIDTH, BLOCK), lambda j: (j, 0)),
            whole,
            whole,
        ],
        out_shape=[
            jax.ShapeDtypeStruct((HEADS, BLOCK, BLOCK), BF),
            jax.ShapeDtypeStruct((1024, BLOCK), F32),
            jax.ShapeDtypeStruct((HEADS, BLOCK), F32),
            jax.ShapeDtypeStruct((HEADS, BLOCK), F32),
        ],
        compiler_params=pltpu.CompilerParams(vmem_limit_bytes=14 * 1024 * 1024),
        cost_estimate=pl.CostEstimate(
            flops=1 << 30, bytes_accessed=4 << 20, transcendentals=1 << 20
        ),
    )(counts, projected, projected, projected)


def forward_kernel(
    counts_ref,
    left_ref,
    right_ref,
    latent_ref,
    weight_ref,
    q_ref,
    own_mixed_ref,
    own_top_ref,
    own_total_ref,
    w_out_ref,
    readout_ref,
    normed_ref,
    khalo_ref,
    vhalo_ref,
    attended_ref,
    stats_ref,
    hidden_ref,
    forecast_ref,
    probs,
    inverse_ref,
    own_inverse_ref,
    stat_rows,
    buffer,
    arrived,
):
    step = pl.program_id(0)

    @pl.when(step == 0)
    def _():
        copies = fetches(weight_ref, buffer, arrived, WIDTH, 1024)
        for place in (0, 4, 1, 5, 2, 6, 3, 7):
            copies[place].start()
        normed_ref[:WIN] = layer_norm(left_ref[...])
        normed_ref[WIN:] = layer_norm(right_ref[...])

    fetch_one(weight_ref, buffer, arrived, WIDTH, 1024, step).wait()
    fetch_one(weight_ref, buffer, arrived, WIDTH, 1024, step + 4).wait()
    khalo_ref[...] = dot_nn(normed_ref[...], buffer[step]).astype(BF)
    vhalo_ref[...] = dot_nn(normed_ref[...], buffer[step + 4]).astype(BF)
    fill = key_fill([(counts_ref[0], WIN), (counts_ref[2], WIN)])
    low_q = iota((BLOCK, PAIR), 1) < HEAD_WIDTH
    low_k = iota(fill.shape, 1) < HEAD_WIDTH
    query_fill = (spare_lane((BLOCK, PAIR)) == 3).astype(BF)
    scores, turned = [], []
    for pair in range(2):
        columns = slice(pair * PAIR, (pair + 1) * PAIR)
        q_pair = q_ref[:, columns] * jnp.asarray(HEAD_WIDTH ** (-0.5), BF)
        k_pair = khalo_ref[:, columns]
        turned.append(vhalo_ref[:, columns].T)
        for half in range(2):
            if half == 0:
                q_head = jnp.where(low_q, q_pair, query_fill)
                k_head = jnp.where(low_k, k_pair, fill)
            else:
                q_head = jnp.where(low_q, query_fill, q_pair)
                k_head = jnp.where(low_k, fill, k_pair)
            scores.append(dot_nt(k_head, q_head))
    tops = []
    for slot in range(4):
        levels = []
        for tile in range(2):
            rows = slice(tile * 128, tile * 128 + 384)
            lanes = slice(tile * 128, tile * 128 + 128)
            first, middle, last = keep_band(scores[slot][rows, lanes], NEVER)
            top = jnp.maximum(
                jnp.max(middle, axis=0, keepdims=True),
                jnp.max(jnp.maximum(first, last), axis=0, keepdims=True),
            )
            top = jnp.maximum(top, own_top_ref[pl.ds(step * 4 + slot, 1), :][:, lanes])
            start = tile * 128
            probs[slot, start : start + 128, lanes] = jnp.exp(first - top).astype(BF)
            probs[slot, start + 128 : start + 256, lanes] = jnp.exp(middle - top).astype(BF)
            probs[slot, start + 256 : start + 384, lanes] = jnp.exp(last - top).astype(BF)
            levels.append(top)
        probs[slot, :128, 128:] = jnp.zeros((128, 128), BF)
        probs[slot, 384:, :128] = jnp.zeros((128, 128), BF)
        tops.append(jnp.concatenate(levels, axis=1))
    ones = jnp.ones((16, fill.shape[0]), BF)
    for pair in range(2):
        halves = []
        for half in range(2):
            slot = pair * 2 + half
            lanes = slice(half * HEAD_WIDTH, (half + 1) * HEAD_WIDTH)
            values = jnp.concatenate([turned[pair][lanes], ones], axis=0)
            mixed = dot_nn(values, probs[slot])
            head = step * 4 + slot
            fade = jnp.exp(own_top_ref[pl.ds(head, 1), :] - tops[slot])
            total = mixed[HEAD_WIDTH : HEAD_WIDTH + 1]
            total += own_total_ref[pl.ds(head, 1), :] * fade
            inverse = 1.0 / total
            own_inverse = fade * inverse
            own_mixed = own_mixed_ref[slot * HEAD_WIDTH : (slot + 1) * HEAD_WIDTH]
            halves.append(mixed[:HEAD_WIDTH] * inverse + own_mixed * own_inverse)
            own_inverse_ref[pl.ds(head, 1), :] = own_inverse
            inverse_ref[pl.ds(head, 1), :] = inverse
            stat_rows[pl.ds(head, 1), :] = tops[slot] + jnp.log(total)
        start = pl.multiple_of(step * WIDTH + pair * PAIR, PAIR)
        attended_ref[:, pl.ds(start, PAIR)] = jnp.concatenate(halves, axis=0).T

    @pl.when(step == 3)
    def _():
        mixed = dot_nn(attended_ref[...].astype(BF), w_out_ref[...])
        hidden = (latent_ref[...].astype(F32) + mixed).astype(BF)
        hidden_ref[...] = hidden
        forecast_ref[...] = dot_nn(hidden, readout_ref[...])
        stat_rows[HEADS:] = jnp.zeros((128 - HEADS, BLOCK), F32)
        stats_ref[...] = stat_rows[...].T


def forward(counts, left, right, latent_own, w_qkv, projected, own, w_out, readout_weight):
    whole = lambda *shape: pl.BlockSpec(shape, lambda j: (0, 0))
    part = lambda rows, first: pl.BlockSpec((rows, WIDTH), lambda j: (0, first + j))
    window = 2 * WIN + BLOCK
    return pl.pallas_call(
        forward_kernel,
        grid=(4,),
        in_specs=[
            pl.BlockSpec(memory_space=pltpu.SMEM),
            whole(WIN, 1024),
            whole(WIN, 1024),
            whole(BLOCK, 1024),
            HBM,
            part(BLOCK, 0),
            pl.BlockSpec((WIDTH, BLOCK), lambda j: (j, 0)),
            whole(HEADS, BLOCK),
            whole(HEADS, BLOCK),
            whole(1024, 1024),
            whole(1024, 128),
        ],
        out_specs=[
            whole(2 * WIN, 1024),
            part(2 * WIN, 0),
            part(2 * WIN, 0),
            whole(BLOCK, 1024),
            whole(BLOCK, 128),
            whole(BLOCK, 1024),
            whole(BLOCK, 128),
            pl.BlockSpec((4, 2 * WIN, BLOCK), lambda j: (j, 0, 0)),
            whole(HEADS, BLOCK),
            whole(HEADS, BLOCK),
        ],
        out_shape=[
            jax.ShapeDtypeStruct((2 * WIN, 1024), BF),
            jax.ShapeDtypeStruct((2 * WIN, 1024), BF),
            jax.ShapeDtypeStruct((2 * WIN, 1024), BF),
            jax.ShapeDtypeStruct((BLOCK, 1024), F32),
            jax.ShapeDtypeStruct((BLOCK, 128), F32),
            jax.ShapeDtypeStruct((BLOCK, 1024), BF),
            jax.ShapeDtypeStruct((BLOCK, 128), F32),
            jax.ShapeDtypeStruct((HEADS, 2 * WIN, BLOCK), BF),
            jax.ShapeDtypeStruct((HEADS, BLOCK), F32),
            jax.ShapeDtypeStruct((HEADS, BLOCK), F32),
        ],
        scratch_shapes=[
            pltpu.VMEM((128, BLOCK), F32),
            pltpu.VMEM((8, 1024, WIDTH), BF),
            pltpu.SemaphoreType.DMA((8,)),
        ],
        compiler_params=pltpu.CompilerParams(vmem_limit_bytes=30 * 1024 * 1024),
        cost_estimate=pl.CostEstimate(
            flops=6 << 30, bytes_accessed=12 << 20, transcendentals=3 << 20
        ),
    )(
        counts,
        left,
        right,
        latent_own,
        in_hbm(w_qkv),
        projected,
        *own,
        w_out,
        readout_weight,
    )


def crps_kernel(counts_ref, own_ref, near_ref, others_ref, target_ref, crps_ref):
    members = 4
    fair_eps = (1.0 - alpha_fair) / members
    coefficient = (1.0 - fair_eps) / (members * (members - 1))
    valid = (iota((BLOCK, 1), 0) < counts_ref[1]).astype(F32)
    forecasts = [own_ref[...], near_ref[...], others_ref[0], others_ref[1]]
    target = target_ref[...]
    error = jnp.zeros_like(target)
    for forecast in forecasts:
        error += smooth_abs(forecast - target)
    spread = jnp.full_like(target, members * smooth_width**0.5)
    for first in range(members):
        for second in range(first + 1, members):
            spread += 2.0 * smooth_abs(forecasts[first] - forecasts[second])
    crps_ref[...] = valid * (error / members - 0.5 * coefficient * spread)


def crps_of(counts, own, near, others, target):
    vmem = pl.BlockSpec(memory_space=pltpu.VMEM)
    return pl.pallas_call(
        crps_kernel,
        in_specs=[pl.BlockSpec(memory_space=pltpu.SMEM)] + [vmem] * 4,
        out_specs=vmem,
        out_shape=jax.ShapeDtypeStruct((BLOCK, 128), F32),
        compiler_params=pltpu.CompilerParams(vmem_limit_bytes=8 * 1024 * 1024),
        cost_estimate=FREE,
    )(counts, own, near, others, in_hbm(target))


def score_kernel(
    counts_ref,
    own_ref,
    near_ref,
    others_ref,
    target_ref,
    attended_ref,
    hidden_ref,
    stats_ref,
    w_out_ref,
    readout_ref,
    packed_ref,
    sent_ref,
    grad_ref,
    small_ref,
):
    members = 4
    fair_eps = (1.0 - alpha_fair) / members
    coefficient = (1.0 - fair_eps) / (members * (members - 1))
    valid = (iota((BLOCK, 1), 0) < counts_ref[1]).astype(F32)
    own = own_ref[...]
    target = target_ref[...]
    pull = jnp.zeros_like(target)
    for other in (near_ref[...], others_ref[0], others_ref[1]):
        pull += smooth_sign(own - other)
    slope = (
        valid / 128 * (smooth_sign(own - target) / members - coefficient * pull)
    ).astype(BF)
    dhidden = dot_nt(slope, readout_ref[...]).astype(BF)
    dattended = dot_nt(dhidden, w_out_ref[...]).astype(BF)
    grad_ref[...] = dattended
    attended = attended_ref[...]
    product = dattended.astype(F32) * attended
    high = product.astype(BF)
    low = (product - high.astype(F32)).astype(BF)
    pick = (iota((1024, 128), 0) // HEAD_WIDTH + HEADS == iota((1024, 128), 1)).astype(BF)
    stats = stats_ref[...] + dot_nn(high, pick) + dot_nn(low, pick)
    first = stats.astype(BF)
    rest = stats - first.astype(F32)
    second = rest.astype(BF)
    third = (rest - second.astype(F32)).astype(BF)
    terms = jnp.zeros((BLOCK, 128), F32)
    for place, term in enumerate((first, second, third)):
        shift = (iota((128, 128), 0) + 32 * place == iota((128, 128), 1)) & (
            iota((128, 128), 0) < 32
        )
        terms += dot_nn(term, shift.astype(BF))
    packed_ref[:, :128] = slope
    packed_ref[:, 128:] = terms.astype(BF)
    sent_ref[...] = packed_ref[...]
    small_ref[:, :128] = dot_tn(attended.astype(BF), slope).astype(BF)
    small_ref[:, 128:] = dot_tn(hidden_ref[...], slope).astype(BF)


def score(counts, own, near, others, target, attended, hidden, stats, w_out, readout_weight):
    vmem = pl.BlockSpec(memory_space=pltpu.VMEM)
    return pl.pallas_call(
        score_kernel,
        in_specs=[pl.BlockSpec(memory_space=pltpu.SMEM)] + [vmem] * 9,
        out_specs=[vmem] * 4,
        out_shape=[
            jax.ShapeDtypeStruct((BLOCK, 256), BF),
            pltpu.HBM((BLOCK, 256), BF),
            jax.ShapeDtypeStruct((BLOCK, 1024), BF),
            jax.ShapeDtypeStruct((1024, 256), BF),
        ],
        compiler_params=pltpu.CompilerParams(vmem_limit_bytes=12 * 1024 * 1024),
    )(counts, own, near, others, target, attended, hidden, stats, w_out, readout_weight)


def query_kernel(
    k_ref,
    v_ref,
    khalo_ref,
    vhalo_ref,
    grad_ref,
    packed_ref,
    probs_ref,
    own_probs_ref,
    inverse_ref,
    own_inverse_ref,
    dq_ref,
    dscores,
    own_dscores,
):
    step = pl.program_id(0)
    low_q = iota((BLOCK, PAIR), 1) < HEAD_WIDTH
    low_k = iota((2 * WIN, PAIR), 1) < HEAD_WIDTH
    own_fill = (spare_lane((BLOCK, PAIR)) < 3).astype(BF)
    halo_fill = (spare_lane((2 * WIN, PAIR)) < 3).astype(BF)
    g_fill = dot_nn(packed_ref[:, 128:], stat_spread(step, HEADS)).astype(BF)
    turned = []
    for pair in range(2):
        columns = slice(pair * PAIR, (pair + 1) * PAIR)
        g_pair = grad_ref[:, columns]
        own_turned = k_ref[:, columns].T
        halo_turned = khalo_ref[:, columns].T
        for half in range(2):
            slot = pair * 2 + half
            pick_q = low_q if half == 0 else ~low_q
            pick_k = low_k if half == 0 else ~low_k
            g_head = jnp.where(pick_q, g_pair, g_fill[:, columns])
            own_change = dot_nt(jnp.where(pick_q, v_ref[:, columns], own_fill), g_head)
            own_dscores[slot] = (own_probs_ref[step * 4 + slot].astype(F32) * own_change).astype(BF)
            change = dot_nt(jnp.where(pick_k, vhalo_ref[:, columns], halo_fill), g_head)
            dscores[slot] = (probs_ref[step * 4 + slot].astype(F32) * change).astype(BF)
            lanes = slice(half * HEAD_WIDTH, (half + 1) * HEAD_WIDTH)
            turned.append((own_turned[lanes], halo_turned[lanes]))
    for slot in range(4):
        row = pl.ds(step * 4 + slot, 1)
        dquery = dot_nn(turned[slot][0], own_dscores[slot]) * own_inverse_ref[row, :]
        dquery += dot_nn(turned[slot][1], dscores[slot]) * inverse_ref[row, :]
        dq_ref[slot * HEAD_WIDTH : (slot + 1) * HEAD_WIDTH] = (
            dquery * HEAD_WIDTH ** (-0.5)
        ).astype(BF)


def query_grads(projected, khalo, vhalo, grad, packed, probs, own_probs, inverse, own_inverse):
    part = lambda rows, first: pl.BlockSpec((rows, WIDTH), lambda j: (0, first + j))
    whole = pl.BlockSpec((HEADS, BLOCK), lambda j: (0, 0))
    return pl.pallas_call(
        query_kernel,
        grid=(4,),
        in_specs=[
            part(BLOCK, 4),
            part(BLOCK, 8),
            part(2 * WIN, 0),
            part(2 * WIN, 0),
            part(BLOCK, 0),
            pl.BlockSpec((BLOCK, 256), lambda j: (0, 0)),
            pl.BlockSpec(memory_space=pltpu.VMEM),
            pl.BlockSpec(memory_space=pltpu.VMEM),
            whole,
            whole,
        ],
        out_specs=pl.BlockSpec((WIDTH, BLOCK), lambda j: (j, 0)),
        out_shape=jax.ShapeDtypeStruct((1024, BLOCK), BF),
        scratch_shapes=[
            pltpu.VMEM((4, 2 * WIN, BLOCK), BF),
            pltpu.VMEM((4, BLOCK, BLOCK), BF),
        ],
        compiler_params=pltpu.CompilerParams(vmem_limit_bytes=16 * 1024 * 1024),
        cost_estimate=pl.CostEstimate(
            flops=6 << 30, bytes_accessed=5 << 20, transcendentals=3 << 20
        ),
    )(
        projected,
        projected,
        khalo,
        vhalo,
        grad,
        packed,
        probs,
        own_probs,
        inverse,
        own_inverse,
    )


def key_kernel(
    counts_ref,
    q_ref,
    k_ref,
    v_ref,
    qhalo_ref,
    grad_ref,
    own_ref,
    left_ref,
    right_ref,
    w_out_ref,
    readout_ref,
    out_ref,
    probs,
    dscores,
    dhidden,
):
    step = pl.program_id(0)

    @pl.when(step == 0)
    def _():
        for slot in range(4):
            for held in (probs, dscores):
                held[slot, :128, 128:] = jnp.zeros((128, 128), BF)
                held[slot, 640:, :128] = jnp.zeros((128, 128), BF)
        dhidden[:WIN] = dot_nt(left_ref[:, :128], readout_ref[...]).astype(BF)
        dhidden[WIN:] = dot_nt(right_ref[:, :128], readout_ref[...]).astype(BF)

    ghalo = dot_nt(dhidden[...], w_out_ref[...]).astype(BF)
    terms = jnp.concatenate(
        [left_ref[:, 128:], own_ref[:, 128:], right_ref[:, 128:]], axis=0
    )
    window = terms.shape[0]
    fill = key_fill([(counts_ref[1], BLOCK)])
    value_fill = (spare_lane(fill.shape) < 3).astype(BF)
    low_q = iota((window, PAIR), 1) < HEAD_WIDTH
    low_k = iota(fill.shape, 1) < HEAD_WIDTH
    ones = (spare_lane((window, WIDTH)) == 3).astype(F32)
    q_fill = (dot_nn(terms, stat_spread(step, 0)) + ones).astype(BF)
    g_fill = dot_nn(terms, stat_spread(step, HEADS)).astype(BF)
    turned = []
    for pair in range(2):
        columns = slice(pair * PAIR, (pair + 1) * PAIR)
        q_pair = jnp.concatenate(
            [qhalo_ref[:WIN, columns], q_ref[:, columns], qhalo_ref[WIN:, columns]], axis=0
        ) * jnp.asarray(HEAD_WIDTH ** (-0.5), BF)
        g_pair = jnp.concatenate(
            [ghalo[:WIN, columns], grad_ref[:, columns], ghalo[WIN:, columns]], axis=0
        )
        k_pair = k_ref[:, columns]
        v_pair = v_ref[:, columns]
        q_turned = q_pair.T
        g_turned = g_pair.T
        for half in range(2):
            slot = pair * 2 + half
            pick_q = low_q if half == 0 else ~low_q
            pick_k = low_k if half == 0 else ~low_k
            q_head = jnp.where(pick_q, q_pair, q_fill[:, columns])
            g_head = jnp.where(pick_q, g_pair, g_fill[:, columns])
            k_head = jnp.where(pick_k, k_pair, fill)
            v_head = jnp.where(pick_k, v_pair, value_fill)
            scores = dot_nt(q_head, k_head)
            change = dot_nt(g_head, v_head)
            for tile in range(2):
                rows = slice(tile * 128, tile * 128 + 640)
                lanes = slice(tile * 128, tile * 128 + 128)
                weight = keep_band(jnp.exp(scores[rows, lanes]), 0.0)
                moved = change[rows, lanes]
                start = tile * 128
                for piece, (low, high) in zip(weight, ((0, 128), (128, 512), (512, 640))):
                    place = slice(start + low, start + high)
                    probs[slot, place, lanes] = piece.astype(BF)
                    dscores[slot, place, lanes] = (piece * moved[low:high]).astype(BF)
            lanes = slice(half * HEAD_WIDTH, (half + 1) * HEAD_WIDTH)
            turned.append((q_turned[lanes], g_turned[lanes]))
    for slot in range(4):
        place = slice(slot * HEAD_WIDTH, (slot + 1) * HEAD_WIDTH)
        out_ref[0, place] = dot_nn(turned[slot][0], dscores[slot]).astype(BF)
        out_ref[1, place] = dot_nn(turned[slot][1], probs[slot]).astype(BF)


def key_grads(counts, projected, qhalo, grad, own, left, right, w_out, readout_weight):
    part = lambda rows, first: pl.BlockSpec((rows, WIDTH), lambda j: (0, first + j))
    whole = lambda *shape: pl.BlockSpec(shape, lambda j: (0, 0))
    window = 2 * WIN + BLOCK
    return pl.pallas_call(
        key_kernel,
        grid=(4,),
        in_specs=[
            pl.BlockSpec(memory_space=pltpu.SMEM),
            part(BLOCK, 0),
            part(BLOCK, 4),
            part(BLOCK, 8),
            part(2 * WIN, 0),
            part(BLOCK, 0),
            whole(BLOCK, 256),
            whole(BLOCK, 256),
            whole(BLOCK, 256),
            pl.BlockSpec((WIDTH, 1024), lambda j: (j, 0)),
            whole(1024, 128),
        ],
        out_specs=pl.BlockSpec((2, WIDTH, BLOCK), lambda j: (0, j, 0)),
        out_shape=jax.ShapeDtypeStruct((2, 1024, BLOCK), BF),
        scratch_shapes=[
            pltpu.VMEM((4, window, BLOCK), BF),
            pltpu.VMEM((4, window, BLOCK), BF),
            pltpu.VMEM((2 * WIN, 1024), BF),
        ],
        compiler_params=pltpu.CompilerParams(vmem_limit_bytes=18 * 1024 * 1024),
        cost_estimate=FREE,
    )(
        counts,
        projected,
        projected,
        projected,
        qhalo,
        in_hbm(grad),
        in_hbm(own),
        in_hbm(left),
        in_hbm(right),
        in_hbm(w_out),
        readout_weight,
    )


AXES = ("x_hi", "core", "y", "x_lo", "z")
MEMBER = ("x_hi", "core")
CELLS = ("y", "x_lo", "z")
CHIPS = ("x_hi", "y", "x_lo", "z")
SWAP = [(0, 1), (1, 0)]


def swap_core(values):
    return lax.ppermute(values, "core", SWAP)


def scatter(partial):
    columns = partial.shape[1]
    return lax.all_to_all(partial.reshape(64, 8, columns), CHIPS, split_axis=0, concat_axis=0)


def add_up(pieces):
    return jnp.sum(pieces.astype(F32), axis=0)


def per_device(latent, counts, w_qkv, w_out, readout_weight, target):
    latent_own = latent[0]
    cell_count = 32
    cell_index = lax.axis_index(CELLS)
    member_index = lax.axis_index(MEMBER)
    core = lax.axis_index("core")
    up = [(i, i + 1) for i in range(cell_count - 1)]
    down = [(i + 1, i) for i in range(cell_count - 1)]
    from_left = lax.ppermute(latent_own, CELLS, up)
    from_right = lax.ppermute(latent_own, CELLS, down)

    own_count = counts[cell_index]
    left_count = jnp.where(cell_index > 0, counts[jnp.maximum(cell_index - 1, 0)], 0)
    right_count = jnp.where(
        cell_index < cell_count - 1, counts[jnp.minimum(cell_index + 1, cell_count - 1)], 0
    )
    scalars = jnp.stack([left_count, own_count, right_count])

    projected, turned = project(latent_own, w_qkv)
    turned_other = swap_core(turned)
    own_probs, *own = own_part(scalars, projected)
    (
        normed_halo,
        khalo,
        vhalo,
        attended,
        stats,
        hidden,
        forecast,
        probs,
        inverse,
        own_inverse,
    ) = forward(
        scalars, from_left, from_right, latent_own, w_qkv, projected, own, w_out, readout_weight
    )
    near = lax.ppermute(forecast, "x_hi", SWAP)
    qhalo = halo_queries(normed_halo, w_qkv)
    near, qhalo = lax.optimization_barrier((near, qhalo))
    others = swap_core(jnp.stack([forecast, near]))
    packed, sent, grad, small = score(
        scalars, forecast, near, others, target, attended, hidden, stats, w_out, readout_weight
    )
    packed_left = lax.ppermute(sent, CELLS, up)
    packed_right = lax.ppermute(sent, CELLS, down)

    dquery = query_grads(
        projected, khalo, vhalo, grad, packed, probs, own_probs, inverse, own_inverse
    )
    dquery, packed_left, packed_right = lax.optimization_barrier(
        (dquery, packed_left, packed_right)
    )

    first_part = partial_sums(
        core, turned, turned_other, dquery, swap_core(dquery), (small, swap_core(small))
    )
    first_part, scalars = lax.optimization_barrier((first_part, scalars))
    first = scatter(first_part)
    pairs = key_grads(
        scalars,
        projected,
        qhalo,
        grad,
        sent,
        packed_left,
        packed_right,
        w_out,
        readout_weight,
    )
    pairs = pairs.reshape(2048, BLOCK)
    second_part = partial_sums(core, turned, turned_other, pairs, swap_core(pairs))
    second_part, first = lax.optimization_barrier((second_part, first))
    second_part, late_near = lax.optimization_barrier((second_part, near))
    second = add_up(scatter(second_part))
    crps_whole = crps_of(scalars, forecast, late_near, others, target)
    crps = lax.dynamic_slice_in_dim(crps_whole, member_index * 32, 32, 1)
    first = add_up(first)
    grad_out = lax.dot_general(
        first[:, 1024:1152],
        readout_weight.astype(F32),
        (((1,), (1,)), ((), ())),
        precision=lax.Precision.HIGHEST,
        preferred_element_type=F32,
    )
    grads = jnp.concatenate([first[:, :1024], second, grad_out, first[:, 1152:]], axis=1)
    return (crps, grads)


def solution(mesh):
    fine = jax.sharding.Mesh(mesh.devices.reshape(2, 2, 4, 2, 4), AXES)
    placed = (P(MEMBER, CELLS, None), P(), P(), P(), P(), P(CELLS, None))
    return jax.shard_map(
        per_device,
        mesh=fine,
        in_specs=placed,
        out_specs=(P(CELLS, MEMBER), P(MEMBER + CELLS, None)),
        check_vma=False,
    )
```
